128 devices in a mesh: seq: 64 (over z_hi, y, x, core), ch: 2 (over z_lo).
Axes of the slice: x: 4, y: 4, z: 4 (z_hi: 2, z_lo: 2; z = z_hi * 2 + z_lo), core: 2. Of those that a mesh axis runs over, the one named last changes fastest.
Arguments:
- tokens: bfloat16 [512, 64, 4096], P(None, 'seq'), may hold values from -6 to 6
- in_weight: bfloat16 [4096, 3, 2048], P('seq', None, 'ch'), may hold values from -0.09375 to 0.09375
- filter_spectrum: float32 [2, 1024, 64, 8], P(None, 'seq', None, 'ch'), may hold values from -6 to 6
- skip_bias: float32 [2048], P('ch'), may hold values from -1 to 1
- out_weight: bfloat16 [2048, 4096], P('ch'), may hold values from -0.125 to 0.125
Outputs:
- mixed: bfloat16 [512, 64, 4096], P('ch', 'seq')
The draws below stay inside these ranges and needn't reach their ends.
All inputs are finite; a program needn't handle non-finite values.
Results may differ from the reference program's by a relative error of at most 0.018.
Values may be sent and summed in bfloat16 or wider, within the bound.
No kernel may reach another device: no remote copies, remote signals or barrier semaphores. Data moves between devices by JAX's collectives and lax.ppermute only.
A program may use at most 128 MiB of HBM per device.

```python
import math
import jax
import jax.numpy as jnp
from jax import lax

D = 4096
GROUP = 256
ROWS = 512
COLS = 64
C = 2048
G = 8
POINTS = 1024
PADDED = 65536


def level_of(stream_key, dims, shards, least, largest):
    factor_of = 1.0
    for position, parts in shards:
        draws = jax.random.uniform(jax.random.fold_in(jax.random.fold_in(stream_key, 6), position), (parts,), jnp.float32, least / len(shards), largest / len(shards))
        factor_of = factor_of * jnp.repeat(jnp.exp(draws), dims[position] // parts).reshape((-1,) + (1,) * (len(dims) - 1 - position))
    return factor_of


def scatter_about(own_key, shape, scale, most, cuts=(), kind=jnp.bfloat16):
    level = level_of(own_key, shape, cuts, -0.22, 0.18) if cuts else 1.0
    result = jax.random.normal(own_key, shape, jnp.float32) * scale * level
    return jnp.minimum(jnp.maximum(result, -most), most).astype(kind)


def setup_inputs(seed: int = 0) -> dict:
    streams_of = jax.random.split(jax.random.key(seed), 6)
    return {
        "tokens": scatter_about(streams_of[0], (ROWS, COLS, D), 1.0, 6.0, ((1, 64),)),
        "in_weight": scatter_about(streams_of[1], (D, 3, C), D ** -0.5, 0.09375, ((0, 64), (2, 2))),
        "filter_spectrum": scatter_about(streams_of[2], (2, POINTS, COLS, G), 1.0, 6.0, ((1, 64), (3, 2)), jnp.float32),
        "skip_bias": jnp.clip(jax.random.uniform(streams_of[3], (C,), jnp.float32, -1.0, 1.0) * level_of(streams_of[3], (C,), ((0, 2),), -0.4, 0.0), -1.0, 1.0),
        "out_weight": scatter_about(streams_of[4], (C, D), C ** -0.5, 0.125, ((0, 2),)),
    }


def rounded(value):
    return lax.optimization_barrier(value.astype(jnp.bfloat16)).astype(jnp.float32)


def reference(tokens, in_weight, filter_spectrum, skip_bias, out_weight):
    flat = tokens.reshape(ROWS * COLS, D)
    gate = jnp.dot(flat, in_weight[:, 0, :], preferred_element_type=jnp.float32).astype(jnp.bfloat16)
    key = jnp.dot(flat, in_weight[:, 1, :], preferred_element_type=jnp.float32).astype(jnp.bfloat16)
    value = jnp.dot(flat, in_weight[:, 2, :], preferred_element_type=jnp.float32).astype(jnp.bfloat16)
    source = (key.astype(jnp.float32) * value.astype(jnp.float32)).reshape(ROWS, COLS, C)
    freq = jnp.arange(POINTS, dtype=jnp.int32)[:, None]
    column = jnp.arange(COLS, dtype=jnp.int32)[None, :]
    phase = ((freq * column) % PADDED).astype(jnp.float32) * (2.0 * math.pi / PADDED)
    cosine = jnp.cos(phase)[:, :, None]
    sine = jnp.sin(phase)[:, :, None]
    grouped = jnp.transpose(source.reshape(ROWS, COLS, G, GROUP), (2, 0, 1, 3))
    spectra = jnp.transpose(filter_spectrum, (3, 0, 1, 2))

    def one_group(pair):
        part, filt = pair
        rowwise = jnp.fft.fft(part, n=POINTS, axis=0)
        real_part = jnp.real(rowwise)
        imag_part = jnp.imag(rowwise)
        turned_re = rounded(real_part * cosine + imag_part * sine)
        turned_im = rounded(imag_part * cosine - real_part * sine)
        spectrum = jnp.fft.fft(turned_re + 1j * turned_im, axis=1)
        filtered = spectrum * (filt[0] + 1j * filt[1])[:, :, None]
        back = jnp.fft.ifft(filtered, axis=1) * COLS
        back_re = jnp.real(back)
        back_im = jnp.imag(back)
        returned_re = rounded(back_re * cosine - back_im * sine)
        returned_im = rounded(back_im * cosine + back_re * sine)
        whole = jnp.fft.ifft(returned_re + 1j * returned_im, axis=0)
        return jnp.real(whole)[:ROWS] * (POINTS / PADDED)

    conv = lax.map(one_group, (grouped, spectra))
    conv = jnp.transpose(conv, (1, 2, 0, 3)).reshape(ROWS, COLS, C)
    gated = (gate.reshape(ROWS, COLS, C).astype(jnp.float32) * (conv + skip_bias * source)).astype(jnp.bfloat16)
    mixed = jnp.dot(gated.reshape(ROWS * COLS, C), out_weight, preferred_element_type=jnp.float32)
    return mixed.astype(jnp.bfloat16).reshape(ROWS, COLS, D)
```

```python
import functools
import math

import jax
import jax.numpy as jnp
import ml_dtypes
import numpy as np
from jax import lax
from jax.experimental import pallas as pl
from jax.experimental.pallas import tpu as pltpu
from jax.sharding import PartitionSpec as P

BF16 = jnp.bfloat16
F32 = jnp.float32
SEQ = 64
CHIPS = 32
SAME_CORE = [[2 * p + j for p in range(CHIPS)] for j in range(2)]


def coords(s):
    return s // 32, (s // 8) % 4, (s // 2) % 4, s % 2


def index_of(z, y, x, c):
    return ((z * 4 + y) * 4 + x) * 2 + c


def send(value, dz=0, dy=0, dx=0, dc=0):
    perm = []
    for s in range(SEQ):
        z, y, x, c = coords(s)
        perm.append((s, index_of((z + dz) % 2, (y + dy) % 4, (x + dx) % 4, c ^ dc)))
    return lax.ppermute(value, "seq", perm)


def split_np(table):
    upper = table.astype(np.float32).astype(ml_dtypes.bfloat16)
    lower = (table - upper.astype(np.float64)).astype(np.float32).astype(ml_dtypes.bfloat16)
    return upper, lower


def split_table(table):
    upper = table.astype(BF16)
    lower = (table - upper.astype(F32)).astype(BF16)
    return upper, lower


def row_tables(rows, padded):
    points = 2 * rows
    a = np.arange(rows)
    k = np.arange(rows)
    phase = 2.0 * np.pi * ((a[:, None] * k[None, :]) % points) / points
    re, im = np.cos(phase), -np.sin(phase)
    im[:, 0] = np.where(a % 2 == 0, 1.0, -1.0)
    forward = np.concatenate([re, im], axis=1)
    scale = np.full((rows,), 2.0)
    scale[0] = 1.0
    inverse = np.concatenate([re * scale, im * scale], axis=1).T / padded
    return forward, inverse


def reorder_kernel(order_ref, a0, a1, b0, b1, out_a, out_b):
    rows = a0.shape[0]
    out_a[:rows, :] = a0[...]
    out_a[rows:, :] = a1[...]
    out_b[:rows, :] = b0[...]
    out_b[rows:, :] = b1[...]


def reorder(order, mine, other):
    rows, width = mine.shape
    blocks = width // 128
    return pl.pallas_call(
        reorder_kernel,
        grid_spec=pltpu.PrefetchScalarGridSpec(
            num_scalar_prefetch=1,
            grid=(blocks,),
            in_specs=[
                pl.BlockSpec((rows, 128), lambda i, o: (0, o[0, i])),
                pl.BlockSpec((rows, 128), lambda i, o: (0, o[0, i])),
                pl.BlockSpec((rows, 128), lambda i, o: (0, o[1, i])),
                pl.BlockSpec((rows, 128), lambda i, o: (0, o[1, i])),
            ],
            out_specs=[
                pl.BlockSpec((2 * rows, 128), lambda i, o: (0, i)),
                pl.BlockSpec((2 * rows, 128), lambda i, o: (0, i)),
            ],
        ),
        out_shape=[jax.ShapeDtypeStruct((2 * rows, width), BF16)] * 2,
        cost_estimate=pl.CostEstimate(flops=0, bytes_accessed=8 * rows * width * 2, transcendentals=0),
        name="reorder_tokens",
    )(order, mine, other, mine, other)


def conv_kernel(x_ref, fwd_ref, inv_ref, tw_ref, a_ref, ai_ref, m_ref, f_ref, y_ref, r_ref, q_ref):
    chips, chans, both = x_ref.shape
    rows = both // 2
    blocks = rows // 128
    for col in range(2):
        x = x_ref[:, :, col * rows : (col + 1) * rows].reshape(chips * chans, rows)
        r = jnp.dot(x, fwd_ref[0], preferred_element_type=F32)
        r += jnp.dot(x, fwd_ref[1], preferred_element_type=F32)
        r = r.reshape(chips, chans, 2 * rows)
        tw = tw_ref[col * chips : (col + 1) * chips, :]
        cos = tw[:, None, :rows]
        sin = tw[:, None, rows:]
        re, im = r[:, :, :rows], r[:, :, rows:]
        turned_re = (re * cos + im * sin).reshape(chips * chans, rows)
        turned_im = (im * cos - re * sin).reshape(chips * chans, rows)
        for k in range(blocks):
            r_ref[col, k] = turned_re[:, k * 128 : (k + 1) * 128]
            r_ref[col, blocks + k] = turned_im[:, k * 128 : (k + 1) * 128]
    half = 2 * chips
    lane = lax.broadcasted_iota(jnp.int32, (2 * half, 128), 1)

    def channel(c, carry):
        pick = pl.ds(c, chips, stride=chans)
        parts = [
            jnp.concatenate([r_ref[col, part * blocks + k, pick, :] for k in range(blocks)], axis=1)
            for part in range(2)
            for col in range(2)
        ]
        turned = jnp.concatenate(parts, axis=0).astype(BF16)
        s = jnp.dot(a_ref[...], turned, preferred_element_type=F32)
        s = s[: 2 * half] + s[2 * half :]
        s_re, s_im = s[:half], s[half:]
        f_re, f_im = f_ref[:, :rows], f_ref[:, rows:]
        filtered = jnp.concatenate(
            [s_re * f_re - s_im * f_im, s_re * f_im + s_im * f_re], axis=0
        ).astype(BF16)
        back = jnp.dot(ai_ref[...], filtered, preferred_element_type=F32)
        back = back[: 2 * half] + back[2 * half :]
        edge = jnp.dot(m_ref[...], turned[:, :128], preferred_element_type=F32)
        edge = edge[: 2 * half] + edge[2 * half :]
        head = jnp.where(lane == 0, edge, back[:, :128])
        back = jnp.concatenate([head, back[:, 128:]], axis=1)
        b_re, b_im = back[:half], back[half:]
        cos, sin = tw_ref[:, :rows], tw_ref[:, rows:]
        out_re = b_re * cos - b_im * sin
        out_im = b_im * cos + b_re * sin
        for col in range(2):
            part = slice(col * chips, (col + 1) * chips)
            for k in range(blocks):
                q_ref[col, k, pick, :] = out_re[part, k * 128 : (k + 1) * 128]
                q_ref[col, blocks + k, pick, :] = out_im[part, k * 128 : (k + 1) * 128]
        return carry

    lax.fori_loop(0, chans, channel, 0)
    for col in range(2):
        q = jnp.concatenate([q_ref[col, k].astype(BF16) for k in range(2 * blocks)], axis=1)
        y = jnp.dot(q, inv_ref[0], preferred_element_type=F32)
        y += jnp.dot(q, inv_ref[1], preferred_element_type=F32)
        y_ref[:, :, col * rows : (col + 1) * rows] = y.astype(BF16).reshape(chips, chans, rows)


def long_conv(x, fwd, inv, tw, a, ai, m, f):
    chips, chans, both = x.shape
    vmem = pl.BlockSpec(memory_space=pltpu.VMEM)
    return pl.pallas_call(
        conv_kernel,
        in_specs=[vmem] * 8,
        out_specs=vmem,
        out_shape=jax.ShapeDtypeStruct(x.shape, BF16),
        scratch_shapes=[
            pltpu.VMEM((2, both // 128, chips * chans, 128), F32),
            pltpu.VMEM((2, both // 128, chips * chans, 128), F32),
        ],
        compiler_params=pltpu.CompilerParams(vmem_limit_bytes=48 * 2**20),
        cost_estimate=pl.CostEstimate(flops=8 * 10**9, bytes_accessed=8 * 2**20, transcendentals=0),
        name="long_conv",
    )(x, fwd, inv, tw, a, ai, m, f)


def cos_sin(product, modulus):
    phase = (product % modulus).astype(F32) * (2.0 * math.pi / modulus)
    return jnp.cos(phase), jnp.sin(phase)


def column_tables(core, filt, rows, cols, padded):
    points = 2 * rows
    i = lax.iota(jnp.int32, cols)
    b = 2 * (i % CHIPS) + ((i // CHIPS) ^ core)
    k1 = lax.iota(jnp.int32, rows)
    tw = jnp.concatenate(cos_sin(b[:, None] * k1[None, :], padded), axis=1)
    k2 = lax.iota(jnp.int32, cols)
    c, s = cos_sin(k2[:, None] * b[None, :], cols)
    a = jnp.block([[c, s], [-s, c]])
    ai = a.T
    f_re, f_im = filt[0], filt[1]
    back_re = jnp.flip(f_re, (0, 1))[rows - 1 : points - 1]
    back_im = jnp.flip(f_im, (0, 1))[rows - 1 : points - 1]
    back_re = jnp.concatenate([back_re[:1], jnp.flip(f_re, (0, 1))[: rows - 1]], axis=0)
    back_im = jnp.concatenate([back_im[:1], jnp.flip(f_im, (0, 1))[: rows - 1]], axis=0)
    h_re = (0.5 * (f_re[:rows] + back_re)).T
    h_im = (0.5 * (f_im[:rows] - back_im)).T
    f = jnp.concatenate([h_re, h_im], axis=1)

    def edge(k):
        d = jnp.mod(b[:, None] - b[None, :], cols)
        dd = b[:, None] - b[None, :]
        ec, es = cos_sin(d[:, :, None] * k2[None, None, :], cols)
        g_re = jnp.sum(ec * f_re[k] - es * f_im[k], axis=-1)
        g_im = jnp.sum(es * f_re[k] + ec * f_im[k], axis=-1)
        tc, ts = cos_sin(jnp.mod(dd * k, padded), padded)
        return g_re * tc - g_im * ts

    zero = jnp.zeros((cols, cols), F32)
    m = jnp.block([[edge(0), zero], [zero, edge(rows)]])

    def stacked(t):
        return jnp.concatenate(split_table(t), axis=0)

    return tw, stacked(a), stacked(ai), stacked(m), f


def dot_t(weight, tokens):
    return lax.dot_general(weight, tokens, (((0,), (1,)), ((), ())), preferred_element_type=F32)


def gather_two(block, first, second):
    d1 = send(block, **{first: -1})
    d3 = send(block, **{first: 1})
    d2 = send(block, **{first: 2})
    line = jnp.concatenate([block, d1, d2, d3], axis=0)
    e1 = send(line, **{second: -1})
    e3 = send(line, **{second: 1})
    half = line.shape[0] // 2
    e2a = send(e1[:half], **{second: -1})
    e2b = send(e3[half:], **{second: 1})
    return line, e1, e2a, e2b, e3


def project(pieces, tokens):
    line, e1, e2a, e2b, e3 = pieces
    n = line.shape[0]
    out = dot_t(line, tokens[:, :n])
    out += dot_t(e1, tokens[:, n : 2 * n])
    out += dot_t(e3, tokens[:, 3 * n :])
    out += dot_t(e2a, tokens[:, 2 * n : 2 * n + n // 2])
    out += dot_t(e2b, tokens[:, 2 * n + n // 2 : 3 * n])
    return out.astype(BF16).astype(F32)


def per_device(tokens, in_weight, filter_spectrum, skip_bias, out_weight):
    rows, _, width = tokens.shape
    cols = SEQ
    padded = 2 * rows * cols
    s = lax.axis_index("seq")
    h = lax.axis_index("ch")
    z, y, x, core = coords(s)
    chan = in_weight.shape[2] // 2
    depth = in_weight.shape[0]

    mine = tokens.reshape(rows, width)
    keep = lax.dynamic_slice_in_dim(in_weight, core * chan, chan, 2)
    give = lax.dynamic_slice_in_dim(in_weight, (1 - core) * chan, chan, 2)
    keep = jnp.concatenate([keep[:, 1], keep[:, 2], keep[:, 0]], axis=1)
    give = jnp.concatenate([give[:, 1], give[:, 2], give[:, 0]], axis=1)
    near = send(give, dc=1)
    far = send(keep[:, : 2 * chan], dz=1)
    far_near = send(give[:, : 2 * chan], dz=1, dc=1)

    def ordered(own, partner):
        return jnp.concatenate(
            [jnp.where(core == 0, own, partner), jnp.where(core == 0, partner, own)], axis=0
        )

    own_z = ordered(keep, near)
    oth_z = ordered(far, far_near)
    block = jnp.concatenate([own_z[:, : 2 * chan], oth_z], axis=0)
    gate_weight = lax.all_gather(
        own_z[:, 2 * chan :], "seq", axis=0, tiled=True, axis_index_groups=SAME_CORE
    )
    key_pieces = gather_two(block[:, :chan], "dx", "dy")
    value_pieces = gather_two(block[:, chan:], "dy", "dx")

    other = send(mine, dc=1)
    order = np.arange(32)
    p_, q_, dz = order // 8, (order // 2) % 4, order % 2
    key_order = ((z ^ dz) * 4 + (y + p_) % 4) * 4 + (x + q_) % 4
    value_order = ((z ^ dz) * 4 + (y + q_) % 4) * 4 + (x + p_) % 4
    tokens_key, tokens_value = reorder(jnp.stack([key_order, value_order]), mine, other)

    half_ow = out_weight.shape[0] // 2
    perm = []
    for t in range(SEQ):
        tz, ty, tx, tc = coords(t)
        for th in range(2):
            perm.append((t * 2 + th, index_of(tz ^ tc, ty, tx, tc) * 2 + 1 - th))
    ow_part = lax.dynamic_slice_in_dim(out_weight, core * half_ow, half_ow, 0)
    ow_same = lax.ppermute(ow_part, ("seq", "ch"), perm)
    ow_cross = send(ow_same, dc=1)

    filt = jnp.transpose(filter_spectrum, (3, 0, 2, 1)).reshape(4, -1)
    filt = lax.all_gather(filt, "seq", axis=0)
    filt = lax.dynamic_index_in_dim(filt, 2 * core + z, 1, keepdims=False)
    filt = filt.reshape(SEQ, 2, cols, 2 * rows // SEQ)
    filt = jnp.transpose(filt, (1, 0, 3, 2)).reshape(2, 2 * rows, cols)
    tw, a, ai, m, f = column_tables(core, filt, rows, cols, padded)
    forward, inverse = row_tables(rows, padded)
    fwd = jnp.asarray(np.stack(split_np(forward)))
    inv = jnp.asarray(np.stack(split_np(inverse)))

    source = project(key_pieces, tokens_key) * project(value_pieces, tokens_value)
    packed = source.astype(BF16).reshape(CHIPS, chan // CHIPS, 2 * rows)
    mine_ch = lax.all_to_all(packed, "seq", 0, 0, axis_index_groups=SAME_CORE)
    conv = long_conv(mine_ch, fwd, inv, tw, a, ai, m, f)
    conv = lax.all_to_all(conv, "seq", 0, 0, axis_index_groups=SAME_CORE)
    conv = conv.reshape(chan, 2 * rows).astype(F32)

    gate = jnp.concatenate([dot_t(gate_weight, mine), dot_t(gate_weight, other)], axis=1)
    gate = gate.astype(BF16).astype(F32)
    skip = lax.dynamic_slice_in_dim(skip_bias, core * chan, chan, 0)[:, None]
    gated = (gate * (conv + skip * source)).astype(BF16)

    kept = rows // 2
    own_here = lax.dynamic_slice(gated, (0, h * kept), (chan, kept))
    own_there = lax.dynamic_slice(gated, (0, (1 - h) * kept), (chan, kept))
    oth_here = lax.dynamic_slice(gated, (0, rows + h * kept), (chan, kept))
    oth_there = lax.dynamic_slice(gated, (0, rows + (1 - h) * kept), (chan, kept))
    swap_ch = [(0, 1), (1, 0)]
    from_h = lax.ppermute(own_there, "ch", swap_ch)
    perm2 = []
    for t in range(SEQ):
        for th in range(2):
            perm2.append((t * 2 + th, (t ^ 1) * 2 + 1 - th))
    from_hc = lax.ppermute(oth_there, ("seq", "ch"), perm2)
    from_c = send(oth_here, dc=1)
    here = ordered(own_here, from_c)

    def out_dot(g, w):
        return lax.dot_general(g, w, (((0,), (0,)), ((), ())), preferred_element_type=F32)

    mixed = out_dot(here, out_weight) + out_dot(from_h, ow_same) + out_dot(from_hc, ow_cross)
    return mixed.astype(BF16).reshape(kept, 1, out_weight.shape[1])


def solution(mesh):
    in_specs = (
        P(None, "seq", None),
        P("seq", None, "ch"),
        P(None, "seq", None, "ch"),
        P("ch"),
        P("ch", None),
    )
    return jax.shard_map(
        per_device, mesh=mesh, in_specs=in_specs, out_specs=P("ch", "seq", None), check_vma=False
    )
```

```python
import functools
import math

import jax
import jax.numpy as jnp
import ml_dtypes
import numpy as np
from jax import lax
from jax.experimental import pallas as pl
from jax.experimental.pallas import tpu as pltpu
from jax.sharding import PartitionSpec as P

BF16 = jnp.bfloat16
F32 = jnp.float32
HIGH = lax.Precision.HIGHEST
SEQ = 64
CHIPS = 32
SAME_CORE = [[2 * p + j for p in range(CHIPS)] for j in range(2)]


def coords(s):
    return s // 32, (s // 8) % 4, (s // 2) % 4, s % 2


def index_of(z, y, x, c):
    return ((z * 4 + y) * 4 + x) * 2 + c


def send(value, dz=0, dy=0, dx=0, dc=0):
    perm = []
    for s in range(SEQ):
        z, y, x, c = coords(s)
        perm.append((s, index_of((z + dz) % 2, (y + dy) % 4, (x + dx) % 4, c ^ dc)))
    return lax.ppermute(value, "seq", perm)


def split_np(table):
    upper = table.astype(np.float32).astype(ml_dtypes.bfloat16)
    lower = (table - upper.astype(np.float64)).astype(np.float32).astype(ml_dtypes.bfloat16)
    return upper, lower


def split_table(table):
    upper = table.astype(BF16)
    lower = (table - upper.astype(F32)).astype(BF16)
    return upper, lower


def row_tables(rows, padded):
    points = 2 * rows
    a = np.arange(rows)
    k = np.arange(rows)
    phase = 2.0 * np.pi * ((a[:, None] * k[None, :]) % points) / points
    re, im = np.cos(phase), -np.sin(phase)
    im[:, 0] = np.where(a % 2 == 0, 1.0, -1.0)
    forward = np.concatenate([re, im], axis=1)
    scale = np.full((rows,), 2.0)
    scale[0] = 1.0
    inverse = np.concatenate([re * scale, im * scale], axis=1).T / padded
    return forward, inverse


def picked(order_ref, row, group, tok_ref):
    blocks = [
        tok_ref[:, pl.ds(pl.multiple_of(order_ref[row, group * 8 + i] * 128, 128), 128)]
        for i in range(8)
    ]
    return jnp.concatenate(blocks, axis=1)


def first_kernel(order_ref, mine_ref, other_ref, *refs):
    weights, (key_ref, value_ref, key_tok_ref, value_tok_ref) = refs[:6], refs[6:]

    def run(tok_ref):
        for row, total_ref, last_ref in ((0, key_ref, key_tok_ref), (1, value_ref, value_tok_ref)):
            line, e1, e3 = weights[3 * row : 3 * row + 3]
            total = jnp.dot(picked(order_ref, row, 0, tok_ref), line[...], preferred_element_type=F32)
            total += jnp.dot(picked(order_ref, row, 1, tok_ref), e1[...], preferred_element_type=F32)
            total += jnp.dot(picked(order_ref, row, 3, tok_ref), e3[...], preferred_element_type=F32)
            total_ref[...] = total
            last_ref[...] = picked(order_ref, row, 2, tok_ref)

    step = pl.program_id(0)

    @pl.when(step < 2)
    def _():
        run(mine_ref)

    @pl.when(step >= 2)
    def _():
        run(other_ref)


def first_part(order, mine, other, key_pieces, value_pieces):
    rows, width = mine.shape
    chan = key_pieces[0].shape[1]
    tile = rows // 2
    weights = [key_pieces[0], key_pieces[1], key_pieces[4]]
    weights += [value_pieces[0], value_pieces[1], value_pieces[4]]
    quarter = width // 4
    return pl.pallas_call(
        first_kernel,
        grid_spec=pltpu.PrefetchScalarGridSpec(
            num_scalar_prefetch=1,
            grid=(4,),
            in_specs=[
                pl.BlockSpec((tile, width), lambda i, o: (jnp.minimum(i, 1), 0)),
                pl.BlockSpec((tile, width), lambda i, o: (jnp.maximum(i - 2, 0), 0)),
            ]
            + [pl.BlockSpec((quarter, chan), lambda i, o: (0, 0))] * 6,
            out_specs=[
                pl.BlockSpec((tile, chan), lambda i, o: (i, 0)),
                pl.BlockSpec((tile, chan), lambda i, o: (i, 0)),
                pl.BlockSpec((tile, quarter), lambda i, o: (i, 0)),
                pl.BlockSpec((tile, quarter), lambda i, o: (i, 0)),
            ],
        ),
        out_shape=[jax.ShapeDtypeStruct((2 * rows, chan), F32)] * 2
        + [jax.ShapeDtypeStruct((2 * rows, quarter), BF16)] * 2,
        compiler_params=pltpu.CompilerParams(vmem_limit_bytes=48 * 2**20),
        cost_estimate=pl.CostEstimate(
            flops=2 * 2 * 2 * rows * 3 * quarter * chan, bytes_accessed=22 * 2**20, transcendentals=0
        ),
        name="first_part",
    )(order, mine, other, *weights)


def last_kernel(key_ref, value_ref, key_tok_ref, value_tok_ref, ka, kb, va, vb, out_ref, send_ref):
    half = ka.shape[0]

    def finish(total_ref, tok_ref, wa, wb):
        total = total_ref[...]
        total += jnp.dot(tok_ref[:, :half], wa[...], preferred_element_type=F32)
        total += jnp.dot(tok_ref[:, half:], wb[...], preferred_element_type=F32)
        return total.astype(BF16).astype(F32)

    source = finish(key_ref, key_tok_ref, ka, kb) * finish(value_ref, value_tok_ref, va, vb)
    source = source.T
    out_ref[...] = source
    send_ref[...] = source.astype(BF16)


def last_part(first, key_pieces, value_pieces):
    total, chan = first[0].shape
    quarter = first[2].shape[1]
    tile = total // 4
    weights = [*key_pieces[2:4], *value_pieces[2:4]]
    return pl.pallas_call(
        last_kernel,
        grid=(4,),
        in_specs=[pl.BlockSpec((tile, chan), lambda i: (i, 0))] * 2
        + [pl.BlockSpec((tile, quarter), lambda i: (i, 0))] * 2
        + [pl.BlockSpec((quarter // 2, chan), lambda i: (0, 0))] * 4,
        out_specs=[pl.BlockSpec((chan, tile), lambda i: (0, i))] * 2,
        out_shape=[
            jax.ShapeDtypeStruct((chan, total), F32),
            jax.ShapeDtypeStruct((chan, total), BF16),
        ],
        compiler_params=pltpu.CompilerParams(vmem_limit_bytes=48 * 2**20),
        cost_estimate=pl.CostEstimate(
            flops=2 * 2 * total * quarter * chan, bytes_accessed=13 * 2**20, transcendentals=0
        ),
        name="last_part",
    )(*first, *weights)


def gate_kernel(mine_ref, other_ref, weight_ref, out_ref):
    step = pl.program_id(0)
    chips, deep, _ = weight_ref.shape
    depth = deep // 4

    def run(tok_ref):
        for k in range(0, 4, 2):
            parts = [
                weight_ref[:, i * depth : (i + 1) * depth, :].reshape(chips * depth, 128)
                for i in (k, k + 1)
            ]
            weight = jnp.concatenate(parts, axis=1)
            gate = jnp.dot(tok_ref[...], weight, preferred_element_type=F32)
            out_ref[k * 128 : (k + 2) * 128, :] = gate.T.astype(BF16)

    @pl.when(step < 2)
    def _():
        run(mine_ref)

    @pl.when(step >= 2)
    def _():
        run(other_ref)


def gate_part(mine, other, gathered):
    rows, width = mine.shape
    chips = gathered.shape[0]
    depth = width // chips
    chan = 4 * 128
    tile = rows // 2
    return pl.pallas_call(
        gate_kernel,
        grid=(4,),
        in_specs=[
            pl.BlockSpec((tile, width), lambda i: (jnp.minimum(i, 1), 0)),
            pl.BlockSpec((tile, width), lambda i: (jnp.maximum(i - 2, 0), 0)),
            pl.BlockSpec((chips, 4 * depth, 128), lambda i: (0, 0, 0)),
        ],
        out_specs=pl.BlockSpec((chan, tile), lambda i: (0, i)),
        out_shape=jax.ShapeDtypeStruct((chan, 2 * rows), BF16),
        compiler_params=pltpu.CompilerParams(vmem_limit_bytes=48 * 2**20),
        cost_estimate=pl.CostEstimate(
            flops=2 * 2 * rows * width * chan, bytes_accessed=13 * 2**20, transcendentals=0
        ),
        name="gate_part",
    )(mine, other, gathered)


def mix_kernel(here, near_h, far_h, w_here, w_near, w_far, out_ref, lhs_ref):
    @pl.when(pl.program_id(0) == 0)
    def _():
        n, m = here.shape[0], near_h.shape[0]
        lhs_ref[:, :n] = here[...].astype(F32).T.astype(BF16)
        lhs_ref[:, n : n + m] = near_h[...].astype(F32).T.astype(BF16)
        lhs_ref[:, n + m :] = far_h[...].astype(F32).T.astype(BF16)

    n, m = here.shape[0], near_h.shape[0]
    total = jnp.dot(lhs_ref[:, :n], w_here[...], preferred_element_type=F32)
    total += jnp.dot(lhs_ref[:, n : n + m], w_near[...], preferred_element_type=F32)
    total += jnp.dot(lhs_ref[:, n + m :], w_far[...], preferred_element_type=F32)
    out_ref[...] = total.astype(BF16)


def mix_part(here, near_h, far_h, w_here, w_near, w_far):
    rows = here.shape[1]
    width = w_here.shape[1]
    tile = width // 8

    def whole(g):
        return pl.BlockSpec(g.shape, lambda i: (0, 0))

    def tiled(w):
        return pl.BlockSpec((w.shape[0], tile), lambda i: (0, i))

    depth = here.shape[0] + near_h.shape[0] + far_h.shape[0]
    return pl.pallas_call(
        mix_kernel,
        grid=(8,),
        in_specs=[whole(here), whole(near_h), whole(far_h), tiled(w_here), tiled(w_near), tiled(w_far)],
        out_specs=pl.BlockSpec((rows, tile), lambda i: (0, i)),
        out_shape=jax.ShapeDtypeStruct((rows, width), BF16),
        scratch_shapes=[pltpu.VMEM((rows, depth), BF16)],
        compiler_params=pltpu.CompilerParams(vmem_limit_bytes=48 * 2**20),
        cost_estimate=pl.CostEstimate(
            flops=2 * rows * depth * width, bytes_accessed=19 * 2**20, transcendentals=0
        ),
        name="mix_part",
    )(here, near_h, far_h, w_here, w_near, w_far)


def filter_kernel(z_ref, x_ref, cs_ref, twist_ref, f_ref, m_ref):
    chips, _, lanes = x_ref.shape
    x = x_ref[...].reshape(2 * chips, 2, 16, lanes)
    points = 2 * chips * 16
    rows, cols = points // 2, lanes // 2
    upper = x[:, 0].reshape(points, lanes)
    lower = x[:, 1].reshape(points, lanes)
    whole = (upper.astype(F32) + lower.astype(F32)).T
    i = lax.broadcasted_iota(jnp.int32, (rows, rows), 0)
    j = lax.broadcasted_iota(jnp.int32, (rows, rows), 1)
    mirror = (i + j == rows).astype(F32).astype(BF16)
    i = lax.broadcasted_iota(jnp.int32, (lanes, lanes), 0)
    j = lax.broadcasted_iota(jnp.int32, (lanes, lanes), 1)
    flip = ((i // cols == j // cols) & (i % cols + j % cols == cols - 1)).astype(F32).astype(BF16)

    def mirrored(part):
        turned = jnp.dot(flip, part[:, rows:], preferred_element_type=F32).astype(BF16)
        return jnp.dot(turned, mirror, preferred_element_type=F32)

    other = mirrored(upper.astype(F32).T.astype(BF16)) + mirrored(lower.astype(F32).T.astype(BF16))
    f_ref[:, :rows] = 0.5 * (whole[:cols, :rows] + other[:cols])
    f_ref[:, rows:] = 0.5 * (whole[cols:, :rows] - other[cols:])
    c, s = cs_ref[0], cs_ref[1]

    def contract(left, right):
        return lax.dot_general(
            left, right, (((0,), (0,)), ((), ())), precision=HIGH, preferred_element_type=F32
        )

    m_ref[...] = jnp.zeros_like(m_ref)
    for n, k in enumerate((0, rows)):
        e_re, e_im = whole[:cols, k : k + 1], whole[cols:, k : k + 1]
        u = c * e_re - s * e_im
        v = s * e_re + c * e_im
        g = contract(u, c) + contract(v, s)
        if n:
            g = g * twist_ref[0] - (contract(v, c) - contract(u, s)) * twist_ref[1]
        g_upper = g.astype(BF16)
        g_lower = (g - g_upper.astype(F32)).astype(BF16)
        spot = slice(n * cols, (n + 1) * cols)
        m_ref[0, spot, spot] = g_upper
        m_ref[1, spot, spot] = g_lower


def filter_part(z, gathered, cs, twist):
    chips = gathered.shape[0]
    cols = cs.shape[1]
    rows = chips * 16
    lanes = 2 * cols
    return pl.pallas_call(
        filter_kernel,
        grid_spec=pltpu.PrefetchScalarGridSpec(
            num_scalar_prefetch=1,
            grid=(1,),
            in_specs=[
                pl.BlockSpec((chips, 64, lanes), lambda i, z: (0, 8 + z[0], 0)),
                pl.BlockSpec(cs.shape, lambda i, z: (0, 0, 0)),
                pl.BlockSpec(twist.shape, lambda i, z: (0, 0, 0)),
            ],
            out_specs=[
                pl.BlockSpec((cols, 2 * rows), lambda i, z: (0, 0)),
                pl.BlockSpec((2, lanes, lanes), lambda i, z: (0, 0, 0)),
            ],
        ),
        out_shape=[
            jax.ShapeDtypeStruct((cols, 2 * rows), F32),
            jax.ShapeDtypeStruct((2, lanes, lanes), BF16),
        ],
        compiler_params=pltpu.CompilerParams(vmem_limit_bytes=32 * 2**20),
        cost_estimate=pl.CostEstimate(flops=10**9, bytes_accessed=2**20, transcendentals=0),
        name="filter_part",
    )(z.reshape(1), gathered, cs, twist)


def conv_kernel(x_ref, fwd_ref, inv_ref, tw_ref, a_ref, ai_ref, m_ref, f_ref, y_ref, r_ref, q_ref):
    chips, chans, both = x_ref.shape
    rows = both // 2
    blocks = rows // 128
    for col in range(2):
        x = x_ref[:, :, col * rows : (col + 1) * rows].reshape(chips * chans, rows)
        r = jnp.dot(x, fwd_ref[0], preferred_element_type=F32)
        r += jnp.dot(x, fwd_ref[1], preferred_element_type=F32)
        r = r.reshape(chips, chans, 2 * rows)
        tw = tw_ref[col * chips : (col + 1) * chips, :]
        cos = tw[:, None, :rows]
        sin = tw[:, None, rows:]
        re, im = r[:, :, :rows], r[:, :, rows:]
        turned_re = (re * cos + im * sin).reshape(chips * chans, rows)
        turned_im = (im * cos - re * sin).reshape(chips * chans, rows)
        for k in range(blocks):
            r_ref[col, k] = turned_re[:, k * 128 : (k + 1) * 128]
            r_ref[col, blocks + k] = turned_im[:, k * 128 : (k + 1) * 128]
    half = 2 * chips
    lane = lax.broadcasted_iota(jnp.int32, (2 * half, 128), 1)

    def channel(c, carry):
        pick = pl.ds(c, chips, stride=chans)
        parts = [
            jnp.concatenate([r_ref[col, part * blocks + k, pick, :] for k in range(blocks)], axis=1)
            for part in range(2)
            for col in range(2)
        ]
        turned = jnp.concatenate(parts, axis=0).astype(BF16)
        s = jnp.dot(a_ref[...], turned, preferred_element_type=F32)
        s = s[: 2 * half] + s[2 * half :]
        s_re, s_im = s[:half], s[half:]
        f_re, f_im = f_ref[:, :rows], f_ref[:, rows:]
        filtered = jnp.concatenate(
            [s_re * f_re - s_im * f_im, s_re * f_im + s_im * f_re], axis=0
        ).astype(BF16)
        back = jnp.dot(ai_ref[...], filtered, preferred_element_type=F32)
        back = back[: 2 * half] + back[2 * half :]
        edge = jnp.dot(m_ref[...], turned[:, :128], preferred_element_type=F32)
        edge = edge[: 2 * half] + edge[2 * half :]
        head = jnp.where(lane == 0, edge, back[:, :128])
        back = jnp.concatenate([head, back[:, 128:]], axis=1)
        b_re, b_im = back[:half], back[half:]
        cos, sin = tw_ref[:, :rows], tw_ref[:, rows:]
        out_re = b_re * cos - b_im * sin
        out_im = b_im * cos + b_re * sin
        for col in range(2):
            part = slice(col * chips, (col + 1) * chips)
            for k in range(blocks):
                q_ref[col, k, pick, :] = out_re[part, k * 128 : (k + 1) * 128]
                q_ref[col, blocks + k, pick, :] = out_im[part, k * 128 : (k + 1) * 128]
        return carry

    lax.fori_loop(0, chans, channel, 0)
    for col in range(2):
        q = jnp.concatenate([q_ref[col, k].astype(BF16) for k in range(2 * blocks)], axis=1)
        y = jnp.dot(q, inv_ref[0], preferred_element_type=F32)
        y += jnp.dot(q, inv_ref[1], preferred_element_type=F32)
        y_ref[:, :, col * rows : (col + 1) * rows] = y.astype(BF16).reshape(chips, chans, rows)


def long_conv(x, fwd, inv, tw, a, ai, m, f):
    chips, chans, both = x.shape
    vmem = pl.BlockSpec(memory_space=pltpu.VMEM)
    return pl.pallas_call(
        conv_kernel,
        in_specs=[vmem] * 8,
        out_specs=vmem,
        out_shape=jax.ShapeDtypeStruct(x.shape, BF16),
        scratch_shapes=[
            pltpu.VMEM((2, both // 128, chips * chans, 128), F32),
            pltpu.VMEM((2, both // 128, chips * chans, 128), F32),
        ],
        compiler_params=pltpu.CompilerParams(vmem_limit_bytes=48 * 2**20),
        cost_estimate=pl.CostEstimate(flops=8 * 10**9, bytes_accessed=8 * 2**20, transcendentals=0),
        name="long_conv",
    )(x, fwd, inv, tw, a, ai, m, f)


def cos_sin(product, modulus):
    phase = (product % modulus).astype(F32) * (2.0 * math.pi / modulus)
    return jnp.cos(phase), jnp.sin(phase)


def column_tables(core, rows, cols, padded):
    i = lax.iota(jnp.int32, cols)
    b = 2 * (i % CHIPS) + ((i // CHIPS) ^ core)
    k1 = lax.iota(jnp.int32, rows)
    tw = jnp.concatenate(cos_sin(b[:, None] * k1[None, :], padded), axis=1)
    k2 = lax.iota(jnp.int32, cols)
    c, s = cos_sin(k2[:, None] * b[None, :], cols)
    a = jnp.block([[c, s], [-s, c]])
    twist = jnp.stack(cos_sin(jnp.mod((b[:, None] - b[None, :]) * rows, padded), padded))

    def stacked(t):
        return jnp.concatenate(split_table(t), axis=0)

    return tw, stacked(a), stacked(a.T), jnp.stack([c, s]), twist


def gather_two(block, first, second):
    d1 = send(block, **{first: -1})
    d3 = send(block, **{first: 1})
    d2 = send(block, **{first: 2})
    line = jnp.concatenate([block, d1, d2, d3], axis=0)
    e1 = send(line, **{second: -1})
    e3 = send(line, **{second: 1})
    half = line.shape[0] // 2
    e2a = send(e1[:half], **{second: -1})
    e2b = send(e3[half:], **{second: 1})
    return line, e1, e2a, e2b, e3


def per_device(tokens, in_weight, filter_spectrum, skip_bias, out_weight):
    rows, _, width = tokens.shape
    cols = SEQ
    padded = 2 * rows * cols
    s = lax.axis_index("seq")
    h = lax.axis_index("ch")
    z, y, x, core = coords(s)
    chan = in_weight.shape[2] // 2
    depth = in_weight.shape[0]

    mine = tokens.reshape(rows, width)
    filt = jnp.transpose(filter_spectrum, (3, 1, 0, 2)).reshape(4, 1, -1, 2 * cols)
    filt = jnp.concatenate(split_table(filt), axis=1).reshape(4, -1, 2 * cols)

    def half_for(c):
        w = lax.dynamic_slice_in_dim(in_weight, c * chan, chan, 2)
        f = lax.dynamic_slice_in_dim(filt, 2 * c, 2, 0)
        g = jnp.concatenate([w[:, 0, i * 128 : (i + 1) * 128] for i in range(chan // 128)], axis=0)
        return jnp.concatenate([w[:, 1], w[:, 2]], axis=0), g.reshape(-1, depth, 128), f

    keep, keep_g, keep_f = half_for(core)
    give, give_g, give_f = half_for(1 - core)
    near_g = send(jnp.concatenate([give_g.reshape(-1, 128), give_f.reshape(-1, 128)], axis=0), dc=1)
    near = send(give, dc=1)
    far = send(keep, dz=1)
    far_near = send(give, dz=1, dc=1)
    other = send(mine, dc=1)

    def ordered(own, partner, axis=0):
        return jnp.concatenate(
            [jnp.where(core == 0, own, partner), jnp.where(core == 0, partner, own)], axis=axis
        )

    key_block = jnp.concatenate(
        [ordered(keep[:depth], near[:depth]), ordered(far[:depth], far_near[:depth])], axis=0
    )
    value_block = jnp.concatenate(
        [ordered(keep[depth:], near[depth:]), ordered(far[depth:], far_near[depth:])], axis=0
    )
    cut = 4 * depth
    gate_block = jnp.concatenate(
        [
            ordered(keep_g, near_g[:cut].reshape(keep_g.shape), 1).reshape(-1, 128),
            ordered(keep_f, near_g[cut:].reshape(keep_f.shape), 1).reshape(-1, 128),
        ],
        axis=0,
    )
    gathered = lax.all_gather(gate_block, "seq", axis=0, axis_index_groups=SAME_CORE)
    ow_part = lax.dynamic_slice_in_dim(
        out_weight, core * (out_weight.shape[0] // 2), out_weight.shape[0] // 2, 0
    )
    key_block, value_block, ow_part = lax.optimization_barrier((key_block, value_block, ow_part))
    key_pieces = gather_two(key_block, "dx", "dy")
    value_pieces = gather_two(value_block, "dy", "dx")

    order = np.arange(32)
    p_, q_, dz = order // 8, (order // 2) % 4, order % 2
    key_order = ((z ^ dz) * 4 + (y + p_) % 4) * 4 + (x + q_) % 4
    value_order = ((z ^ dz) * 4 + (y + q_) % 4) * 4 + (x + p_) % 4
    first = first_part(jnp.stack([key_order, value_order]), mine, other, key_pieces, value_pieces)

    perm = []
    for t in range(SEQ):
        tz, ty, tx, tc = coords(t)
        for th in range(2):
            perm.append((t * 2 + th, index_of(tz ^ tc, ty, tx, tc) * 2 + 1 - th))
    ow_same = lax.ppermute(ow_part, ("seq", "ch"), perm)
    ow_cross = send(ow_same, dc=1)

    source, packed = last_part(first, key_pieces, value_pieces)
    packed = packed.reshape(CHIPS, chan // CHIPS, 2 * rows)
    mine_ch = lax.all_to_all(packed, "seq", 0, 0, axis_index_groups=SAME_CORE)

    tw, a, ai, cs, twist = column_tables(core, rows, cols, padded)
    f, m = filter_part(z, gathered, cs, twist)
    m = m.reshape(-1, 2 * cols)
    forward, inverse = row_tables(rows, padded)
    fwd = jnp.asarray(np.stack(split_np(forward)))
    inv = jnp.asarray(np.stack(split_np(inverse)))
    conv = long_conv(mine_ch, fwd, inv, tw, a, ai, m, f)
    conv = lax.all_to_all(conv, "seq", 0, 0, axis_index_groups=SAME_CORE)
    conv = conv.reshape(chan, 2 * rows).astype(F32)

    gate = gate_part(mine, other, gathered).astype(F32)
    skip = lax.dynamic_slice_in_dim(skip_bias, core * chan, chan, 0)[:, None]
    gated = (gate * (conv + skip * source)).astype(BF16)

    kept = rows // 2
    own_here = lax.dynamic_slice(gated, (0, h * kept), (chan, kept))
    own_there = lax.dynamic_slice(gated, (0, (1 - h) * kept), (chan, kept))
    oth_here = lax.dynamic_slice(gated, (0, rows + h * kept), (chan, kept))
    oth_there = lax.dynamic_slice(gated, (0, rows + (1 - h) * kept), (chan, kept))
    swap_ch = [(0, 1), (1, 0)]
    from_h = lax.ppermute(own_there, "ch", swap_ch)
    perm2 = []
    for t in range(SEQ):
        for th in range(2):
            perm2.append((t * 2 + th, (t ^ 1) * 2 + 1 - th))
    from_hc = lax.ppermute(oth_there, ("seq", "ch"), perm2)
    from_c = send(oth_here, dc=1)
    here = ordered(own_here, from_c)

    mixed = mix_part(here, from_h, from_hc, out_weight, ow_same, ow_cross)
    return mixed.reshape(kept, 1, width)


def solution(mesh):
    in_specs = (
        P(None, "seq", None),
        P("seq", None, "ch"),
        P(None, "seq", None, "ch"),
        P("ch"),
        P("ch", None),
    )
    return jax.shard_map(
        per_device, mesh=mesh, in_specs=in_specs, out_specs=P("ch", "seq", None), check_vma=False
    )
```

```python
import functools
import math

import jax
import jax.numpy as jnp
import ml_dtypes
import numpy as np
from jax import lax
from jax.experimental import pallas as pl
from jax.experimental.pallas import tpu as pltpu
from jax.sharding import PartitionSpec as P

BF16 = jnp.bfloat16
F32 = jnp.float32
HIGH = lax.Precision.HIGHEST
SEQ = 64
CHIPS = 32
SAME_CORE = [[2 * p + j for p in range(CHIPS)] for j in range(2)]


def coords(s):
    return s // 32, (s // 8) % 4, (s // 2) % 4, s % 2


def index_of(z, y, x, c):
    return ((z * 4 + y) * 4 + x) * 2 + c


def send(value, dz=0, dy=0, dx=0, dc=0):
    perm = []
    for s in range(SEQ):
        z, y, x, c = coords(s)
        perm.append((s, index_of((z + dz) % 2, (y + dy) % 4, (x + dx) % 4, c ^ dc)))
    return lax.ppermute(value, "seq", perm)


def split_np(table):
    upper = table.astype(np.float32).astype(ml_dtypes.bfloat16)
    lower = (table - upper.astype(np.float64)).astype(np.float32).astype(ml_dtypes.bfloat16)
    return upper, lower


def split_table(table):
    upper = table.astype(BF16)
    lower = (table - upper.astype(F32)).astype(BF16)
    return upper, lower


def row_tables(rows, padded):
    points = 2 * rows
    a = np.arange(rows)
    k = np.arange(rows)
    phase = 2.0 * np.pi * ((a[:, None] * k[None, :]) % points) / points
    re, im = np.cos(phase), -np.sin(phase)
    im[:, 0] = np.where(a % 2 == 0, 1.0, -1.0)
    forward = np.concatenate([re, im], axis=1)
    scale = np.full((rows,), 2.0)
    scale[0] = 1.0
    inverse = np.concatenate([re * scale, im * scale], axis=1).T / padded
    return forward, inverse


def picked(order_ref, row, group, tok_ref):
    blocks = [
        tok_ref[:, pl.ds(pl.multiple_of(order_ref[row, group * 8 + i] * 128, 128), 128)]
        for i in range(8)
    ]
    return jnp.concatenate(blocks, axis=1)


def first_kernel(order_ref, mine_ref, other_ref, *refs):
    weights, (key_ref, value_ref, key_tok_ref, value_tok_ref) = refs[:6], refs[6:]

    def run(tok_ref):
        for row, total_ref, last_ref in ((0, key_ref, key_tok_ref), (1, value_ref, value_tok_ref)):
            line, e1, e3 = weights[3 * row : 3 * row + 3]
            total = jnp.dot(picked(order_ref, row, 0, tok_ref), line[...], preferred_element_type=F32)
            total += jnp.dot(picked(order_ref, row, 1, tok_ref), e1[...], preferred_element_type=F32)
            total += jnp.dot(picked(order_ref, row, 3, tok_ref), e3[...], preferred_element_type=F32)
            total_ref[...] = total
            last_ref[...] = picked(order_ref, row, 2, tok_ref)

    step = pl.program_id(0)

    @pl.when(step < 2)
    def _():
        run(mine_ref)

    @pl.when(step >= 2)
    def _():
        run(other_ref)


def first_part(order, mine, other, key_pieces, value_pieces):
    rows, width = mine.shape
    chan = key_pieces[0].shape[1]
    tile = rows // 2
    weights = [key_pieces[0], key_pieces[1], key_pieces[4]]
    weights += [value_pieces[0], value_pieces[1], value_pieces[4]]
    quarter = width // 4
    return pl.pallas_call(
        first_kernel,
        grid_spec=pltpu.PrefetchScalarGridSpec(
            num_scalar_prefetch=1,
            grid=(4,),
            in_specs=[
                pl.BlockSpec((tile, width), lambda i, o: (jnp.minimum(i, 1), 0)),
                pl.BlockSpec((tile, width), lambda i, o: (jnp.maximum(i - 2, 0), 0)),
            ]
            + [pl.BlockSpec((quarter, chan), lambda i, o: (0, 0))] * 6,
            out_specs=[
                pl.BlockSpec((tile, chan), lambda i, o: (i, 0)),
                pl.BlockSpec((tile, chan), lambda i, o: (i, 0)),
                pl.BlockSpec((tile, quarter), lambda i, o: (i, 0)),
                pl.BlockSpec((tile, quarter), lambda i, o: (i, 0)),
            ],
        ),
        out_shape=[jax.ShapeDtypeStruct((2 * rows, chan), F32)] * 2
        + [jax.ShapeDtypeStruct((2 * rows, quarter), BF16)] * 2,
        compiler_params=pltpu.CompilerParams(vmem_limit_bytes=48 * 2**20),
        cost_estimate=pl.CostEstimate(
            flops=2 * 2 * 2 * rows * 3 * quarter * chan, bytes_accessed=22 * 2**20, transcendentals=0
        ),
        name="first_part",
    )(order, mine, other, *weights)


def last_kernel(key_ref, value_ref, key_tok_ref, value_tok_ref, ka, kb, va, vb, out_ref, send_ref):
    half = ka.shape[0]

    def finish(total_ref, tok_ref, wa, wb):
        total = total_ref[...]
        total += jnp.dot(tok_ref[:, :half], wa[...], preferred_element_type=F32)
        total += jnp.dot(tok_ref[:, half:], wb[...], preferred_element_type=F32)
        return total.astype(BF16).astype(F32)

    source = finish(key_ref, key_tok_ref, ka, kb) * finish(value_ref, value_tok_ref, va, vb)
    source = source.T
    out_ref[...] = source
    send_ref[...] = source.astype(BF16)


def last_part(first, key_pieces, value_pieces):
    total, chan = first[0].shape
    quarter = first[2].shape[1]
    tile = total // 4
    weights = [*key_pieces[2:4], *value_pieces[2:4]]
    return pl.pallas_call(
        last_kernel,
        grid=(4,),
        in_specs=[pl.BlockSpec((tile, chan), lambda i: (i, 0))] * 2
        + [pl.BlockSpec((tile, quarter), lambda i: (i, 0))] * 2
        + [pl.BlockSpec((quarter // 2, chan), lambda i: (0, 0))] * 4,
        out_specs=[pl.BlockSpec((chan, tile), lambda i: (0, i))] * 2,
        out_shape=[
            jax.ShapeDtypeStruct((chan, total), F32),
            jax.ShapeDtypeStruct((chan, total), BF16),
        ],
        compiler_params=pltpu.CompilerParams(vmem_limit_bytes=48 * 2**20),
        cost_estimate=pl.CostEstimate(
            flops=2 * 2 * total * quarter * chan, bytes_accessed=13 * 2**20, transcendentals=0
        ),
        name="last_part",
    )(*first, *weights)


def gate_kernel(mine_ref, other_ref, weight_ref, out_ref):
    step = pl.program_id(0)
    chips, deep, _ = weight_ref.shape
    depth = deep // 4

    def run(tok_ref):
        for k in range(0, 4, 2):
            parts = [
                weight_ref[:, i * depth : (i + 1) * depth, :].reshape(chips * depth, 128)
                for i in (k, k + 1)
            ]
            weight = jnp.concatenate(parts, axis=1)
            gate = jnp.dot(tok_ref[...], weight, preferred_element_type=F32)
            out_ref[k * 128 : (k + 2) * 128, :] = gate.T.astype(BF16)

    @pl.when(step < 2)
    def _():
        run(mine_ref)

    @pl.when(step >= 2)
    def _():
        run(other_ref)


def gate_part(mine, other, gathered):
    rows, width = mine.shape
    chips = gathered.shape[0]
    depth = width // chips
    chan = 4 * 128
    tile = rows // 2
    return pl.pallas_call(
        gate_kernel,
        grid=(4,),
        in_specs=[
            pl.BlockSpec((tile, width), lambda i: (jnp.minimum(i, 1), 0)),
            pl.BlockSpec((tile, width), lambda i: (jnp.maximum(i - 2, 0), 0)),
            pl.BlockSpec((chips, 4 * depth, 128), lambda i: (0, 0, 0)),
        ],
        out_specs=pl.BlockSpec((chan, tile), lambda i: (0, i)),
        out_shape=jax.ShapeDtypeStruct((chan, 2 * rows), BF16),
        compiler_params=pltpu.CompilerParams(vmem_limit_bytes=48 * 2**20),
        cost_estimate=pl.CostEstimate(
            flops=2 * 2 * rows * width * chan, bytes_accessed=13 * 2**20, transcendentals=0
        ),
        name="gate_part",
    )(mine, other, gathered)


def turn(ref):
    return ref[...].astype(F32).T.astype(BF16)


def mix_kernel(here, w_here, out_ref, lhs_ref):
    @pl.when(pl.program_id(0) == 0)
    def _():
        lhs_ref[...] = turn(here)

    out_ref[...] = jnp.dot(lhs_ref[...], w_here[...], preferred_element_type=F32)


def mix_more_kernel(total_ref, near_h, far_h, w_near, w_far, out_ref, lhs_ref):
    m = near_h.shape[0]

    @pl.when(pl.program_id(0) == 0)
    def _():
        lhs_ref[:, :m] = turn(near_h)
        lhs_ref[:, m:] = turn(far_h)

    total = total_ref[...]
    total += jnp.dot(lhs_ref[:, :m], w_near[...], preferred_element_type=F32)
    total += jnp.dot(lhs_ref[:, m:], w_far[...], preferred_element_type=F32)
    out_ref[...] = total.astype(BF16)


def mix_part(total, parts, weights):
    rows = parts[0].shape[1]
    width = weights[0].shape[1]
    tile = width // 4
    depth = sum(p.shape[0] for p in parts)
    totals = [] if total is None else [total]

    def whole(g):
        return pl.BlockSpec(g.shape, lambda i: (0, 0))

    def tiled(w):
        return pl.BlockSpec((w.shape[0], tile), lambda i: (0, i))

    return pl.pallas_call(
        mix_kernel if total is None else mix_more_kernel,
        grid=(4,),
        in_specs=[tiled(t) for t in totals] + [whole(p) for p in parts] + [tiled(w) for w in weights],
        out_specs=pl.BlockSpec((rows, tile), lambda i: (0, i)),
        out_shape=jax.ShapeDtypeStruct((rows, width), F32 if total is None else BF16),
        scratch_shapes=[pltpu.VMEM((rows, depth), BF16)],
        compiler_params=pltpu.CompilerParams(vmem_limit_bytes=48 * 2**20),
        cost_estimate=pl.CostEstimate(
            flops=2 * rows * depth * width, bytes_accessed=12 * 2**20, transcendentals=0
        ),
        name="mix_part" if total is None else "mix_more",
    )(*totals, *parts, *weights)


def filter_kernel(z_ref, x_ref, cs_ref, twist_ref, f_ref, m_ref):
    chips, _, lanes = x_ref.shape
    x = x_ref[...].reshape(2 * chips, 2, 16, lanes)
    points = 2 * chips * 16
    rows, cols = points // 2, lanes // 2
    upper = x[:, 0].reshape(points, lanes)
    lower = x[:, 1].reshape(points, lanes)
    whole = (upper.astype(F32) + lower.astype(F32)).T
    i = lax.broadcasted_iota(jnp.int32, (rows, rows), 0)
    j = lax.broadcasted_iota(jnp.int32, (rows, rows), 1)
    mirror = (i + j == rows).astype(F32).astype(BF16)
    i = lax.broadcasted_iota(jnp.int32, (lanes, lanes), 0)
    j = lax.broadcasted_iota(jnp.int32, (lanes, lanes), 1)
    flip = ((i // cols == j // cols) & (i % cols + j % cols == cols - 1)).astype(F32).astype(BF16)

    def mirrored(part):
        turned = jnp.dot(flip, part[:, rows:], preferred_element_type=F32).astype(BF16)
        return jnp.dot(turned, mirror, preferred_element_type=F32)

    other = mirrored(upper.astype(F32).T.astype(BF16)) + mirrored(lower.astype(F32).T.astype(BF16))
    f_ref[:, :rows] = 0.5 * (whole[:cols, :rows] + other[:cols])
    f_ref[:, rows:] = 0.5 * (whole[cols:, :rows] - other[cols:])
    c, s = cs_ref[0], cs_ref[1]

    def contract(left, right):
        return lax.dot_general(
            left, right, (((0,), (0,)), ((), ())), precision=HIGH, preferred_element_type=F32
        )

    m_ref[...] = jnp.zeros_like(m_ref)
    for n, k in enumerate((0, rows)):
        e_re, e_im = whole[:cols, k : k + 1], whole[cols:, k : k + 1]
        u = c * e_re - s * e_im
        v = s * e_re + c * e_im
        g = contract(u, c) + contract(v, s)
        if n:
            g = g * twist_ref[0] - (contract(v, c) - contract(u, s)) * twist_ref[1]
        for start in (n * cols, lanes + n * cols):
            spot = slice(start, start + cols)
            m_ref[spot, spot] = g.astype(BF16)


def filter_part(z, gathered, cs, twist):
    chips = gathered.shape[0]
    cols = cs.shape[1]
    rows = chips * 16
    lanes = 2 * cols
    return pl.pallas_call(
        filter_kernel,
        grid_spec=pltpu.PrefetchScalarGridSpec(
            num_scalar_prefetch=1,
            grid=(1,),
            in_specs=[
                pl.BlockSpec((chips, 64, lanes), lambda i, z: (0, 8 + z[0], 0)),
                pl.BlockSpec(cs.shape, lambda i, z: (0, 0, 0)),
                pl.BlockSpec(twist.shape, lambda i, z: (0, 0, 0)),
            ],
            out_specs=[
                pl.BlockSpec((cols, 2 * rows), lambda i, z: (0, 0)),
                pl.BlockSpec((2 * lanes, 2 * lanes), lambda i, z: (0, 0)),
            ],
        ),
        out_shape=[
            jax.ShapeDtypeStruct((cols, 2 * rows), F32),
            jax.ShapeDtypeStruct((2 * lanes, 2 * lanes), BF16),
        ],
        compiler_params=pltpu.CompilerParams(vmem_limit_bytes=32 * 2**20),
        cost_estimate=pl.CostEstimate(flops=10**9, bytes_accessed=2**20, transcendentals=0),
        name="filter_part",
    )(z.reshape(1), gathered, cs, twist)


def conv_kernel(
    x_ref, fwd_hbm, inv_hbm, tw_hbm, a_ref, ai_ref, m_ref, f_ref, y_ref, fwd_ref, inv_ref, tw_ref, r_ref, q_ref, sems
):
    copies = [
        pltpu.make_async_copy(src, dst, sems.at[i])
        for i, (src, dst) in enumerate(((fwd_hbm, fwd_ref), (tw_hbm, tw_ref), (inv_hbm, inv_ref)))
    ]
    for copy in copies:
        copy.start()
    chips, chans, both = x_ref.shape
    rows = both // 2
    blocks = rows // 128
    half = 2 * chips
    copies[0].wait()
    for col in range(2):
        x = x_ref[:, :, col * rows : (col + 1) * rows].reshape(chips * chans, rows)
        r = jnp.dot(x, fwd_ref[0], preferred_element_type=F32)
        r += jnp.dot(x, fwd_ref[1], preferred_element_type=F32)
        r = r.reshape(chips, chans, 2 * rows)
        if col == 0:
            copies[1].wait()
        tw = tw_ref[col * chips : (col + 1) * chips, :]
        cos = tw[:, None, :rows]
        sin = tw[:, None, rows:]
        re, im = r[:, :, :rows], r[:, :, rows:]
        turned_re = (re * cos + im * sin).reshape(chips * chans, rows)
        turned_im = (im * cos - re * sin).reshape(chips * chans, rows)
        for k in range(blocks):
            r_ref[col, k] = turned_re[:, k * 128 : (k + 1) * 128]
            r_ref[col, blocks + k] = turned_im[:, k * 128 : (k + 1) * 128]
    lane = lax.broadcasted_iota(jnp.int32, (4 * half, 128), 1)

    def pair(n, carry):
        picks = [pl.ds(2 * n + i, chips, stride=chans) for i in range(2)]
        parts = [
            jnp.concatenate([r_ref[col, part * blocks + k, pick, :] for k in range(blocks)], axis=1)
            for pick in picks
            for part in range(2)
            for col in range(2)
        ]
        turned = jnp.concatenate(parts, axis=0).astype(BF16)
        s = jnp.dot(a_ref[...], turned, preferred_element_type=F32)
        f_re, f_im = f_ref[:, :rows], f_ref[:, rows:]
        filtered = []
        for i in range(2):
            s_re = s[2 * i * half : (2 * i + 1) * half]
            s_im = s[(2 * i + 1) * half : (2 * i + 2) * half]
            filtered += [s_re * f_re - s_im * f_im, s_re * f_im + s_im * f_re]
        filtered = jnp.concatenate(filtered, axis=0).astype(BF16)
        back = jnp.dot(ai_ref[...], filtered, preferred_element_type=F32)
        edge = jnp.dot(m_ref[...], turned[:, :128], preferred_element_type=F32)
        head = jnp.where(lane == 0, edge, back[:, :128])
        back = jnp.concatenate([head, back[:, 128:]], axis=1)
        cos, sin = tw_ref[:, :rows], tw_ref[:, rows:]
        for i, pick in enumerate(picks):
            b_re = back[2 * i * half : (2 * i + 1) * half]
            b_im = back[(2 * i + 1) * half : (2 * i + 2) * half]
            out_re = b_re * cos - b_im * sin
            out_im = b_im * cos + b_re * sin
            for col in range(2):
                part = slice(col * chips, (col + 1) * chips)
                for k in range(blocks):
                    q_ref[col, k, pick, :] = out_re[part, k * 128 : (k + 1) * 128]
                    q_ref[col, blocks + k, pick, :] = out_im[part, k * 128 : (k + 1) * 128]
        return carry

    lax.fori_loop(0, chans // 2, pair, 0, unroll=2)
    copies[2].wait()
    for col in range(2):
        q = jnp.concatenate([q_ref[col, k].astype(BF16) for k in range(2 * blocks)], axis=1)
        y = jnp.dot(q, inv_ref[0], preferred_element_type=F32)
        y += jnp.dot(q, inv_ref[1], preferred_element_type=F32)
        y_ref[:, :, col * rows : (col + 1) * rows] = y.astype(BF16).reshape(chips, chans, rows)


def long_conv(x, fwd, inv, tw, a, ai, m, f):
    chips, chans, both = x.shape
    vmem = pl.BlockSpec(memory_space=pltpu.VMEM)
    hbm = pl.BlockSpec(memory_space=pl.ANY)
    return pl.pallas_call(
        conv_kernel,
        in_specs=[vmem, hbm, hbm, hbm, vmem, vmem, vmem, vmem],
        out_specs=vmem,
        out_shape=jax.ShapeDtypeStruct(x.shape, BF16),
        scratch_shapes=[
            pltpu.VMEM(fwd.shape, BF16),
            pltpu.VMEM(inv.shape, BF16),
            pltpu.VMEM(tw.shape, F32),
            pltpu.VMEM((2, both // 128, chips * chans, 128), F32),
            pltpu.VMEM((2, both // 128, chips * chans, 128), F32),
            pltpu.SemaphoreType.DMA((3,)),
        ],
        compiler_params=pltpu.CompilerParams(vmem_limit_bytes=48 * 2**20),
        cost_estimate=pl.CostEstimate(flops=8 * 10**9, bytes_accessed=8 * 2**20, transcendentals=0),
        name="long_conv",
    )(x, fwd, inv, tw, a, ai, m, f)


def cos_sin(product, modulus):
    phase = (product % modulus).astype(F32) * (2.0 * math.pi / modulus)
    return jnp.cos(phase), jnp.sin(phase)


def twice(t):
    zero = jnp.zeros_like(t)
    return jnp.block([[t, zero], [zero, t]])


def column_tables(core, rows, cols, padded):
    i = lax.iota(jnp.int32, cols)
    b = 2 * (i % CHIPS) + ((i // CHIPS) ^ core)
    k1 = lax.iota(jnp.int32, rows)
    tw = jnp.concatenate(cos_sin(b[:, None] * k1[None, :], padded), axis=1)
    k2 = lax.iota(jnp.int32, cols)
    c, s = cos_sin(k2[:, None] * b[None, :], cols)
    a = jnp.block([[c, s], [-s, c]])
    twist = jnp.stack(cos_sin(jnp.mod((b[:, None] - b[None, :]) * rows, padded), padded))

    return tw, twice(a.astype(BF16)), twice(a.T.astype(BF16)), jnp.stack([c, s]), twist


def gather_line(block, axis):
    d1 = send(block, **{axis: -1})
    d3 = send(block, **{axis: 1})
    d2 = send(block, **{axis: 2})
    return jnp.concatenate([block, d1, d2, d3], axis=0)


def gather_lines(line, axis):
    e1 = send(line, **{axis: -1})
    e3 = send(line, **{axis: 1})
    half = line.shape[0] // 2
    e2a = send(e1[:half], **{axis: -1})
    e2b = send(e3[half:], **{axis: 1})
    return line, e1, e2a, e2b, e3


def per_device(tokens, in_weight, filter_spectrum, skip_bias, out_weight):
    rows, _, width = tokens.shape
    cols = SEQ
    padded = 2 * rows * cols
    s = lax.axis_index("seq")
    h = lax.axis_index("ch")
    z, y, x, core = coords(s)
    chan = in_weight.shape[2] // 2
    depth = in_weight.shape[0]

    mine = tokens.reshape(rows, width)
    filt = jnp.transpose(filter_spectrum, (3, 1, 0, 2)).reshape(4, 1, -1, 2 * cols)
    filt = jnp.concatenate(split_table(filt), axis=1).reshape(4, -1, 2 * cols)

    def half_for(c):
        w = lax.dynamic_slice_in_dim(in_weight, c * chan, chan, 2)
        f = lax.dynamic_slice_in_dim(filt, 2 * c, 2, 0)
        g = jnp.concatenate([w[:, 0, i * 128 : (i + 1) * 128] for i in range(chan // 128)], axis=0)
        return jnp.concatenate([w[:, 1], w[:, 2]], axis=0), g.reshape(-1, depth, 128), f

    keep, keep_g, keep_f = half_for(core)
    give, give_g, give_f = half_for(1 - core)
    near_g = send(jnp.concatenate([give_g.reshape(-1, 128), give_f.reshape(-1, 128)], axis=0), dc=1)
    near = send(give, dc=1)
    far = send(keep, dz=1)
    far_near = send(give, dz=1, dc=1)
    other = send(mine, dc=1)

    def ordered(own, partner, axis=0):
        return jnp.concatenate(
            [jnp.where(core == 0, own, partner), jnp.where(core == 0, partner, own)], axis=axis
        )

    key_block = jnp.concatenate(
        [ordered(keep[:depth], near[:depth]), ordered(far[:depth], far_near[:depth])], axis=0
    )
    value_block = jnp.concatenate(
        [ordered(keep[depth:], near[depth:]), ordered(far[depth:], far_near[depth:])], axis=0
    )
    cut = 4 * depth
    gate_block = jnp.concatenate(
        [
            ordered(keep_g, near_g[:cut].reshape(keep_g.shape), 1).reshape(-1, 128),
            ordered(keep_f, near_g[cut:].reshape(keep_f.shape), 1).reshape(-1, 128),
        ],
        axis=0,
    )
    gathered = lax.all_gather(gate_block, "seq", axis=0, axis_index_groups=SAME_CORE)
    key_line, value_line, late = lax.optimization_barrier(
        (gather_line(key_block, "dx"), gather_line(value_block, "dy"), core)
    )
    half_ow = out_weight.shape[0] // 2
    ow_part = lax.dynamic_slice_in_dim(out_weight, late * half_ow, half_ow, 0)
    key_pieces = gather_lines(key_line, "dy")
    value_pieces = gather_lines(value_line, "dx")

    order = np.arange(32)
    p_, q_, dz = order // 8, (order // 2) % 4, order % 2
    key_order = ((z ^ dz) * 4 + (y + p_) % 4) * 4 + (x + q_) % 4
    value_order = ((z ^ dz) * 4 + (y + q_) % 4) * 4 + (x + p_) % 4
    first = first_part(jnp.stack([key_order, value_order]), mine, other, key_pieces, value_pieces)

    perm = []
    for t in range(SEQ):
        tz, ty, tx, tc = coords(t)
        for th in range(2):
            perm.append((t * 2 + th, index_of(tz ^ tc, ty, tx, tc) * 2 + 1 - th))
    ow_same = lax.ppermute(ow_part, ("seq", "ch"), perm)
    ow_cross = send(ow_same, dc=1)

    source, packed = last_part(first, key_pieces, value_pieces)
    packed = packed.reshape(CHIPS, chan // CHIPS, 2 * rows)
    mine_ch = lax.all_to_all(packed, "seq", 0, 0, axis_index_groups=SAME_CORE)

    tw, a, ai, cs, twist = column_tables(core, rows, cols, padded)
    f, m = filter_part(z, gathered, cs, twist)
    forward, inverse = row_tables(rows, padded)
    fwd = jnp.asarray(np.stack(split_np(forward)))
    inv = jnp.asarray(np.stack(split_np(inverse)))
    conv = long_conv(mine_ch, fwd, inv, tw, a, ai, m, f)
    conv = lax.all_to_all(conv, "seq", 0, 0, axis_index_groups=SAME_CORE)
    conv = conv.reshape(chan, 2 * rows).astype(F32)

    gate = gate_part(mine, other, gathered).astype(F32)
    skip = lax.dynamic_slice_in_dim(skip_bias, core * chan, chan, 0)[:, None]
    gated = (gate * (conv + skip * source)).astype(BF16)

    kept = rows // 2
    own_here = lax.dynamic_slice(gated, (0, h * kept), (chan, kept))
    own_there = lax.dynamic_slice(gated, (0, (1 - h) * kept), (chan, kept))
    oth_here = lax.dynamic_slice(gated, (0, rows + h * kept), (chan, kept))
    oth_there = lax.dynamic_slice(gated, (0, rows + (1 - h) * kept), (chan, kept))
    swap_ch = [(0, 1), (1, 0)]
    from_h = lax.ppermute(own_there, "ch", swap_ch)
    perm2 = []
    for t in range(SEQ):
        for th in range(2):
            perm2.append((t * 2 + th, (t ^ 1) * 2 + 1 - th))
    from_hc = lax.ppermute(oth_there, ("seq", "ch"), perm2)
    from_c = send(oth_here, dc=1)
    here = ordered(own_here, from_c)

    mixed = mix_part(None, [here], [out_weight])
    mixed = mix_part(mixed, [from_h, from_hc], [ow_same, ow_cross])
    return mixed.reshape(kept, 1, width)


def solution(mesh):
    in_specs = (
        P(None, "seq", None),
        P("seq", None, "ch"),
        P(None, "seq", None, "ch"),
        P("ch"),
        P("ch", None),
    )
    return jax.shard_map(
        per_device, mesh=mesh, in_specs=in_specs, out_specs=P("ch", "seq", None), check_vma=False
    )
```

```python
import functools
import math

import jax
import jax.numpy as jnp
import ml_dtypes
import numpy as np
from jax import lax
from jax.experimental import pallas as pl
from jax.experimental.pallas import tpu as pltpu
from jax.sharding import PartitionSpec as P

BF16 = jnp.bfloat16
F32 = jnp.float32
HIGH = lax.Precision.HIGHEST
SEQ = 64
VMEM = 60 * 2**20
CHIPS = 32
SAME_CORE = [[2 * p + j for p in range(CHIPS)] for j in range(2)]


def coords(s):
    return s // 32, (s // 8) % 4, (s // 2) % 4, s % 2


def index_of(z, y, x, c):
    return ((z * 4 + y) * 4 + x) * 2 + c


def send(value, dz=0, dy=0, dx=0, dc=0):
    perm = []
    for s in range(SEQ):
        z, y, x, c = coords(s)
        perm.append((s, index_of((z + dz) % 2, (y + dy) % 4, (x + dx) % 4, c ^ dc)))
    return lax.ppermute(value, "seq", perm)


def split_np(table):
    upper = table.astype(np.float32).astype(ml_dtypes.bfloat16)
    lower = (table - upper.astype(np.float64)).astype(np.float32).astype(ml_dtypes.bfloat16)
    return upper, lower


def split_table(table):
    upper = table.astype(BF16)
    lower = (table - upper.astype(F32)).astype(BF16)
    return upper, lower


def row_tables(rows, padded):
    points = 2 * rows
    a = np.arange(rows)
    k = np.arange(rows)
    phase = 2.0 * np.pi * ((a[:, None] * k[None, :]) % points) / points
    re, im = np.cos(phase), -np.sin(phase)
    im[:, 0] = np.where(a % 2 == 0, 1.0, -1.0)
    forward = np.concatenate([re, im], axis=1)
    scale = np.full((rows,), 2.0)
    scale[0] = 1.0
    inverse = np.concatenate([re * scale, im * scale], axis=1).T / padded
    return forward, inverse


def picked(order_ref, row, group, tok_ref):
    blocks = [
        tok_ref[:, pl.ds(pl.multiple_of(order_ref[row, group * 8 + i] * 128, 128), 128)]
        for i in range(8)
    ]
    return jnp.concatenate(blocks, axis=1)


def first_kernel(order_ref, mine_ref, other_ref, *refs):
    weights, (key_ref, value_ref, key_tok_ref, value_tok_ref) = refs[:6], refs[6:]

    def run(tok_ref):
        for row, total_ref, last_ref in ((0, key_ref, key_tok_ref), (1, value_ref, value_tok_ref)):
            line, e1, e3 = weights[3 * row : 3 * row + 3]
            total = jnp.dot(picked(order_ref, row, 0, tok_ref), line[...], preferred_element_type=F32)
            total += jnp.dot(picked(order_ref, row, 1, tok_ref), e1[...], preferred_element_type=F32)
            total += jnp.dot(picked(order_ref, row, 3, tok_ref), e3[...], preferred_element_type=F32)
            total_ref[...] = total
            last_ref[...] = picked(order_ref, row, 2, tok_ref)

    step = pl.program_id(0)

    @pl.when(step < 2)
    def _():
        run(mine_ref)

    @pl.when(step >= 2)
    def _():
        run(other_ref)


def first_part(order, mine, other, key_pieces, value_pieces):
    rows, width = mine.shape
    chan = key_pieces[0].shape[1]
    tile = rows // 2
    weights = [key_pieces[0], key_pieces[1], key_pieces[4]]
    weights += [value_pieces[0], value_pieces[1], value_pieces[4]]
    quarter = width // 4
    return pl.pallas_call(
        first_kernel,
        grid_spec=pltpu.PrefetchScalarGridSpec(
            num_scalar_prefetch=1,
            grid=(4,),
            in_specs=[
                pl.BlockSpec((tile, width), lambda i, o: (jnp.minimum(i, 1), 0)),
                pl.BlockSpec((tile, width), lambda i, o: (jnp.maximum(i - 2, 0), 0)),
            ]
            + [pl.BlockSpec((quarter, chan), lambda i, o: (0, 0))] * 6,
            out_specs=[
                pl.BlockSpec((tile, chan), lambda i, o: (i, 0)),
                pl.BlockSpec((tile, chan), lambda i, o: (i, 0)),
                pl.BlockSpec((tile, quarter), lambda i, o: (i, 0)),
                pl.BlockSpec((tile, quarter), lambda i, o: (i, 0)),
            ],
        ),
        out_shape=[jax.ShapeDtypeStruct((2 * rows, chan), F32)] * 2
        + [jax.ShapeDtypeStruct((2 * rows, quarter), BF16)] * 2,
        compiler_params=pltpu.CompilerParams(vmem_limit_bytes=VMEM),
        cost_estimate=pl.CostEstimate(
            flops=2 * 2 * 2 * rows * 3 * quarter * chan, bytes_accessed=22 * 2**20, transcendentals=0
        ),
        name="first_part",
    )(order, mine, other, *weights)


def last_kernel(key_ref, value_ref, key_tok_ref, value_tok_ref, ka, kb, va, vb, out_ref, send_ref):
    half = ka.shape[0]

    def finish(total_ref, tok_ref, wa, wb):
        total = total_ref[...]
        total += jnp.dot(tok_ref[:, :half], wa[...], preferred_element_type=F32)
        total += jnp.dot(tok_ref[:, half:], wb[...], preferred_element_type=F32)
        return total.astype(BF16).astype(F32)

    source = finish(key_ref, key_tok_ref, ka, kb) * finish(value_ref, value_tok_ref, va, vb)
    source = source.T
    out_ref[...] = source
    send_ref[...] = source.astype(BF16)


def last_part(first, key_pieces, value_pieces):
    total, chan = first[0].shape
    quarter = first[2].shape[1]
    tile = total // 4
    weights = [*key_pieces[2:4], *value_pieces[2:4]]
    return pl.pallas_call(
        last_kernel,
        grid=(4,),
        in_specs=[pl.BlockSpec((tile, chan), lambda i: (i, 0))] * 2
        + [pl.BlockSpec((tile, quarter), lambda i: (i, 0))] * 2
        + [pl.BlockSpec((quarter // 2, chan), lambda i: (0, 0))] * 4,
        out_specs=[pl.BlockSpec((chan, tile), lambda i: (0, i))] * 2,
        out_shape=[
            jax.ShapeDtypeStruct((chan, total), F32),
            jax.ShapeDtypeStruct((chan, total), BF16),
        ],
        compiler_params=pltpu.CompilerParams(vmem_limit_bytes=VMEM),
        cost_estimate=pl.CostEstimate(
            flops=2 * 2 * total * quarter * chan, bytes_accessed=13 * 2**20, transcendentals=0
        ),
        name="last_part",
    )(*first, *weights)


def gate_kernel(mine_ref, other_ref, weight_ref, out_ref):
    step = pl.program_id(0)
    chips, deep, _ = weight_ref.shape
    depth = deep // 4

    def run(tok_ref):
        for k in range(0, 4, 2):
            parts = [
                weight_ref[:, i * depth : (i + 1) * depth, :].reshape(chips * depth, 128)
                for i in (k, k + 1)
            ]
            weight = jnp.concatenate(parts, axis=1)
            gate = jnp.dot(tok_ref[...], weight, preferred_element_type=F32)
            out_ref[k * 128 : (k + 2) * 128, :] = gate.T.astype(BF16)

    @pl.when(step < 2)
    def _():
        run(mine_ref)

    @pl.when(step >= 2)
    def _():
        run(other_ref)


def gate_part(mine, other, gathered):
    rows, width = mine.shape
    chips = gathered.shape[0]
    depth = width // chips
    chan = 4 * 128
    tile = rows // 2
    return pl.pallas_call(
        gate_kernel,
        grid=(4,),
        in_specs=[
            pl.BlockSpec((tile, width), lambda i: (jnp.minimum(i, 1), 0)),
            pl.BlockSpec((tile, width), lambda i: (jnp.maximum(i - 2, 0), 0)),
            pl.BlockSpec((chips, 4 * depth, 128), lambda i: (0, 0, 0)),
        ],
        out_specs=pl.BlockSpec((chan, tile), lambda i: (0, i)),
        out_shape=jax.ShapeDtypeStruct((chan, 2 * rows), BF16),
        compiler_params=pltpu.CompilerParams(vmem_limit_bytes=VMEM),
        cost_estimate=pl.CostEstimate(
            flops=2 * 2 * rows * width * chan, bytes_accessed=13 * 2**20, transcendentals=0
        ),
        name="gate_part",
    )(mine, other, gathered)


def turn(ref):
    return ref[...].astype(F32).T.astype(BF16)


def mix_kernel(here, w_here, out_ref, lhs_ref):
    @pl.when(pl.program_id(0) == 0)
    def _():
        lhs_ref[...] = turn(here)

    out_ref[...] = jnp.dot(lhs_ref[...], w_here[...], preferred_element_type=F32)


def mix_more_kernel(total_ref, near_h, far_h, w_near, w_far, out_ref, lhs_ref):
    m = near_h.shape[0]

    @pl.when(pl.program_id(0) == 0)
    def _():
        lhs_ref[:, :m] = turn(near_h)
        lhs_ref[:, m:] = turn(far_h)

    total = total_ref[...]
    total += jnp.dot(lhs_ref[:, :m], w_near[...], preferred_element_type=F32)
    total += jnp.dot(lhs_ref[:, m:], w_far[...], preferred_element_type=F32)
    out_ref[...] = total.astype(BF16)


def mix_part(total, parts, weights):
    rows = parts[0].shape[1]
    width = weights[0].shape[1]
    tile = width // 4
    depth = sum(p.shape[0] for p in parts)
    totals = [] if total is None else [total]

    def whole(g):
        return pl.BlockSpec(g.shape, lambda i: (0, 0))

    def tiled(w):
        return pl.BlockSpec((w.shape[0], tile), lambda i: (0, i))

    return pl.pallas_call(
        mix_kernel if total is None else mix_more_kernel,
        grid=(4,),
        in_specs=[tiled(t) for t in totals] + [whole(p) for p in parts] + [tiled(w) for w in weights],
        out_specs=pl.BlockSpec((rows, tile), lambda i: (0, i)),
        out_shape=jax.ShapeDtypeStruct((rows, width), F32 if total is None else BF16),
        scratch_shapes=[pltpu.VMEM((rows, depth), BF16)],
        compiler_params=pltpu.CompilerParams(vmem_limit_bytes=VMEM),
        cost_estimate=pl.CostEstimate(
            flops=2 * rows * depth * width, bytes_accessed=12 * 2**20, transcendentals=0
        ),
        name="mix_part" if total is None else "mix_more",
    )(*totals, *parts, *weights)


def filter_kernel(z_ref, x_ref, cs_ref, twist_ref, f_ref, m_ref):
    chips, _, lanes = x_ref.shape
    x = x_ref[...].reshape(2 * chips, 2, 16, lanes)
    points = 2 * chips * 16
    rows, cols = points // 2, lanes // 2
    upper = x[:, 0].reshape(points, lanes)
    lower = x[:, 1].reshape(points, lanes)
    whole = (upper.astype(F32) + lower.astype(F32)).T
    i = lax.broadcasted_iota(jnp.int32, (rows, rows), 0)
    j = lax.broadcasted_iota(jnp.int32, (rows, rows), 1)
    mirror = (i + j == rows).astype(F32).astype(BF16)
    i = lax.broadcasted_iota(jnp.int32, (lanes, lanes), 0)
    j = lax.broadcasted_iota(jnp.int32, (lanes, lanes), 1)
    flip = ((i // cols == j // cols) & (i % cols + j % cols == cols - 1)).astype(F32).astype(BF16)

    def mirrored(part):
        turned = jnp.dot(flip, part[:, rows:], preferred_element_type=F32).astype(BF16)
        return jnp.dot(turned, mirror, preferred_element_type=F32)

    other = mirrored(upper.astype(F32).T.astype(BF16)) + mirrored(lower.astype(F32).T.astype(BF16))
    f_ref[:, :rows] = 0.5 * (whole[:cols, :rows] + other[:cols])
    f_ref[:, rows:] = 0.5 * (whole[cols:, :rows] - other[cols:])
    c, s = cs_ref[0], cs_ref[1]

    def contract(left, right):
        return lax.dot_general(
            left, right, (((0,), (0,)), ((), ())), precision=HIGH, preferred_element_type=F32
        )

    m_ref[...] = jnp.zeros_like(m_ref)
    for n, k in enumerate((0, rows)):
        e_re, e_im = whole[:cols, k : k + 1], whole[cols:, k : k + 1]
        u = c * e_re - s * e_im
        v = s * e_re + c * e_im
        g = contract(u, c) + contract(v, s)
        if n:
            g = g * twist_ref[0] - (contract(v, c) - contract(u, s)) * twist_ref[1]
        for start in (n * cols, lanes + n * cols):
            spot = slice(start, start + cols)
            m_ref[spot, spot] = g.astype(BF16)


def filter_part(z, gathered, cs, twist):
    chips = gathered.shape[0]
    cols = cs.shape[1]
    rows = chips * 16
    lanes = 2 * cols
    return pl.pallas_call(
        filter_kernel,
        grid_spec=pltpu.PrefetchScalarGridSpec(
            num_scalar_prefetch=1,
            grid=(1,),
            in_specs=[
                pl.BlockSpec((chips, 64, lanes), lambda i, z: (0, 8 + z[0], 0)),
                pl.BlockSpec(cs.shape, lambda i, z: (0, 0, 0)),
                pl.BlockSpec(twist.shape, lambda i, z: (0, 0, 0)),
            ],
            out_specs=[
                pl.BlockSpec((cols, 2 * rows), lambda i, z: (0, 0)),
                pl.BlockSpec((2 * lanes, 2 * lanes), lambda i, z: (0, 0)),
            ],
        ),
        out_shape=[
            jax.ShapeDtypeStruct((cols, 2 * rows), F32),
            jax.ShapeDtypeStruct((2 * lanes, 2 * lanes), BF16),
        ],
        compiler_params=pltpu.CompilerParams(vmem_limit_bytes=VMEM),
        cost_estimate=pl.CostEstimate(flops=10**9, bytes_accessed=2**20, transcendentals=0),
        name="filter_part",
    )(z.reshape(1), gathered, cs, twist)


def conv_kernel(
    x_ref, fwd_hbm, inv_hbm, tw_hbm, a_ref, ai_ref, m_ref, f_ref, y_ref, fwd_ref, inv_ref, tw_ref, r_ref, q_ref, sems
):
    copies = [
        pltpu.make_async_copy(src, dst, sems.at[i])
        for i, (src, dst) in enumerate(((fwd_hbm, fwd_ref), (tw_hbm, tw_ref), (inv_hbm, inv_ref)))
    ]
    for copy in copies:
        copy.start()
    chips, chans, both = x_ref.shape
    rows = both // 2
    blocks = rows // 128
    half = 2 * chips
    copies[0].wait()
    for col in range(2):
        x = x_ref[:, :, col * rows : (col + 1) * rows].reshape(chips * chans, rows)
        r = jnp.dot(x, fwd_ref[0], preferred_element_type=F32)
        r += jnp.dot(x, fwd_ref[1], preferred_element_type=F32)
        r = r.reshape(chips, chans, 2 * rows)
        if col == 0:
            copies[1].wait()
        tw = tw_ref[col * chips : (col + 1) * chips, :]
        cos = tw[:, None, :rows]
        sin = tw[:, None, rows:]
        re, im = r[:, :, :rows], r[:, :, rows:]
        turned_re = (re * cos + im * sin).reshape(chips * chans, rows)
        turned_im = (im * cos - re * sin).reshape(chips * chans, rows)
        for k in range(blocks):
            r_ref[col, k] = turned_re[:, k * 128 : (k + 1) * 128]
            r_ref[col, blocks + k] = turned_im[:, k * 128 : (k + 1) * 128]
    lane = lax.broadcasted_iota(jnp.int32, (4 * half, 128), 1)

    def pair(n, carry):
        picks = [pl.ds(2 * n + i, chips, stride=chans) for i in range(2)]
        parts = [
            jnp.concatenate([r_ref[col, part * blocks + k, pick, :] for k in range(blocks)], axis=1)
            for pick in picks
            for part in range(2)
            for col in range(2)
        ]
        turned = jnp.concatenate(parts, axis=0).astype(BF16)
        s = jnp.dot(a_ref[...], turned, preferred_element_type=F32)
        f_re, f_im = f_ref[:, :rows], f_ref[:, rows:]
        filtered = []
        for i in range(2):
            s_re = s[2 * i * half : (2 * i + 1) * half]
            s_im = s[(2 * i + 1) * half : (2 * i + 2) * half]
            filtered += [s_re * f_re - s_im * f_im, s_re * f_im + s_im * f_re]
        filtered = jnp.concatenate(filtered, axis=0).astype(BF16)
        back = jnp.dot(ai_ref[...], filtered, preferred_element_type=F32)
        edge = jnp.dot(m_ref[...], turned[:, :128], preferred_element_type=F32)
        head = jnp.where(lane == 0, edge, back[:, :128])
        back = jnp.concatenate([head, back[:, 128:]], axis=1)
        cos, sin = tw_ref[:, :rows], tw_ref[:, rows:]
        for i, pick in enumerate(picks):
            b_re = back[2 * i * half : (2 * i + 1) * half]
            b_im = back[(2 * i + 1) * half : (2 * i + 2) * half]
            out_re = b_re * cos - b_im * sin
            out_im = b_im * cos + b_re * sin
            for col in range(2):
                part = slice(col * chips, (col + 1) * chips)
                for k in range(blocks):
                    q_ref[col, k, pick, :] = out_re[part, k * 128 : (k + 1) * 128]
                    q_ref[col, blocks + k, pick, :] = out_im[part, k * 128 : (k + 1) * 128]
        return carry

    lax.fori_loop(0, chans // 2, pair, 0, unroll=2)
    copies[2].wait()
    for col in range(2):
        q = jnp.concatenate([q_ref[col, k].astype(BF16) for k in range(2 * blocks)], axis=1)
        y = jnp.dot(q, inv_ref[0], preferred_element_type=F32)
        y += jnp.dot(q, inv_ref[1], preferred_element_type=F32)
        y_ref[:, :, col * rows : (col + 1) * rows] = y.astype(BF16).reshape(chips, chans, rows)


def long_conv(x, fwd, inv, tw, a, ai, m, f):
    chips, chans, both = x.shape
    vmem = pl.BlockSpec(memory_space=pltpu.VMEM)
    hbm = pl.BlockSpec(memory_space=pl.ANY)
    return pl.pallas_call(
        conv_kernel,
        in_specs=[vmem, hbm, hbm, hbm, vmem, vmem, vmem, vmem],
        out_specs=vmem,
        out_shape=jax.ShapeDtypeStruct(x.shape, BF16),
        scratch_shapes=[
            pltpu.VMEM(fwd.shape, BF16),
            pltpu.VMEM(inv.shape, BF16),
            pltpu.VMEM(tw.shape, F32),
            pltpu.VMEM((2, both // 128, chips * chans, 128), F32),
            pltpu.VMEM((2, both // 128, chips * chans, 128), F32),
            pltpu.SemaphoreType.DMA((3,)),
        ],
        compiler_params=pltpu.CompilerParams(vmem_limit_bytes=VMEM),
        cost_estimate=pl.CostEstimate(flops=8 * 10**9, bytes_accessed=8 * 2**20, transcendentals=0),
        name="long_conv",
    )(x, fwd, inv, tw, a, ai, m, f)


def cos_sin(product, modulus):
    phase = (product % modulus).astype(F32) * (2.0 * math.pi / modulus)
    return jnp.cos(phase), jnp.sin(phase)


def twice(t):
    zero = jnp.zeros_like(t)
    return jnp.block([[t, zero], [zero, t]])


def column_tables(core, rows, cols, padded):
    i = lax.iota(jnp.int32, cols)
    b = 2 * (i % CHIPS) + ((i // CHIPS) ^ core)
    k1 = lax.iota(jnp.int32, rows)
    tw = jnp.concatenate(cos_sin(b[:, None] * k1[None, :], padded), axis=1)
    k2 = lax.iota(jnp.int32, cols)
    c, s = cos_sin(k2[:, None] * b[None, :], cols)
    a = jnp.block([[c, s], [-s, c]])
    twist = jnp.stack(cos_sin(jnp.mod((b[:, None] - b[None, :]) * rows, padded), padded))

    return tw, twice(a.astype(BF16)), twice(a.T.astype(BF16)), jnp.stack([c, s]), twist


def gather_line(block, axis):
    d1 = send(block, **{axis: -1})
    d3 = send(block, **{axis: 1})
    d2 = send(block, **{axis: 2})
    return jnp.concatenate([block, d1, d2, d3], axis=0)


def gather_lines(line, axis):
    e1 = send(line, **{axis: -1})
    e3 = send(line, **{axis: 1})
    half = line.shape[0] // 2
    e2a = send(e1[:half], **{axis: -1})
    e2b = send(e3[half:], **{axis: 1})
    return line, e1, e2a, e2b, e3


def per_device(tokens, in_weight, filter_spectrum, skip_bias, out_weight):
    rows, _, width = tokens.shape
    cols = SEQ
    padded = 2 * rows * cols
    s = lax.axis_index("seq")
    h = lax.axis_index("ch")
    z, y, x, core = coords(s)
    chan = in_weight.shape[2] // 2
    depth = in_weight.shape[0]

    mine = tokens.reshape(rows, width)
    filt = jnp.transpose(filter_spectrum, (3, 1, 0, 2)).reshape(4, 1, -1, 2 * cols)
    filt = jnp.concatenate(split_table(filt), axis=1).reshape(4, -1, 2 * cols)

    def half_for(c):
        w = lax.dynamic_slice_in_dim(in_weight, c * chan, chan, 2)
        f = lax.dynamic_slice_in_dim(filt, 2 * c, 2, 0)
        g = jnp.concatenate([w[:, 0, i * 128 : (i + 1) * 128] for i in range(chan // 128)], axis=0)
        return jnp.concatenate([w[:, 1], w[:, 2]], axis=0), g.reshape(-1, depth, 128), f

    keep, keep_g, keep_f = half_for(core)
    give, give_g, give_f = half_for(1 - core)
    near_g = send(jnp.concatenate([give_g.reshape(-1, 128), give_f.reshape(-1, 128)], axis=0), dc=1)
    near = send(give, dc=1)
    far = send(keep, dz=1)
    far_near = send(give, dz=1, dc=1)
    other = send(mine, dc=1)

    def ordered(own, partner, axis=0):
        return jnp.concatenate(
            [jnp.where(core == 0, own, partner), jnp.where(core == 0, partner, own)], axis=axis
        )

    key_block = jnp.concatenate(
        [ordered(keep[:depth], near[:depth]), ordered(far[:depth], far_near[:depth])], axis=0
    )
    value_block = jnp.concatenate(
        [ordered(keep[depth:], near[depth:]), ordered(far[depth:], far_near[depth:])], axis=0
    )
    cut = 4 * depth
    gate_block = jnp.concatenate(
        [
            ordered(keep_g, near_g[:cut].reshape(keep_g.shape), 1).reshape(-1, 128),
            ordered(keep_f, near_g[cut:].reshape(keep_f.shape), 1).reshape(-1, 128),
        ],
        axis=0,
    )
    gathered = lax.all_gather(gate_block, "seq", axis=0, axis_index_groups=SAME_CORE)
    key_block, value_block, other = lax.optimization_barrier((key_block, value_block, other))
    key_line, value_line, late = lax.optimization_barrier(
        (gather_line(key_block, "dx"), gather_line(value_block, "dy"), core)
    )
    half_ow = out_weight.shape[0] // 2
    ow_part = lax.dynamic_slice_in_dim(out_weight, late * half_ow, half_ow, 0)
    key_pieces = gather_lines(key_line, "dy")
    value_pieces = gather_lines(value_line, "dx")

    order = np.arange(32)
    p_, q_, dz = order // 8, (order // 2) % 4, order % 2
    key_order = ((z ^ dz) * 4 + (y + p_) % 4) * 4 + (x + q_) % 4
    value_order = ((z ^ dz) * 4 + (y + q_) % 4) * 4 + (x + p_) % 4
    first = first_part(jnp.stack([key_order, value_order]), mine, other, key_pieces, value_pieces)

    perm = []
    for t in range(SEQ):
        tz, ty, tx, tc = coords(t)
        for th in range(2):
            perm.append((t * 2 + th, index_of(tz ^ tc, ty, tx, tc) * 2 + 1 - th))
    ow_same = lax.ppermute(ow_part, ("seq", "ch"), perm)
    ow_cross = send(ow_same, dc=1)

    source, packed = last_part(first, key_pieces, value_pieces)
    packed = packed.reshape(CHIPS, chan // CHIPS, 2 * rows)
    mine_ch = lax.all_to_all(packed, "seq", 0, 0, axis_index_groups=SAME_CORE)

    tw, a, ai, cs, twist = column_tables(core, rows, cols, padded)
    f, m = filter_part(z, gathered, cs, twist)
    forward, inverse = row_tables(rows, padded)
    fwd = jnp.asarray(np.stack(split_np(forward)))
    inv = jnp.asarray(np.stack(split_np(inverse)))
    conv = long_conv(mine_ch, fwd, inv, tw, a, ai, m, f)
    conv = lax.all_to_all(conv, "seq", 0, 0, axis_index_groups=SAME_CORE)
    conv = conv.reshape(chan, 2 * rows).astype(F32)

    gate = gate_part(mine, other, gathered).astype(F32)
    skip = lax.dynamic_slice_in_dim(skip_bias, core * chan, chan, 0)[:, None]
    gated = (gate * (conv + skip * source)).astype(BF16)

    kept = rows // 2
    own_here = lax.dynamic_slice(gated, (0, h * kept), (chan, kept))
    own_there = lax.dynamic_slice(gated, (0, (1 - h) * kept), (chan, kept))
    oth_here = lax.dynamic_slice(gated, (0, rows + h * kept), (chan, kept))
    oth_there = lax.dynamic_slice(gated, (0, rows + (1 - h) * kept), (chan, kept))
    swap_ch = [(0, 1), (1, 0)]
    from_h = lax.ppermute(own_there, "ch", swap_ch)
    perm2 = []
    for t in range(SEQ):
        for th in range(2):
            perm2.append((t * 2 + th, (t ^ 1) * 2 + 1 - th))
    from_hc = lax.ppermute(oth_there, ("seq", "ch"), perm2)
    from_c = send(oth_here, dc=1)
    here = ordered(own_here, from_c)

    mixed = mix_part(None, [here], [out_weight])
    mixed = mix_part(mixed, [from_h, from_hc], [ow_same, ow_cross])
    return mixed.reshape(kept, 1, width)


def solution(mesh):
    in_specs = (
        P(None, "seq", None),
        P("seq", None, "ch"),
        P(None, "seq", None, "ch"),
        P("ch"),
        P("ch", None),
    )
    return jax.shard_map(
        per_device, mesh=mesh, in_specs=in_specs, out_specs=P("ch", "seq", None), check_vma=False
    )
```

```python
import functools
import math

import jax
import jax.numpy as jnp
import ml_dtypes
import numpy as np
from jax import lax
from jax.experimental import pallas as pl
from jax.experimental.pallas import tpu as pltpu
from jax.sharding import PartitionSpec as P

BF16 = jnp.bfloat16
F32 = jnp.float32
HIGH = lax.Precision.HIGHEST
SEQ = 64
VMEM = 60 * 2**20
CHIPS = 32
SAME_CORE = [[2 * p + j for p in range(CHIPS)] for j in range(2)]


def coords(s):
    return s // 32, (s // 8) % 4, (s // 2) % 4, s % 2


def index_of(z, y, x, c):
    return ((z * 4 + y) * 4 + x) * 2 + c


def send(value, dz=0, dy=0, dx=0, dc=0):
    perm = []
    for s in range(SEQ):
        z, y, x, c = coords(s)
        perm.append((s, index_of((z + dz) % 2, (y + dy) % 4, (x + dx) % 4, c ^ dc)))
    return lax.ppermute(value, "seq", perm)


def split_table(table):
    upper = table.astype(BF16)
    lower = (table - upper.astype(F32)).astype(BF16)
    return upper, lower


def row_tables(rows, padded):
    points = 2 * rows
    a = np.arange(rows)
    k = np.arange(rows)
    phase = 2.0 * np.pi * ((a[:, None] * k[None, :]) % points) / points
    re, im = np.cos(phase), -np.sin(phase)
    im[:, 0] = np.where(a % 2 == 0, 1.0, -1.0)
    forward = np.concatenate([re, im], axis=1)
    scale = np.full((rows,), 2.0)
    scale[0] = 1.0
    inverse = np.concatenate([re * scale, im * scale], axis=1).T / padded
    return forward, inverse


def picked(order_ref, row, group, tok_ref):
    blocks = [
        tok_ref[:, pl.ds(pl.multiple_of(order_ref[row, group * 8 + i] * 128, 128), 128)]
        for i in range(8)
    ]
    return jnp.concatenate(blocks, axis=1)


def by_column(run, mine_ref, other_ref):
    step = pl.program_id(0)

    @pl.when(step < 2)
    def _():
        run(mine_ref)

    @pl.when(step >= 2)
    def _():
        run(other_ref)


def first_kernel(order_ref, mine_ref, other_ref, key_line, value_line, *outs):
    key_ref, value_ref, key_tok_ref, value_tok_ref = outs

    def run(tok_ref):
        for row, line, total_ref, last_ref in (
            (0, key_line, key_ref, key_tok_ref),
            (1, value_line, value_ref, value_tok_ref),
        ):
            total_ref[...] = jnp.dot(
                picked(order_ref, row, 0, tok_ref), line[...], preferred_element_type=F32
            )
            last_ref[...] = picked(order_ref, row, 2, tok_ref)

    by_column(run, mine_ref, other_ref)


def second_kernel(order_ref, mine_ref, other_ref, key_in, value_in, k1, k3, v1, v3, key_ref, value_ref):
    def run(tok_ref):
        for row, before, e1, e3, total_ref in (
            (0, key_in, k1, k3, key_ref),
            (1, value_in, v1, v3, value_ref),
        ):
            total = before[...]
            total += jnp.dot(picked(order_ref, row, 1, tok_ref), e1[...], preferred_element_type=F32)
            total += jnp.dot(picked(order_ref, row, 3, tok_ref), e3[...], preferred_element_type=F32)
            total_ref[...] = total

    by_column(run, mine_ref, other_ref)


def sum_part(kernel, name, order, mine, other, totals, weights, last):
    rows, width = mine.shape
    chan = weights[0].shape[1]
    tile = rows // 2
    quarter = width // 4
    by_row = [pl.BlockSpec((tile, chan), lambda i, o: (i, 0))] * 2
    tokens_out = [pl.BlockSpec((tile, quarter), lambda i, o: (i, 0))] * 2
    shapes = [jax.ShapeDtypeStruct((2 * rows, chan), F32)] * 2
    token_shapes = [jax.ShapeDtypeStruct((2 * rows, quarter), BF16)] * 2
    return pl.pallas_call(
        kernel,
        grid_spec=pltpu.PrefetchScalarGridSpec(
            num_scalar_prefetch=1,
            grid=(4,),
            in_specs=[
                pl.BlockSpec((tile, width), lambda i, o: (jnp.minimum(i, 1), 0)),
                pl.BlockSpec((tile, width), lambda i, o: (jnp.maximum(i - 2, 0), 0)),
            ]
            + by_row[: len(totals)]
            + [pl.BlockSpec((quarter, chan), lambda i, o: (0, 0))] * len(weights),
            out_specs=by_row + (tokens_out if last else []),
        ),
        out_shape=shapes + (token_shapes if last else []),
        compiler_params=pltpu.CompilerParams(vmem_limit_bytes=VMEM),
        cost_estimate=pl.CostEstimate(
            flops=2 * 2 * rows * quarter * chan * len(weights), bytes_accessed=18 * 2**20, transcendentals=0
        ),
        name=name,
    )(order, mine, other, *totals, *weights)


def last_kernel(key_ref, value_ref, key_tok_ref, value_tok_ref, ka, kb, va, vb, out_ref, send_ref):
    half = ka.shape[0]

    def finish(total_ref, tok_ref, wa, wb):
        total = total_ref[...]
        total += jnp.dot(tok_ref[:, :half], wa[...], preferred_element_type=F32)
        total += jnp.dot(tok_ref[:, half:], wb[...], preferred_element_type=F32)
        return total.astype(BF16).astype(F32)

    source = finish(key_ref, key_tok_ref, ka, kb) * finish(value_ref, value_tok_ref, va, vb)
    source = source.T
    out_ref[...] = source
    send_ref[...] = source.astype(BF16)


def last_part(totals, tokens, weights):
    total, chan = totals[0].shape
    quarter = tokens[0].shape[1]
    tile = total // 4
    return pl.pallas_call(
        last_kernel,
        grid=(4,),
        in_specs=[pl.BlockSpec((tile, chan), lambda i: (i, 0))] * 2
        + [pl.BlockSpec((tile, quarter), lambda i: (i, 0))] * 2
        + [pl.BlockSpec((quarter // 2, chan), lambda i: (0, 0))] * 4,
        out_specs=[pl.BlockSpec((chan, tile), lambda i: (0, i))] * 2,
        out_shape=[
            jax.ShapeDtypeStruct((chan, total), F32),
            jax.ShapeDtypeStruct((chan, total), BF16),
        ],
        compiler_params=pltpu.CompilerParams(vmem_limit_bytes=VMEM),
        cost_estimate=pl.CostEstimate(
            flops=2 * 2 * total * quarter * chan, bytes_accessed=13 * 2**20, transcendentals=0
        ),
        name="last_part",
    )(*totals, *tokens, *weights)


def gate_kernel(mine_ref, other_ref, weight_ref, out_ref):
    chips, deep, chan = weight_ref.shape

    def run(tok_ref):
        weight = weight_ref[...].reshape(chips * deep, chan)
        gate = jnp.dot(tok_ref[...], weight, preferred_element_type=F32)
        out_ref[...] = gate.T.astype(BF16)

    by_column(run, mine_ref, other_ref)


def gate_part(mine, other, gathered):
    rows, width = mine.shape
    chips, _, chan = gathered.shape
    tile = rows // 2
    return pl.pallas_call(
        gate_kernel,
        grid=(4,),
        in_specs=[
            pl.BlockSpec((tile, width), lambda i: (jnp.minimum(i, 1), 0)),
            pl.BlockSpec((tile, width), lambda i: (jnp.maximum(i - 2, 0), 0)),
            pl.BlockSpec((chips, width // chips, chan), lambda i: (0, 0, 0)),
        ],
        out_specs=pl.BlockSpec((chan, tile), lambda i: (0, i)),
        out_shape=jax.ShapeDtypeStruct((chan, 2 * rows), BF16),
        compiler_params=pltpu.CompilerParams(vmem_limit_bytes=VMEM),
        cost_estimate=pl.CostEstimate(
            flops=2 * 2 * rows * width * chan, bytes_accessed=13 * 2**20, transcendentals=0
        ),
        name="gate_part",
    )(mine, other, gathered)


def turn(ref):
    return ref[...].astype(F32).T.astype(BF16)


def mix_kernel(here, w_here, out_ref, lhs_ref):
    @pl.when(pl.program_id(0) == 0)
    def _():
        lhs_ref[...] = turn(here)

    out_ref[...] = jnp.dot(lhs_ref[...], w_here[...], preferred_element_type=F32)


def mix_more_kernel(total_ref, near_h, far_h, w_near, w_far, out_ref, lhs_ref):
    m = near_h.shape[0]

    @pl.when(pl.program_id(0) == 0)
    def _():
        lhs_ref[:, :m] = turn(near_h)
        lhs_ref[:, m:] = turn(far_h)

    total = total_ref[...]
    total += jnp.dot(lhs_ref[:, :m], w_near[...], preferred_element_type=F32)
    total += jnp.dot(lhs_ref[:, m:], w_far[...], preferred_element_type=F32)
    out_ref[...] = total.astype(BF16)


def mix_part(total, parts, weights):
    rows = parts[0].shape[1]
    width = weights[0].shape[1]
    tile = width // 4
    depth = sum(p.shape[0] for p in parts)
    totals = [] if total is None else [total]

    def whole(g):
        return pl.BlockSpec(g.shape, lambda i: (0, 0))

    def tiled(w):
        return pl.BlockSpec((w.shape[0], tile), lambda i: (0, i))

    return pl.pallas_call(
        mix_kernel if total is None else mix_more_kernel,
        grid=(4,),
        in_specs=[tiled(t) for t in totals] + [whole(p) for p in parts] + [tiled(w) for w in weights],
        out_specs=pl.BlockSpec((rows, tile), lambda i: (0, i)),
        out_shape=jax.ShapeDtypeStruct((rows, width), F32 if total is None else BF16),
        scratch_shapes=[pltpu.VMEM((rows, depth), BF16)],
        compiler_params=pltpu.CompilerParams(vmem_limit_bytes=VMEM),
        cost_estimate=pl.CostEstimate(
            flops=2 * rows * depth * width, bytes_accessed=12 * 2**20, transcendentals=0
        ),
        name="mix_part" if total is None else "mix_more",
    )(*totals, *parts, *weights)


def filter_kernel(z_ref, x_ref, cs_ref, twist_ref, f_ref, m_ref):
    chips, _, lanes = x_ref.shape
    lanes = lanes // 2
    points = 2 * chips * 16
    rows, cols = points // 2, lanes // 2

    def part(n):
        rows_of = slice(16 * n, 16 * (n + 1))
        cores = [x_ref[:, rows_of, c * lanes : (c + 1) * lanes] for c in range(2)]
        return jnp.stack(cores, axis=1).reshape(points, lanes)

    upper, lower = part(0), part(1)
    whole = (upper.astype(F32) + lower.astype(F32)).T
    i = lax.broadcasted_iota(jnp.int32, (rows, rows), 0)
    j = lax.broadcasted_iota(jnp.int32, (rows, rows), 1)
    mirror = (i + j == rows).astype(F32).astype(BF16)
    i = lax.broadcasted_iota(jnp.int32, (lanes, lanes), 0)
    j = lax.broadcasted_iota(jnp.int32, (lanes, lanes), 1)
    flip = ((i // cols == j // cols) & (i % cols + j % cols == cols - 1)).astype(F32).astype(BF16)

    def mirrored(part):
        turned = jnp.dot(flip, part[:, rows:], preferred_element_type=F32).astype(BF16)
        return jnp.dot(turned, mirror, preferred_element_type=F32)

    other = mirrored(upper.astype(F32).T.astype(BF16)) + mirrored(lower.astype(F32).T.astype(BF16))
    f_ref[:, :rows] = 0.5 * (whole[:cols, :rows] + other[:cols])
    f_ref[:, rows:] = 0.5 * (whole[cols:, :rows] - other[cols:])
    c, s = cs_ref[0], cs_ref[1]

    def contract(left, right):
        return lax.dot_general(
            left, right, (((0,), (0,)), ((), ())), precision=HIGH, preferred_element_type=F32
        )

    m_ref[...] = jnp.zeros_like(m_ref)
    for n, k in enumerate((0, rows)):
        e_re, e_im = whole[:cols, k : k + 1], whole[cols:, k : k + 1]
        u = c * e_re - s * e_im
        v = s * e_re + c * e_im
        g = contract(u, c) + contract(v, s)
        if n:
            g = g * twist_ref[0] - (contract(v, c) - contract(u, s)) * twist_ref[1]
        for start in (n * cols, lanes + n * cols):
            spot = slice(start, start + cols)
            m_ref[spot, spot] = g.astype(BF16)


def filter_part(z, gathered, cs, twist):
    chips = gathered.shape[0]
    cols = cs.shape[1]
    rows = chips * 16
    lanes = 2 * cols
    return pl.pallas_call(
        filter_kernel,
        grid_spec=pltpu.PrefetchScalarGridSpec(
            num_scalar_prefetch=1,
            grid=(1,),
            in_specs=[
                pl.BlockSpec((chips, 32, 2 * lanes), lambda i, z: (0, 4, z[0])),
                pl.BlockSpec(cs.shape, lambda i, z: (0, 0, 0)),
                pl.BlockSpec(twist.shape, lambda i, z: (0, 0, 0)),
            ],
            out_specs=[
                pl.BlockSpec((cols, 2 * rows), lambda i, z: (0, 0)),
                pl.BlockSpec((2 * lanes, 2 * lanes), lambda i, z: (0, 0)),
            ],
        ),
        out_shape=[
            jax.ShapeDtypeStruct((cols, 2 * rows), F32),
            jax.ShapeDtypeStruct((2 * lanes, 2 * lanes), BF16),
        ],
        compiler_params=pltpu.CompilerParams(vmem_limit_bytes=VMEM),
        cost_estimate=pl.CostEstimate(flops=10**9, bytes_accessed=2**20, transcendentals=0),
        name="filter_part",
    )(z.reshape(1), gathered, cs, twist)


def conv_kernel(
    x_ref, fwd_hbm, inv_hbm, tw_hbm, a_ref, ai_ref, m_ref, f_ref, y_ref, fwd_ref, inv_ref, tw_ref, r_ref, q_ref, sems
):
    copies = [
        pltpu.make_async_copy(src, dst, sems.at[i])
        for i, (src, dst) in enumerate(((fwd_hbm, fwd_ref), (tw_hbm, tw_ref), (inv_hbm, inv_ref)))
    ]
    for copy in copies:
        copy.start()
    chips, chans, both = x_ref.shape
    rows = both // 2
    blocks = rows // 128
    half = 2 * chips
    copies[0].wait()
    for col in range(2):
        x = x_ref[:, :, col * rows : (col + 1) * rows].reshape(chips * chans, rows)
        r = jnp.dot(x, fwd_ref[...], preferred_element_type=F32)
        r = r.reshape(chips, chans, 2 * rows)
        if col == 0:
            copies[1].wait()
        tw = tw_ref[col * chips : (col + 1) * chips, :]
        cos = tw[:, None, :rows]
        sin = tw[:, None, rows:]
        re, im = r[:, :, :rows], r[:, :, rows:]
        turned_re = (re * cos + im * sin).reshape(chips * chans, rows)
        turned_im = (im * cos - re * sin).reshape(chips * chans, rows)
        for k in range(blocks):
            r_ref[col, k] = turned_re[:, k * 128 : (k + 1) * 128]
            r_ref[col, blocks + k] = turned_im[:, k * 128 : (k + 1) * 128]
    lane = lax.broadcasted_iota(jnp.int32, (4 * half, 128), 1)

    def pair(n, carry):
        picks = [pl.ds(2 * n + i, chips, stride=chans) for i in range(2)]
        parts = [
            jnp.concatenate([r_ref[col, part * blocks + k, pick, :] for k in range(blocks)], axis=1)
            for pick in picks
            for part in range(2)
            for col in range(2)
        ]
        turned = jnp.concatenate(parts, axis=0).astype(BF16)
        s = jnp.dot(a_ref[...], turned, preferred_element_type=F32)
        f_re, f_im = f_ref[:, :rows], f_ref[:, rows:]
        filtered = []
        for i in range(2):
            s_re = s[2 * i * half : (2 * i + 1) * half]
            s_im = s[(2 * i + 1) * half : (2 * i + 2) * half]
            filtered += [s_re * f_re - s_im * f_im, s_re * f_im + s_im * f_re]
        filtered = jnp.concatenate(filtered, axis=0).astype(BF16)
        back = jnp.dot(ai_ref[...], filtered, preferred_element_type=F32)
        edge = jnp.dot(m_ref[...], turned[:, :128], preferred_element_type=F32)
        head = jnp.where(lane == 0, edge, back[:, :128])
        back = jnp.concatenate([head, back[:, 128:]], axis=1)
        cos, sin = tw_ref[:, :rows], tw_ref[:, rows:]
        for i, pick in enumerate(picks):
            b_re = back[2 * i * half : (2 * i + 1) * half]
            b_im = back[(2 * i + 1) * half : (2 * i + 2) * half]
            out_re = b_re * cos - b_im * sin
            out_im = b_im * cos + b_re * sin
            for col in range(2):
                part = slice(col * chips, (col + 1) * chips)
                for k in range(blocks):
                    q_ref[col, k, pick, :] = out_re[part, k * 128 : (k + 1) * 128]
                    q_ref[col, blocks + k, pick, :] = out_im[part, k * 128 : (k + 1) * 128]
        return carry

    lax.fori_loop(0, chans // 2, pair, 0, unroll=2)
    copies[2].wait()
    for col in range(2):
        q = jnp.concatenate([q_ref[col, k].astype(BF16) for k in range(2 * blocks)], axis=1)
        y = jnp.dot(q, inv_ref[...], preferred_element_type=F32)
        y_ref[:, :, col * rows : (col + 1) * rows] = y.astype(BF16).reshape(chips, chans, rows)


def long_conv(x, fwd, inv, tw, a, ai, m, f):
    chips, chans, both = x.shape
    vmem = pl.BlockSpec(memory_space=pltpu.VMEM)
    hbm = pl.BlockSpec(memory_space=pl.ANY)
    return pl.pallas_call(
        conv_kernel,
        in_specs=[vmem, hbm, hbm, hbm, vmem, vmem, vmem, vmem],
        out_specs=vmem,
        out_shape=jax.ShapeDtypeStruct(x.shape, BF16),
        scratch_shapes=[
            pltpu.VMEM(fwd.shape, BF16),
            pltpu.VMEM(inv.shape, BF16),
            pltpu.VMEM(tw.shape, F32),
            pltpu.VMEM((2, both // 128, chips * chans, 128), F32),
            pltpu.VMEM((2, both // 128, chips * chans, 128), F32),
            pltpu.SemaphoreType.DMA((3,)),
        ],
        compiler_params=pltpu.CompilerParams(vmem_limit_bytes=VMEM),
        cost_estimate=pl.CostEstimate(flops=8 * 10**9, bytes_accessed=8 * 2**20, transcendentals=0),
        name="long_conv",
    )(x, fwd, inv, tw, a, ai, m, f)


def cos_sin(product, modulus):
    phase = (product % modulus).astype(F32) * (2.0 * math.pi / modulus)
    return jnp.cos(phase), jnp.sin(phase)


def twice(t):
    zero = jnp.zeros_like(t)
    return jnp.block([[t, zero], [zero, t]])


def column_tables(core, rows, cols, padded):
    i = lax.iota(jnp.int32, cols)
    b = 2 * (i % CHIPS) + ((i // CHIPS) ^ core)
    k1 = lax.iota(jnp.int32, rows)
    tw = jnp.concatenate(cos_sin(b[:, None] * k1[None, :], padded), axis=1)
    k2 = lax.iota(jnp.int32, cols)
    c, s = cos_sin(k2[:, None] * b[None, :], cols)
    a = jnp.block([[c, s], [-s, c]])
    twist = jnp.stack(cos_sin(jnp.mod((b[:, None] - b[None, :]) * rows, padded), padded))

    return tw, twice(a.astype(BF16)), twice(a.T.astype(BF16)), jnp.stack([c, s]), twist


def gather_line(block, axis):
    d1 = send(block, **{axis: -1})
    d3 = send(block, **{axis: 1})
    d2 = send(block, **{axis: 2})
    return jnp.concatenate([block, d1, d2, d3], axis=0)


def per_device(tokens, in_weight, filter_spectrum, skip_bias, out_weight):
    rows, _, width = tokens.shape
    cols = SEQ
    padded = 2 * rows * cols
    s = lax.axis_index("seq")
    h = lax.axis_index("ch")
    z, y, x, core = coords(s)
    chan = in_weight.shape[2] // 2
    depth = in_weight.shape[0]

    mine = tokens.reshape(rows, width)
    filt = jnp.transpose(filter_spectrum, (3, 1, 0, 2)).reshape(4, -1, 2 * cols)
    filt = jnp.concatenate(split_table(filt), axis=1)

    def half_for(c):
        w = lax.dynamic_slice_in_dim(in_weight, c * chan, chan, 2)
        f = lax.dynamic_slice_in_dim(filt, 2 * c, 2, 0)
        return jnp.transpose(w, (1, 0, 2)).reshape(3 * depth, chan), jnp.concatenate([f[0], f[1]], axis=1)

    keep, keep_f = half_for(core)
    give, give_f = half_for(1 - core)
    far_near = send(give[depth:], dz=1, dc=1)
    far = send(keep[depth:], dz=1)
    near = send(give, dc=1)
    near_f = send(give_f, dc=1)
    other = send(mine, dc=1)

    def ordered(own, partner, axis=0):
        return jnp.concatenate(
            [jnp.where(core == 0, own, partner), jnp.where(core == 0, partner, own)], axis=axis
        )

    def block_of(n):
        own, away = slice(n * depth, (n + 1) * depth), slice((n - 1) * depth, n * depth)
        return jnp.concatenate([ordered(keep[own], near[own]), ordered(far[away], far_near[away])], axis=0)

    key_block, value_block = block_of(1), block_of(2)
    f_lanes = 2 * cols
    gate_block = jnp.concatenate(
        [
            ordered(keep[:depth], near[:depth]),
            jnp.concatenate(
                [
                    ordered(keep_f[:, :f_lanes], near_f[:, :f_lanes], 1),
                    ordered(keep_f[:, f_lanes:], near_f[:, f_lanes:], 1),
                ],
                axis=1,
            ),
        ],
        axis=0,
    )
    gathered = lax.all_gather(gate_block, "seq", axis=0, axis_index_groups=SAME_CORE)
    key_block, value_block, other = lax.optimization_barrier((key_block, value_block, other))
    half_ow = out_weight.shape[0] // 2
    ow_part = lax.dynamic_slice_in_dim(out_weight, core * half_ow, half_ow, 0)
    key_line, value_line, ow_part = lax.optimization_barrier(
        (gather_line(key_block, "dx"), gather_line(value_block, "dy"), ow_part)
    )

    order = np.arange(32)
    p_, q_, dz = order // 8, (order // 2) % 4, order % 2
    key_order = ((z ^ dz) * 4 + (y + p_) % 4) * 4 + (x + q_) % 4
    value_order = ((z ^ dz) * 4 + (y + q_) % 4) * 4 + (x + p_) % 4
    order = jnp.stack([key_order, value_order])
    first = sum_part(first_kernel, "first_part", order, mine, other, [], [key_line, value_line], True)
    near_lines = [send(key_line, dy=-1), send(key_line, dy=1), send(value_line, dx=-1), send(value_line, dx=1)]
    near_lines, first = lax.optimization_barrier((near_lines, first))
    half = key_line.shape[0] // 2
    last_lines = [
        send(near_lines[0][:half], dy=-1),
        send(near_lines[1][half:], dy=1),
        send(near_lines[2][:half], dx=-1),
        send(near_lines[3][half:], dx=1),
    ]
    totals = sum_part(second_kernel, "second_part", order, mine, other, first[:2], near_lines, False)

    perm = []
    for t in range(SEQ):
        tz, ty, tx, tc = coords(t)
        for th in range(2):
            perm.append((t * 2 + th, index_of(tz ^ tc, ty, tx, tc) * 2 + 1 - th))
    ow_same = lax.ppermute(ow_part, ("seq", "ch"), perm)
    ow_cross = send(ow_same, dc=1)

    source, packed = last_part(totals, first[2:], last_lines)
    packed = packed.reshape(CHIPS, chan // CHIPS, 2 * rows)
    mine_ch = lax.all_to_all(packed, "seq", 0, 0, axis_index_groups=SAME_CORE)

    tw, a, ai, cs, twist = column_tables(core, rows, cols, padded)
    f, m = filter_part(z, gathered, cs, twist)
    forward, inverse = row_tables(rows, padded)
    fwd = jnp.asarray(forward.astype(np.float32).astype(ml_dtypes.bfloat16))
    inv = jnp.asarray(inverse.astype(np.float32).astype(ml_dtypes.bfloat16))
    conv = long_conv(mine_ch, fwd, inv, tw, a, ai, m, f)
    conv = lax.all_to_all(conv, "seq", 0, 0, axis_index_groups=SAME_CORE)
    conv = conv.reshape(chan, 2 * rows).astype(F32)

    gate = gate_part(mine, other, gathered).astype(F32)
    skip = lax.dynamic_slice_in_dim(skip_bias, core * chan, chan, 0)[:, None]
    gated = (gate * (conv + skip * source)).astype(BF16)

    kept = rows // 2
    own_here = lax.dynamic_slice(gated, (0, h * kept), (chan, kept))
    own_there = lax.dynamic_slice(gated, (0, (1 - h) * kept), (chan, kept))
    oth_here = lax.dynamic_slice(gated, (0, rows + h * kept), (chan, kept))
    oth_there = lax.dynamic_slice(gated, (0, rows + (1 - h) * kept), (chan, kept))
    swap_ch = [(0, 1), (1, 0)]
    from_h = lax.ppermute(own_there, "ch", swap_ch)
    perm2 = []
    for t in range(SEQ):
        for th in range(2):
            perm2.append((t * 2 + th, (t ^ 1) * 2 + 1 - th))
    from_hc = lax.ppermute(oth_there, ("seq", "ch"), perm2)
    from_c = send(oth_here, dc=1)
    here = ordered(own_here, from_c)

    mixed = mix_part(None, [here], [out_weight])
    mixed = mix_part(mixed, [from_h, from_hc], [ow_same, ow_cross])
    return mixed.reshape(kept, 1, width)


def solution(mesh):
    in_specs = (
        P(None, "seq", None),
        P("seq", None, "ch"),
        P(None, "seq", None, "ch"),
        P("ch"),
        P("ch", None),
    )
    return jax.shard_map(
        per_device, mesh=mesh, in_specs=in_specs, out_specs=P("ch", "seq", None), check_vma=False
    )
```

```python
import functools
import math

import jax
import jax.numpy as jnp
import ml_dtypes
import numpy as np
from jax import lax
from jax.experimental import pallas as pl
from jax.experimental.pallas import tpu as pltpu
from jax.sharding import PartitionSpec as P

BF16 = jnp.bfloat16
F32 = jnp.float32
HIGH = lax.Precision.HIGHEST
SEQ = 64
VMEM = 60 * 2**20
CHIPS = 32
SAME_CORE = [[2 * p + j for p in range(CHIPS)] for j in range(2)]


def coords(s):
    return s // 32, (s // 8) % 4, (s // 2) % 4, s % 2


def index_of(z, y, x, c):
    return ((z * 4 + y) * 4 + x) * 2 + c


def send(value, dz=0, dy=0, dx=0, dc=0):
    perm = []
    for s in range(SEQ):
        z, y, x, c = coords(s)
        perm.append((s, index_of((z + dz) % 2, (y + dy) % 4, (x + dx) % 4, c ^ dc)))
    return lax.ppermute(value, "seq", perm)


def split_table(table):
    upper = table.astype(BF16)
    lower = (table - upper.astype(F32)).astype(BF16)
    return upper, lower


def row_tables(rows, padded):
    points = 2 * rows
    a = np.arange(rows)
    k = np.arange(rows)
    phase = 2.0 * np.pi * ((a[:, None] * k[None, :]) % points) / points
    re, im = np.cos(phase), -np.sin(phase)
    im[:, 0] = np.where(a % 2 == 0, 1.0, -1.0)
    forward = np.concatenate([re, im], axis=1)
    scale = np.full((rows,), 2.0)
    scale[0] = 1.0
    inverse = np.concatenate([re * scale, im * scale], axis=1).T / padded
    return forward, inverse


def picked(order_ref, row, group, tok_ref):
    blocks = [
        tok_ref[:, pl.ds(pl.multiple_of(order_ref[row, group * 8 + i] * 128, 128), 128)]
        for i in range(8)
    ]
    return jnp.concatenate(blocks, axis=1)


def by_column(run, mine_ref, other_ref):
    step = pl.program_id(0)

    @pl.when(step < 2)
    def _():
        run(mine_ref)

    @pl.when(step >= 2)
    def _():
        run(other_ref)


def first_kernel(order_ref, mine_ref, other_ref, key_line, value_line, *outs):
    key_ref, value_ref, key_tok_ref, value_tok_ref = outs

    def run(tok_ref):
        for row, line, total_ref, last_ref in (
            (0, key_line, key_ref, key_tok_ref),
            (1, value_line, value_ref, value_tok_ref),
        ):
            total_ref[...] = jnp.dot(
                picked(order_ref, row, 0, tok_ref), line[...], preferred_element_type=F32
            )
            last_ref[...] = picked(order_ref, row, 2, tok_ref)

    by_column(run, mine_ref, other_ref)


def second_kernel(order_ref, mine_ref, other_ref, key_in, value_in, k1, k3, v1, v3, key_ref, value_ref):
    def run(tok_ref):
        for row, before, e1, e3, total_ref in (
            (0, key_in, k1, k3, key_ref),
            (1, value_in, v1, v3, value_ref),
        ):
            total = before[...]
            total += jnp.dot(picked(order_ref, row, 1, tok_ref), e1[...], preferred_element_type=F32)
            total += jnp.dot(picked(order_ref, row, 3, tok_ref), e3[...], preferred_element_type=F32)
            total_ref[...] = total

    by_column(run, mine_ref, other_ref)


def sum_part(kernel, name, order, mine, other, totals, weights, last):
    rows, width = mine.shape
    chan = weights[0].shape[1]
    tile = rows // 2
    quarter = width // 4
    by_row = [pl.BlockSpec((tile, chan), lambda i, o: (i, 0))] * 2
    tokens_out = [pl.BlockSpec((tile, quarter), lambda i, o: (i, 0))] * 2
    shapes = [jax.ShapeDtypeStruct((2 * rows, chan), F32)] * 2
    token_shapes = [jax.ShapeDtypeStruct((2 * rows, quarter), BF16)] * 2
    return pl.pallas_call(
        kernel,
        grid_spec=pltpu.PrefetchScalarGridSpec(
            num_scalar_prefetch=1,
            grid=(4,),
            in_specs=[
                pl.BlockSpec((tile, width), lambda i, o: (jnp.minimum(i, 1), 0)),
                pl.BlockSpec((tile, width), lambda i, o: (jnp.maximum(i - 2, 0), 0)),
            ]
            + by_row[: len(totals)]
            + [pl.BlockSpec((quarter, chan), lambda i, o: (0, 0))] * len(weights),
            out_specs=by_row + (tokens_out if last else []),
        ),
        out_shape=shapes + (token_shapes if last else []),
        compiler_params=pltpu.CompilerParams(vmem_limit_bytes=VMEM),
        cost_estimate=pl.CostEstimate(
            flops=2 * 2 * rows * quarter * chan * len(weights), bytes_accessed=18 * 2**20, transcendentals=0
        ),
        name=name,
    )(order, mine, other, *totals, *weights)


def cut_kernel(k1, k3, v1, v3, o1, o2, o3, o4, sems):
    half = o1.shape[0]
    copies = [
        pltpu.make_async_copy(src.at[pl.ds(start, half)], dst, sems.at[i])
        for i, (src, start, dst) in enumerate(((k1, 0, o1), (k3, half, o2), (v1, 0, o3), (v3, half, o4)))
    ]
    for copy in copies:
        copy.start()
    for copy in copies:
        copy.wait()


def cut_halves(lines):
    hbm = pl.BlockSpec(memory_space=pl.ANY)
    rows, width = lines[0].shape
    return pl.pallas_call(
        cut_kernel,
        in_specs=[hbm] * 4,
        out_specs=[hbm] * 4,
        out_shape=[jax.ShapeDtypeStruct((rows // 2, width), BF16)] * 4,
        scratch_shapes=[pltpu.SemaphoreType.DMA((4,))],
        compiler_params=pltpu.CompilerParams(vmem_limit_bytes=VMEM),
        cost_estimate=pl.CostEstimate(flops=0, bytes_accessed=4 * rows * width * 2, transcendentals=0),
        name="cut_halves",
    )(*lines)


def last_kernel(key_ref, value_ref, key_tok_ref, value_tok_ref, ka, kb, va, vb, send_ref):
    half = ka.shape[0]

    def finish(total_ref, tok_ref, wa, wb):
        total = total_ref[...]
        total += jnp.dot(tok_ref[:, :half], wa[...], preferred_element_type=F32)
        total += jnp.dot(tok_ref[:, half:], wb[...], preferred_element_type=F32)
        return total.astype(BF16).astype(F32)

    source = finish(key_ref, key_tok_ref, ka, kb) * finish(value_ref, value_tok_ref, va, vb)
    send_ref[...] = source.T.astype(BF16)


def last_part(totals, tokens, weights):
    total, chan = totals[0].shape
    quarter = tokens[0].shape[1]
    tile = total // 4
    return pl.pallas_call(
        last_kernel,
        grid=(4,),
        in_specs=[pl.BlockSpec((tile, chan), lambda i: (i, 0))] * 2
        + [pl.BlockSpec((tile, quarter), lambda i: (i, 0))] * 2
        + [pl.BlockSpec((quarter // 2, chan), lambda i: (0, 0))] * 4,
        out_specs=pl.BlockSpec((chan, tile), lambda i: (0, i)),
        out_shape=jax.ShapeDtypeStruct((chan, total), BF16),
        compiler_params=pltpu.CompilerParams(vmem_limit_bytes=VMEM),
        cost_estimate=pl.CostEstimate(
            flops=2 * 2 * total * quarter * chan, bytes_accessed=13 * 2**20, transcendentals=0
        ),
        name="last_part",
    )(*totals, *tokens, *weights)


def gate_kernel(mine_ref, other_ref, weight_ref, out_ref):
    chips, deep, chan = weight_ref.shape

    def run(tok_ref):
        weight = weight_ref[...].reshape(chips * deep, chan)
        gate = jnp.dot(tok_ref[...], weight, preferred_element_type=F32)
        out_ref[...] = gate.T.astype(BF16)

    by_column(run, mine_ref, other_ref)


def gate_part(mine, other, gathered):
    rows, width = mine.shape
    chips, _, chan = gathered.shape
    tile = rows // 2
    return pl.pallas_call(
        gate_kernel,
        grid=(4,),
        in_specs=[
            pl.BlockSpec((tile, width), lambda i: (jnp.minimum(i, 1), 0)),
            pl.BlockSpec((tile, width), lambda i: (jnp.maximum(i - 2, 0), 0)),
            pl.BlockSpec((chips, width // chips, chan), lambda i: (0, 0, 0)),
        ],
        out_specs=pl.BlockSpec((chan, tile), lambda i: (0, i)),
        out_shape=jax.ShapeDtypeStruct((chan, 2 * rows), BF16),
        compiler_params=pltpu.CompilerParams(vmem_limit_bytes=VMEM),
        cost_estimate=pl.CostEstimate(
            flops=2 * 2 * rows * width * chan, bytes_accessed=13 * 2**20, transcendentals=0
        ),
        name="gate_part",
    )(mine, other, gathered)


def turn(ref):
    return ref[...].astype(F32).T.astype(BF16)


def mix_kernel(here, w_here, out_ref, lhs_ref):
    @pl.when(pl.program_id(0) == 0)
    def _():
        lhs_ref[...] = turn(here)

    out_ref[...] = jnp.dot(lhs_ref[...], w_here[...], preferred_element_type=F32)


def mix_more_kernel(total_ref, near_h, far_h, w_near, w_far, out_ref, lhs_ref):
    m = near_h.shape[0]

    @pl.when(pl.program_id(0) == 0)
    def _():
        lhs_ref[:, :m] = turn(near_h)
        lhs_ref[:, m:] = turn(far_h)

    total = total_ref[...]
    total += jnp.dot(lhs_ref[:, :m], w_near[...], preferred_element_type=F32)
    total += jnp.dot(lhs_ref[:, m:], w_far[...], preferred_element_type=F32)
    out_ref[...] = total.astype(BF16)


def mix_part(total, parts, weights):
    rows = parts[0].shape[1]
    width = weights[0].shape[1]
    tile = width // 4
    depth = sum(p.shape[0] for p in parts)
    totals = [] if total is None else [total]

    def whole(g):
        return pl.BlockSpec(g.shape, lambda i: (0, 0))

    def tiled(w):
        return pl.BlockSpec((w.shape[0], tile), lambda i: (0, i))

    return pl.pallas_call(
        mix_kernel if total is None else mix_more_kernel,
        grid=(4,),
        in_specs=[tiled(t) for t in totals] + [whole(p) for p in parts] + [tiled(w) for w in weights],
        out_specs=pl.BlockSpec((rows, tile), lambda i: (0, i)),
        out_shape=jax.ShapeDtypeStruct((rows, width), F32 if total is None else BF16),
        scratch_shapes=[pltpu.VMEM((rows, depth), BF16)],
        compiler_params=pltpu.CompilerParams(vmem_limit_bytes=VMEM),
        cost_estimate=pl.CostEstimate(
            flops=2 * rows * depth * width, bytes_accessed=12 * 2**20, transcendentals=0
        ),
        name="mix_part" if total is None else "mix_more",
    )(*totals, *parts, *weights)


def filter_kernel(z_ref, x_ref, cs_ref, twist_ref, f_ref, m_ref):
    chips, _, lanes = x_ref.shape
    lanes = lanes // 2
    points = 2 * chips * 16
    rows, cols = points // 2, lanes // 2

    def part(n):
        rows_of = slice(16 * n, 16 * (n + 1))
        cores = [x_ref[:, rows_of, c * lanes : (c + 1) * lanes] for c in range(2)]
        return jnp.stack(cores, axis=1).reshape(points, lanes)

    upper, lower = part(0), part(1)
    whole = (upper.astype(F32) + lower.astype(F32)).T
    i = lax.broadcasted_iota(jnp.int32, (rows, rows), 0)
    j = lax.broadcasted_iota(jnp.int32, (rows, rows), 1)
    mirror = (i + j == rows).astype(F32).astype(BF16)
    i = lax.broadcasted_iota(jnp.int32, (lanes, lanes), 0)
    j = lax.broadcasted_iota(jnp.int32, (lanes, lanes), 1)
    flip = ((i // cols == j // cols) & (i % cols + j % cols == cols - 1)).astype(F32).astype(BF16)

    def mirrored(part):
        turned = jnp.dot(flip, part[:, rows:], preferred_element_type=F32).astype(BF16)
        return jnp.dot(turned, mirror, preferred_element_type=F32)

    other = mirrored(upper.astype(F32).T.astype(BF16)) + mirrored(lower.astype(F32).T.astype(BF16))
    f_ref[:, :rows] = 0.5 * (whole[:cols, :rows] + other[:cols])
    f_ref[:, rows:] = 0.5 * (whole[cols:, :rows] - other[cols:])
    c, s = cs_ref[0], cs_ref[1]

    def contract(left, right):
        return lax.dot_general(
            left, right, (((0,), (0,)), ((), ())), precision=HIGH, preferred_element_type=F32
        )

    m_ref[...] = jnp.zeros_like(m_ref)
    for n, k in enumerate((0, rows)):
        e_re, e_im = whole[:cols, k : k + 1], whole[cols:, k : k + 1]
        u = c * e_re - s * e_im
        v = s * e_re + c * e_im
        g = contract(u, c) + contract(v, s)
        if n:
            g = g * twist_ref[0] - (contract(v, c) - contract(u, s)) * twist_ref[1]
        for start in (n * cols, lanes + n * cols):
            spot = slice(start, start + cols)
            m_ref[spot, spot] = g.astype(BF16)


def filter_part(z, gathered, cs, twist):
    chips = gathered.shape[0]
    cols = cs.shape[1]
    rows = chips * 16
    lanes = 2 * cols
    return pl.pallas_call(
        filter_kernel,
        grid_spec=pltpu.PrefetchScalarGridSpec(
            num_scalar_prefetch=1,
            grid=(1,),
            in_specs=[
                pl.BlockSpec((chips, 32, 2 * lanes), lambda i, z: (0, 4, z[0])),
                pl.BlockSpec(cs.shape, lambda i, z: (0, 0, 0)),
                pl.BlockSpec(twist.shape, lambda i, z: (0, 0, 0)),
            ],
            out_specs=[
                pl.BlockSpec((cols, 2 * rows), lambda i, z: (0, 0)),
                pl.BlockSpec((2 * lanes, 2 * lanes), lambda i, z: (0, 0)),
            ],
        ),
        out_shape=[
            jax.ShapeDtypeStruct((cols, 2 * rows), F32),
            jax.ShapeDtypeStruct((2 * lanes, 2 * lanes), BF16),
        ],
        compiler_params=pltpu.CompilerParams(vmem_limit_bytes=VMEM),
        cost_estimate=pl.CostEstimate(flops=10**9, bytes_accessed=2**20, transcendentals=0),
        name="filter_part",
    )(z.reshape(1), gathered, cs, twist)


def conv_kernel(
    x_ref, fwd_hbm, inv_hbm, tw_hbm, a_ref, ai_ref, m_ref, f_ref, y_ref, fwd_ref, inv_ref, tw_ref, r_ref, q_ref, sems
):
    copies = [
        pltpu.make_async_copy(src, dst, sems.at[i])
        for i, (src, dst) in enumerate(((fwd_hbm, fwd_ref), (tw_hbm, tw_ref), (inv_hbm, inv_ref)))
    ]
    for copy in copies:
        copy.start()
    chips, chans, both = x_ref.shape
    rows = both // 2
    blocks = rows // 128
    half = 2 * chips
    copies[0].wait()
    for col in range(2):
        x = x_ref[:, :, col * rows : (col + 1) * rows].reshape(chips * chans, rows)
        r = jnp.dot(x, fwd_ref[...], preferred_element_type=F32)
        r = r.reshape(chips, chans, 2 * rows)
        if col == 0:
            copies[1].wait()
        tw = tw_ref[col * chips : (col + 1) * chips, :]
        cos = tw[:, None, :rows]
        sin = tw[:, None, rows:]
        re, im = r[:, :, :rows], r[:, :, rows:]
        turned_re = (re * cos + im * sin).reshape(chips * chans, rows)
        turned_im = (im * cos - re * sin).reshape(chips * chans, rows)
        for k in range(blocks):
            r_ref[col, k] = turned_re[:, k * 128 : (k + 1) * 128]
            r_ref[col, blocks + k] = turned_im[:, k * 128 : (k + 1) * 128]
    lane = lax.broadcasted_iota(jnp.int32, (4 * half, 128), 1)

    def pair(n, carry):
        picks = [pl.ds(2 * n + i, chips, stride=chans) for i in range(2)]
        parts = [
            jnp.concatenate([r_ref[col, part * blocks + k, pick, :] for k in range(blocks)], axis=1)
            for pick in picks
            for part in range(2)
            for col in range(2)
        ]
        turned = jnp.concatenate(parts, axis=0).astype(BF16)
        s = jnp.dot(a_ref[...], turned, preferred_element_type=F32)
        f_re, f_im = f_ref[:, :rows], f_ref[:, rows:]
        filtered = []
        for i in range(2):
            s_re = s[2 * i * half : (2 * i + 1) * half]
            s_im = s[(2 * i + 1) * half : (2 * i + 2) * half]
            filtered += [s_re * f_re - s_im * f_im, s_re * f_im + s_im * f_re]
        filtered = jnp.concatenate(filtered, axis=0).astype(BF16)
        back = jnp.dot(ai_ref[...], filtered, preferred_element_type=F32)
        edge = jnp.dot(m_ref[...], turned[:, :128], preferred_element_type=F32)
        head = jnp.where(lane == 0, edge, back[:, :128])
        back = jnp.concatenate([head, back[:, 128:]], axis=1)
        cos, sin = tw_ref[:, :rows], tw_ref[:, rows:]
        for i, pick in enumerate(picks):
            b_re = back[2 * i * half : (2 * i + 1) * half]
            b_im = back[(2 * i + 1) * half : (2 * i + 2) * half]
            out_re = b_re * cos - b_im * sin
            out_im = b_im * cos + b_re * sin
            for col in range(2):
                part = slice(col * chips, (col + 1) * chips)
                for k in range(blocks):
                    q_ref[col, k, pick, :] = out_re[part, k * 128 : (k + 1) * 128]
                    q_ref[col, blocks + k, pick, :] = out_im[part, k * 128 : (k + 1) * 128]
        return carry

    lax.fori_loop(0, chans // 2, pair, 0, unroll=2)
    copies[2].wait()
    for col in range(2):
        q = jnp.concatenate([q_ref[col, k].astype(BF16) for k in range(2 * blocks)], axis=1)
        y = jnp.dot(q, inv_ref[...], preferred_element_type=F32)
        y_ref[:, :, col * rows : (col + 1) * rows] = y.astype(BF16).reshape(chips, chans, rows)


def long_conv(x, fwd, inv, tw, a, ai, m, f):
    chips, chans, both = x.shape
    vmem = pl.BlockSpec(memory_space=pltpu.VMEM)
    hbm = pl.BlockSpec(memory_space=pl.ANY)
    return pl.pallas_call(
        conv_kernel,
        in_specs=[vmem, hbm, hbm, hbm, vmem, vmem, vmem, vmem],
        out_specs=vmem,
        out_shape=jax.ShapeDtypeStruct(x.shape, BF16),
        scratch_shapes=[
            pltpu.VMEM(fwd.shape, BF16),
            pltpu.VMEM(inv.shape, BF16),
            pltpu.VMEM(tw.shape, F32),
            pltpu.VMEM((2, both // 128, chips * chans, 128), F32),
            pltpu.VMEM((2, both // 128, chips * chans, 128), F32),
            pltpu.SemaphoreType.DMA((3,)),
        ],
        compiler_params=pltpu.CompilerParams(vmem_limit_bytes=VMEM),
        cost_estimate=pl.CostEstimate(flops=8 * 10**9, bytes_accessed=8 * 2**20, transcendentals=0),
        name="long_conv",
    )(x, fwd, inv, tw, a, ai, m, f)


def cos_sin(product, modulus):
    phase = (product % modulus).astype(F32) * (2.0 * math.pi / modulus)
    return jnp.cos(phase), jnp.sin(phase)


def twice(t):
    zero = jnp.zeros_like(t)
    return jnp.block([[t, zero], [zero, t]])


def column_tables(core, rows, cols, padded):
    i = lax.iota(jnp.int32, cols)
    b = 2 * (i % CHIPS) + ((i // CHIPS) ^ core)
    k1 = lax.iota(jnp.int32, rows)
    tw = jnp.concatenate(cos_sin(b[:, None] * k1[None, :], padded), axis=1)
    k2 = lax.iota(jnp.int32, cols)
    c, s = cos_sin(k2[:, None] * b[None, :], cols)
    a = jnp.block([[c, s], [-s, c]])
    twist = jnp.stack(cos_sin(jnp.mod((b[:, None] - b[None, :]) * rows, padded), padded))

    return tw, twice(a.astype(BF16)), twice(a.T.astype(BF16)), jnp.stack([c, s]), twist


def gather_line(block, axis):
    d1 = send(block, **{axis: -1})
    d3 = send(block, **{axis: 1})
    d2 = send(block, **{axis: 2})
    return jnp.concatenate([block, d1, d2, d3], axis=0)


def per_device(tokens, in_weight, filter_spectrum, skip_bias, out_weight):
    rows, _, width = tokens.shape
    cols = SEQ
    padded = 2 * rows * cols
    s = lax.axis_index("seq")
    h = lax.axis_index("ch")
    z, y, x, core = coords(s)
    chan = in_weight.shape[2] // 2
    depth = in_weight.shape[0]

    mine = tokens.reshape(rows, width)
    filt = jnp.transpose(filter_spectrum, (3, 1, 0, 2)).reshape(4, -1, 2 * cols)
    filt = jnp.concatenate(split_table(filt), axis=1)

    def half_for(c):
        w = lax.dynamic_slice_in_dim(in_weight, c * chan, chan, 2)
        f = lax.dynamic_slice_in_dim(filt, 2 * c, 2, 0)
        return jnp.transpose(w, (1, 0, 2)).reshape(3 * depth, chan), jnp.concatenate([f[0], f[1]], axis=1)

    keep, keep_f = half_for(core)
    give, give_f = half_for(1 - core)
    far_near = send(give[depth:], dz=1, dc=1)
    far = send(keep[depth:], dz=1)
    near = send(give, dc=1)
    near_f = send(give_f, dc=1)
    other = send(mine, dc=1)

    def ordered(own, partner, axis=0):
        return jnp.concatenate(
            [jnp.where(core == 0, own, partner), jnp.where(core == 0, partner, own)], axis=axis
        )

    def block_of(n):
        own, away = slice(n * depth, (n + 1) * depth), slice((n - 1) * depth, n * depth)
        return jnp.concatenate([ordered(keep[own], near[own]), ordered(far[away], far_near[away])], axis=0)

    key_block, value_block = block_of(1), block_of(2)
    f_lanes = 2 * cols
    gate_block = jnp.concatenate(
        [
            ordered(keep[:depth], near[:depth]),
            jnp.concatenate(
                [
                    ordered(keep_f[:, :f_lanes], near_f[:, :f_lanes], 1),
                    ordered(keep_f[:, f_lanes:], near_f[:, f_lanes:], 1),
                ],
                axis=1,
            ),
        ],
        axis=0,
    )
    gathered = lax.all_gather(gate_block, "seq", axis=0, axis_index_groups=SAME_CORE)
    key_block, value_block, other = lax.optimization_barrier((key_block, value_block, other))
    half_ow = out_weight.shape[0] // 2
    ow_part = lax.dynamic_slice_in_dim(out_weight, core * half_ow, half_ow, 0)
    key_line, value_line, ow_part = lax.optimization_barrier(
        (gather_line(key_block, "dx"), gather_line(value_block, "dy"), ow_part)
    )

    order = np.arange(32)
    p_, q_, dz = order // 8, (order // 2) % 4, order % 2
    key_order = ((z ^ dz) * 4 + (y + p_) % 4) * 4 + (x + q_) % 4
    value_order = ((z ^ dz) * 4 + (y + q_) % 4) * 4 + (x + p_) % 4
    order = jnp.stack([key_order, value_order])
    first = sum_part(first_kernel, "first_part", order, mine, other, [], [key_line, value_line], True)
    near_lines = [send(key_line, dy=-1), send(key_line, dy=1), send(value_line, dx=-1), send(value_line, dx=1)]
    near_lines, first = lax.optimization_barrier((near_lines, first))
    halves = cut_halves(near_lines)
    last_lines = [
        send(halves[0], dy=-1),
        send(halves[1], dy=1),
        send(halves[2], dx=-1),
        send(halves[3], dx=1),
    ]
    totals = sum_part(second_kernel, "second_part", order, mine, other, first[:2], near_lines, False)

    perm = []
    for t in range(SEQ):
        tz, ty, tx, tc = coords(t)
        for th in range(2):
            perm.append((t * 2 + th, index_of(tz ^ tc, ty, tx, tc) * 2 + 1 - th))
    ow_same = lax.ppermute(ow_part, ("seq", "ch"), perm)
    ow_cross = send(ow_same, dc=1)

    source = last_part(totals, first[2:], last_lines)
    packed = source.reshape(CHIPS, chan // CHIPS, 2 * rows)
    mine_ch = lax.all_to_all(packed, "seq", 0, 0, axis_index_groups=SAME_CORE)

    tw, a, ai, cs, twist = column_tables(core, rows, cols, padded)
    f, m = filter_part(z, gathered, cs, twist)
    forward, inverse = row_tables(rows, padded)
    fwd = jnp.asarray(forward.astype(np.float32).astype(ml_dtypes.bfloat16))
    inv = jnp.asarray(inverse.astype(np.float32).astype(ml_dtypes.bfloat16))
    conv = long_conv(mine_ch, fwd, inv, tw, a, ai, m, f)
    conv = lax.all_to_all(conv, "seq", 0, 0, axis_index_groups=SAME_CORE)
    conv = conv.reshape(chan, 2 * rows).astype(F32)

    gate = gate_part(mine, other, gathered).astype(F32)
    skip = lax.dynamic_slice_in_dim(skip_bias, core * chan, chan, 0)[:, None]
    gated = (gate * (conv + skip * source.astype(F32))).astype(BF16)

    kept = rows // 2
    own_here = lax.dynamic_slice(gated, (0, h * kept), (chan, kept))
    own_there = lax.dynamic_slice(gated, (0, (1 - h) * kept), (chan, kept))
    oth_here = lax.dynamic_slice(gated, (0, rows + h * kept), (chan, kept))
    oth_there = lax.dynamic_slice(gated, (0, rows + (1 - h) * kept), (chan, kept))
    swap_ch = [(0, 1), (1, 0)]
    from_h = lax.ppermute(own_there, "ch", swap_ch)
    perm2 = []
    for t in range(SEQ):
        for th in range(2):
            perm2.append((t * 2 + th, (t ^ 1) * 2 + 1 - th))
    from_hc = lax.ppermute(oth_there, ("seq", "ch"), perm2)
    from_c = send(oth_here, dc=1)
    here = ordered(own_here, from_c)

    mixed = mix_part(None, [here], [out_weight])
    mixed = mix_part(mixed, [from_h, from_hc], [ow_same, ow_cross])
    return mixed.reshape(kept, 1, width)


def solution(mesh):
    in_specs = (
        P(None, "seq", None),
        P("seq", None, "ch"),
        P(None, "seq", None, "ch"),
        P("ch"),
        P("ch", None),
    )
    return jax.shard_map(
        per_device, mesh=mesh, in_specs=in_specs, out_specs=P("ch", "seq", None), check_vma=False
    )
```

```python
import functools
import math

import jax
import jax.numpy as jnp
import ml_dtypes
import numpy as np
from jax import lax
from jax.experimental import pallas as pl
from jax.experimental.pallas import tpu as pltpu
from jax.sharding import PartitionSpec as P

BF16 = jnp.bfloat16
F32 = jnp.float32
HIGH = lax.Precision.HIGHEST
SEQ = 64
VMEM = 60 * 2**20
CHIPS = 32
SAME_CORE = [[2 * p + j for p in range(CHIPS)] for j in range(2)]


def coords(s):
    return s // 32, (s // 8) % 4, (s // 2) % 4, s % 2


def index_of(z, y, x, c):
    return ((z * 4 + y) * 4 + x) * 2 + c


def send(value, dz=0, dy=0, dx=0, dc=0):
    perm = []
    for s in range(SEQ):
        z, y, x, c = coords(s)
        perm.append((s, index_of((z + dz) % 2, (y + dy) % 4, (x + dx) % 4, c ^ dc)))
    return lax.ppermute(value, "seq", perm)


def split_table(table):
    upper = table.astype(BF16)
    lower = (table - upper.astype(F32)).astype(BF16)
    return upper, lower


def row_tables(rows, padded):
    points = 2 * rows
    a = np.arange(rows)
    k = np.arange(rows)
    phase = 2.0 * np.pi * ((a[:, None] * k[None, :]) % points) / points
    re, im = np.cos(phase), -np.sin(phase)
    im[:, 0] = np.where(a % 2 == 0, 1.0, -1.0)
    forward = np.concatenate([re, im], axis=1)
    scale = np.full((rows,), 2.0)
    scale[0] = 1.0
    inverse = np.concatenate([re * scale, im * scale], axis=1).T / padded
    return forward, inverse


def picked(order_ref, row, group, tok_ref):
    blocks = [
        tok_ref[:, pl.ds(pl.multiple_of(order_ref[row, group * 8 + i] * 128, 128), 128)]
        for i in range(8)
    ]
    return jnp.concatenate(blocks, axis=1)


def by_column(run, mine_ref, other_ref):
    step = pl.program_id(0)

    @pl.when(step < 2)
    def _():
        run(mine_ref)

    @pl.when(step >= 2)
    def _():
        run(other_ref)


def first_kernel(order_ref, mine_ref, other_ref, key_line, value_line, *outs):
    key_ref, value_ref, key_tok_ref, value_tok_ref = outs

    def run(tok_ref):
        for row, line, total_ref, last_ref in (
            (0, key_line, key_ref, key_tok_ref),
            (1, value_line, value_ref, value_tok_ref),
        ):
            total_ref[...] = jnp.dot(
                picked(order_ref, row, 0, tok_ref), line[...], preferred_element_type=F32
            )
            last_ref[...] = picked(order_ref, row, 2, tok_ref)

    by_column(run, mine_ref, other_ref)


def second_kernel(order_ref, mine_ref, other_ref, key_in, value_in, k1, k3, v1, v3, key_ref, value_ref):
    def run(tok_ref):
        for row, before, e1, e3, total_ref in (
            (0, key_in, k1, k3, key_ref),
            (1, value_in, v1, v3, value_ref),
        ):
            total = before[...]
            total += jnp.dot(picked(order_ref, row, 1, tok_ref), e1[...], preferred_element_type=F32)
            total += jnp.dot(picked(order_ref, row, 3, tok_ref), e3[...], preferred_element_type=F32)
            total_ref[...] = total

    by_column(run, mine_ref, other_ref)


def sum_part(kernel, name, order, mine, other, totals, weights, last):
    rows, width = mine.shape
    chan = weights[0].shape[1]
    tile = rows // 2
    quarter = width // 4
    by_row = [pl.BlockSpec((tile, chan), lambda i, o: (i, 0))] * 2
    tokens_out = [pl.BlockSpec((tile, quarter), lambda i, o: (i, 0))] * 2
    shapes = [jax.ShapeDtypeStruct((2 * rows, chan), F32)] * 2
    token_shapes = [jax.ShapeDtypeStruct((2 * rows, quarter), BF16)] * 2
    return pl.pallas_call(
        kernel,
        grid_spec=pltpu.PrefetchScalarGridSpec(
            num_scalar_prefetch=1,
            grid=(4,),
            in_specs=[
                pl.BlockSpec((tile, width), lambda i, o: (jnp.minimum(i, 1), 0)),
                pl.BlockSpec((tile, width), lambda i, o: (jnp.maximum(i - 2, 0), 0)),
            ]
            + by_row[: len(totals)]
            + [pl.BlockSpec((quarter, chan), lambda i, o: (0, 0))] * len(weights),
            out_specs=by_row + (tokens_out if last else []),
        ),
        out_shape=shapes + (token_shapes if last else []),
        compiler_params=pltpu.CompilerParams(vmem_limit_bytes=VMEM),
        cost_estimate=pl.CostEstimate(
            flops=2 * 2 * rows * quarter * chan * len(weights), bytes_accessed=18 * 2**20, transcendentals=0
        ),
        name=name,
    )(order, mine, other, *totals, *weights)


def cut_kernel(*refs):
    for src, dst in zip(refs[:4], refs[4:], strict=True):
        dst[...] = src[...]


def cut_halves(lines):
    rows, width = lines[0].shape
    tile = rows // 4
    upper = pl.BlockSpec((tile, width), lambda i: (i, 0))
    lower = pl.BlockSpec((tile, width), lambda i: (i + 2, 0))
    return pl.pallas_call(
        cut_kernel,
        grid=(2,),
        in_specs=[upper, lower, upper, lower],
        out_specs=[upper] * 4,
        out_shape=[jax.ShapeDtypeStruct((rows // 2, width), BF16)] * 4,
        compiler_params=pltpu.CompilerParams(vmem_limit_bytes=VMEM),
        cost_estimate=pl.CostEstimate(flops=0, bytes_accessed=4 * rows * width * 2, transcendentals=0),
        name="cut_halves",
    )(*lines)


def last_kernel(key_ref, value_ref, key_tok_ref, value_tok_ref, ka, kb, va, vb, send_ref):
    half = ka.shape[0]

    def finish(total_ref, tok_ref, wa, wb):
        total = total_ref[...]
        total += jnp.dot(tok_ref[:, :half], wa[...], preferred_element_type=F32)
        total += jnp.dot(tok_ref[:, half:], wb[...], preferred_element_type=F32)
        return total.astype(BF16).astype(F32)

    source = finish(key_ref, key_tok_ref, ka, kb) * finish(value_ref, value_tok_ref, va, vb)
    send_ref[...] = source.T.astype(BF16)


def last_part(totals, tokens, weights):
    total, chan = totals[0].shape
    quarter = tokens[0].shape[1]
    tile = total // 4
    return pl.pallas_call(
        last_kernel,
        grid=(4,),
        in_specs=[pl.BlockSpec((tile, chan), lambda i: (i, 0))] * 2
        + [pl.BlockSpec((tile, quarter), lambda i: (i, 0))] * 2
        + [pl.BlockSpec((quarter // 2, chan), lambda i: (0, 0))] * 4,
        out_specs=pl.BlockSpec((chan, tile), lambda i: (0, i)),
        out_shape=jax.ShapeDtypeStruct((chan, total), BF16),
        compiler_params=pltpu.CompilerParams(vmem_limit_bytes=VMEM),
        cost_estimate=pl.CostEstimate(
            flops=2 * 2 * total * quarter * chan, bytes_accessed=13 * 2**20, transcendentals=0
        ),
        name="last_part",
    )(*totals, *tokens, *weights)


def gate_kernel(mine_ref, other_ref, weight_ref, out_ref):
    chips, deep, chan = weight_ref.shape

    def run(tok_ref):
        weight = weight_ref[...].reshape(chips * deep, chan)
        gate = jnp.dot(tok_ref[...], weight, preferred_element_type=F32)
        out_ref[...] = gate.T.astype(BF16)

    by_column(run, mine_ref, other_ref)


def gate_part(mine, other, gathered):
    rows, width = mine.shape
    chips, _, chan = gathered.shape
    tile = rows // 2
    return pl.pallas_call(
        gate_kernel,
        grid=(4,),
        in_specs=[
            pl.BlockSpec((tile, width), lambda i: (jnp.minimum(i, 1), 0)),
            pl.BlockSpec((tile, width), lambda i: (jnp.maximum(i - 2, 0), 0)),
            pl.BlockSpec((chips, width // chips, chan), lambda i: (0, 0, 0)),
        ],
        out_specs=pl.BlockSpec((chan, tile), lambda i: (0, i)),
        out_shape=jax.ShapeDtypeStruct((chan, 2 * rows), BF16),
        compiler_params=pltpu.CompilerParams(vmem_limit_bytes=VMEM),
        cost_estimate=pl.CostEstimate(
            flops=2 * 2 * rows * width * chan, bytes_accessed=13 * 2**20, transcendentals=0
        ),
        name="gate_part",
    )(mine, other, gathered)


def turn(ref):
    return ref[...].astype(F32).T.astype(BF16)


def mix_kernel(here, w_here, out_ref, lhs_ref):
    @pl.when(pl.program_id(0) == 0)
    def _():
        lhs_ref[...] = turn(here)

    out_ref[...] = jnp.dot(lhs_ref[...], w_here[...], preferred_element_type=F32)


def mix_more_kernel(total_ref, near_h, far_h, w_near, w_far, out_ref, lhs_ref):
    m = near_h.shape[0]

    @pl.when(pl.program_id(0) == 0)
    def _():
        lhs_ref[:, :m] = turn(near_h)
        lhs_ref[:, m:] = turn(far_h)

    total = total_ref[...]
    total += jnp.dot(lhs_ref[:, :m], w_near[...], preferred_element_type=F32)
    total += jnp.dot(lhs_ref[:, m:], w_far[...], preferred_element_type=F32)
    out_ref[...] = total.astype(BF16)


def mix_part(total, parts, weights):
    rows = parts[0].shape[1]
    width = weights[0].shape[1]
    tile = width // 4
    depth = sum(p.shape[0] for p in parts)
    totals = [] if total is None else [total]

    def whole(g):
        return pl.BlockSpec(g.shape, lambda i: (0, 0))

    def tiled(w):
        return pl.BlockSpec((w.shape[0], tile), lambda i: (0, i))

    return pl.pallas_call(
        mix_kernel if total is None else mix_more_kernel,
        grid=(4,),
        in_specs=[tiled(t) for t in totals] + [whole(p) for p in parts] + [tiled(w) for w in weights],
        out_specs=pl.BlockSpec((rows, tile), lambda i: (0, i)),
        out_shape=jax.ShapeDtypeStruct((rows, width), F32 if total is None else BF16),
        scratch_shapes=[pltpu.VMEM((rows, depth), BF16)],
        compiler_params=pltpu.CompilerParams(vmem_limit_bytes=VMEM),
        cost_estimate=pl.CostEstimate(
            flops=2 * rows * depth * width, bytes_accessed=12 * 2**20, transcendentals=0
        ),
        name="mix_part" if total is None else "mix_more",
    )(*totals, *parts, *weights)


def filter_kernel(z_ref, x_ref, cs_ref, twist_ref, f_ref, m_ref):
    chips, _, lanes = x_ref.shape
    lanes = lanes // 2
    points = 2 * chips * 16
    rows, cols = points // 2, lanes // 2

    def part(n):
        rows_of = slice(16 * n, 16 * (n + 1))
        cores = [x_ref[:, rows_of, c * lanes : (c + 1) * lanes] for c in range(2)]
        return jnp.stack(cores, axis=1).reshape(points, lanes)

    upper, lower = part(0), part(1)
    whole = (upper.astype(F32) + lower.astype(F32)).T
    i = lax.broadcasted_iota(jnp.int32, (rows, rows), 0)
    j = lax.broadcasted_iota(jnp.int32, (rows, rows), 1)
    mirror = (i + j == rows).astype(F32).astype(BF16)
    i = lax.broadcasted_iota(jnp.int32, (lanes, lanes), 0)
    j = lax.broadcasted_iota(jnp.int32, (lanes, lanes), 1)
    flip = ((i // cols == j // cols) & (i % cols + j % cols == cols - 1)).astype(F32).astype(BF16)

    def mirrored(part):
        turned = jnp.dot(flip, part[:, rows:], preferred_element_type=F32).astype(BF16)
        return jnp.dot(turned, mirror, preferred_element_type=F32)

    other = mirrored(upper.astype(F32).T.astype(BF16)) + mirrored(lower.astype(F32).T.astype(BF16))
    f_ref[:, :rows] = 0.5 * (whole[:cols, :rows] + other[:cols])
    f_ref[:, rows:] = 0.5 * (whole[cols:, :rows] - other[cols:])
    c, s = cs_ref[0], cs_ref[1]

    def contract(left, right):
        return lax.dot_general(
            left, right, (((0,), (0,)), ((), ())), precision=HIGH, preferred_element_type=F32
        )

    m_ref[...] = jnp.zeros_like(m_ref)
    for n, k in enumerate((0, rows)):
        e_re, e_im = whole[:cols, k : k + 1], whole[cols:, k : k + 1]
        u = c * e_re - s * e_im
        v = s * e_re + c * e_im
        g = contract(u, c) + contract(v, s)
        if n:
            g = g * twist_ref[0] - (contract(v, c) - contract(u, s)) * twist_ref[1]
        for start in (n * cols, lanes + n * cols):
            spot = slice(start, start + cols)
            m_ref[spot, spot] = g.astype(BF16)


def filter_part(z, gathered, cs, twist):
    chips = gathered.shape[0]
    cols = cs.shape[1]
    rows = chips * 16
    lanes = 2 * cols
    return pl.pallas_call(
        filter_kernel,
        grid_spec=pltpu.PrefetchScalarGridSpec(
            num_scalar_prefetch=1,
            grid=(1,),
            in_specs=[
                pl.BlockSpec((chips, 32, 2 * lanes), lambda i, z: (0, 4, z[0])),
                pl.BlockSpec(cs.shape, lambda i, z: (0, 0, 0)),
                pl.BlockSpec(twist.shape, lambda i, z: (0, 0, 0)),
            ],
            out_specs=[
                pl.BlockSpec((cols, 2 * rows), lambda i, z: (0, 0)),
                pl.BlockSpec((2 * lanes, 2 * lanes), lambda i, z: (0, 0)),
            ],
        ),
        out_shape=[
            jax.ShapeDtypeStruct((cols, 2 * rows), F32),
            jax.ShapeDtypeStruct((2 * lanes, 2 * lanes), BF16),
        ],
        compiler_params=pltpu.CompilerParams(vmem_limit_bytes=VMEM),
        cost_estimate=pl.CostEstimate(flops=10**9, bytes_accessed=2**20, transcendentals=0),
        name="filter_part",
    )(z.reshape(1), gathered, cs, twist)


def conv_kernel(
    x_ref, fwd_hbm, inv_hbm, tw_hbm, a_ref, ai_ref, m_ref, f_ref, y_ref, fwd_ref, inv_ref, tw_ref, r_ref, q_ref, sems
):
    copies = [
        pltpu.make_async_copy(src, dst, sems.at[i])
        for i, (src, dst) in enumerate(((fwd_hbm, fwd_ref), (tw_hbm, tw_ref), (inv_hbm, inv_ref)))
    ]
    for copy in copies:
        copy.start()
    chips, chans, both = x_ref.shape
    rows = both // 2
    blocks = rows // 128
    half = 2 * chips
    copies[0].wait()
    for col in range(2):
        x = x_ref[:, :, col * rows : (col + 1) * rows].reshape(chips * chans, rows)
        r = jnp.dot(x, fwd_ref[...], preferred_element_type=F32)
        r = r.reshape(chips, chans, 2 * rows)
        if col == 0:
            copies[1].wait()
        tw = tw_ref[col * chips : (col + 1) * chips, :]
        cos = tw[:, None, :rows]
        sin = tw[:, None, rows:]
        re, im = r[:, :, :rows], r[:, :, rows:]
        turned_re = (re * cos + im * sin).reshape(chips * chans, rows)
        turned_im = (im * cos - re * sin).reshape(chips * chans, rows)
        for k in range(blocks):
            r_ref[col, k] = turned_re[:, k * 128 : (k + 1) * 128]
            r_ref[col, blocks + k] = turned_im[:, k * 128 : (k + 1) * 128]
    lane = lax.broadcasted_iota(jnp.int32, (4 * half, 128), 1)

    def pair(n, carry):
        picks = [pl.ds(2 * n + i, chips, stride=chans) for i in range(2)]
        parts = [
            jnp.concatenate([r_ref[col, part * blocks + k, pick, :] for k in range(blocks)], axis=1)
            for pick in picks
            for part in range(2)
            for col in range(2)
        ]
        turned = jnp.concatenate(parts, axis=0).astype(BF16)
        s = jnp.dot(a_ref[...], turned, preferred_element_type=F32)
        f_re, f_im = f_ref[:, :rows], f_ref[:, rows:]
        filtered = []
        for i in range(2):
            s_re = s[2 * i * half : (2 * i + 1) * half]
            s_im = s[(2 * i + 1) * half : (2 * i + 2) * half]
            filtered += [s_re * f_re - s_im * f_im, s_re * f_im + s_im * f_re]
        filtered = jnp.concatenate(filtered, axis=0).astype(BF16)
        back = jnp.dot(ai_ref[...], filtered, preferred_element_type=F32)
        edge = jnp.dot(m_ref[...], turned[:, :128], preferred_element_type=F32)
        head = jnp.where(lane == 0, edge, back[:, :128])
        back = jnp.concatenate([head, back[:, 128:]], axis=1)
        cos, sin = tw_ref[:, :rows], tw_ref[:, rows:]
        for i, pick in enumerate(picks):
            b_re = back[2 * i * half : (2 * i + 1) * half]
            b_im = back[(2 * i + 1) * half : (2 * i + 2) * half]
            out_re = b_re * cos - b_im * sin
            out_im = b_im * cos + b_re * sin
            for col in range(2):
                part = slice(col * chips, (col + 1) * chips)
                for k in range(blocks):
                    q_ref[col, k, pick, :] = out_re[part, k * 128 : (k + 1) * 128]
                    q_ref[col, blocks + k, pick, :] = out_im[part, k * 128 : (k + 1) * 128]
        return carry

    lax.fori_loop(0, chans // 2, pair, 0, unroll=2)
    copies[2].wait()
    for col in range(2):
        q = jnp.concatenate([q_ref[col, k].astype(BF16) for k in range(2 * blocks)], axis=1)
        y = jnp.dot(q, inv_ref[...], preferred_element_type=F32)
        y_ref[:, :, col * rows : (col + 1) * rows] = y.astype(BF16).reshape(chips, chans, rows)


def long_conv(x, fwd, inv, tw, a, ai, m, f):
    chips, chans, both = x.shape
    vmem = pl.BlockSpec(memory_space=pltpu.VMEM)
    hbm = pl.BlockSpec(memory_space=pl.ANY)
    return pl.pallas_call(
        conv_kernel,
        in_specs=[vmem, hbm, hbm, hbm, vmem, vmem, vmem, vmem],
        out_specs=vmem,
        out_shape=jax.ShapeDtypeStruct(x.shape, BF16),
        scratch_shapes=[
            pltpu.VMEM(fwd.shape, BF16),
            pltpu.VMEM(inv.shape, BF16),
            pltpu.VMEM(tw.shape, F32),
            pltpu.VMEM((2, both // 128, chips * chans, 128), F32),
            pltpu.VMEM((2, both // 128, chips * chans, 128), F32),
            pltpu.SemaphoreType.DMA((3,)),
        ],
        compiler_params=pltpu.CompilerParams(vmem_limit_bytes=VMEM),
        cost_estimate=pl.CostEstimate(flops=8 * 10**9, bytes_accessed=8 * 2**20, transcendentals=0),
        name="long_conv",
    )(x, fwd, inv, tw, a, ai, m, f)


def cos_sin(product, modulus):
    phase = (product % modulus).astype(F32) * (2.0 * math.pi / modulus)
    return jnp.cos(phase), jnp.sin(phase)


def twice(t):
    zero = jnp.zeros_like(t)
    return jnp.block([[t, zero], [zero, t]])


def column_tables(core, rows, cols, padded):
    i = lax.iota(jnp.int32, cols)
    b = 2 * (i % CHIPS) + ((i // CHIPS) ^ core)
    k1 = lax.iota(jnp.int32, rows)
    tw = jnp.concatenate(cos_sin(b[:, None] * k1[None, :], padded), axis=1)
    k2 = lax.iota(jnp.int32, cols)
    c, s = cos_sin(k2[:, None] * b[None, :], cols)
    a = jnp.block([[c, s], [-s, c]])
    twist = jnp.stack(cos_sin(jnp.mod((b[:, None] - b[None, :]) * rows, padded), padded))

    return tw, twice(a.astype(BF16)), twice(a.T.astype(BF16)), jnp.stack([c, s]), twist


def gather_line(block, axis):
    d1 = send(block, **{axis: -1})
    d3 = send(block, **{axis: 1})
    d2 = send(block, **{axis: 2})
    return jnp.concatenate([block, d1, d2, d3], axis=0)


def per_device(tokens, in_weight, filter_spectrum, skip_bias, out_weight):
    rows, _, width = tokens.shape
    cols = SEQ
    padded = 2 * rows * cols
    s = lax.axis_index("seq")
    h = lax.axis_index("ch")
    z, y, x, core = coords(s)
    chan = in_weight.shape[2] // 2
    depth = in_weight.shape[0]

    mine = tokens.reshape(rows, width)
    filt = jnp.transpose(filter_spectrum, (3, 1, 0, 2)).reshape(4, -1, 2 * cols)
    filt = jnp.concatenate(split_table(filt), axis=1)

    def half_for(c):
        w = lax.dynamic_slice_in_dim(in_weight, c * chan, chan, 2)
        f = lax.dynamic_slice_in_dim(filt, 2 * c, 2, 0)
        return jnp.transpose(w, (1, 0, 2)).reshape(3 * depth, chan), jnp.concatenate([f[0], f[1]], axis=1)

    keep, keep_f = half_for(core)
    give, give_f = half_for(1 - core)
    far_near = send(give[depth:], dz=1, dc=1)
    far = send(keep[depth:], dz=1)
    near = send(give, dc=1)
    near_f = send(give_f, dc=1)
    other = send(mine, dc=1)

    def ordered(own, partner, axis=0):
        return jnp.concatenate(
            [jnp.where(core == 0, own, partner), jnp.where(core == 0, partner, own)], axis=axis
        )

    def block_of(n):
        own, away = slice(n * depth, (n + 1) * depth), slice((n - 1) * depth, n * depth)
        return jnp.concatenate([ordered(keep[own], near[own]), ordered(far[away], far_near[away])], axis=0)

    key_block, value_block = block_of(1), block_of(2)
    f_lanes = 2 * cols
    gate_block = jnp.concatenate(
        [
            ordered(keep[:depth], near[:depth]),
            jnp.concatenate(
                [
                    ordered(keep_f[:, :f_lanes], near_f[:, :f_lanes], 1),
                    ordered(keep_f[:, f_lanes:], near_f[:, f_lanes:], 1),
                ],
                axis=1,
            ),
        ],
        axis=0,
    )
    gathered = lax.all_gather(gate_block, "seq", axis=0, axis_index_groups=SAME_CORE)
    key_block, value_block, other = lax.optimization_barrier((key_block, value_block, other))
    half_ow = out_weight.shape[0] // 2
    ow_part = lax.dynamic_slice_in_dim(out_weight, core * half_ow, half_ow, 0)
    key_line, value_line, ow_part = lax.optimization_barrier(
        (gather_line(key_block, "dx"), gather_line(value_block, "dy"), ow_part)
    )

    order = np.arange(32)
    p_, q_, dz = order // 8, (order // 2) % 4, order % 2
    key_order = ((z ^ dz) * 4 + (y + p_) % 4) * 4 + (x + q_) % 4
    value_order = ((z ^ dz) * 4 + (y + q_) % 4) * 4 + (x + p_) % 4
    order = jnp.stack([key_order, value_order])
    first = sum_part(first_kernel, "first_part", order, mine, other, [], [key_line, value_line], True)
    near_lines = [send(key_line, dy=-1), send(key_line, dy=1), send(value_line, dx=-1), send(value_line, dx=1)]
    near_lines, first = lax.optimization_barrier((near_lines, first))
    halves = cut_halves(near_lines)
    last_lines = [
        send(halves[0], dy=-1),
        send(halves[1], dy=1),
        send(halves[2], dx=-1),
        send(halves[3], dx=1),
    ]
    totals = sum_part(second_kernel, "second_part", order, mine, other, first[:2], near_lines, False)

    perm = []
    for t in range(SEQ):
        tz, ty, tx, tc = coords(t)
        for th in range(2):
            perm.append((t * 2 + th, index_of(tz ^ tc, ty, tx, tc) * 2 + 1 - th))
    ow_same = lax.ppermute(ow_part, ("seq", "ch"), perm)
    ow_cross = send(ow_same, dc=1)

    source = last_part(totals, first[2:], last_lines)
    packed = source.reshape(CHIPS, chan // CHIPS, 2 * rows)
    mine_ch = lax.all_to_all(packed, "seq", 0, 0, axis_index_groups=SAME_CORE)

    tw, a, ai, cs, twist = column_tables(core, rows, cols, padded)
    f, m = filter_part(z, gathered, cs, twist)
    forward, inverse = row_tables(rows, padded)
    fwd = jnp.asarray(forward.astype(np.float32).astype(ml_dtypes.bfloat16))
    inv = jnp.asarray(inverse.astype(np.float32).astype(ml_dtypes.bfloat16))
    conv = long_conv(mine_ch, fwd, inv, tw, a, ai, m, f)
    conv = lax.all_to_all(conv, "seq", 0, 0, axis_index_groups=SAME_CORE)
    conv = conv.reshape(chan, 2 * rows).astype(F32)

    gate = gate_part(mine, other, gathered).astype(F32)
    skip = lax.dynamic_slice_in_dim(skip_bias, core * chan, chan, 0)[:, None]
    gated = (gate * (conv + skip * source.astype(F32))).astype(BF16)

    kept = rows // 2
    own_here = lax.dynamic_slice(gated, (0, h * kept), (chan, kept))
    own_there = lax.dynamic_slice(gated, (0, (1 - h) * kept), (chan, kept))
    oth_here = lax.dynamic_slice(gated, (0, rows + h * kept), (chan, kept))
    oth_there = lax.dynamic_slice(gated, (0, rows + (1 - h) * kept), (chan, kept))
    swap_ch = [(0, 1), (1, 0)]
    from_h = lax.ppermute(own_there, "ch", swap_ch)
    perm2 = []
    for t in range(SEQ):
        for th in range(2):
            perm2.append((t * 2 + th, (t ^ 1) * 2 + 1 - th))
    from_hc = lax.ppermute(oth_there, ("seq", "ch"), perm2)
    from_c = send(oth_here, dc=1)
    here = ordered(own_here, from_c)

    mixed = mix_part(None, [here], [out_weight])
    mixed = mix_part(mixed, [from_h, from_hc], [ow_same, ow_cross])
    return mixed.reshape(kept, 1, width)


def solution(mesh):
    in_specs = (
        P(None, "seq", None),
        P("seq", None, "ch"),
        P(None, "seq", None, "ch"),
        P("ch"),
        P("ch", None),
    )
    return jax.shard_map(
        per_device, mesh=mesh, in_specs=in_specs, out_specs=P("ch", "seq", None), check_vma=False
    )
```

```python
import functools
import math

import jax
import jax.numpy as jnp
import ml_dtypes
import numpy as np
from jax import lax
from jax.experimental import pallas as pl
from jax.experimental.pallas import tpu as pltpu
from jax.sharding import PartitionSpec as P

BF16 = jnp.bfloat16
F32 = jnp.float32
HIGH = lax.Precision.HIGHEST
SEQ = 64
VMEM = 60 * 2**20
CHIPS = 32
SAME_CORE = [[2 * p + j for p in range(CHIPS)] for j in range(2)]


def coords(s):
    return s // 32, (s // 8) % 4, (s // 2) % 4, s % 2


def index_of(z, y, x, c):
    return ((z * 4 + y) * 4 + x) * 2 + c


def send(value, dz=0, dy=0, dx=0, dc=0):
    perm = []
    for s in range(SEQ):
        z, y, x, c = coords(s)
        perm.append((s, index_of((z + dz) % 2, (y + dy) % 4, (x + dx) % 4, c ^ dc)))
    return lax.ppermute(value, "seq", perm)


def split_table(table):
    upper = table.astype(BF16)
    lower = (table - upper.astype(F32)).astype(BF16)
    return upper, lower


def row_tables(rows, padded):
    points = 2 * rows
    a = np.arange(rows)
    k = np.arange(rows)
    phase = 2.0 * np.pi * ((a[:, None] * k[None, :]) % points) / points
    re, im = np.cos(phase), -np.sin(phase)
    im[:, 0] = np.where(a % 2 == 0, 1.0, -1.0)
    forward = np.concatenate([re, im], axis=1)
    scale = np.full((rows,), 2.0)
    scale[0] = 1.0
    inverse = np.concatenate([re * scale, im * scale], axis=1).T / padded
    return forward, inverse


def picked(order_ref, row, group, tok_ref):
    blocks = [
        tok_ref[:, pl.ds(pl.multiple_of(order_ref[row, group * 8 + i] * 128, 128), 128)]
        for i in range(8)
    ]
    return jnp.concatenate(blocks, axis=1)


def by_column(run, mine_ref, other_ref):
    step = pl.program_id(0)

    @pl.when(step < 2)
    def _():
        run(mine_ref)

    @pl.when(step >= 2)
    def _():
        run(other_ref)


def first_kernel(order_ref, mine_ref, other_ref, key_line, value_line, *outs):
    key_ref, value_ref, key_tok_ref, value_tok_ref = outs

    def run(tok_ref):
        for row, line, total_ref, last_ref in (
            (0, key_line, key_ref, key_tok_ref),
            (1, value_line, value_ref, value_tok_ref),
        ):
            total_ref[...] = jnp.dot(
                picked(order_ref, row, 0, tok_ref), line[...], preferred_element_type=F32
            )
            last_ref[...] = picked(order_ref, row, 2, tok_ref)

    by_column(run, mine_ref, other_ref)


def second_kernel(order_ref, mine_ref, other_ref, key_in, value_in, k1, k3, v1, v3, key_ref, value_ref):
    def run(tok_ref):
        for row, before, e1, e3, total_ref in (
            (0, key_in, k1, k3, key_ref),
            (1, value_in, v1, v3, value_ref),
        ):
            total = before[...]
            total += jnp.dot(picked(order_ref, row, 1, tok_ref), e1[...], preferred_element_type=F32)
            total += jnp.dot(picked(order_ref, row, 3, tok_ref), e3[...], preferred_element_type=F32)
            total_ref[...] = total

    by_column(run, mine_ref, other_ref)


def sum_part(kernel, name, order, mine, other, totals, weights, last):
    rows, width = mine.shape
    chan = weights[0].shape[1]
    tile = rows // 2
    quarter = width // 4
    by_row = [pl.BlockSpec((tile, chan), lambda i, o: (i, 0))] * 2
    tokens_out = [pl.BlockSpec((tile, quarter), lambda i, o: (i, 0))] * 2
    shapes = [jax.ShapeDtypeStruct((2 * rows, chan), F32)] * 2
    token_shapes = [jax.ShapeDtypeStruct((2 * rows, quarter), BF16)] * 2
    return pl.pallas_call(
        kernel,
        grid_spec=pltpu.PrefetchScalarGridSpec(
            num_scalar_prefetch=1,
            grid=(4,),
            in_specs=[
                pl.BlockSpec((tile, width), lambda i, o: (jnp.minimum(i, 1), 0)),
                pl.BlockSpec((tile, width), lambda i, o: (jnp.maximum(i - 2, 0), 0)),
            ]
            + by_row[: len(totals)]
            + [pl.BlockSpec((quarter, chan), lambda i, o: (0, 0))] * len(weights),
            out_specs=by_row + (tokens_out if last else []),
        ),
        out_shape=shapes + (token_shapes if last else []),
        compiler_params=pltpu.CompilerParams(vmem_limit_bytes=VMEM),
        cost_estimate=pl.CostEstimate(
            flops=2 * 2 * rows * quarter * chan * len(weights), bytes_accessed=18 * 2**20, transcendentals=0
        ),
        name=name,
    )(order, mine, other, *totals, *weights)


def cut_kernel(*refs):
    for src, dst in zip(refs[:4], refs[4:], strict=True):
        dst[...] = src[...]


def cut_halves(lines):
    rows, width = lines[0].shape
    tile = rows // 4
    upper = pl.BlockSpec((tile, width), lambda i: (i, 0))
    lower = pl.BlockSpec((tile, width), lambda i: (i + 2, 0))
    return pl.pallas_call(
        cut_kernel,
        grid=(2,),
        in_specs=[upper, lower, upper, lower],
        out_specs=[upper] * 4,
        out_shape=[jax.ShapeDtypeStruct((rows // 2, width), BF16)] * 4,
        compiler_params=pltpu.CompilerParams(vmem_limit_bytes=VMEM),
        cost_estimate=pl.CostEstimate(flops=0, bytes_accessed=4 * rows * width * 2, transcendentals=0),
        name="cut_halves",
    )(*lines)


def last_kernel(key_ref, value_ref, key_tok_ref, value_tok_ref, ka, kb, va, vb, send_ref):
    half = ka.shape[0]

    def finish(total_ref, tok_ref, wa, wb):
        total = total_ref[...]
        total += jnp.dot(tok_ref[:, :half], wa[...], preferred_element_type=F32)
        total += jnp.dot(tok_ref[:, half:], wb[...], preferred_element_type=F32)
        return total.astype(BF16).astype(F32)

    source = finish(key_ref, key_tok_ref, ka, kb) * finish(value_ref, value_tok_ref, va, vb)
    send_ref[...] = source.T.astype(BF16)


def last_part(totals, tokens, weights):
    total, chan = totals[0].shape
    quarter = tokens[0].shape[1]
    tile = total // 4
    return pl.pallas_call(
        last_kernel,
        grid=(4,),
        in_specs=[pl.BlockSpec((tile, chan), lambda i: (i, 0))] * 2
        + [pl.BlockSpec((tile, quarter), lambda i: (i, 0))] * 2
        + [pl.BlockSpec((quarter // 2, chan), lambda i: (0, 0))] * 4,
        out_specs=pl.BlockSpec((chan, tile), lambda i: (0, i)),
        out_shape=jax.ShapeDtypeStruct((chan, total), BF16),
        compiler_params=pltpu.CompilerParams(vmem_limit_bytes=VMEM),
        cost_estimate=pl.CostEstimate(
            flops=2 * 2 * total * quarter * chan, bytes_accessed=13 * 2**20, transcendentals=0
        ),
        name="last_part",
    )(*totals, *tokens, *weights)


def gate_kernel(mine_ref, other_ref, weight_ref, out_ref):
    chips, deep, chan = weight_ref.shape

    def run(tok_ref):
        weight = weight_ref[...].reshape(chips * deep, chan)
        gate = jnp.dot(tok_ref[...], weight, preferred_element_type=F32)
        out_ref[...] = gate.T.astype(BF16)

    by_column(run, mine_ref, other_ref)


def gate_part(mine, other, gathered):
    rows, width = mine.shape
    chips, _, chan = gathered.shape
    tile = rows // 2
    return pl.pallas_call(
        gate_kernel,
        grid=(4,),
        in_specs=[
            pl.BlockSpec((tile, width), lambda i: (jnp.minimum(i, 1), 0)),
            pl.BlockSpec((tile, width), lambda i: (jnp.maximum(i - 2, 0), 0)),
            pl.BlockSpec((chips, width // chips, chan), lambda i: (0, 0, 0)),
        ],
        out_specs=pl.BlockSpec((chan, tile), lambda i: (0, i)),
        out_shape=jax.ShapeDtypeStruct((chan, 2 * rows), BF16),
        compiler_params=pltpu.CompilerParams(vmem_limit_bytes=VMEM),
        cost_estimate=pl.CostEstimate(
            flops=2 * 2 * rows * width * chan, bytes_accessed=13 * 2**20, transcendentals=0
        ),
        name="gate_part",
    )(mine, other, gathered)


def turn(ref):
    return ref[...].astype(F32).T.astype(BF16)


def mix_kernel(here, w_here, out_ref, lhs_ref):
    @pl.when(pl.program_id(0) == 0)
    def _():
        lhs_ref[...] = turn(here)

    out_ref[...] = jnp.dot(lhs_ref[...], w_here[...], preferred_element_type=F32)


def mix_more_kernel(total_ref, near_h, far_h, w_near, w_far, out_ref, lhs_ref):
    m = near_h.shape[0]

    @pl.when(pl.program_id(0) == 0)
    def _():
        lhs_ref[:, :m] = turn(near_h)
        lhs_ref[:, m:] = turn(far_h)

    total = total_ref[...]
    total += jnp.dot(lhs_ref[:, :m], w_near[...], preferred_element_type=F32)
    total += jnp.dot(lhs_ref[:, m:], w_far[...], preferred_element_type=F32)
    out_ref[...] = total.astype(BF16)


def mix_part(total, parts, weights):
    rows = parts[0].shape[1]
    width = weights[0].shape[1]
    tile = width // 4
    depth = sum(p.shape[0] for p in parts)
    totals = [] if total is None else [total]

    def whole(g):
        return pl.BlockSpec(g.shape, lambda i: (0, 0))

    def tiled(w):
        return pl.BlockSpec((w.shape[0], tile), lambda i: (0, i))

    return pl.pallas_call(
        mix_kernel if total is None else mix_more_kernel,
        grid=(4,),
        in_specs=[tiled(t) for t in totals] + [whole(p) for p in parts] + [tiled(w) for w in weights],
        out_specs=pl.BlockSpec((rows, tile), lambda i: (0, i)),
        out_shape=jax.ShapeDtypeStruct((rows, width), F32 if total is None else BF16),
        scratch_shapes=[pltpu.VMEM((rows, depth), BF16)],
        compiler_params=pltpu.CompilerParams(vmem_limit_bytes=VMEM),
        cost_estimate=pl.CostEstimate(
            flops=2 * rows * depth * width, bytes_accessed=12 * 2**20, transcendentals=0
        ),
        name="mix_part" if total is None else "mix_more",
    )(*totals, *parts, *weights)


def filter_kernel(z_ref, x_ref, cs_ref, twist_ref, f_ref, m_ref):
    chips, _, lanes = x_ref.shape
    lanes = lanes // 2
    points = 2 * chips * 16
    rows, cols = points // 2, lanes // 2

    def part(n):
        rows_of = slice(16 * n, 16 * (n + 1))
        cores = [x_ref[:, rows_of, c * lanes : (c + 1) * lanes] for c in range(2)]
        return jnp.stack(cores, axis=1).reshape(points, lanes)

    upper, lower = part(0), part(1)
    whole = (upper.astype(F32) + lower.astype(F32)).T
    i = lax.broadcasted_iota(jnp.int32, (rows, rows), 0)
    j = lax.broadcasted_iota(jnp.int32, (rows, rows), 1)
    mirror = (i + j == rows).astype(F32).astype(BF16)
    i = lax.broadcasted_iota(jnp.int32, (lanes, lanes), 0)
    j = lax.broadcasted_iota(jnp.int32, (lanes, lanes), 1)
    flip = ((i // cols == j // cols) & (i % cols + j % cols == cols - 1)).astype(F32).astype(BF16)

    def mirrored(part):
        turned = jnp.dot(flip, part[:, rows:], preferred_element_type=F32).astype(BF16)
        return jnp.dot(turned, mirror, preferred_element_type=F32)

    other = mirrored(upper.astype(F32).T.astype(BF16)) + mirrored(lower.astype(F32).T.astype(BF16))
    f_ref[:, :rows] = 0.5 * (whole[:cols, :rows] + other[:cols])
    f_ref[:, rows:] = 0.5 * (whole[cols:, :rows] - other[cols:])
    c, s = cs_ref[0], cs_ref[1]

    def contract(left, right):
        return lax.dot_general(
            left, right, (((0,), (0,)), ((), ())), precision=HIGH, preferred_element_type=F32
        )

    m_ref[...] = jnp.zeros_like(m_ref)
    for n, k in enumerate((0, rows)):
        e_re, e_im = whole[:cols, k : k + 1], whole[cols:, k : k + 1]
        u = c * e_re - s * e_im
        v = s * e_re + c * e_im
        g = contract(u, c) + contract(v, s)
        if n:
            g = g * twist_ref[0] - (contract(v, c) - contract(u, s)) * twist_ref[1]
        for start in (n * cols, lanes + n * cols):
            spot = slice(start, start + cols)
            m_ref[spot, spot] = g.astype(BF16)


def filter_part(z, gathered, cs, twist):
    chips = gathered.shape[0]
    cols = cs.shape[1]
    rows = chips * 16
    lanes = 2 * cols
    return pl.pallas_call(
        filter_kernel,
        grid_spec=pltpu.PrefetchScalarGridSpec(
            num_scalar_prefetch=1,
            grid=(1,),
            in_specs=[
                pl.BlockSpec((chips, 32, 2 * lanes), lambda i, z: (0, 4, z[0])),
                pl.BlockSpec(cs.shape, lambda i, z: (0, 0, 0)),
                pl.BlockSpec(twist.shape, lambda i, z: (0, 0, 0)),
            ],
            out_specs=[
                pl.BlockSpec((cols, 2 * rows), lambda i, z: (0, 0)),
                pl.BlockSpec((2 * lanes, 2 * lanes), lambda i, z: (0, 0)),
            ],
        ),
        out_shape=[
            jax.ShapeDtypeStruct((cols, 2 * rows), F32),
            jax.ShapeDtypeStruct((2 * lanes, 2 * lanes), BF16),
        ],
        compiler_params=pltpu.CompilerParams(vmem_limit_bytes=VMEM),
        cost_estimate=pl.CostEstimate(flops=10**9, bytes_accessed=2**20, transcendentals=0),
        name="filter_part",
    )(z.reshape(1), gathered, cs, twist)


def conv_kernel(
    x_ref, fwd_hbm, inv_hbm, tw_hbm, a_ref, ai_ref, m_ref, f_ref, y_ref, fwd_ref, inv_ref, tw_ref, r_ref, q_ref, sems
):
    copies = [
        pltpu.make_async_copy(src, dst, sems.at[i])
        for i, (src, dst) in enumerate(((fwd_hbm, fwd_ref), (tw_hbm, tw_ref), (inv_hbm, inv_ref)))
    ]
    for copy in copies:
        copy.start()
    chips, chans, both = x_ref.shape
    rows = both // 2
    blocks = rows // 128
    half = 2 * chips
    copies[0].wait()
    for col in range(2):
        x = x_ref[:, :, col * rows : (col + 1) * rows].reshape(chips * chans, rows)
        r = jnp.dot(x, fwd_ref[...], preferred_element_type=F32)
        r = r.reshape(chips, chans, 2 * rows)
        if col == 0:
            copies[1].wait()
        tw = tw_ref[col * chips : (col + 1) * chips, :]
        cos = tw[:, None, :rows]
        sin = tw[:, None, rows:]
        re, im = r[:, :, :rows], r[:, :, rows:]
        turned_re = (re * cos + im * sin).reshape(chips * chans, rows)
        turned_im = (im * cos - re * sin).reshape(chips * chans, rows)
        for k in range(blocks):
            r_ref[col, k] = turned_re[:, k * 128 : (k + 1) * 128]
            r_ref[col, blocks + k] = turned_im[:, k * 128 : (k + 1) * 128]
    lane = lax.broadcasted_iota(jnp.int32, (4 * half, 128), 1)

    def pair(n, carry):
        picks = [pl.ds(2 * n + i, chips, stride=chans) for i in range(2)]
        parts = [
            jnp.concatenate([r_ref[col, part * blocks + k, pick, :] for k in range(blocks)], axis=1)
            for pick in picks
            for part in range(2)
            for col in range(2)
        ]
        turned = jnp.concatenate(parts, axis=0).astype(BF16)
        s = jnp.dot(a_ref[...], turned, preferred_element_type=F32)
        f_re, f_im = f_ref[:, :rows], f_ref[:, rows:]
        filtered = []
        for i in range(2):
            s_re = s[2 * i * half : (2 * i + 1) * half]
            s_im = s[(2 * i + 1) * half : (2 * i + 2) * half]
            filtered += [s_re * f_re - s_im * f_im, s_re * f_im + s_im * f_re]
        filtered = jnp.concatenate(filtered, axis=0).astype(BF16)
        back = jnp.dot(ai_ref[...], filtered, preferred_element_type=F32)
        edge = jnp.dot(m_ref[...], turned[:, :128], preferred_element_type=F32)
        head = jnp.where(lane == 0, edge, back[:, :128])
        back = jnp.concatenate([head, back[:, 128:]], axis=1)
        cos, sin = tw_ref[:, :rows], tw_ref[:, rows:]
        for i, pick in enumerate(picks):
            b_re = back[2 * i * half : (2 * i + 1) * half]
            b_im = back[(2 * i + 1) * half : (2 * i + 2) * half]
            out_re = b_re * cos - b_im * sin
            out_im = b_im * cos + b_re * sin
            for col in range(2):
                part = slice(col * chips, (col + 1) * chips)
                for k in range(blocks):
                    q_ref[col, k, pick, :] = out_re[part, k * 128 : (k + 1) * 128]
                    q_ref[col, blocks + k, pick, :] = out_im[part, k * 128 : (k + 1) * 128]
        return carry

    lax.fori_loop(0, chans // 2, pair, 0, unroll=2)
    copies[2].wait()
    for col in range(2):
        q = jnp.concatenate([q_ref[col, k].astype(BF16) for k in range(2 * blocks)], axis=1)
        y = jnp.dot(q, inv_ref[...], preferred_element_type=F32)
        y_ref[:, :, col * rows : (col + 1) * rows] = y.astype(BF16).reshape(chips, chans, rows)


def long_conv(x, fwd, inv, tw, a, ai, m, f):
    chips, chans, both = x.shape
    vmem = pl.BlockSpec(memory_space=pltpu.VMEM)
    hbm = pl.BlockSpec(memory_space=pl.ANY)
    return pl.pallas_call(
        conv_kernel,
        in_specs=[vmem, hbm, hbm, hbm, vmem, vmem, vmem, vmem],
        out_specs=vmem,
        out_shape=jax.ShapeDtypeStruct(x.shape, BF16),
        scratch_shapes=[
            pltpu.VMEM(fwd.shape, BF16),
            pltpu.VMEM(inv.shape, BF16),
            pltpu.VMEM(tw.shape, F32),
            pltpu.VMEM((2, both // 128, chips * chans, 128), F32),
            pltpu.VMEM((2, both // 128, chips * chans, 128), F32),
            pltpu.SemaphoreType.DMA((3,)),
        ],
        compiler_params=pltpu.CompilerParams(vmem_limit_bytes=VMEM),
        cost_estimate=pl.CostEstimate(flops=8 * 10**9, bytes_accessed=8 * 2**20, transcendentals=0),
        name="long_conv",
    )(x, fwd, inv, tw, a, ai, m, f)


def cos_sin(product, modulus):
    phase = (product % modulus).astype(F32) * (2.0 * math.pi / modulus)
    return jnp.cos(phase), jnp.sin(phase)


def twice(t):
    zero = jnp.zeros_like(t)
    return jnp.block([[t, zero], [zero, t]])


def column_tables(core, rows, cols, padded):
    i = lax.iota(jnp.int32, cols)
    b = 2 * (i % CHIPS) + ((i // CHIPS) ^ core)
    k1 = lax.iota(jnp.int32, rows)
    tw = jnp.concatenate(cos_sin(b[:, None] * k1[None, :], padded), axis=1)
    k2 = lax.iota(jnp.int32, cols)
    c, s = cos_sin(k2[:, None] * b[None, :], cols)
    a = jnp.block([[c, s], [-s, c]])
    twist = jnp.stack(cos_sin(jnp.mod((b[:, None] - b[None, :]) * rows, padded), padded))

    return tw, twice(a.astype(BF16)), twice(a.T.astype(BF16)), jnp.stack([c, s]), twist


def gather_line(block, axis):
    d1 = send(block, **{axis: -1})
    d3 = send(block, **{axis: 1})
    d2 = send(block, **{axis: 2})
    return jnp.concatenate([block, d1, d2, d3], axis=0)


def per_device(tokens, in_weight, filter_spectrum, skip_bias, out_weight):
    rows, _, width = tokens.shape
    cols = SEQ
    padded = 2 * rows * cols
    s = lax.axis_index("seq")
    h = lax.axis_index("ch")
    z, y, x, core = coords(s)
    chan = in_weight.shape[2] // 2
    depth = in_weight.shape[0]

    mine = tokens.reshape(rows, width)
    filt = jnp.transpose(filter_spectrum, (3, 1, 0, 2)).reshape(4, -1, 2 * cols)
    filt = jnp.concatenate(split_table(filt), axis=1)

    def half_for(c):
        w = lax.dynamic_slice_in_dim(in_weight, c * chan, chan, 2)
        f = lax.dynamic_slice_in_dim(filt, 2 * c, 2, 0)
        return jnp.transpose(w, (1, 0, 2)).reshape(3 * depth, chan), jnp.concatenate([f[0], f[1]], axis=1)

    keep, keep_f = half_for(core)
    give, give_f = half_for(1 - core)
    far_near = send(give[depth:], dz=1, dc=1)
    far = send(keep[depth:], dz=1)
    near = send(give, dc=1)
    near_f = send(give_f, dc=1)
    other = send(mine, dc=1)

    def ordered(own, partner, axis=0):
        return jnp.concatenate(
            [jnp.where(core == 0, own, partner), jnp.where(core == 0, partner, own)], axis=axis
        )

    def block_of(n):
        own, away = slice(n * depth, (n + 1) * depth), slice((n - 1) * depth, n * depth)
        return jnp.concatenate([ordered(keep[own], near[own]), ordered(far[away], far_near[away])], axis=0)

    key_block, value_block = block_of(1), block_of(2)
    f_lanes = 2 * cols
    gate_block = jnp.concatenate(
        [
            ordered(keep[:depth], near[:depth]),
            jnp.concatenate(
                [
                    ordered(keep_f[:, :f_lanes], near_f[:, :f_lanes], 1),
                    ordered(keep_f[:, f_lanes:], near_f[:, f_lanes:], 1),
                ],
                axis=1,
            ),
        ],
        axis=0,
    )
    gathered = lax.all_gather(gate_block, "seq", axis=0, axis_index_groups=SAME_CORE)
    key_block, value_block, other = lax.optimization_barrier((key_block, value_block, other))
    half_ow = out_weight.shape[0] // 2
    ow_part = lax.dynamic_slice_in_dim(out_weight, core * half_ow, half_ow, 0)
    key_line, value_line, ow_part = lax.optimization_barrier(
        (gather_line(key_block, "dx"), gather_line(value_block, "dy"), ow_part)
    )

    order = np.arange(32)
    p_, q_, dz = order // 8, (order // 2) % 4, order % 2
    key_order = ((z ^ dz) * 4 + (y + p_) % 4) * 4 + (x + q_) % 4
    value_order = ((z ^ dz) * 4 + (y + q_) % 4) * 4 + (x + p_) % 4
    order = jnp.stack([key_order, value_order])
    first = sum_part(first_kernel, "first_part", order, mine, other, [], [key_line, value_line], True)
    near_lines = [send(key_line, dy=-1), send(key_line, dy=1), send(value_line, dx=-1), send(value_line, dx=1)]
    near_lines, first = lax.optimization_barrier((near_lines, first))
    halves = cut_halves(near_lines)
    last_lines = [
        send(halves[0], dy=-1),
        send(halves[1], dy=1),
        send(halves[2], dx=-1),
        send(halves[3], dx=1),
    ]
    totals = sum_part(second_kernel, "second_part", order, mine, other, first[:2], near_lines, False)

    perm = []
    for t in range(SEQ):
        tz, ty, tx, tc = coords(t)
        for th in range(2):
            perm.append((t * 2 + th, index_of(tz ^ tc, ty, tx, tc) * 2 + 1 - th))
    ow_same = lax.ppermute(ow_part, ("seq", "ch"), perm)

    source = last_part(totals, first[2:], last_lines)
    packed = source.reshape(CHIPS, chan // CHIPS, 2 * rows)
    mine_ch = lax.all_to_all(packed, "seq", 0, 0, axis_index_groups=SAME_CORE)
    mine_ch, ow_same = lax.optimization_barrier((mine_ch, ow_same))
    ow_cross = send(ow_same, dc=1)

    tw, a, ai, cs, twist = column_tables(core, rows, cols, padded)
    f, m = filter_part(z, gathered, cs, twist)
    forward, inverse = row_tables(rows, padded)
    fwd = jnp.asarray(forward.astype(np.float32).astype(ml_dtypes.bfloat16))
    inv = jnp.asarray(inverse.astype(np.float32).astype(ml_dtypes.bfloat16))
    conv = long_conv(mine_ch, fwd, inv, tw, a, ai, m, f)
    conv = lax.all_to_all(conv, "seq", 0, 0, axis_index_groups=SAME_CORE)
    conv = conv.reshape(chan, 2 * rows).astype(F32)

    gate = gate_part(mine, other, gathered).astype(F32)
    skip = lax.dynamic_slice_in_dim(skip_bias, core * chan, chan, 0)[:, None]
    gated = (gate * (conv + skip * source.astype(F32))).astype(BF16)

    kept = rows // 2
    own_here = lax.dynamic_slice(gated, (0, h * kept), (chan, kept))
    own_there = lax.dynamic_slice(gated, (0, (1 - h) * kept), (chan, kept))
    oth_here = lax.dynamic_slice(gated, (0, rows + h * kept), (chan, kept))
    oth_there = lax.dynamic_slice(gated, (0, rows + (1 - h) * kept), (chan, kept))
    swap_ch = [(0, 1), (1, 0)]
    from_h = lax.ppermute(own_there, "ch", swap_ch)
    perm2 = []
    for t in range(SEQ):
        for th in range(2):
            perm2.append((t * 2 + th, (t ^ 1) * 2 + 1 - th))
    from_hc = lax.ppermute(oth_there, ("seq", "ch"), perm2)
    from_c = send(oth_here, dc=1)
    here = ordered(own_here, from_c)

    mixed = mix_part(None, [here], [out_weight])
    mixed = mix_part(mixed, [from_h, from_hc], [ow_same, ow_cross])
    return mixed.reshape(kept, 1, width)


def solution(mesh):
    in_specs = (
        P(None, "seq", None),
        P("seq", None, "ch"),
        P(None, "seq", None, "ch"),
        P("ch"),
        P("ch", None),
    )
    return jax.shard_map(
        per_device, mesh=mesh, in_specs=in_specs, out_specs=P("ch", "seq", None), check_vma=False
    )
```

```python
import functools
import math

import jax
import jax.numpy as jnp
import ml_dtypes
import numpy as np
from jax import lax
from jax.experimental import pallas as pl
from jax.experimental.pallas import tpu as pltpu
from jax.sharding import PartitionSpec as P

BF16 = jnp.bfloat16
F32 = jnp.float32
HIGH = lax.Precision.HIGHEST
SEQ = 64
VMEM = 60 * 2**20
CHIPS = 32
SAME_CORE = [[2 * p + j for p in range(CHIPS)] for j in range(2)]


def coords(s):
    return s // 32, (s // 8) % 4, (s // 2) % 4, s % 2


def index_of(z, y, x, c):
    return ((z * 4 + y) * 4 + x) * 2 + c


def send(value, dz=0, dy=0, dx=0, dc=0):
    perm = []
    for s in range(SEQ):
        z, y, x, c = coords(s)
        perm.append((s, index_of((z + dz) % 2, (y + dy) % 4, (x + dx) % 4, c ^ dc)))
    return lax.ppermute(value, "seq", perm)


def split_table(table):
    upper = table.astype(BF16)
    lower = (table - upper.astype(F32)).astype(BF16)
    return upper, lower


def row_tables(rows, padded):
    points = 2 * rows
    a = np.arange(rows)
    k = np.arange(rows)
    phase = 2.0 * np.pi * ((a[:, None] * k[None, :]) % points) / points
    re, im = np.cos(phase), -np.sin(phase)
    im[:, 0] = np.where(a % 2 == 0, 1.0, -1.0)
    forward = np.concatenate([re, im], axis=1)
    scale = np.full((rows,), 2.0)
    scale[0] = 1.0
    inverse = np.concatenate([re * scale, im * scale], axis=1).T / padded
    return forward, inverse


def picked(order_ref, row, group, tok_ref):
    blocks = [
        tok_ref[:, pl.ds(pl.multiple_of(order_ref[row, group * 8 + i] * 128, 128), 128)]
        for i in range(8)
    ]
    return jnp.concatenate(blocks, axis=1)


def by_column(run, mine_ref, other_ref):
    step = pl.program_id(0)

    @pl.when(step < 2)
    def _():
        run(mine_ref)

    @pl.when(step >= 2)
    def _():
        run(other_ref)


def first_kernel(order_ref, mine_ref, other_ref, key_line, value_line, *outs):
    key_ref, value_ref, key_tok_ref, value_tok_ref = outs

    def run(tok_ref):
        for row, line, total_ref, last_ref in (
            (0, key_line, key_ref, key_tok_ref),
            (1, value_line, value_ref, value_tok_ref),
        ):
            total_ref[...] = jnp.dot(
                picked(order_ref, row, 0, tok_ref), line[...], preferred_element_type=F32
            )
            last_ref[...] = picked(order_ref, row, 2, tok_ref)

    by_column(run, mine_ref, other_ref)


def second_kernel(order_ref, mine_ref, other_ref, key_in, value_in, k1, k3, v1, v3, key_ref, value_ref):
    def run(tok_ref):
        for row, before, e1, e3, total_ref in (
            (0, key_in, k1, k3, key_ref),
            (1, value_in, v1, v3, value_ref),
        ):
            total = before[...]
            total += jnp.dot(picked(order_ref, row, 1, tok_ref), e1[...], preferred_element_type=F32)
            total += jnp.dot(picked(order_ref, row, 3, tok_ref), e3[...], preferred_element_type=F32)
            total_ref[...] = total

    by_column(run, mine_ref, other_ref)


def sum_part(kernel, name, order, mine, other, totals, weights, last):
    rows, width = mine.shape
    chan = weights[0].shape[1]
    tile = rows // 2
    quarter = width // 4
    by_row = [pl.BlockSpec((tile, chan), lambda i, o: (i, 0))] * 2
    tokens_out = [pl.BlockSpec((tile, quarter), lambda i, o: (i, 0))] * 2
    shapes = [jax.ShapeDtypeStruct((2 * rows, chan), F32)] * 2
    token_shapes = [jax.ShapeDtypeStruct((2 * rows, quarter), BF16)] * 2
    return pl.pallas_call(
        kernel,
        grid_spec=pltpu.PrefetchScalarGridSpec(
            num_scalar_prefetch=1,
            grid=(4,),
            in_specs=[
                pl.BlockSpec((tile, width), lambda i, o: (jnp.minimum(i, 1), 0)),
                pl.BlockSpec((tile, width), lambda i, o: (jnp.maximum(i - 2, 0), 0)),
            ]
            + by_row[: len(totals)]
            + [pl.BlockSpec((quarter, chan), lambda i, o: (0, 0))] * len(weights),
            out_specs=by_row + (tokens_out if last else []),
        ),
        out_shape=shapes + (token_shapes if last else []),
        compiler_params=pltpu.CompilerParams(vmem_limit_bytes=VMEM),
        cost_estimate=pl.CostEstimate(
            flops=2 * 2 * rows * quarter * chan * len(weights), bytes_accessed=18 * 2**20, transcendentals=0
        ),
        name=name,
    )(order, mine, other, *totals, *weights)


def cut_kernel(*refs):
    for src, dst in zip(refs[:4], refs[4:], strict=True):
        dst[...] = src[...]


def cut_halves(lines):
    rows, width = lines[0].shape
    tile = rows // 4
    upper = pl.BlockSpec((tile, width), lambda i: (i, 0))
    lower = pl.BlockSpec((tile, width), lambda i: (i + 2, 0))
    return pl.pallas_call(
        cut_kernel,
        grid=(2,),
        in_specs=[upper, lower, upper, lower],
        out_specs=[upper] * 4,
        out_shape=[jax.ShapeDtypeStruct((rows // 2, width), BF16)] * 4,
        compiler_params=pltpu.CompilerParams(vmem_limit_bytes=VMEM),
        cost_estimate=pl.CostEstimate(flops=0, bytes_accessed=4 * rows * width * 2, transcendentals=0),
        name="cut_halves",
    )(*lines)


def last_kernel(key_ref, value_ref, key_tok_ref, value_tok_ref, ka, kb, va, vb, send_ref):
    half = ka.shape[0]

    def finish(total_ref, tok_ref, wa, wb):
        total = total_ref[...]
        total += jnp.dot(tok_ref[:, :half], wa[...], preferred_element_type=F32)
        total += jnp.dot(tok_ref[:, half:], wb[...], preferred_element_type=F32)
        return total.astype(BF16).astype(F32)

    source = finish(key_ref, key_tok_ref, ka, kb) * finish(value_ref, value_tok_ref, va, vb)
    send_ref[...] = source.T.astype(BF16)


def last_part(totals, tokens, weights):
    total, chan = totals[0].shape
    quarter = tokens[0].shape[1]
    tile = total // 4
    return pl.pallas_call(
        last_kernel,
        grid=(4,),
        in_specs=[pl.BlockSpec((tile, chan), lambda i: (i, 0))] * 2
        + [pl.BlockSpec((tile, quarter), lambda i: (i, 0))] * 2
        + [pl.BlockSpec((quarter // 2, chan), lambda i: (0, 0))] * 4,
        out_specs=pl.BlockSpec((chan, tile), lambda i: (0, i)),
        out_shape=jax.ShapeDtypeStruct((chan, total), BF16),
        compiler_params=pltpu.CompilerParams(vmem_limit_bytes=VMEM),
        cost_estimate=pl.CostEstimate(
            flops=2 * 2 * total * quarter * chan, bytes_accessed=13 * 2**20, transcendentals=0
        ),
        name="last_part",
    )(*totals, *tokens, *weights)


def gate_kernel(mine_ref, other_ref, weight_ref, out_ref):
    chips, deep, chan = weight_ref.shape

    def run(tok_ref):
        weight = weight_ref[...].reshape(chips * deep, chan)
        gate = jnp.dot(tok_ref[...], weight, preferred_element_type=F32)
        out_ref[...] = gate.T.astype(BF16)

    by_column(run, mine_ref, other_ref)


def gate_part(mine, other, gathered):
    rows, width = mine.shape
    chips, _, chan = gathered.shape
    tile = rows // 2
    return pl.pallas_call(
        gate_kernel,
        grid=(4,),
        in_specs=[
            pl.BlockSpec((tile, width), lambda i: (jnp.minimum(i, 1), 0)),
            pl.BlockSpec((tile, width), lambda i: (jnp.maximum(i - 2, 0), 0)),
            pl.BlockSpec((chips, width // chips, chan), lambda i: (0, 0, 0)),
        ],
        out_specs=pl.BlockSpec((chan, tile), lambda i: (0, i)),
        out_shape=jax.ShapeDtypeStruct((chan, 2 * rows), BF16),
        compiler_params=pltpu.CompilerParams(vmem_limit_bytes=VMEM),
        cost_estimate=pl.CostEstimate(
            flops=2 * 2 * rows * width * chan, bytes_accessed=13 * 2**20, transcendentals=0
        ),
        name="gate_part",
    )(mine, other, gathered)


def turn(ref):
    return ref[...].astype(F32).T.astype(BF16)


def mix_kernel(here, w_here, out_ref, lhs_ref):
    @pl.when(pl.program_id(0) == 0)
    def _():
        lhs_ref[...] = turn(here)

    out_ref[...] = jnp.dot(lhs_ref[...], w_here[...], preferred_element_type=F32)


def mix_more_kernel(total_ref, near_h, far_h, w_near, w_far, out_ref, lhs_ref):
    m = near_h.shape[0]

    @pl.when(pl.program_id(0) == 0)
    def _():
        lhs_ref[:, :m] = turn(near_h)
        lhs_ref[:, m:] = turn(far_h)

    total = total_ref[...]
    total += jnp.dot(lhs_ref[:, :m], w_near[...], preferred_element_type=F32)
    total += jnp.dot(lhs_ref[:, m:], w_far[...], preferred_element_type=F32)
    out_ref[...] = total.astype(BF16)


def mix_part(total, parts, weights):
    rows = parts[0].shape[1]
    width = weights[0].shape[1]
    tile = width // 4
    depth = sum(p.shape[0] for p in parts)
    totals = [] if total is None else [total]

    def whole(g):
        return pl.BlockSpec(g.shape, lambda i: (0, 0))

    def tiled(w):
        return pl.BlockSpec((w.shape[0], tile), lambda i: (0, i))

    return pl.pallas_call(
        mix_kernel if total is None else mix_more_kernel,
        grid=(4,),
        in_specs=[tiled(t) for t in totals] + [whole(p) for p in parts] + [tiled(w) for w in weights],
        out_specs=pl.BlockSpec((rows, tile), lambda i: (0, i)),
        out_shape=jax.ShapeDtypeStruct((rows, width), F32 if total is None else BF16),
        scratch_shapes=[pltpu.VMEM((rows, depth), BF16)],
        compiler_params=pltpu.CompilerParams(vmem_limit_bytes=VMEM),
        cost_estimate=pl.CostEstimate(
            flops=2 * rows * depth * width, bytes_accessed=12 * 2**20, transcendentals=0
        ),
        name="mix_part" if total is None else "mix_more",
    )(*totals, *parts, *weights)


def filter_kernel(z_ref, x_ref, cs_ref, twist_ref, f_ref, m_ref):
    chips, _, lanes = x_ref.shape
    lanes = lanes // 2
    points = 2 * chips * 16
    rows, cols = points // 2, lanes // 2

    def part(n):
        rows_of = slice(16 * n, 16 * (n + 1))
        cores = [x_ref[:, rows_of, c * lanes : (c + 1) * lanes] for c in range(2)]
        return jnp.stack(cores, axis=1).reshape(points, lanes)

    upper, lower = part(0), part(1)
    whole = (upper.astype(F32) + lower.astype(F32)).T
    i = lax.broadcasted_iota(jnp.int32, (rows, rows), 0)
    j = lax.broadcasted_iota(jnp.int32, (rows, rows), 1)
    mirror = (i + j == rows).astype(F32).astype(BF16)
    i = lax.broadcasted_iota(jnp.int32, (lanes, lanes), 0)
    j = lax.broadcasted_iota(jnp.int32, (lanes, lanes), 1)
    flip = ((i // cols == j // cols) & (i % cols + j % cols == cols - 1)).astype(F32).astype(BF16)

    def mirrored(part):
        turned = jnp.dot(flip, part[:, rows:], preferred_element_type=F32).astype(BF16)
        return jnp.dot(turned, mirror, preferred_element_type=F32)

    other = mirrored(upper.astype(F32).T.astype(BF16)) + mirrored(lower.astype(F32).T.astype(BF16))
    f_ref[:, :rows] = 0.5 * (whole[:cols, :rows] + other[:cols])
    f_ref[:, rows:] = 0.5 * (whole[cols:, :rows] - other[cols:])
    c, s = cs_ref[0], cs_ref[1]

    def contract(left, right):
        return lax.dot_general(
            left, right, (((0,), (0,)), ((), ())), precision=HIGH, preferred_element_type=F32
        )

    m_ref[...] = jnp.zeros_like(m_ref)
    for n, k in enumerate((0, rows)):
        e_re, e_im = whole[:cols, k : k + 1], whole[cols:, k : k + 1]
        u = c * e_re - s * e_im
        v = s * e_re + c * e_im
        g = contract(u, c) + contract(v, s)
        if n:
            g = g * twist_ref[0] - (contract(v, c) - contract(u, s)) * twist_ref[1]
        for start in (n * cols, lanes + n * cols):
            spot = slice(start, start + cols)
            m_ref[spot, spot] = g.astype(BF16)


def filter_part(z, gathered, cs, twist):
    chips = gathered.shape[0]
    cols = cs.shape[1]
    rows = chips * 16
    lanes = 2 * cols
    return pl.pallas_call(
        filter_kernel,
        grid_spec=pltpu.PrefetchScalarGridSpec(
            num_scalar_prefetch=1,
            grid=(1,),
            in_specs=[
                pl.BlockSpec((chips, 32, 2 * lanes), lambda i, z: (0, 4, z[0])),
                pl.BlockSpec(cs.shape, lambda i, z: (0, 0, 0)),
                pl.BlockSpec(twist.shape, lambda i, z: (0, 0, 0)),
            ],
            out_specs=[
                pl.BlockSpec((cols, 2 * rows), lambda i, z: (0, 0)),
                pl.BlockSpec((2 * lanes, 2 * lanes), lambda i, z: (0, 0)),
            ],
        ),
        out_shape=[
            jax.ShapeDtypeStruct((cols, 2 * rows), F32),
            jax.ShapeDtypeStruct((2 * lanes, 2 * lanes), BF16),
        ],
        compiler_params=pltpu.CompilerParams(vmem_limit_bytes=VMEM),
        cost_estimate=pl.CostEstimate(flops=10**9, bytes_accessed=2**20, transcendentals=0),
        name="filter_part",
    )(z.reshape(1), gathered, cs, twist)


def conv_kernel(
    x_ref, fwd_hbm, inv_hbm, tw_hbm, a_ref, ai_ref, m_ref, f_ref, y_ref, fwd_ref, inv_ref, tw_ref, r_ref, q_ref, sems
):
    copies = [
        pltpu.make_async_copy(src, dst, sems.at[i])
        for i, (src, dst) in enumerate(((fwd_hbm, fwd_ref), (tw_hbm, tw_ref), (inv_hbm, inv_ref)))
    ]
    for copy in copies:
        copy.start()
    chips, chans, both = x_ref.shape
    rows = both // 2
    blocks = rows // 128
    half = 2 * chips
    copies[0].wait()
    for col in range(2):
        x = x_ref[:, :, col * rows : (col + 1) * rows].reshape(chips * chans, rows)
        r = jnp.dot(x, fwd_ref[...], preferred_element_type=F32)
        r = r.reshape(chips, chans, 2 * rows)
        if col == 0:
            copies[1].wait()
        tw = tw_ref[col * chips : (col + 1) * chips, :]
        cos = tw[:, None, :rows]
        sin = tw[:, None, rows:]
        re, im = r[:, :, :rows], r[:, :, rows:]
        turned_re = (re * cos + im * sin).reshape(chips * chans, rows)
        turned_im = (im * cos - re * sin).reshape(chips * chans, rows)
        for k in range(blocks):
            r_ref[col, k] = turned_re[:, k * 128 : (k + 1) * 128]
            r_ref[col, blocks + k] = turned_im[:, k * 128 : (k + 1) * 128]
    lane = lax.broadcasted_iota(jnp.int32, (4 * half, 128), 1)

    def pair(n, carry):
        picks = [pl.ds(2 * n + i, chips, stride=chans) for i in range(2)]
        parts = [
            jnp.concatenate([r_ref[col, part * blocks + k, pick, :] for k in range(blocks)], axis=1)
            for pick in picks
            for part in range(2)
            for col in range(2)
        ]
        turned = jnp.concatenate(parts, axis=0).astype(BF16)
        s = jnp.dot(a_ref[...], turned, preferred_element_type=F32)
        f_re, f_im = f_ref[:, :rows], f_ref[:, rows:]
        filtered = []
        for i in range(2):
            s_re = s[2 * i * half : (2 * i + 1) * half]
            s_im = s[(2 * i + 1) * half : (2 * i + 2) * half]
            filtered += [s_re * f_re - s_im * f_im, s_re * f_im + s_im * f_re]
        filtered = jnp.concatenate(filtered, axis=0).astype(BF16)
        back = jnp.dot(ai_ref[...], filtered, preferred_element_type=F32)
        edge = jnp.dot(m_ref[...], turned[:, :128], preferred_element_type=F32)
        head = jnp.where(lane == 0, edge, back[:, :128])
        back = jnp.concatenate([head, back[:, 128:]], axis=1)
        cos, sin = tw_ref[:, :rows], tw_ref[:, rows:]
        for i, pick in enumerate(picks):
            b_re = back[2 * i * half : (2 * i + 1) * half]
            b_im = back[(2 * i + 1) * half : (2 * i + 2) * half]
            out_re = b_re * cos - b_im * sin
            out_im = b_im * cos + b_re * sin
            for col in range(2):
                part = slice(col * chips, (col + 1) * chips)
                for k in range(blocks):
                    q_ref[col, k, pick, :] = out_re[part, k * 128 : (k + 1) * 128]
                    q_ref[col, blocks + k, pick, :] = out_im[part, k * 128 : (k + 1) * 128]
        return carry

    lax.fori_loop(0, chans // 2, pair, 0, unroll=2)
    copies[2].wait()
    for col in range(2):
        q = jnp.concatenate([q_ref[col, k].astype(BF16) for k in range(2 * blocks)], axis=1)
        y = jnp.dot(q, inv_ref[...], preferred_element_type=F32)
        y_ref[:, :, col * rows : (col + 1) * rows] = y.astype(BF16).reshape(chips, chans, rows)


def long_conv(x, fwd, inv, tw, a, ai, m, f):
    chips, chans, both = x.shape
    vmem = pl.BlockSpec(memory_space=pltpu.VMEM)
    hbm = pl.BlockSpec(memory_space=pl.ANY)
    return pl.pallas_call(
        conv_kernel,
        in_specs=[vmem, hbm, hbm, hbm, vmem, vmem, vmem, vmem],
        out_specs=vmem,
        out_shape=jax.ShapeDtypeStruct(x.shape, BF16),
        scratch_shapes=[
            pltpu.VMEM(fwd.shape, BF16),
            pltpu.VMEM(inv.shape, BF16),
            pltpu.VMEM(tw.shape, F32),
            pltpu.VMEM((2, both // 128, chips * chans, 128), F32),
            pltpu.VMEM((2, both // 128, chips * chans, 128), F32),
            pltpu.SemaphoreType.DMA((3,)),
        ],
        compiler_params=pltpu.CompilerParams(vmem_limit_bytes=VMEM),
        cost_estimate=pl.CostEstimate(flops=8 * 10**9, bytes_accessed=8 * 2**20, transcendentals=0),
        name="long_conv",
    )(x, fwd, inv, tw, a, ai, m, f)


def cos_sin(product, modulus):
    phase = (product % modulus).astype(F32) * (2.0 * math.pi / modulus)
    return jnp.cos(phase), jnp.sin(phase)


def twice(t):
    zero = jnp.zeros_like(t)
    return jnp.block([[t, zero], [zero, t]])


def column_tables(core, rows, cols, padded):
    i = lax.iota(jnp.int32, cols)
    b = 2 * (i % CHIPS) + ((i // CHIPS) ^ core)
    k1 = lax.iota(jnp.int32, rows)
    tw = jnp.concatenate(cos_sin(b[:, None] * k1[None, :], padded), axis=1)
    k2 = lax.iota(jnp.int32, cols)
    c, s = cos_sin(k2[:, None] * b[None, :], cols)
    a = jnp.block([[c, s], [-s, c]])
    twist = jnp.stack(cos_sin(jnp.mod((b[:, None] - b[None, :]) * rows, padded), padded))

    return tw, twice(a.astype(BF16)), twice(a.T.astype(BF16)), jnp.stack([c, s]), twist


def gather_line(block, axis):
    d1 = send(block, **{axis: -1})
    d3 = send(block, **{axis: 1})
    d2 = send(block, **{axis: 2})
    return jnp.concatenate([block, d1, d2, d3], axis=0)


def per_device(tokens, in_weight, filter_spectrum, skip_bias, out_weight):
    rows, _, width = tokens.shape
    cols = SEQ
    padded = 2 * rows * cols
    s = lax.axis_index("seq")
    h = lax.axis_index("ch")
    z, y, x, core = coords(s)
    chan = in_weight.shape[2] // 2
    depth = in_weight.shape[0]

    mine = tokens.reshape(rows, width)
    filt = jnp.transpose(filter_spectrum, (3, 1, 0, 2)).reshape(4, -1, 2 * cols)
    filt = jnp.concatenate(split_table(filt), axis=1)

    def half_for(c):
        w = lax.dynamic_slice_in_dim(in_weight, c * chan, chan, 2)
        f = lax.dynamic_slice_in_dim(filt, 2 * c, 2, 0)
        return jnp.transpose(w, (1, 0, 2)).reshape(3 * depth, chan), jnp.concatenate([f[0], f[1]], axis=1)

    keep, keep_f = half_for(core)
    give, give_f = half_for(1 - core)
    far_near = send(give[depth:], dz=1, dc=1)
    far = send(keep[depth:], dz=1)
    near = send(give, dc=1)
    near_f = send(give_f, dc=1)
    other = send(mine, dc=1)

    def ordered(own, partner, axis=0):
        return jnp.concatenate(
            [jnp.where(core == 0, own, partner), jnp.where(core == 0, partner, own)], axis=axis
        )

    def block_of(n):
        own, away = slice(n * depth, (n + 1) * depth), slice((n - 1) * depth, n * depth)
        return jnp.concatenate([ordered(keep[own], near[own]), ordered(far[away], far_near[away])], axis=0)

    key_block, value_block = block_of(1), block_of(2)
    f_lanes = 2 * cols
    gate_block = jnp.concatenate(
        [
            ordered(keep[:depth], near[:depth]),
            jnp.concatenate(
                [
                    ordered(keep_f[:, :f_lanes], near_f[:, :f_lanes], 1),
                    ordered(keep_f[:, f_lanes:], near_f[:, f_lanes:], 1),
                ],
                axis=1,
            ),
        ],
        axis=0,
    )
    gathered = lax.all_gather(gate_block, "seq", axis=0, axis_index_groups=SAME_CORE)
    key_block, value_block, other = lax.optimization_barrier((key_block, value_block, other))
    half_ow = out_weight.shape[0] // 2
    ow_part = lax.dynamic_slice_in_dim(out_weight, core * half_ow, half_ow, 0)
    key_line, value_line, ow_part = lax.optimization_barrier(
        (gather_line(key_block, "dx"), gather_line(value_block, "dy"), ow_part)
    )

    order = np.arange(32)
    p_, q_, dz = order // 8, (order // 2) % 4, order % 2
    key_order = ((z ^ dz) * 4 + (y + p_) % 4) * 4 + (x + q_) % 4
    value_order = ((z ^ dz) * 4 + (y + q_) % 4) * 4 + (x + p_) % 4
    order = jnp.stack([key_order, value_order])
    first = sum_part(first_kernel, "first_part", order, mine, other, [], [key_line, value_line], True)
    near_lines = [send(key_line, dy=-1), send(key_line, dy=1), send(value_line, dx=-1), send(value_line, dx=1)]
    tables = column_tables(core, rows, cols, padded)
    near_lines, first, tables = lax.optimization_barrier((near_lines, first, tables))
    halves = cut_halves(near_lines)
    last_lines = [
        send(halves[0], dy=-1),
        send(halves[1], dy=1),
        send(halves[2], dx=-1),
        send(halves[3], dx=1),
    ]
    totals = sum_part(second_kernel, "second_part", order, mine, other, first[:2], near_lines, False)

    perm = []
    for t in range(SEQ):
        tz, ty, tx, tc = coords(t)
        for th in range(2):
            perm.append((t * 2 + th, index_of(tz ^ tc, ty, tx, tc) * 2 + 1 - th))
    ow_same = lax.ppermute(ow_part, ("seq", "ch"), perm)

    source = last_part(totals, first[2:], last_lines)
    packed = source.reshape(CHIPS, chan // CHIPS, 2 * rows)
    mine_ch = lax.all_to_all(packed, "seq", 0, 0, axis_index_groups=SAME_CORE)

    tw, a, ai, cs, twist = tables
    f, m = filter_part(z, gathered, cs, twist)
    forward, inverse = row_tables(rows, padded)
    fwd = jnp.asarray(forward.astype(np.float32).astype(ml_dtypes.bfloat16))
    inv = jnp.asarray(inverse.astype(np.float32).astype(ml_dtypes.bfloat16))
    conv = long_conv(mine_ch, fwd, inv, tw, a, ai, m, f)
    conv, ow_same = lax.optimization_barrier((conv, ow_same))
    ow_cross = send(ow_same, dc=1)
    conv = lax.all_to_all(conv, "seq", 0, 0, axis_index_groups=SAME_CORE)
    conv = conv.reshape(chan, 2 * rows).astype(F32)

    gate = gate_part(mine, other, gathered).astype(F32)
    skip = lax.dynamic_slice_in_dim(skip_bias, core * chan, chan, 0)[:, None]
    gated = (gate * (conv + skip * source.astype(F32))).astype(BF16)

    kept = rows // 2
    own_here = lax.dynamic_slice(gated, (0, h * kept), (chan, kept))
    own_there = lax.dynamic_slice(gated, (0, (1 - h) * kept), (chan, kept))
    oth_here = lax.dynamic_slice(gated, (0, rows + h * kept), (chan, kept))
    oth_there = lax.dynamic_slice(gated, (0, rows + (1 - h) * kept), (chan, kept))
    swap_ch = [(0, 1), (1, 0)]
    from_h = lax.ppermute(own_there, "ch", swap_ch)
    perm2 = []
    for t in range(SEQ):
        for th in range(2):
            perm2.append((t * 2 + th, (t ^ 1) * 2 + 1 - th))
    from_hc = lax.ppermute(oth_there, ("seq", "ch"), perm2)
    from_c = send(oth_here, dc=1)
    here = ordered(own_here, from_c)

    mixed = mix_part(None, [here], [out_weight])
    mixed = mix_part(mixed, [from_h, from_hc], [ow_same, ow_cross])
    return mixed.reshape(kept, 1, width)


def solution(mesh):
    in_specs = (
        P(None, "seq", None),
        P("seq", None, "ch"),
        P(None, "seq", None, "ch"),
        P("ch"),
        P("ch", None),
    )
    return jax.shard_map(
        per_device, mesh=mesh, in_specs=in_specs, out_specs=P("ch", "seq", None), check_vma=False
    )
```

```python
import functools
import math

import jax
import jax.numpy as jnp
import ml_dtypes
import numpy as np
from jax import lax
from jax.experimental import pallas as pl
from jax.experimental.pallas import tpu as pltpu
from jax.sharding import PartitionSpec as P

BF16 = jnp.bfloat16
F32 = jnp.float32
HIGH = lax.Precision.HIGHEST
SEQ = 64
VMEM = 60 * 2**20
CHIPS = 32
SAME_CORE = [[2 * p + j for p in range(CHIPS)] for j in range(2)]


def coords(s):
    return s // 32, (s // 8) % 4, (s // 2) % 4, s % 2


def index_of(z, y, x, c):
    return ((z * 4 + y) * 4 + x) * 2 + c


def send(value, dz=0, dy=0, dx=0, dc=0):
    perm = []
    for s in range(SEQ):
        z, y, x, c = coords(s)
        perm.append((s, index_of((z + dz) % 2, (y + dy) % 4, (x + dx) % 4, c ^ dc)))
    return lax.ppermute(value, "seq", perm)


def split_table(table):
    upper = table.astype(BF16)
    lower = (table - upper.astype(F32)).astype(BF16)
    return upper, lower


def row_tables(rows, padded):
    points = 2 * rows
    a = np.arange(rows)
    k = np.arange(rows)
    phase = 2.0 * np.pi * ((a[:, None] * k[None, :]) % points) / points
    re, im = np.cos(phase), -np.sin(phase)
    im[:, 0] = np.where(a % 2 == 0, 1.0, -1.0)
    forward = np.concatenate([re, im], axis=1)
    scale = np.full((rows,), 2.0)
    scale[0] = 1.0
    inverse = np.concatenate([re * scale, im * scale], axis=1).T / padded
    return forward, inverse


def picked(order_ref, row, group, tok_ref):
    blocks = [
        tok_ref[:, pl.ds(pl.multiple_of(order_ref[row, group * 8 + i] * 128, 128), 128)]
        for i in range(8)
    ]
    return jnp.concatenate(blocks, axis=1)


def stacked(ref, parts):
    stride = ref.shape[0] // parts
    return jnp.concatenate([ref[stride * i : stride * i + stride - 16] for i in range(parts)], axis=0)


def by_column(run, mine_ref, other_ref):
    step = pl.program_id(0)

    @pl.when(step < 2)
    def _():
        run(mine_ref)

    @pl.when(step >= 2)
    def _():
        run(other_ref)


def first_kernel(order_ref, mine_ref, other_ref, key_line, value_line, *outs):
    key_ref, value_ref, key_tok_ref, value_tok_ref = outs

    def run(tok_ref):
        for row, line, total_ref, last_ref in (
            (0, key_line, key_ref, key_tok_ref),
            (1, value_line, value_ref, value_tok_ref),
        ):
            total_ref[...] = jnp.dot(
                picked(order_ref, row, 0, tok_ref), stacked(line, 4), preferred_element_type=F32
            )
            last_ref[...] = picked(order_ref, row, 2, tok_ref)

    by_column(run, mine_ref, other_ref)


def second_kernel(order_ref, mine_ref, other_ref, key_in, value_in, k1, k3, v1, v3, key_ref, value_ref):
    def run(tok_ref):
        for row, before, e1, e3, total_ref in (
            (0, key_in, k1, k3, key_ref),
            (1, value_in, v1, v3, value_ref),
        ):
            total = before[...]
            total += jnp.dot(picked(order_ref, row, 1, tok_ref), stacked(e1, 4), preferred_element_type=F32)
            total += jnp.dot(picked(order_ref, row, 3, tok_ref), stacked(e3, 4), preferred_element_type=F32)
            total_ref[...] = total

    by_column(run, mine_ref, other_ref)


def sum_part(kernel, name, order, mine, other, totals, weights, last):
    rows, width = mine.shape
    chan = weights[0].shape[1]
    tile = rows // 2
    quarter = width // 4
    by_row = [pl.BlockSpec((tile, chan), lambda i, o: (i, 0))] * 2
    tokens_out = [pl.BlockSpec((tile, quarter), lambda i, o: (i, 0))] * 2
    shapes = [jax.ShapeDtypeStruct((2 * rows, chan), F32)] * 2
    token_shapes = [jax.ShapeDtypeStruct((2 * rows, quarter), BF16)] * 2
    return pl.pallas_call(
        kernel,
        grid_spec=pltpu.PrefetchScalarGridSpec(
            num_scalar_prefetch=1,
            grid=(4,),
            in_specs=[
                pl.BlockSpec((tile, width), lambda i, o: (jnp.minimum(i, 1), 0)),
                pl.BlockSpec((tile, width), lambda i, o: (jnp.maximum(i - 2, 0), 0)),
            ]
            + by_row[: len(totals)]
            + [pl.BlockSpec(weights[0].shape, lambda i, o: (0, 0))] * len(weights),
            out_specs=by_row + (tokens_out if last else []),
        ),
        out_shape=shapes + (token_shapes if last else []),
        compiler_params=pltpu.CompilerParams(vmem_limit_bytes=VMEM),
        cost_estimate=pl.CostEstimate(
            flops=2 * 2 * rows * quarter * chan * len(weights), bytes_accessed=18 * 2**20, transcendentals=0
        ),
        name=name,
    )(order, mine, other, *totals, *weights)


def cut_kernel(*refs):
    for src, dst in zip(refs[:4], refs[4:], strict=True):
        dst[...] = src[...]


def cut_halves(lines):
    rows, width = lines[0].shape
    tile = rows // 4
    upper = pl.BlockSpec((tile, width), lambda i: (i, 0))
    lower = pl.BlockSpec((tile, width), lambda i: (i + 2, 0))
    return pl.pallas_call(
        cut_kernel,
        grid=(2,),
        in_specs=[upper, lower, upper, lower],
        out_specs=[upper] * 4,
        out_shape=[jax.ShapeDtypeStruct((rows // 2, width), BF16)] * 4,
        compiler_params=pltpu.CompilerParams(vmem_limit_bytes=VMEM),
        cost_estimate=pl.CostEstimate(flops=0, bytes_accessed=4 * rows * width * 2, transcendentals=0),
        name="cut_halves",
    )(*lines)


def last_kernel(key_ref, value_ref, key_tok_ref, value_tok_ref, ka, kb, va, vb, source_ref, gate_ref):
    half = key_tok_ref.shape[1] // 2
    chan = source_ref.shape[0]

    def finish(total_ref, tok_ref, wa, wb):
        total = total_ref[...]
        total += jnp.dot(tok_ref[:, :half], stacked(wa, 2), preferred_element_type=F32)
        total += jnp.dot(tok_ref[:, half:], stacked(wb, 2), preferred_element_type=F32)
        return total.astype(BF16).astype(F32)

    key = finish(key_ref, key_tok_ref, ka, kb)
    value = finish(value_ref, value_tok_ref, va, vb)
    source_ref[...] = (key[:, :chan] * value[:, :chan]).T.astype(BF16)
    gate_ref[: chan // 2, :] = key[:, chan:].T.astype(BF16)
    gate_ref[chan // 2 :, :] = value[:, chan:].T.astype(BF16)


def last_part(totals, tokens, weights):
    total, wide = totals[0].shape
    quarter = tokens[0].shape[1]
    tile = total // 4
    chan = wide * 2 // 3
    return pl.pallas_call(
        last_kernel,
        grid=(4,),
        in_specs=[pl.BlockSpec((tile, wide), lambda i: (i, 0))] * 2
        + [pl.BlockSpec((tile, quarter), lambda i: (i, 0))] * 2
        + [pl.BlockSpec(weights[0].shape, lambda i: (0, 0))] * 4,
        out_specs=[pl.BlockSpec((chan, tile), lambda i: (0, i))] * 2,
        out_shape=[jax.ShapeDtypeStruct((chan, total), BF16)] * 2,
        compiler_params=pltpu.CompilerParams(vmem_limit_bytes=VMEM),
        cost_estimate=pl.CostEstimate(
            flops=2 * 2 * total * quarter * wide, bytes_accessed=16 * 2**20, transcendentals=0
        ),
        name="last_part",
    )(*totals, *tokens, *weights)


def turn(ref):
    return ref[...].astype(F32).T.astype(BF16)


def mix_kernel(here, w_here, out_ref, lhs_ref):
    @pl.when(pl.program_id(0) == 0)
    def _():
        lhs_ref[...] = turn(here)

    out_ref[...] = jnp.dot(lhs_ref[...], w_here[...], preferred_element_type=F32)


def mix_more_kernel(total_ref, near_h, far_h, w_near, w_far, out_ref, lhs_ref):
    m = near_h.shape[0]

    @pl.when(pl.program_id(0) == 0)
    def _():
        lhs_ref[:, :m] = turn(near_h)
        lhs_ref[:, m:] = turn(far_h)

    total = total_ref[...]
    total += jnp.dot(lhs_ref[:, :m], w_near[...], preferred_element_type=F32)
    total += jnp.dot(lhs_ref[:, m:], w_far[...], preferred_element_type=F32)
    out_ref[...] = total.astype(BF16)


def mix_part(total, parts, weights):
    rows = parts[0].shape[1]
    width = weights[0].shape[1]
    tile = width // 4
    depth = sum(p.shape[0] for p in parts)
    totals = [] if total is None else [total]

    def whole(g):
        return pl.BlockSpec(g.shape, lambda i: (0, 0))

    def tiled(w):
        return pl.BlockSpec((w.shape[0], tile), lambda i: (0, i))

    return pl.pallas_call(
        mix_kernel if total is None else mix_more_kernel,
        grid=(4,),
        in_specs=[tiled(t) for t in totals] + [whole(p) for p in parts] + [tiled(w) for w in weights],
        out_specs=pl.BlockSpec((rows, tile), lambda i: (0, i)),
        out_shape=jax.ShapeDtypeStruct((rows, width), F32 if total is None else BF16),
        scratch_shapes=[pltpu.VMEM((rows, depth), BF16)],
        compiler_params=pltpu.CompilerParams(vmem_limit_bytes=VMEM),
        cost_estimate=pl.CostEstimate(
            flops=2 * rows * depth * width, bytes_accessed=12 * 2**20, transcendentals=0
        ),
        name="mix_part" if total is None else "mix_more",
    )(*totals, *parts, *weights)


def filter_kernel(order_ref, *refs):
    pieces, (cs_ref, twist_ref, f_ref, m_ref, natural_ref) = refs[:32], refs[32:]
    points, lanes = natural_ref.shape[1:]
    rows, cols = points // 2, lanes // 2
    for row in range(2):
        for n in range(16):
            for dz in range(2):
                chip = order_ref[row, 2 * n + dz]
                for c in range(2):
                    start = pl.multiple_of(chip * 32 + 16 * c, 16)
                    spot = (2 * dz + c) * lanes
                    natural_ref[row, pl.ds(start, 16), :] = pieces[16 * row + n][:, spot : spot + lanes]
    upper, lower = natural_ref[0], natural_ref[1]
    whole = (upper.astype(F32) + lower.astype(F32)).T
    i = lax.broadcasted_iota(jnp.int32, (rows, rows), 0)
    j = lax.broadcasted_iota(jnp.int32, (rows, rows), 1)
    mirror = (i + j == rows).astype(F32).astype(BF16)
    i = lax.broadcasted_iota(jnp.int32, (lanes, lanes), 0)
    j = lax.broadcasted_iota(jnp.int32, (lanes, lanes), 1)
    flip = ((i // cols == j // cols) & (i % cols + j % cols == cols - 1)).astype(F32).astype(BF16)

    def mirrored(part):
        turned = jnp.dot(flip, part[:, rows:], preferred_element_type=F32).astype(BF16)
        return jnp.dot(turned, mirror, preferred_element_type=F32)

    other = mirrored(upper.astype(F32).T.astype(BF16)) + mirrored(lower.astype(F32).T.astype(BF16))
    f_ref[:, :rows] = 0.5 * (whole[:cols, :rows] + other[:cols])
    f_ref[:, rows:] = 0.5 * (whole[cols:, :rows] - other[cols:])
    c, s = cs_ref[0], cs_ref[1]

    def contract(left, right):
        return lax.dot_general(
            left, right, (((0,), (0,)), ((), ())), precision=HIGH, preferred_element_type=F32
        )

    m_ref[...] = jnp.zeros_like(m_ref)
    for n, k in enumerate((0, rows)):
        e_re, e_im = whole[:cols, k : k + 1], whole[cols:, k : k + 1]
        u = c * e_re - s * e_im
        v = s * e_re + c * e_im
        g = contract(u, c) + contract(v, s)
        if n:
            g = g * twist_ref[0] - (contract(v, c) - contract(u, s)) * twist_ref[1]
        for start in (n * cols, lanes + n * cols):
            spot = slice(start, start + cols)
            m_ref[spot, spot] = g.astype(BF16)


def filter_part(order, key_lines, value_lines, cs, twist):
    cols = cs.shape[1]
    lanes = 2 * cols
    points = 16 * SEQ
    rows = points // 2
    specs, operands = [], []
    for lines in (key_lines, value_lines):
        for line, parts in zip(lines, (4, 4, 2, 2, 4), strict=True):
            stride = line.shape[0] // parts // 16
            for i in range(parts):
                at = stride * (i + 1) - 1
                specs.append(pl.BlockSpec((16, 4 * lanes), lambda i, o, at=at: (at, 0)))
                operands.append(line)
    return pl.pallas_call(
        filter_kernel,
        grid_spec=pltpu.PrefetchScalarGridSpec(
            num_scalar_prefetch=1,
            grid=(1,),
            in_specs=specs
            + [
                pl.BlockSpec(cs.shape, lambda i, o: (0, 0, 0)),
                pl.BlockSpec(twist.shape, lambda i, o: (0, 0, 0)),
            ],
            out_specs=[
                pl.BlockSpec((cols, 2 * rows), lambda i, o: (0, 0)),
                pl.BlockSpec((2 * lanes, 2 * lanes), lambda i, o: (0, 0)),
            ],
            scratch_shapes=[pltpu.VMEM((2, points, lanes), BF16)],
        ),
        out_shape=[
            jax.ShapeDtypeStruct((cols, 2 * rows), F32),
            jax.ShapeDtypeStruct((2 * lanes, 2 * lanes), BF16),
        ],
        compiler_params=pltpu.CompilerParams(vmem_limit_bytes=VMEM),
        cost_estimate=pl.CostEstimate(flops=10**9, bytes_accessed=2**20, transcendentals=0),
        name="filter_part",
    )(order, *operands, cs, twist)


def conv_kernel(
    x_ref, fwd_hbm, inv_hbm, tw_hbm, a_ref, ai_ref, m_ref, f_ref, y_ref, fwd_ref, inv_ref, tw_ref, r_ref, q_ref, sems
):
    copies = [
        pltpu.make_async_copy(src, dst, sems.at[i])
        for i, (src, dst) in enumerate(((fwd_hbm, fwd_ref), (tw_hbm, tw_ref), (inv_hbm, inv_ref)))
    ]
    for copy in copies:
        copy.start()
    chips, chans, both = x_ref.shape
    rows = both // 2
    blocks = rows // 128
    half = 2 * chips
    copies[0].wait()
    for col in range(2):
        x = x_ref[:, :, col * rows : (col + 1) * rows].reshape(chips * chans, rows)
        r = jnp.dot(x, fwd_ref[...], preferred_element_type=F32)
        r = r.reshape(chips, chans, 2 * rows)
        if col == 0:
            copies[1].wait()
        tw = tw_ref[col * chips : (col + 1) * chips, :]
        cos = tw[:, None, :rows]
        sin = tw[:, None, rows:]
        re, im = r[:, :, :rows], r[:, :, rows:]
        turned_re = (re * cos + im * sin).reshape(chips * chans, rows)
        turned_im = (im * cos - re * sin).reshape(chips * chans, rows)
        for k in range(blocks):
            r_ref[col, k] = turned_re[:, k * 128 : (k + 1) * 128]
            r_ref[col, blocks + k] = turned_im[:, k * 128 : (k + 1) * 128]
    lane = lax.broadcasted_iota(jnp.int32, (4 * half, 128), 1)

    def pair(n, carry):
        picks = [pl.ds(2 * n + i, chips, stride=chans) for i in range(2)]
        parts = [
            jnp.concatenate([r_ref[col, part * blocks + k, pick, :] for k in range(blocks)], axis=1)
            for pick in picks
            for part in range(2)
            for col in range(2)
        ]
        turned = jnp.concatenate(parts, axis=0).astype(BF16)
        s = jnp.dot(a_ref[...], turned, preferred_element_type=F32)
        f_re, f_im = f_ref[:, :rows], f_ref[:, rows:]
        filtered = []
        for i in range(2):
            s_re = s[2 * i * half : (2 * i + 1) * half]
            s_im = s[(2 * i + 1) * half : (2 * i + 2) * half]
            filtered += [s_re * f_re - s_im * f_im, s_re * f_im + s_im * f_re]
        filtered = jnp.concatenate(filtered, axis=0).astype(BF16)
        back = jnp.dot(ai_ref[...], filtered, preferred_element_type=F32)
        edge = jnp.dot(m_ref[...], turned[:, :128], preferred_element_type=F32)
        head = jnp.where(lane == 0, edge, back[:, :128])
        back = jnp.concatenate([head, back[:, 128:]], axis=1)
        cos, sin = tw_ref[:, :rows], tw_ref[:, rows:]
        for i, pick in enumerate(picks):
            b_re = back[2 * i * half : (2 * i + 1) * half]
            b_im = back[(2 * i + 1) * half : (2 * i + 2) * half]
            out_re = b_re * cos - b_im * sin
            out_im = b_im * cos + b_re * sin
            for col in range(2):
                part = slice(col * chips, (col + 1) * chips)
                for k in range(blocks):
                    q_ref[col, k, pick, :] = out_re[part, k * 128 : (k + 1) * 128]
                    q_ref[col, blocks + k, pick, :] = out_im[part, k * 128 : (k + 1) * 128]
        return carry

    lax.fori_loop(0, chans // 2, pair, 0, unroll=2)
    copies[2].wait()
    for col in range(2):
        q = jnp.concatenate([q_ref[col, k].astype(BF16) for k in range(2 * blocks)], axis=1)
        y = jnp.dot(q, inv_ref[...], preferred_element_type=F32)
        y_ref[:, :, col * rows : (col + 1) * rows] = y.astype(BF16).reshape(chips, chans, rows)


def long_conv(x, fwd, inv, tw, a, ai, m, f):
    chips, chans, both = x.shape
    vmem = pl.BlockSpec(memory_space=pltpu.VMEM)
    hbm = pl.BlockSpec(memory_space=pl.ANY)
    return pl.pallas_call(
        conv_kernel,
        in_specs=[vmem, hbm, hbm, hbm, vmem, vmem, vmem, vmem],
        out_specs=vmem,
        out_shape=jax.ShapeDtypeStruct(x.shape, BF16),
        scratch_shapes=[
            pltpu.VMEM(fwd.shape, BF16),
            pltpu.VMEM(inv.shape, BF16),
            pltpu.VMEM(tw.shape, F32),
            pltpu.VMEM((2, both // 128, chips * chans, 128), F32),
            pltpu.VMEM((2, both // 128, chips * chans, 128), F32),
            pltpu.SemaphoreType.DMA((3,)),
        ],
        compiler_params=pltpu.CompilerParams(vmem_limit_bytes=VMEM),
        cost_estimate=pl.CostEstimate(flops=8 * 10**9, bytes_accessed=8 * 2**20, transcendentals=0),
        name="long_conv",
    )(x, fwd, inv, tw, a, ai, m, f)


def cos_sin(product, modulus):
    phase = (product % modulus).astype(F32) * (2.0 * math.pi / modulus)
    return jnp.cos(phase), jnp.sin(phase)


def twice(t):
    zero = jnp.zeros_like(t)
    return jnp.block([[t, zero], [zero, t]])


def column_tables(core, rows, cols, padded):
    i = lax.iota(jnp.int32, cols)
    b = 2 * (i % CHIPS) + ((i // CHIPS) ^ core)
    k1 = lax.iota(jnp.int32, rows)
    tw = jnp.concatenate(cos_sin(b[:, None] * k1[None, :], padded), axis=1)
    k2 = lax.iota(jnp.int32, cols)
    c, s = cos_sin(k2[:, None] * b[None, :], cols)
    a = jnp.block([[c, s], [-s, c]])
    twist = jnp.stack(cos_sin(jnp.mod((b[:, None] - b[None, :]) * rows, padded), padded))

    return tw, twice(a.astype(BF16)), twice(a.T.astype(BF16)), jnp.stack([c, s]), twist


def gather_line(block, axis):
    d1 = send(block, **{axis: -1})
    d3 = send(block, **{axis: 1})
    d2 = send(block, **{axis: 2})
    return jnp.concatenate([block, d1, d2, d3], axis=0)


def per_device(tokens, in_weight, filter_spectrum, skip_bias, out_weight):
    rows, _, width = tokens.shape
    cols = SEQ
    padded = 2 * rows * cols
    s = lax.axis_index("seq")
    h = lax.axis_index("ch")
    z, y, x, core = coords(s)
    chan = in_weight.shape[2] // 2
    depth = in_weight.shape[0]

    mine = tokens.reshape(rows, width)
    filt = jnp.transpose(filter_spectrum, (3, 1, 0, 2)).reshape(4, -1, 2 * cols)
    filt = jnp.concatenate(split_table(filt), axis=1)

    def half_for(c):
        w = lax.dynamic_slice_in_dim(in_weight, c * chan, chan, 2)
        return jnp.transpose(w, (1, 0, 2)).reshape(3 * depth, chan)

    def load(w, c, z_to):
        f = lax.dynamic_index_in_dim(filt, 2 * c + z_to, 0, keepdims=False)
        return jnp.concatenate([w, jnp.pad(f, ((0, 0), (0, chan - 2 * cols)))], axis=0)

    keep, give = half_for(core), half_for(1 - core)
    far = send(load(keep, core, 1 - z), dz=1)
    far_near = send(load(give, 1 - core, 1 - z), dz=1, dc=1)
    near = send(load(give, 1 - core, z), dc=1)
    keep = load(keep, core, z)
    other = send(mine, dc=1)

    def ordered(own, partner, axis=0):
        return jnp.concatenate(
            [jnp.where(core == 0, own, partner), jnp.where(core == 0, partner, own)], axis=axis
        )

    def block_of(n):
        part = slice(n * depth, (n + 1) * depth)
        w = jnp.concatenate([ordered(keep[part], near[part]), ordered(far[part], far_near[part])], axis=0)
        part, lanes = slice(0, depth), slice((n - 1) * chan // 2, n * chan // 2)
        g = jnp.concatenate(
            [
                ordered(keep[part, lanes], near[part, lanes]),
                ordered(far[part, lanes], far_near[part, lanes]),
            ],
            axis=0,
        )
        part, lanes = slice(3 * depth + 16 * (n - 1), 3 * depth + 16 * n), slice(0, 2 * cols)
        f = jnp.concatenate(
            [
                ordered(keep[part, lanes], near[part, lanes], 1),
                ordered(far[part, lanes], far_near[part, lanes], 1),
            ],
            axis=1,
        )
        return jnp.concatenate(
            [jnp.concatenate([w, f], axis=0), jnp.pad(g, ((0, 16), (0, 0)))], axis=1
        )

    key_block, value_block, other = lax.optimization_barrier((block_of(1), block_of(2), other))
    half_ow = out_weight.shape[0] // 2
    ow_part = lax.dynamic_slice_in_dim(out_weight, core * half_ow, half_ow, 0)
    key_line, value_line, ow_part = lax.optimization_barrier(
        (gather_line(key_block, "dx"), gather_line(value_block, "dy"), ow_part)
    )

    order = np.arange(32)
    p_, q_, dz = order // 8, (order // 2) % 4, order % 2
    key_order = ((z ^ dz) * 4 + (y + p_) % 4) * 4 + (x + q_) % 4
    value_order = ((z ^ dz) * 4 + (y + q_) % 4) * 4 + (x + p_) % 4
    order = jnp.stack([key_order, value_order])
    first = sum_part(first_kernel, "first_part", order, mine, other, [], [key_line, value_line], True)
    near_lines = [send(key_line, dy=-1), send(key_line, dy=1), send(value_line, dx=-1), send(value_line, dx=1)]
    tables = column_tables(core, rows, cols, padded)
    near_lines, first, tables = lax.optimization_barrier((near_lines, first, tables))
    halves = cut_halves(near_lines)
    last_lines = [
        send(halves[0], dy=-1),
        send(halves[1], dy=1),
        send(halves[2], dx=-1),
        send(halves[3], dx=1),
    ]
    totals = sum_part(second_kernel, "second_part", order, mine, other, first[:2], near_lines, False)

    perm = []
    for t in range(SEQ):
        tz, ty, tx, tc = coords(t)
        for th in range(2):
            perm.append((t * 2 + th, index_of(tz ^ tc, ty, tx, tc) * 2 + 1 - th))
    ow_same = lax.ppermute(ow_part, ("seq", "ch"), perm)

    source, gate = last_part(totals, first[2:], last_lines)
    packed = source.reshape(CHIPS, chan // CHIPS, 2 * rows)
    mine_ch = lax.all_to_all(packed, "seq", 0, 0, axis_index_groups=SAME_CORE)

    tw, a, ai, cs, twist = tables
    k1_, k3_, v1_, v3_ = near_lines
    f, m = filter_part(
        order,
        [key_line, k1_, last_lines[0], last_lines[1], k3_],
        [value_line, v1_, last_lines[2], last_lines[3], v3_],
        cs,
        twist,
    )
    forward, inverse = row_tables(rows, padded)
    fwd = jnp.asarray(forward.astype(np.float32).astype(ml_dtypes.bfloat16))
    inv = jnp.asarray(inverse.astype(np.float32).astype(ml_dtypes.bfloat16))
    conv = long_conv(mine_ch, fwd, inv, tw, a, ai, m, f)
    conv = lax.all_to_all(conv, "seq", 0, 0, axis_index_groups=SAME_CORE)
    conv, ow_same = lax.optimization_barrier((conv, ow_same))
    ow_cross = send(ow_same, dc=1)
    conv = conv.reshape(chan, 2 * rows).astype(F32)

    gate = gate.astype(F32)
    skip = lax.dynamic_slice_in_dim(skip_bias, core * chan, chan, 0)[:, None]
    gated = (gate * (conv + skip * source.astype(F32))).astype(BF16)

    kept = rows // 2
    own_here = lax.dynamic_slice(gated, (0, h * kept), (chan, kept))
    own_there = lax.dynamic_slice(gated, (0, (1 - h) * kept), (chan, kept))
    oth_here = lax.dynamic_slice(gated, (0, rows + h * kept), (chan, kept))
    oth_there = lax.dynamic_slice(gated, (0, rows + (1 - h) * kept), (chan, kept))
    swap_ch = [(0, 1), (1, 0)]
    from_h = lax.ppermute(own_there, "ch", swap_ch)
    perm2 = []
    for t in range(SEQ):
        for th in range(2):
            perm2.append((t * 2 + th, (t ^ 1) * 2 + 1 - th))
    from_hc = lax.ppermute(oth_there, ("seq", "ch"), perm2)
    from_c = send(oth_here, dc=1)
    here = ordered(own_here, from_c)

    mixed = mix_part(None, [here], [out_weight])
    mixed = mix_part(mixed, [from_h, from_hc], [ow_same, ow_cross])
    return mixed.reshape(kept, 1, width)


def solution(mesh):
    in_specs = (
        P(None, "seq", None),
        P("seq", None, "ch"),
        P(None, "seq", None, "ch"),
        P("ch"),
        P("ch", None),
    )
    return jax.shard_map(
        per_device, mesh=mesh, in_specs=in_specs, out_specs=P("ch", "seq", None), check_vma=False
    )
```

```python
import functools
import math

import jax
import jax.numpy as jnp
import ml_dtypes
import numpy as np
from jax import lax
from jax.experimental import pallas as pl
from jax.experimental.pallas import tpu as pltpu
from jax.sharding import PartitionSpec as P

BF16 = jnp.bfloat16
F32 = jnp.float32
HIGH = lax.Precision.HIGHEST
SEQ = 64
VMEM = 60 * 2**20
CHIPS = 32
SAME_CORE = [[2 * p + j for p in range(CHIPS)] for j in range(2)]


def coords(s):
    return s // 32, (s // 8) % 4, (s // 2) % 4, s % 2


def index_of(z, y, x, c):
    return ((z * 4 + y) * 4 + x) * 2 + c


def send(value, dz=0, dy=0, dx=0, dc=0):
    perm = []
    for s in range(SEQ):
        z, y, x, c = coords(s)
        perm.append((s, index_of((z + dz) % 2, (y + dy) % 4, (x + dx) % 4, c ^ dc)))
    return lax.ppermute(value, "seq", perm)


def split_table(table):
    upper = table.astype(BF16)
    lower = (table - upper.astype(F32)).astype(BF16)
    return upper, lower


def row_tables(rows, padded):
    points = 2 * rows
    a = np.arange(rows)
    k = np.arange(rows)
    phase = 2.0 * np.pi * ((a[:, None] * k[None, :]) % points) / points
    re, im = np.cos(phase), -np.sin(phase)
    im[:, 0] = np.where(a % 2 == 0, 1.0, -1.0)
    forward = np.concatenate([re, im], axis=1)
    scale = np.full((rows,), 2.0)
    scale[0] = 1.0
    inverse = np.concatenate([re * scale, im * scale], axis=1).T / padded
    return forward, inverse


def picked(order_ref, row, group, tok_ref):
    blocks = [
        tok_ref[:, pl.ds(pl.multiple_of(order_ref[row, group * 8 + i] * 128, 128), 128)]
        for i in range(8)
    ]
    return jnp.concatenate(blocks, axis=1)


def stacked(ref, parts):
    stride = ref.shape[0] // parts
    return jnp.concatenate([ref[stride * i : stride * i + stride - 16] for i in range(parts)], axis=0)


def by_column(run, mine_ref, other_ref):
    step = pl.program_id(0)

    @pl.when(step < 2)
    def _():
        run(mine_ref)

    @pl.when(step >= 2)
    def _():
        run(other_ref)


def first_kernel(order_ref, mine_ref, other_ref, key_line, value_line, *outs):
    key_ref, value_ref, key_tok_ref, value_tok_ref = outs

    def run(tok_ref):
        for row, line, total_ref, last_ref in (
            (0, key_line, key_ref, key_tok_ref),
            (1, value_line, value_ref, value_tok_ref),
        ):
            total_ref[...] = jnp.dot(
                picked(order_ref, row, 0, tok_ref), stacked(line, 4), preferred_element_type=F32
            )
            last_ref[...] = picked(order_ref, row, 2, tok_ref)

    by_column(run, mine_ref, other_ref)


def second_kernel(order_ref, mine_ref, other_ref, key_in, value_in, k1, k3, v1, v3, key_ref, value_ref):
    def run(tok_ref):
        for row, before, e1, e3, total_ref in (
            (0, key_in, k1, k3, key_ref),
            (1, value_in, v1, v3, value_ref),
        ):
            total = before[...]
            total += jnp.dot(picked(order_ref, row, 1, tok_ref), stacked(e1, 4), preferred_element_type=F32)
            total += jnp.dot(picked(order_ref, row, 3, tok_ref), stacked(e3, 4), preferred_element_type=F32)
            total_ref[...] = total

    by_column(run, mine_ref, other_ref)


def sum_part(kernel, name, order, mine, other, totals, weights, last):
    rows, width = mine.shape
    chan = weights[0].shape[1]
    tile = rows // 2
    quarter = width // 4
    by_row = [pl.BlockSpec((tile, chan), lambda i, o: (i, 0))] * 2
    tokens_out = [pl.BlockSpec((tile, quarter), lambda i, o: (i, 0))] * 2
    shapes = [jax.ShapeDtypeStruct((2 * rows, chan), F32)] * 2
    token_shapes = [jax.ShapeDtypeStruct((2 * rows, quarter), BF16)] * 2
    return pl.pallas_call(
        kernel,
        grid_spec=pltpu.PrefetchScalarGridSpec(
            num_scalar_prefetch=1,
            grid=(4,),
            in_specs=[
                pl.BlockSpec((tile, width), lambda i, o: (jnp.minimum(i, 1), 0)),
                pl.BlockSpec((tile, width), lambda i, o: (jnp.maximum(i - 2, 0), 0)),
            ]
            + by_row[: len(totals)]
            + [pl.BlockSpec(weights[0].shape, lambda i, o: (0, 0))] * len(weights),
            out_specs=by_row + (tokens_out if last else []),
        ),
        out_shape=shapes + (token_shapes if last else []),
        compiler_params=pltpu.CompilerParams(vmem_limit_bytes=VMEM),
        cost_estimate=pl.CostEstimate(
            flops=2 * 2 * rows * quarter * chan * len(weights), bytes_accessed=18 * 2**20, transcendentals=0
        ),
        name=name,
    )(order, mine, other, *totals, *weights)


def cut_kernel(*refs):
    for src, dst in zip(refs[:4], refs[4:], strict=True):
        dst[...] = src[...]


def cut_halves(lines):
    rows, width = lines[0].shape
    tile = rows // 4
    upper = pl.BlockSpec((tile, width), lambda i: (i, 0))
    lower = pl.BlockSpec((tile, width), lambda i: (i + 2, 0))
    return pl.pallas_call(
        cut_kernel,
        grid=(2,),
        in_specs=[upper, lower, upper, lower],
        out_specs=[upper] * 4,
        out_shape=[jax.ShapeDtypeStruct((rows // 2, width), BF16)] * 4,
        compiler_params=pltpu.CompilerParams(vmem_limit_bytes=VMEM),
        cost_estimate=pl.CostEstimate(flops=0, bytes_accessed=4 * rows * width * 2, transcendentals=0),
        name="cut_halves",
    )(*lines)


def last_kernel(key_ref, value_ref, key_tok_ref, value_tok_ref, ka, kb, va, vb, source_ref, gate_ref):
    half = key_tok_ref.shape[1] // 2
    chan = source_ref.shape[0]

    def finish(total_ref, tok_ref, wa, wb):
        total = total_ref[...]
        total += jnp.dot(tok_ref[:, :half], stacked(wa, 2), preferred_element_type=F32)
        total += jnp.dot(tok_ref[:, half:], stacked(wb, 2), preferred_element_type=F32)
        return total.astype(BF16).astype(F32)

    key = finish(key_ref, key_tok_ref, ka, kb)
    value = finish(value_ref, value_tok_ref, va, vb)
    source_ref[...] = (key[:, :chan] * value[:, :chan]).T.astype(BF16)
    gate_ref[: chan // 2, :] = key[:, chan:].T.astype(BF16)
    gate_ref[chan // 2 :, :] = value[:, chan:].T.astype(BF16)


def last_part(totals, tokens, weights):
    total, wide = totals[0].shape
    quarter = tokens[0].shape[1]
    tile = total // 4
    chan = wide * 2 // 3
    return pl.pallas_call(
        last_kernel,
        grid=(4,),
        in_specs=[pl.BlockSpec((tile, wide), lambda i: (i, 0))] * 2
        + [pl.BlockSpec((tile, quarter), lambda i: (i, 0))] * 2
        + [pl.BlockSpec(weights[0].shape, lambda i: (0, 0))] * 4,
        out_specs=[pl.BlockSpec((chan, tile), lambda i: (0, i))] * 2,
        out_shape=[jax.ShapeDtypeStruct((chan, total), BF16)] * 2,
        compiler_params=pltpu.CompilerParams(vmem_limit_bytes=VMEM),
        cost_estimate=pl.CostEstimate(
            flops=2 * 2 * total * quarter * wide, bytes_accessed=16 * 2**20, transcendentals=0
        ),
        name="last_part",
    )(*totals, *tokens, *weights)


def turn(ref):
    return ref[...].astype(F32).T.astype(BF16)


def mix_kernel(here, w_here, out_ref, lhs_ref):
    @pl.when(pl.program_id(0) == 0)
    def _():
        lhs_ref[...] = turn(here)

    out_ref[...] = jnp.dot(lhs_ref[...], w_here[...], preferred_element_type=F32)


def mix_more_kernel(total_ref, near_h, far_h, w_near, w_far, out_ref, lhs_ref):
    m = near_h.shape[0]

    @pl.when(pl.program_id(0) == 0)
    def _():
        lhs_ref[:, :m] = turn(near_h)
        lhs_ref[:, m:] = turn(far_h)

    total = total_ref[...]
    total += jnp.dot(lhs_ref[:, :m], w_near[...], preferred_element_type=F32)
    total += jnp.dot(lhs_ref[:, m:], w_far[...], preferred_element_type=F32)
    out_ref[...] = total.astype(BF16)


def mix_part(total, parts, weights):
    rows = parts[0].shape[1]
    width = weights[0].shape[1]
    tile = width // 4
    depth = sum(p.shape[0] for p in parts)
    totals = [] if total is None else [total]

    def whole(g):
        return pl.BlockSpec(g.shape, lambda i: (0, 0))

    def tiled(w):
        return pl.BlockSpec((w.shape[0], tile), lambda i: (0, i))

    return pl.pallas_call(
        mix_kernel if total is None else mix_more_kernel,
        grid=(4,),
        in_specs=[tiled(t) for t in totals] + [whole(p) for p in parts] + [tiled(w) for w in weights],
        out_specs=pl.BlockSpec((rows, tile), lambda i: (0, i)),
        out_shape=jax.ShapeDtypeStruct((rows, width), F32 if total is None else BF16),
        scratch_shapes=[pltpu.VMEM((rows, depth), BF16)],
        compiler_params=pltpu.CompilerParams(vmem_limit_bytes=VMEM),
        cost_estimate=pl.CostEstimate(
            flops=2 * rows * depth * width, bytes_accessed=12 * 2**20, transcendentals=0
        ),
        name="mix_part" if total is None else "mix_more",
    )(*totals, *parts, *weights)


def filter_kernel(order_ref, *refs):
    pieces, (cs_ref, twist_ref, f_ref, m_ref, natural_ref) = refs[:32], refs[32:]
    points, lanes = natural_ref.shape[1:]
    rows, cols = points // 2, lanes // 2
    for row in range(2):
        for n in range(16):
            for dz in range(2):
                chip = order_ref[row, 2 * n + dz]
                for c in range(2):
                    start = pl.multiple_of(chip * 32 + 16 * c, 16)
                    spot = (2 * dz + c) * lanes
                    natural_ref[row, pl.ds(start, 16), :] = pieces[16 * row + n][:, spot : spot + lanes]
    upper, lower = natural_ref[0], natural_ref[1]
    whole = (upper.astype(F32) + lower.astype(F32)).T
    i = lax.broadcasted_iota(jnp.int32, (rows, rows), 0)
    j = lax.broadcasted_iota(jnp.int32, (rows, rows), 1)
    mirror = (i + j == rows).astype(F32).astype(BF16)
    i = lax.broadcasted_iota(jnp.int32, (lanes, lanes), 0)
    j = lax.broadcasted_iota(jnp.int32, (lanes, lanes), 1)
    flip = ((i // cols == j // cols) & (i % cols + j % cols == cols - 1)).astype(F32).astype(BF16)

    def mirrored(part):
        turned = jnp.dot(flip, part[:, rows:], preferred_element_type=F32).astype(BF16)
        return jnp.dot(turned, mirror, preferred_element_type=F32)

    other = mirrored(upper.astype(F32).T.astype(BF16)) + mirrored(lower.astype(F32).T.astype(BF16))
    f_ref[:, :rows] = 0.5 * (whole[:cols, :rows] + other[:cols])
    f_ref[:, rows:] = 0.5 * (whole[cols:, :rows] - other[cols:])
    c, s = cs_ref[0], cs_ref[1]

    def contract(left, right):
        return lax.dot_general(
            left, right, (((0,), (0,)), ((), ())), precision=HIGH, preferred_element_type=F32
        )

    m_ref[...] = jnp.zeros_like(m_ref)
    for n, k in enumerate((0, rows)):
        e_re, e_im = whole[:cols, k : k + 1], whole[cols:, k : k + 1]
        u = c * e_re - s * e_im
        v = s * e_re + c * e_im
        g = contract(u, c) + contract(v, s)
        if n:
            g = g * twist_ref[0] - (contract(v, c) - contract(u, s)) * twist_ref[1]
        for start in (n * cols, lanes + n * cols):
            spot = slice(start, start + cols)
            m_ref[spot, spot] = g.astype(BF16)


def filter_part(order, key_lines, value_lines, cs, twist):
    cols = cs.shape[1]
    lanes = 2 * cols
    points = 16 * SEQ
    rows = points // 2
    specs, operands = [], []
    for lines in (key_lines, value_lines):
        for line, parts in zip(lines, (4, 4, 2, 2, 4), strict=True):
            stride = line.shape[0] // parts // 16
            for i in range(parts):
                at = stride * (i + 1) - 1
                specs.append(pl.BlockSpec((16, 4 * lanes), lambda i, o, at=at: (at, 0)))
                operands.append(line)
    return pl.pallas_call(
        filter_kernel,
        grid_spec=pltpu.PrefetchScalarGridSpec(
            num_scalar_prefetch=1,
            grid=(1,),
            in_specs=specs
            + [
                pl.BlockSpec(cs.shape, lambda i, o: (0, 0, 0)),
                pl.BlockSpec(twist.shape, lambda i, o: (0, 0, 0)),
            ],
            out_specs=[
                pl.BlockSpec((cols, 2 * rows), lambda i, o: (0, 0)),
                pl.BlockSpec((2 * lanes, 2 * lanes), lambda i, o: (0, 0)),
            ],
            scratch_shapes=[pltpu.VMEM((2, points, lanes), BF16)],
        ),
        out_shape=[
            jax.ShapeDtypeStruct((cols, 2 * rows), F32),
            jax.ShapeDtypeStruct((2 * lanes, 2 * lanes), BF16),
        ],
        compiler_params=pltpu.CompilerParams(vmem_limit_bytes=VMEM),
        cost_estimate=pl.CostEstimate(flops=10**9, bytes_accessed=2**20, transcendentals=0),
        name="filter_part",
    )(order, *operands, cs, twist)


def conv_kernel(
    x_ref, fwd_hbm, inv_hbm, tw_hbm, a_ref, ai_ref, m_ref, f_ref, y_ref, fwd_ref, inv_ref, tw_ref, r_ref, q_ref, sems
):
    copies = [
        pltpu.make_async_copy(src, dst, sems.at[i])
        for i, (src, dst) in enumerate(((fwd_hbm, fwd_ref), (tw_hbm, tw_ref), (inv_hbm, inv_ref)))
    ]
    for copy in copies:
        copy.start()
    chips, chans, both = x_ref.shape
    rows = both // 2
    blocks = rows // 128
    half = 2 * chips
    copies[0].wait()
    for col in range(2):
        x = x_ref[:, :, col * rows : (col + 1) * rows].reshape(chips * chans, rows)
        r = jnp.dot(x, fwd_ref[...], preferred_element_type=F32)
        r = r.reshape(chips, chans, 2 * rows)
        if col == 0:
            copies[1].wait()
        tw = tw_ref[col * chips : (col + 1) * chips, :]
        cos = tw[:, None, :rows]
        sin = tw[:, None, rows:]
        re, im = r[:, :, :rows], r[:, :, rows:]
        turned_re = (re * cos + im * sin).reshape(chips * chans, rows)
        turned_im = (im * cos - re * sin).reshape(chips * chans, rows)
        for k in range(blocks):
            r_ref[col, k] = turned_re[:, k * 128 : (k + 1) * 128]
            r_ref[col, blocks + k] = turned_im[:, k * 128 : (k + 1) * 128]
    lane = lax.broadcasted_iota(jnp.int32, (4 * half, 128), 1)

    def pair(n, carry):
        picks = [pl.ds(2 * n + i, chips, stride=chans) for i in range(2)]
        parts = [
            jnp.concatenate([r_ref[col, part * blocks + k, pick, :] for k in range(blocks)], axis=1)
            for pick in picks
            for part in range(2)
            for col in range(2)
        ]
        turned = jnp.concatenate(parts, axis=0).astype(BF16)
        s = jnp.dot(a_ref[...], turned, preferred_element_type=F32)
        f_re, f_im = f_ref[:, :rows], f_ref[:, rows:]
        filtered = []
        for i in range(2):
            s_re = s[2 * i * half : (2 * i + 1) * half]
            s_im = s[(2 * i + 1) * half : (2 * i + 2) * half]
            filtered += [s_re * f_re - s_im * f_im, s_re * f_im + s_im * f_re]
        filtered = jnp.concatenate(filtered, axis=0).astype(BF16)
        back = jnp.dot(ai_ref[...], filtered, preferred_element_type=F32)
        edge = jnp.dot(m_ref[...], turned[:, :128], preferred_element_type=F32)
        head = jnp.where(lane == 0, edge, back[:, :128])
        back = jnp.concatenate([head, back[:, 128:]], axis=1)
        cos, sin = tw_ref[:, :rows], tw_ref[:, rows:]
        for i, pick in enumerate(picks):
            b_re = back[2 * i * half : (2 * i + 1) * half]
            b_im = back[(2 * i + 1) * half : (2 * i + 2) * half]
            out_re = b_re * cos - b_im * sin
            out_im = b_im * cos + b_re * sin
            for col in range(2):
                part = slice(col * chips, (col + 1) * chips)
                for k in range(blocks):
                    q_ref[col, k, pick, :] = out_re[part, k * 128 : (k + 1) * 128]
                    q_ref[col, blocks + k, pick, :] = out_im[part, k * 128 : (k + 1) * 128]
        return carry

    lax.fori_loop(0, chans // 2, pair, 0, unroll=2)
    copies[2].wait()
    for col in range(2):
        q = jnp.concatenate([q_ref[col, k].astype(BF16) for k in range(2 * blocks)], axis=1)
        y = jnp.dot(q, inv_ref[...], preferred_element_type=F32)
        y_ref[:, :, col * rows : (col + 1) * rows] = y.astype(BF16).reshape(chips, chans, rows)


def long_conv(x, fwd, inv, tw, a, ai, m, f):
    chips, chans, both = x.shape
    vmem = pl.BlockSpec(memory_space=pltpu.VMEM)
    hbm = pl.BlockSpec(memory_space=pl.ANY)
    return pl.pallas_call(
        conv_kernel,
        in_specs=[vmem, hbm, hbm, hbm, vmem, vmem, vmem, vmem],
        out_specs=vmem,
        out_shape=jax.ShapeDtypeStruct(x.shape, BF16),
        scratch_shapes=[
            pltpu.VMEM(fwd.shape, BF16),
            pltpu.VMEM(inv.shape, BF16),
            pltpu.VMEM(tw.shape, F32),
            pltpu.VMEM((2, both // 128, chips * chans, 128), F32),
            pltpu.VMEM((2, both // 128, chips * chans, 128), F32),
            pltpu.SemaphoreType.DMA((3,)),
        ],
        compiler_params=pltpu.CompilerParams(vmem_limit_bytes=VMEM),
        cost_estimate=pl.CostEstimate(flops=8 * 10**9, bytes_accessed=8 * 2**20, transcendentals=0),
        name="long_conv",
    )(x, fwd, inv, tw, a, ai, m, f)


def cos_sin(product, modulus):
    phase = (product % modulus).astype(F32) * (2.0 * math.pi / modulus)
    return jnp.cos(phase), jnp.sin(phase)


def twice(t):
    zero = jnp.zeros_like(t)
    return jnp.block([[t, zero], [zero, t]])


def column_tables(core, rows, cols, padded):
    i = lax.iota(jnp.int32, cols)
    b = 2 * (i % CHIPS) + ((i // CHIPS) ^ core)
    k1 = lax.iota(jnp.int32, rows)
    tw = jnp.concatenate(cos_sin(b[:, None] * k1[None, :], padded), axis=1)
    k2 = lax.iota(jnp.int32, cols)
    c, s = cos_sin(k2[:, None] * b[None, :], cols)
    a = jnp.block([[c, s], [-s, c]])
    twist = jnp.stack(cos_sin(jnp.mod((b[:, None] - b[None, :]) * rows, padded), padded))

    return tw, twice(a.astype(BF16)), twice(a.T.astype(BF16)), jnp.stack([c, s]), twist


def gather_line(block, axis):
    d1 = send(block, **{axis: -1})
    d3 = send(block, **{axis: 1})
    d2 = send(block, **{axis: 2})
    return jnp.concatenate([block, d1, d2, d3], axis=0)


def per_device(tokens, in_weight, filter_spectrum, skip_bias, out_weight):
    rows, _, width = tokens.shape
    cols = SEQ
    padded = 2 * rows * cols
    s = lax.axis_index("seq")
    h = lax.axis_index("ch")
    z, y, x, core = coords(s)
    chan = in_weight.shape[2] // 2
    depth = in_weight.shape[0]

    mine = tokens.reshape(rows, width)
    filt = jnp.transpose(filter_spectrum, (3, 1, 0, 2)).reshape(4, -1, 2 * cols)
    filt = jnp.concatenate(split_table(filt), axis=1)

    def half_for(c):
        w = lax.dynamic_slice_in_dim(in_weight, c * chan, chan, 2)
        return jnp.transpose(w, (1, 0, 2)).reshape(3 * depth, chan)

    def load(w, c, z_to):
        f = lax.dynamic_index_in_dim(filt, 2 * c + z_to, 0, keepdims=False)
        return jnp.concatenate([w, jnp.pad(f, ((0, 0), (0, chan - 2 * cols)))], axis=0)

    keep, give = half_for(core), half_for(1 - core)
    far = send(load(keep, core, 1 - z), dz=1)
    far_near = send(load(give, 1 - core, 1 - z), dz=1, dc=1)
    near = send(load(give, 1 - core, z), dc=1)
    keep = load(keep, core, z)
    other = send(mine, dc=1)

    def ordered(own, partner, axis=0):
        return jnp.concatenate(
            [jnp.where(core == 0, own, partner), jnp.where(core == 0, partner, own)], axis=axis
        )

    def block_of(n):
        part = slice(n * depth, (n + 1) * depth)
        w = jnp.concatenate([ordered(keep[part], near[part]), ordered(far[part], far_near[part])], axis=0)
        part, lanes = slice(0, depth), slice((n - 1) * chan // 2, n * chan // 2)
        g = jnp.concatenate(
            [
                ordered(keep[part, lanes], near[part, lanes]),
                ordered(far[part, lanes], far_near[part, lanes]),
            ],
            axis=0,
        )
        part, lanes = slice(3 * depth + 16 * (n - 1), 3 * depth + 16 * n), slice(0, 2 * cols)
        f = jnp.concatenate(
            [
                ordered(keep[part, lanes], near[part, lanes], 1),
                ordered(far[part, lanes], far_near[part, lanes], 1),
            ],
            axis=1,
        )
        return jnp.concatenate(
            [jnp.concatenate([w, f], axis=0), jnp.pad(g, ((0, 16), (0, 0)))], axis=1
        )

    half_ow = out_weight.shape[0] // 2
    ow_part = lax.dynamic_slice_in_dim(out_weight, core * half_ow, half_ow, 0)
    key_block, value_block, other, ow_part = lax.optimization_barrier(
        (block_of(1), block_of(2), other, ow_part)
    )
    key_line, value_line, ow_part = lax.optimization_barrier(
        (gather_line(key_block, "dx"), gather_line(value_block, "dy"), ow_part)
    )

    order = np.arange(32)
    p_, q_, dz = order // 8, (order // 2) % 4, order % 2
    key_order = ((z ^ dz) * 4 + (y + p_) % 4) * 4 + (x + q_) % 4
    value_order = ((z ^ dz) * 4 + (y + q_) % 4) * 4 + (x + p_) % 4
    order = jnp.stack([key_order, value_order])
    first = sum_part(first_kernel, "first_part", order, mine, other, [], [key_line, value_line], True)
    near_lines = [send(key_line, dy=-1), send(key_line, dy=1), send(value_line, dx=-1), send(value_line, dx=1)]
    tables = column_tables(core, rows, cols, padded)
    near_lines, first, tables = lax.optimization_barrier((near_lines, first, tables))
    halves = cut_halves(near_lines)
    last_lines = [
        send(halves[0], dy=-1),
        send(halves[1], dy=1),
        send(halves[2], dx=-1),
        send(halves[3], dx=1),
    ]
    totals = sum_part(second_kernel, "second_part", order, mine, other, first[:2], near_lines, False)

    perm = []
    for t in range(SEQ):
        tz, ty, tx, tc = coords(t)
        for th in range(2):
            perm.append((t * 2 + th, index_of(tz ^ tc, ty, tx, tc) * 2 + 1 - th))
    ow_same = lax.ppermute(ow_part, ("seq", "ch"), perm)

    source, gate = last_part(totals, first[2:], last_lines)
    packed = source.reshape(CHIPS, chan // CHIPS, 2 * rows)
    mine_ch = lax.all_to_all(packed, "seq", 0, 0, axis_index_groups=SAME_CORE)

    tw, a, ai, cs, twist = tables
    k1_, k3_, v1_, v3_ = near_lines
    f, m = filter_part(
        order,
        [key_line, k1_, last_lines[0], last_lines[1], k3_],
        [value_line, v1_, last_lines[2], last_lines[3], v3_],
        cs,
        twist,
    )
    forward, inverse = row_tables(rows, padded)
    fwd = jnp.asarray(forward.astype(np.float32).astype(ml_dtypes.bfloat16))
    inv = jnp.asarray(inverse.astype(np.float32).astype(ml_dtypes.bfloat16))
    mine_ch, ow_same, f, m = lax.optimization_barrier((mine_ch, ow_same, f, m))
    ow_cross = send(ow_same, dc=1)
    conv = long_conv(mine_ch, fwd, inv, tw, a, ai, m, f)
    conv = lax.all_to_all(conv, "seq", 0, 0, axis_index_groups=SAME_CORE)
    conv = conv.reshape(chan, 2 * rows).astype(F32)

    gate = gate.astype(F32)
    skip = lax.dynamic_slice_in_dim(skip_bias, core * chan, chan, 0)[:, None]
    gated = (gate * (conv + skip * source.astype(F32))).astype(BF16)

    kept = rows // 2
    own_here = lax.dynamic_slice(gated, (0, h * kept), (chan, kept))
    own_there = lax.dynamic_slice(gated, (0, (1 - h) * kept), (chan, kept))
    oth_here = lax.dynamic_slice(gated, (0, rows + h * kept), (chan, kept))
    oth_there = lax.dynamic_slice(gated, (0, rows + (1 - h) * kept), (chan, kept))
    swap_ch = [(0, 1), (1, 0)]
    from_h = lax.ppermute(own_there, "ch", swap_ch)
    perm2 = []
    for t in range(SEQ):
        for th in range(2):
            perm2.append((t * 2 + th, (t ^ 1) * 2 + 1 - th))
    from_hc = lax.ppermute(oth_there, ("seq", "ch"), perm2)
    from_c = send(oth_here, dc=1)
    here = ordered(own_here, from_c)

    mixed = mix_part(None, [here], [out_weight])
    mixed = mix_part(mixed, [from_h, from_hc], [ow_same, ow_cross])
    return mixed.reshape(kept, 1, width)


def solution(mesh):
    in_specs = (
        P(None, "seq", None),
        P("seq", None, "ch"),
        P(None, "seq", None, "ch"),
        P("ch"),
        P("ch", None),
    )
    return jax.shard_map(
        per_device, mesh=mesh, in_specs=in_specs, out_specs=P("ch", "seq", None), check_vma=False
    )
```

```python
import functools
import math

import jax
import jax.numpy as jnp
import ml_dtypes
import numpy as np
from jax import lax
from jax.experimental import pallas as pl
from jax.experimental.pallas import tpu as pltpu
from jax.sharding import PartitionSpec as P

BF16 = jnp.bfloat16
F32 = jnp.float32
HIGH = lax.Precision.HIGHEST
SEQ = 64
VMEM = 60 * 2**20
CHIPS = 32
SAME_CORE = [[2 * p + j for p in range(CHIPS)] for j in range(2)]


def coords(s):
    return s // 32, (s // 8) % 4, (s // 2) % 4, s % 2


def index_of(z, y, x, c):
    return ((z * 4 + y) * 4 + x) * 2 + c


def send(value, dz=0, dy=0, dx=0, dc=0):
    perm = []
    for s in range(SEQ):
        z, y, x, c = coords(s)
        perm.append((s, index_of((z + dz) % 2, (y + dy) % 4, (x + dx) % 4, c ^ dc)))
    return lax.ppermute(value, "seq", perm)


def split_table(table):
    upper = table.astype(BF16)
    lower = (table - upper.astype(F32)).astype(BF16)
    return upper, lower


def row_tables(rows, padded):
    points = 2 * rows
    a = np.arange(rows)
    k = np.arange(rows)
    phase = 2.0 * np.pi * ((a[:, None] * k[None, :]) % points) / points
    re, im = np.cos(phase), -np.sin(phase)
    im[:, 0] = np.where(a % 2 == 0, 1.0, -1.0)
    forward = np.concatenate([re, im], axis=1)
    scale = np.full((rows,), 2.0)
    scale[0] = 1.0
    inverse = np.concatenate([re * scale, im * scale], axis=1).T / padded
    return forward, inverse


def picked(order_ref, row, group, tok_ref):
    blocks = [
        tok_ref[:, pl.ds(pl.multiple_of(order_ref[row, group * 8 + i] * 128, 128), 128)]
        for i in range(8)
    ]
    return jnp.concatenate(blocks, axis=1)


def stacked(ref, parts):
    stride = ref.shape[0] // parts
    return jnp.concatenate([ref[stride * i : stride * i + stride - 16] for i in range(parts)], axis=0)


def by_column(run, mine_ref, other_ref):
    step = pl.program_id(0)

    @pl.when(step < 2)
    def _():
        run(mine_ref)

    @pl.when(step >= 2)
    def _():
        run(other_ref)


def first_kernel(order_ref, mine_ref, other_ref, key_line, value_line, *outs):
    key_ref, value_ref, key_tok_ref, value_tok_ref = outs

    def run(tok_ref):
        for row, line, total_ref, last_ref in (
            (0, key_line, key_ref, key_tok_ref),
            (1, value_line, value_ref, value_tok_ref),
        ):
            total_ref[...] = jnp.dot(
                picked(order_ref, row, 0, tok_ref), stacked(line, 4), preferred_element_type=F32
            )
            last_ref[...] = picked(order_ref, row, 2, tok_ref)

    by_column(run, mine_ref, other_ref)


def second_kernel(order_ref, mine_ref, other_ref, key_in, value_in, k1, k3, v1, v3, key_ref, value_ref):
    def run(tok_ref):
        for row, before, e1, e3, total_ref in (
            (0, key_in, k1, k3, key_ref),
            (1, value_in, v1, v3, value_ref),
        ):
            total = before[...]
            total += jnp.dot(picked(order_ref, row, 1, tok_ref), stacked(e1, 4), preferred_element_type=F32)
            total += jnp.dot(picked(order_ref, row, 3, tok_ref), stacked(e3, 4), preferred_element_type=F32)
            total_ref[...] = total

    by_column(run, mine_ref, other_ref)


def sum_part(kernel, name, order, mine, other, totals, weights, last):
    rows, width = mine.shape
    chan = weights[0].shape[1]
    tile = rows // 2
    quarter = width // 4
    by_row = [pl.BlockSpec((tile, chan), lambda i, o: (i, 0))] * 2
    tokens_out = [pl.BlockSpec((tile, quarter), lambda i, o: (i, 0))] * 2
    shapes = [jax.ShapeDtypeStruct((2 * rows, chan), F32)] * 2
    token_shapes = [jax.ShapeDtypeStruct((2 * rows, quarter), BF16)] * 2
    return pl.pallas_call(
        kernel,
        grid_spec=pltpu.PrefetchScalarGridSpec(
            num_scalar_prefetch=1,
            grid=(4,),
            in_specs=[
                pl.BlockSpec((tile, width), lambda i, o: (jnp.minimum(i, 1), 0)),
                pl.BlockSpec((tile, width), lambda i, o: (jnp.maximum(i - 2, 0), 0)),
            ]
            + by_row[: len(totals)]
            + [pl.BlockSpec(weights[0].shape, lambda i, o: (0, 0))] * len(weights),
            out_specs=by_row + (tokens_out if last else []),
        ),
        out_shape=shapes + (token_shapes if last else []),
        compiler_params=pltpu.CompilerParams(vmem_limit_bytes=VMEM),
        cost_estimate=pl.CostEstimate(
            flops=2 * 2 * rows * quarter * chan * len(weights), bytes_accessed=18 * 2**20, transcendentals=0
        ),
        name=name,
    )(order, mine, other, *totals, *weights)


def cut_kernel(*refs):
    for src, dst in zip(refs[:4], refs[4:], strict=True):
        dst[...] = src[...]


def cut_halves(lines):
    rows, width = lines[0].shape
    tile = rows // 4
    upper = pl.BlockSpec((tile, width), lambda i: (i, 0))
    lower = pl.BlockSpec((tile, width), lambda i: (i + 2, 0))
    return pl.pallas_call(
        cut_kernel,
        grid=(2,),
        in_specs=[upper, lower, upper, lower],
        out_specs=[upper] * 4,
        out_shape=[jax.ShapeDtypeStruct((rows // 2, width), BF16)] * 4,
        compiler_params=pltpu.CompilerParams(vmem_limit_bytes=VMEM),
        cost_estimate=pl.CostEstimate(flops=0, bytes_accessed=4 * rows * width * 2, transcendentals=0),
        name="cut_halves",
    )(*lines)


def last_kernel(key_ref, value_ref, key_tok_ref, value_tok_ref, ka, kb, va, vb, source_ref, gate_ref):
    half = key_tok_ref.shape[1] // 2
    chan = source_ref.shape[0]

    def finish(total_ref, tok_ref, wa, wb):
        total = total_ref[...]
        total += jnp.dot(tok_ref[:, :half], stacked(wa, 2), preferred_element_type=F32)
        total += jnp.dot(tok_ref[:, half:], stacked(wb, 2), preferred_element_type=F32)
        return total.astype(BF16).astype(F32)

    key = finish(key_ref, key_tok_ref, ka, kb)
    value = finish(value_ref, value_tok_ref, va, vb)
    source_ref[...] = (key[:, :chan] * value[:, :chan]).T.astype(BF16)
    gate_ref[: chan // 2, :] = key[:, chan:].T.astype(BF16)
    gate_ref[chan // 2 :, :] = value[:, chan:].T.astype(BF16)


def last_part(totals, tokens, weights):
    total, wide = totals[0].shape
    quarter = tokens[0].shape[1]
    tile = total // 4
    chan = wide * 2 // 3
    return pl.pallas_call(
        last_kernel,
        grid=(4,),
        in_specs=[pl.BlockSpec((tile, wide), lambda i: (i, 0))] * 2
        + [pl.BlockSpec((tile, quarter), lambda i: (i, 0))] * 2
        + [pl.BlockSpec(weights[0].shape, lambda i: (0, 0))] * 4,
        out_specs=[pl.BlockSpec((chan, tile), lambda i: (0, i))] * 2,
        out_shape=[jax.ShapeDtypeStruct((chan, total), BF16)] * 2,
        compiler_params=pltpu.CompilerParams(vmem_limit_bytes=VMEM),
        cost_estimate=pl.CostEstimate(
            flops=2 * 2 * total * quarter * wide, bytes_accessed=16 * 2**20, transcendentals=0
        ),
        name="last_part",
    )(*totals, *tokens, *weights)


def turn(ref):
    return ref[...].astype(F32).T.astype(BF16)


def mix_kernel(here, w_here, out_ref, lhs_ref):
    @pl.when(pl.program_id(0) == 0)
    def _():
        lhs_ref[...] = turn(here)

    out_ref[...] = jnp.dot(lhs_ref[...], w_here[...], preferred_element_type=F32)


def mix_more_kernel(total_ref, near_h, far_h, w_near, w_far, out_ref, lhs_ref):
    m = near_h.shape[0]

    @pl.when(pl.program_id(0) == 0)
    def _():
        lhs_ref[:, :m] = turn(near_h)
        lhs_ref[:, m:] = turn(far_h)

    total = total_ref[...]
    total += jnp.dot(lhs_ref[:, :m], w_near[...], preferred_element_type=F32)
    total += jnp.dot(lhs_ref[:, m:], w_far[...], preferred_element_type=F32)
    out_ref[...] = total.astype(BF16)


def mix_part(total, parts, weights):
    rows = parts[0].shape[1]
    width = weights[0].shape[1]
    tile = width // 4
    depth = sum(p.shape[0] for p in parts)
    totals = [] if total is None else [total]

    def whole(g):
        return pl.BlockSpec(g.shape, lambda i: (0, 0))

    def tiled(w):
        return pl.BlockSpec((w.shape[0], tile), lambda i: (0, i))

    return pl.pallas_call(
        mix_kernel if total is None else mix_more_kernel,
        grid=(4,),
        in_specs=[tiled(t) for t in totals] + [whole(p) for p in parts] + [tiled(w) for w in weights],
        out_specs=pl.BlockSpec((rows, tile), lambda i: (0, i)),
        out_shape=jax.ShapeDtypeStruct((rows, width), F32 if total is None else BF16),
        scratch_shapes=[pltpu.VMEM((rows, depth), BF16)],
        compiler_params=pltpu.CompilerParams(vmem_limit_bytes=VMEM),
        cost_estimate=pl.CostEstimate(
            flops=2 * rows * depth * width, bytes_accessed=12 * 2**20, transcendentals=0
        ),
        name="mix_part" if total is None else "mix_more",
    )(*totals, *parts, *weights)


def filter_kernel(order_ref, *refs):
    pieces, (cs_ref, twist_ref, f_ref, m_ref, natural_ref) = refs[:32], refs[32:]
    points, lanes = natural_ref.shape[1:]
    rows, cols = points // 2, lanes // 2
    for row in range(2):
        for n in range(16):
            for dz in range(2):
                chip = order_ref[row, 2 * n + dz]
                for c in range(2):
                    start = pl.multiple_of(chip * 32 + 16 * c, 16)
                    spot = (2 * dz + c) * lanes
                    natural_ref[row, pl.ds(start, 16), :] = pieces[16 * row + n][:, spot : spot + lanes]
    upper, lower = natural_ref[0], natural_ref[1]
    whole = (upper.astype(F32) + lower.astype(F32)).T
    i = lax.broadcasted_iota(jnp.int32, (rows, rows), 0)
    j = lax.broadcasted_iota(jnp.int32, (rows, rows), 1)
    mirror = (i + j == rows).astype(F32).astype(BF16)
    i = lax.broadcasted_iota(jnp.int32, (lanes, lanes), 0)
    j = lax.broadcasted_iota(jnp.int32, (lanes, lanes), 1)
    flip = ((i // cols == j // cols) & (i % cols + j % cols == cols - 1)).astype(F32).astype(BF16)

    def mirrored(part):
        turned = jnp.dot(flip, part[:, rows:], preferred_element_type=F32).astype(BF16)
        return jnp.dot(turned, mirror, preferred_element_type=F32)

    other = mirrored(upper.astype(F32).T.astype(BF16)) + mirrored(lower.astype(F32).T.astype(BF16))
    f_ref[:, :rows] = 0.5 * (whole[:cols, :rows] + other[:cols])
    f_ref[:, rows:] = 0.5 * (whole[cols:, :rows] - other[cols:])
    c, s = cs_ref[0], cs_ref[1]

    def contract(left, right):
        return lax.dot_general(
            left, right, (((0,), (0,)), ((), ())), precision=HIGH, preferred_element_type=F32
        )

    m_ref[...] = jnp.zeros_like(m_ref)
    for n, k in enumerate((0, rows)):
        e_re, e_im = whole[:cols, k : k + 1], whole[cols:, k : k + 1]
        u = c * e_re - s * e_im
        v = s * e_re + c * e_im
        g = contract(u, c) + contract(v, s)
        if n:
            g = g * twist_ref[0] - (contract(v, c) - contract(u, s)) * twist_ref[1]
        for start in (n * cols, lanes + n * cols):
            spot = slice(start, start + cols)
            m_ref[spot, spot] = g.astype(BF16)


def filter_part(order, key_lines, value_lines, cs, twist):
    cols = cs.shape[1]
    lanes = 2 * cols
    points = 16 * SEQ
    rows = points // 2
    specs, operands = [], []
    for lines in (key_lines, value_lines):
        for line, parts in zip(lines, (4, 4, 2, 2, 4), strict=True):
            stride = line.shape[0] // parts // 16
            for i in range(parts):
                at = stride * (i + 1) - 1
                specs.append(pl.BlockSpec((16, 4 * lanes), lambda i, o, at=at: (at, 0)))
                operands.append(line)
    return pl.pallas_call(
        filter_kernel,
        grid_spec=pltpu.PrefetchScalarGridSpec(
            num_scalar_prefetch=1,
            grid=(1,),
            in_specs=specs
            + [
                pl.BlockSpec(cs.shape, lambda i, o: (0, 0, 0)),
                pl.BlockSpec(twist.shape, lambda i, o: (0, 0, 0)),
            ],
            out_specs=[
                pl.BlockSpec((cols, 2 * rows), lambda i, o: (0, 0)),
                pl.BlockSpec((2 * lanes, 2 * lanes), lambda i, o: (0, 0)),
            ],
            scratch_shapes=[pltpu.VMEM((2, points, lanes), BF16)],
        ),
        out_shape=[
            jax.ShapeDtypeStruct((cols, 2 * rows), F32),
            jax.ShapeDtypeStruct((2 * lanes, 2 * lanes), BF16),
        ],
        compiler_params=pltpu.CompilerParams(vmem_limit_bytes=VMEM),
        cost_estimate=pl.CostEstimate(flops=10**9, bytes_accessed=2**20, transcendentals=0),
        name="filter_part",
    )(order, *operands, cs, twist)


def conv_kernel(
    x_ref, fwd_hbm, inv_hbm, tw_hbm, a_ref, ai_ref, m_ref, f_ref, y_ref, fwd_ref, inv_ref, tw_ref, r_ref, q_ref, sems
):
    copies = [
        pltpu.make_async_copy(src, dst, sems.at[i])
        for i, (src, dst) in enumerate(((fwd_hbm, fwd_ref), (tw_hbm, tw_ref), (inv_hbm, inv_ref)))
    ]
    for copy in copies:
        copy.start()
    chips, chans, both = x_ref.shape
    rows = both // 2
    blocks = rows // 128
    half = 2 * chips
    copies[0].wait()
    for col in range(2):
        x = x_ref[:, :, col * rows : (col + 1) * rows].reshape(chips * chans, rows)
        r = jnp.dot(x, fwd_ref[...], preferred_element_type=F32)
        r = r.reshape(chips, chans, 2 * rows)
        if col == 0:
            copies[1].wait()
        tw = tw_ref[col * chips : (col + 1) * chips, :]
        cos = tw[:, None, :rows]
        sin = tw[:, None, rows:]
        re, im = r[:, :, :rows], r[:, :, rows:]
        turned_re = (re * cos + im * sin).reshape(chips * chans, rows)
        turned_im = (im * cos - re * sin).reshape(chips * chans, rows)
        for k in range(blocks):
            r_ref[col, k] = turned_re[:, k * 128 : (k + 1) * 128]
            r_ref[col, blocks + k] = turned_im[:, k * 128 : (k + 1) * 128]
    lane = lax.broadcasted_iota(jnp.int32, (4 * half, 128), 1)

    def pair(n, carry):
        picks = [pl.ds(2 * n + i, chips, stride=chans) for i in range(2)]
        parts = [
            jnp.concatenate([r_ref[col, part * blocks + k, pick, :] for k in range(blocks)], axis=1)
            for pick in picks
            for part in range(2)
            for col in range(2)
        ]
        turned = jnp.concatenate(parts, axis=0).astype(BF16)
        s = jnp.dot(a_ref[...], turned, preferred_element_type=F32)
        f_re, f_im = f_ref[:, :rows], f_ref[:, rows:]
        filtered = []
        for i in range(2):
            s_re = s[2 * i * half : (2 * i + 1) * half]
            s_im = s[(2 * i + 1) * half : (2 * i + 2) * half]
            filtered += [s_re * f_re - s_im * f_im, s_re * f_im + s_im * f_re]
        filtered = jnp.concatenate(filtered, axis=0).astype(BF16)
        back = jnp.dot(ai_ref[...], filtered, preferred_element_type=F32)
        edge = jnp.dot(m_ref[...], turned[:, :128], preferred_element_type=F32)
        head = jnp.where(lane == 0, edge, back[:, :128])
        back = jnp.concatenate([head, back[:, 128:]], axis=1)
        cos, sin = tw_ref[:, :rows], tw_ref[:, rows:]
        for i, pick in enumerate(picks):
            b_re = back[2 * i * half : (2 * i + 1) * half]
            b_im = back[(2 * i + 1) * half : (2 * i + 2) * half]
            out_re = b_re * cos - b_im * sin
            out_im = b_im * cos + b_re * sin
            for col in range(2):
                part = slice(col * chips, (col + 1) * chips)
                for k in range(blocks):
                    q_ref[col, k, pick, :] = out_re[part, k * 128 : (k + 1) * 128]
                    q_ref[col, blocks + k, pick, :] = out_im[part, k * 128 : (k + 1) * 128]
        return carry

    lax.fori_loop(0, chans // 2, pair, 0, unroll=4)
    copies[2].wait()
    for col in range(2):
        q = jnp.concatenate([q_ref[col, k].astype(BF16) for k in range(2 * blocks)], axis=1)
        y = jnp.dot(q, inv_ref[...], preferred_element_type=F32)
        y_ref[:, :, col * rows : (col + 1) * rows] = y.astype(BF16).reshape(chips, chans, rows)


def long_conv(x, fwd, inv, tw, a, ai, m, f):
    chips, chans, both = x.shape
    vmem = pl.BlockSpec(memory_space=pltpu.VMEM)
    hbm = pl.BlockSpec(memory_space=pl.ANY)
    return pl.pallas_call(
        conv_kernel,
        in_specs=[vmem, hbm, hbm, hbm, vmem, vmem, vmem, vmem],
        out_specs=vmem,
        out_shape=jax.ShapeDtypeStruct(x.shape, BF16),
        scratch_shapes=[
            pltpu.VMEM(fwd.shape, BF16),
            pltpu.VMEM(inv.shape, BF16),
            pltpu.VMEM(tw.shape, F32),
            pltpu.VMEM((2, both // 128, chips * chans, 128), F32),
            pltpu.VMEM((2, both // 128, chips * chans, 128), F32),
            pltpu.SemaphoreType.DMA((3,)),
        ],
        compiler_params=pltpu.CompilerParams(vmem_limit_bytes=VMEM),
        cost_estimate=pl.CostEstimate(flops=8 * 10**9, bytes_accessed=8 * 2**20, transcendentals=0),
        name="long_conv",
    )(x, fwd, inv, tw, a, ai, m, f)


def cos_sin(product, modulus):
    phase = (product % modulus).astype(F32) * (2.0 * math.pi / modulus)
    return jnp.cos(phase), jnp.sin(phase)


def twice(t):
    zero = jnp.zeros_like(t)
    return jnp.block([[t, zero], [zero, t]])


def column_tables(core, rows, cols, padded):
    i = lax.iota(jnp.int32, cols)
    b = 2 * (i % CHIPS) + ((i // CHIPS) ^ core)
    k1 = lax.iota(jnp.int32, rows)
    tw = jnp.concatenate(cos_sin(b[:, None] * k1[None, :], padded), axis=1)
    k2 = lax.iota(jnp.int32, cols)
    c, s = cos_sin(k2[:, None] * b[None, :], cols)
    a = jnp.block([[c, s], [-s, c]])
    twist = jnp.stack(cos_sin(jnp.mod((b[:, None] - b[None, :]) * rows, padded), padded))

    return tw, twice(a.astype(BF16)), twice(a.T.astype(BF16)), jnp.stack([c, s]), twist


def gather_line(block, axis):
    d1 = send(block, **{axis: -1})
    d3 = send(block, **{axis: 1})
    d2 = send(block, **{axis: 2})
    return jnp.concatenate([block, d1, d2, d3], axis=0)


def per_device(tokens, in_weight, filter_spectrum, skip_bias, out_weight):
    rows, _, width = tokens.shape
    cols = SEQ
    padded = 2 * rows * cols
    s = lax.axis_index("seq")
    h = lax.axis_index("ch")
    z, y, x, core = coords(s)
    chan = in_weight.shape[2] // 2
    depth = in_weight.shape[0]

    mine = tokens.reshape(rows, width)
    filt = jnp.transpose(filter_spectrum, (3, 1, 0, 2)).reshape(4, -1, 2 * cols)
    filt = jnp.concatenate(split_table(filt), axis=1)

    def half_for(c):
        w = lax.dynamic_slice_in_dim(in_weight, c * chan, chan, 2)
        return jnp.transpose(w, (1, 0, 2)).reshape(3 * depth, chan)

    def load(w, c, z_to):
        f = lax.dynamic_index_in_dim(filt, 2 * c + z_to, 0, keepdims=False)
        return jnp.concatenate([w, jnp.pad(f, ((0, 0), (0, chan - 2 * cols)))], axis=0)

    keep, give = half_for(core), half_for(1 - core)
    far = send(load(keep, core, 1 - z), dz=1)
    far_near = send(load(give, 1 - core, 1 - z), dz=1, dc=1)
    near = send(load(give, 1 - core, z), dc=1)
    keep = load(keep, core, z)
    other = send(mine, dc=1)

    def ordered(own, partner, axis=0):
        return jnp.concatenate(
            [jnp.where(core == 0, own, partner), jnp.where(core == 0, partner, own)], axis=axis
        )

    def block_of(n):
        part = slice(n * depth, (n + 1) * depth)
        w = jnp.concatenate([ordered(keep[part], near[part]), ordered(far[part], far_near[part])], axis=0)
        part, lanes = slice(0, depth), slice((n - 1) * chan // 2, n * chan // 2)
        g = jnp.concatenate(
            [
                ordered(keep[part, lanes], near[part, lanes]),
                ordered(far[part, lanes], far_near[part, lanes]),
            ],
            axis=0,
        )
        part, lanes = slice(3 * depth + 16 * (n - 1), 3 * depth + 16 * n), slice(0, 2 * cols)
        f = jnp.concatenate(
            [
                ordered(keep[part, lanes], near[part, lanes], 1),
                ordered(far[part, lanes], far_near[part, lanes], 1),
            ],
            axis=1,
        )
        return jnp.concatenate(
            [jnp.concatenate([w, f], axis=0), jnp.pad(g, ((0, 16), (0, 0)))], axis=1
        )

    half_ow = out_weight.shape[0] // 2
    ow_part = lax.dynamic_slice_in_dim(out_weight, core * half_ow, half_ow, 0)
    key_block, value_block, other, ow_part = lax.optimization_barrier(
        (block_of(1), block_of(2), other, ow_part)
    )
    key_line, value_line, ow_part = lax.optimization_barrier(
        (gather_line(key_block, "dx"), gather_line(value_block, "dy"), ow_part)
    )

    order = np.arange(32)
    p_, q_, dz = order // 8, (order // 2) % 4, order % 2
    key_order = ((z ^ dz) * 4 + (y + p_) % 4) * 4 + (x + q_) % 4
    value_order = ((z ^ dz) * 4 + (y + q_) % 4) * 4 + (x + p_) % 4
    order = jnp.stack([key_order, value_order])
    first = sum_part(first_kernel, "first_part", order, mine, other, [], [key_line, value_line], True)
    near_lines = [send(key_line, dy=-1), send(key_line, dy=1), send(value_line, dx=-1), send(value_line, dx=1)]
    tables = column_tables(core, rows, cols, padded)
    near_lines, first, tables = lax.optimization_barrier((near_lines, first, tables))
    halves = cut_halves(near_lines)
    last_lines = [
        send(halves[0], dy=-1),
        send(halves[1], dy=1),
        send(halves[2], dx=-1),
        send(halves[3], dx=1),
    ]
    totals = sum_part(second_kernel, "second_part", order, mine, other, first[:2], near_lines, False)

    perm = []
    for t in range(SEQ):
        tz, ty, tx, tc = coords(t)
        for th in range(2):
            perm.append((t * 2 + th, index_of(tz ^ tc, ty, tx, tc) * 2 + 1 - th))
    ow_same = lax.ppermute(ow_part, ("seq", "ch"), perm)

    source, gate = last_part(totals, first[2:], last_lines)
    packed = source.reshape(CHIPS, chan // CHIPS, 2 * rows)
    mine_ch = lax.all_to_all(packed, "seq", 0, 0, axis_index_groups=SAME_CORE)

    tw, a, ai, cs, twist = tables
    k1_, k3_, v1_, v3_ = near_lines
    f, m = filter_part(
        order,
        [key_line, k1_, last_lines[0], last_lines[1], k3_],
        [value_line, v1_, last_lines[2], last_lines[3], v3_],
        cs,
        twist,
    )
    forward, inverse = row_tables(rows, padded)
    fwd = jnp.asarray(forward.astype(np.float32).astype(ml_dtypes.bfloat16))
    inv = jnp.asarray(inverse.astype(np.float32).astype(ml_dtypes.bfloat16))
    mine_ch, f, m = lax.optimization_barrier((mine_ch, f, m))
    conv = long_conv(mine_ch, fwd, inv, tw, a, ai, m, f)
    conv = lax.all_to_all(conv, "seq", 0, 0, axis_index_groups=SAME_CORE)
    conv = conv.reshape(chan, 2 * rows).astype(F32)

    gate = gate.astype(F32)
    skip = lax.dynamic_slice_in_dim(skip_bias, core * chan, chan, 0)[:, None]
    gated = (gate * (conv + skip * source.astype(F32))).astype(BF16)

    kept = rows // 2
    own_here = lax.dynamic_slice(gated, (0, h * kept), (chan, kept))
    own_there = lax.dynamic_slice(gated, (0, (1 - h) * kept), (chan, kept))
    oth_here = lax.dynamic_slice(gated, (0, rows + h * kept), (chan, kept))
    oth_there = lax.dynamic_slice(gated, (0, rows + (1 - h) * kept), (chan, kept))
    swap_ch = [(0, 1), (1, 0)]
    from_h = lax.ppermute(own_there, "ch", swap_ch)
    perm2 = []
    for t in range(SEQ):
        for th in range(2):
            perm2.append((t * 2 + th, (t ^ 1) * 2 + 1 - th))
    from_hc = lax.ppermute(oth_there, ("seq", "ch"), perm2)
    from_c = send(oth_here, dc=1)
    from_c, ow_same = lax.optimization_barrier((from_c, ow_same))
    ow_cross = send(ow_same, dc=1)
    here = ordered(own_here, from_c)

    mixed = mix_part(None, [here], [out_weight])
    mixed = mix_part(mixed, [from_h, from_hc], [ow_same, ow_cross])
    return mixed.reshape(kept, 1, width)


def solution(mesh):
    in_specs = (
        P(None, "seq", None),
        P("seq", None, "ch"),
        P(None, "seq", None, "ch"),
        P("ch"),
        P("ch", None),
    )
    return jax.shard_map(
        per_device, mesh=mesh, in_specs=in_specs, out_specs=P("ch", "seq", None), check_vma=False
    )
```

```python
import functools
import math

import jax
import jax.numpy as jnp
import ml_dtypes
import numpy as np
from jax import lax
from jax.experimental import pallas as pl
from jax.experimental.pallas import tpu as pltpu
from jax.sharding import PartitionSpec as P

BF16 = jnp.bfloat16
F32 = jnp.float32
HIGH = lax.Precision.HIGHEST
SEQ = 64
VMEM = 60 * 2**20
CHIPS = 32
SAME_CORE = [[2 * p + j for p in range(CHIPS)] for j in range(2)]


def coords(s):
    return s // 32, (s // 8) % 4, (s // 2) % 4, s % 2


def index_of(z, y, x, c):
    return ((z * 4 + y) * 4 + x) * 2 + c


def send(value, dz=0, dy=0, dx=0, dc=0):
    perm = []
    for s in range(SEQ):
        z, y, x, c = coords(s)
        perm.append((s, index_of((z + dz) % 2, (y + dy) % 4, (x + dx) % 4, c ^ dc)))
    return lax.ppermute(value, "seq", perm)


def split_table(table):
    upper = table.astype(BF16)
    lower = (table - upper.astype(F32)).astype(BF16)
    return upper, lower


def row_tables(rows, padded):
    points = 2 * rows
    a = np.arange(rows)
    k = np.arange(rows)
    phase = 2.0 * np.pi * ((a[:, None] * k[None, :]) % points) / points
    re, im = np.cos(phase), -np.sin(phase)
    im[:, 0] = np.where(a % 2 == 0, 1.0, -1.0)
    forward = np.concatenate([re, im], axis=1)
    scale = np.full((rows,), 2.0)
    scale[0] = 1.0
    inverse = np.concatenate([re * scale, im * scale], axis=1).T / padded
    return forward, inverse


def picked(order_ref, row, group, tok_ref):
    blocks = [
        tok_ref[:, pl.ds(pl.multiple_of(order_ref[row, group * 8 + i] * 128, 128), 128)]
        for i in range(8)
    ]
    return jnp.concatenate(blocks, axis=1)


def stacked(ref, parts):
    stride = ref.shape[0] // parts
    return jnp.concatenate([ref[stride * i : stride * i + stride - 16] for i in range(parts)], axis=0)


def by_column(run, mine_ref, other_ref):
    step = pl.program_id(0)

    @pl.when(step < 2)
    def _():
        run(mine_ref)

    @pl.when(step >= 2)
    def _():
        run(other_ref)


def first_kernel(order_ref, mine_ref, other_ref, key_line, value_line, *outs):
    key_ref, value_ref, key_tok_ref, value_tok_ref = outs

    def run(tok_ref):
        for row, line, total_ref, last_ref in (
            (0, key_line, key_ref, key_tok_ref),
            (1, value_line, value_ref, value_tok_ref),
        ):
            total_ref[...] = jnp.dot(
                picked(order_ref, row, 0, tok_ref), stacked(line, 4), preferred_element_type=F32
            )
            last_ref[...] = picked(order_ref, row, 2, tok_ref)

    by_column(run, mine_ref, other_ref)


def second_kernel(order_ref, mine_ref, other_ref, key_in, value_in, k1, k3, v1, v3, key_ref, value_ref):
    def run(tok_ref):
        for row, before, e1, e3, total_ref in (
            (0, key_in, k1, k3, key_ref),
            (1, value_in, v1, v3, value_ref),
        ):
            total = before[...]
            total += jnp.dot(picked(order_ref, row, 1, tok_ref), stacked(e1, 4), preferred_element_type=F32)
            total += jnp.dot(picked(order_ref, row, 3, tok_ref), stacked(e3, 4), preferred_element_type=F32)
            total_ref[...] = total

    by_column(run, mine_ref, other_ref)


def sum_part(kernel, name, order, mine, other, totals, weights, last):
    rows, width = mine.shape
    chan = weights[0].shape[1]
    tile = rows // 2
    quarter = width // 4
    by_row = [pl.BlockSpec((tile, chan), lambda i, o: (i, 0))] * 2
    tokens_out = [pl.BlockSpec((tile, quarter), lambda i, o: (i, 0))] * 2
    shapes = [jax.ShapeDtypeStruct((2 * rows, chan), F32)] * 2
    token_shapes = [jax.ShapeDtypeStruct((2 * rows, quarter), BF16)] * 2
    return pl.pallas_call(
        kernel,
        grid_spec=pltpu.PrefetchScalarGridSpec(
            num_scalar_prefetch=1,
            grid=(4,),
            in_specs=[
                pl.BlockSpec((tile, width), lambda i, o: (jnp.minimum(i, 1), 0)),
                pl.BlockSpec((tile, width), lambda i, o: (jnp.maximum(i - 2, 0), 0)),
            ]
            + by_row[: len(totals)]
            + [pl.BlockSpec(weights[0].shape, lambda i, o: (0, 0))] * len(weights),
            out_specs=by_row + (tokens_out if last else []),
        ),
        out_shape=shapes + (token_shapes if last else []),
        compiler_params=pltpu.CompilerParams(vmem_limit_bytes=VMEM),
        cost_estimate=pl.CostEstimate(
            flops=2 * 2 * rows * quarter * chan * len(weights), bytes_accessed=18 * 2**20, transcendentals=0
        ),
        name=name,
    )(order, mine, other, *totals, *weights)


def cut_kernel(*refs):
    for src, dst in zip(refs[:4], refs[4:], strict=True):
        dst[...] = src[...]


def cut_halves(lines):
    rows, width = lines[0].shape
    tile = rows // 4
    upper = pl.BlockSpec((tile, width), lambda i: (i, 0))
    lower = pl.BlockSpec((tile, width), lambda i: (i + 2, 0))
    return pl.pallas_call(
        cut_kernel,
        grid=(2,),
        in_specs=[upper, lower, upper, lower],
        out_specs=[upper] * 4,
        out_shape=[jax.ShapeDtypeStruct((rows // 2, width), BF16)] * 4,
        compiler_params=pltpu.CompilerParams(vmem_limit_bytes=VMEM),
        cost_estimate=pl.CostEstimate(flops=0, bytes_accessed=4 * rows * width * 2, transcendentals=0),
        name="cut_halves",
    )(*lines)


def last_kernel(key_ref, value_ref, key_tok_ref, value_tok_ref, ka, kb, va, vb, source_ref, gate_ref):
    half = key_tok_ref.shape[1] // 2
    chan = source_ref.shape[0]

    def finish(total_ref, tok_ref, wa, wb):
        total = total_ref[...]
        total += jnp.dot(tok_ref[:, :half], stacked(wa, 2), preferred_element_type=F32)
        total += jnp.dot(tok_ref[:, half:], stacked(wb, 2), preferred_element_type=F32)
        return total.astype(BF16).astype(F32)

    key = finish(key_ref, key_tok_ref, ka, kb)
    value = finish(value_ref, value_tok_ref, va, vb)
    source_ref[...] = (key[:, :chan] * value[:, :chan]).T.astype(BF16)
    gate_ref[: chan // 2, :] = key[:, chan:].T.astype(BF16)
    gate_ref[chan // 2 :, :] = value[:, chan:].T.astype(BF16)


def last_part(totals, tokens, weights):
    total, wide = totals[0].shape
    quarter = tokens[0].shape[1]
    tile = total // 4
    chan = wide * 2 // 3
    return pl.pallas_call(
        last_kernel,
        grid=(4,),
        in_specs=[pl.BlockSpec((tile, wide), lambda i: (i, 0))] * 2
        + [pl.BlockSpec((tile, quarter), lambda i: (i, 0))] * 2
        + [pl.BlockSpec(weights[0].shape, lambda i: (0, 0))] * 4,
        out_specs=[pl.BlockSpec((chan, tile), lambda i: (0, i))] * 2,
        out_shape=[jax.ShapeDtypeStruct((chan, total), BF16)] * 2,
        compiler_params=pltpu.CompilerParams(vmem_limit_bytes=VMEM),
        cost_estimate=pl.CostEstimate(
            flops=2 * 2 * total * quarter * wide, bytes_accessed=16 * 2**20, transcendentals=0
        ),
        name="last_part",
    )(*totals, *tokens, *weights)


def turn(ref):
    return ref[...].astype(F32).T.astype(BF16)


def mix_kernel(here, w_here, out_ref, lhs_ref):
    @pl.when(pl.program_id(0) == 0)
    def _():
        lhs_ref[...] = turn(here)

    out_ref[...] = jnp.dot(lhs_ref[...], w_here[...], preferred_element_type=F32)


def mix_more_kernel(total_ref, near_h, far_h, w_near, w_far, out_ref, lhs_ref):
    m = near_h.shape[0]

    @pl.when(pl.program_id(0) == 0)
    def _():
        lhs_ref[:, :m] = turn(near_h)
        lhs_ref[:, m:] = turn(far_h)

    total = total_ref[...]
    total += jnp.dot(lhs_ref[:, :m], w_near[...], preferred_element_type=F32)
    total += jnp.dot(lhs_ref[:, m:], w_far[...], preferred_element_type=F32)
    out_ref[...] = total.astype(BF16)


def mix_part(total, parts, weights):
    rows = parts[0].shape[1]
    width = weights[0].shape[1]
    tile = width // 4
    depth = sum(p.shape[0] for p in parts)
    totals = [] if total is None else [total]

    def whole(g):
        return pl.BlockSpec(g.shape, lambda i: (0, 0))

    def tiled(w):
        return pl.BlockSpec((w.shape[0], tile), lambda i: (0, i))

    return pl.pallas_call(
        mix_kernel if total is None else mix_more_kernel,
        grid=(4,),
        in_specs=[tiled(t) for t in totals] + [whole(p) for p in parts] + [tiled(w) for w in weights],
        out_specs=pl.BlockSpec((rows, tile), lambda i: (0, i)),
        out_shape=jax.ShapeDtypeStruct((rows, width), F32 if total is None else BF16),
        scratch_shapes=[pltpu.VMEM((rows, depth), BF16)],
        compiler_params=pltpu.CompilerParams(vmem_limit_bytes=VMEM),
        cost_estimate=pl.CostEstimate(
            flops=2 * rows * depth * width, bytes_accessed=12 * 2**20, transcendentals=0
        ),
        name="mix_part" if total is None else "mix_more",
    )(*totals, *parts, *weights)


def filter_kernel(order_ref, *refs):
    pieces, (cs_ref, twist_ref, f_ref, m_ref, natural_ref) = refs[:32], refs[32:]
    points, lanes = natural_ref.shape[1:]
    rows, cols = points // 2, lanes // 2
    for row in range(2):
        for n in range(16):
            for dz in range(2):
                chip = order_ref[row, 2 * n + dz]
                for c in range(2):
                    start = pl.multiple_of(chip * 32 + 16 * c, 16)
                    spot = (2 * dz + c) * lanes
                    natural_ref[row, pl.ds(start, 16), :] = pieces[16 * row + n][:, spot : spot + lanes]
    upper, lower = natural_ref[0], natural_ref[1]
    whole = (upper.astype(F32) + lower.astype(F32)).T
    i = lax.broadcasted_iota(jnp.int32, (rows, rows), 0)
    j = lax.broadcasted_iota(jnp.int32, (rows, rows), 1)
    mirror = (i + j == rows).astype(F32).astype(BF16)
    i = lax.broadcasted_iota(jnp.int32, (lanes, lanes), 0)
    j = lax.broadcasted_iota(jnp.int32, (lanes, lanes), 1)
    flip = ((i // cols == j // cols) & (i % cols + j % cols == cols - 1)).astype(F32).astype(BF16)

    def mirrored(part):
        turned = jnp.dot(flip, part[:, rows:], preferred_element_type=F32).astype(BF16)
        return jnp.dot(turned, mirror, preferred_element_type=F32)

    other = mirrored(upper.astype(F32).T.astype(BF16)) + mirrored(lower.astype(F32).T.astype(BF16))
    f_ref[:, :rows] = 0.5 * (whole[:cols, :rows] + other[:cols])
    f_ref[:, rows:] = 0.5 * (whole[cols:, :rows] - other[cols:])
    c, s = cs_ref[0], cs_ref[1]

    def contract(left, right):
        return lax.dot_general(
            left, right, (((0,), (0,)), ((), ())), precision=HIGH, preferred_element_type=F32
        )

    m_ref[...] = jnp.zeros_like(m_ref)
    for n, k in enumerate((0, rows)):
        e_re, e_im = whole[:cols, k : k + 1], whole[cols:, k : k + 1]
        u = c * e_re - s * e_im
        v = s * e_re + c * e_im
        g = contract(u, c) + contract(v, s)
        if n:
            g = g * twist_ref[0] - (contract(v, c) - contract(u, s)) * twist_ref[1]
        for start in (n * cols, lanes + n * cols):
            spot = slice(start, start + cols)
            m_ref[spot, spot] = g.astype(BF16)


def filter_part(order, key_lines, value_lines, cs, twist):
    cols = cs.shape[1]
    lanes = 2 * cols
    points = 16 * SEQ
    rows = points // 2
    specs, operands = [], []
    for lines in (key_lines, value_lines):
        for line, parts in zip(lines, (4, 4, 2, 2, 4), strict=True):
            stride = line.shape[0] // parts // 16
            for i in range(parts):
                at = stride * (i + 1) - 1
                specs.append(pl.BlockSpec((16, 4 * lanes), lambda i, o, at=at: (at, 0)))
                operands.append(line)
    return pl.pallas_call(
        filter_kernel,
        grid_spec=pltpu.PrefetchScalarGridSpec(
            num_scalar_prefetch=1,
            grid=(1,),
            in_specs=specs
            + [
                pl.BlockSpec(cs.shape, lambda i, o: (0, 0, 0)),
                pl.BlockSpec(twist.shape, lambda i, o: (0, 0, 0)),
            ],
            out_specs=[
                pl.BlockSpec((cols, 2 * rows), lambda i, o: (0, 0)),
                pl.BlockSpec((2 * lanes, 2 * lanes), lambda i, o: (0, 0)),
            ],
            scratch_shapes=[pltpu.VMEM((2, points, lanes), BF16)],
        ),
        out_shape=[
            jax.ShapeDtypeStruct((cols, 2 * rows), F32),
            jax.ShapeDtypeStruct((2 * lanes, 2 * lanes), BF16),
        ],
        compiler_params=pltpu.CompilerParams(vmem_limit_bytes=VMEM),
        cost_estimate=pl.CostEstimate(flops=10**9, bytes_accessed=2**20, transcendentals=0),
        name="filter_part",
    )(order, *operands, cs, twist)


def conv_kernel(
    x_ref, fwd_hbm, inv_hbm, tw_hbm, a_ref, ai_ref, m_ref, f_ref, y_ref, fwd_ref, inv_ref, tw_ref, r_ref, q_ref, sems
):
    copies = [
        pltpu.make_async_copy(src, dst, sems.at[i])
        for i, (src, dst) in enumerate(((fwd_hbm, fwd_ref), (tw_hbm, tw_ref), (inv_hbm, inv_ref)))
    ]
    for copy in copies:
        copy.start()
    chips, chans, both = x_ref.shape
    rows = both // 2
    blocks = rows // 128
    half = 2 * chips
    copies[0].wait()
    for col in range(2):
        x = x_ref[:, :, col * rows : (col + 1) * rows].reshape(chips * chans, rows)
        r = jnp.dot(x, fwd_ref[...], preferred_element_type=F32)
        r = r.reshape(chips, chans, 2 * rows)
        if col == 0:
            copies[1].wait()
        tw = tw_ref[col * chips : (col + 1) * chips, :]
        cos = tw[:, None, :rows]
        sin = tw[:, None, rows:]
        re, im = r[:, :, :rows], r[:, :, rows:]
        turned_re = (re * cos + im * sin).reshape(chips * chans, rows)
        turned_im = (im * cos - re * sin).reshape(chips * chans, rows)
        for k in range(blocks):
            r_ref[col, k] = turned_re[:, k * 128 : (k + 1) * 128]
            r_ref[col, blocks + k] = turned_im[:, k * 128 : (k + 1) * 128]
    lane = lax.broadcasted_iota(jnp.int32, (4 * half, 128), 1)

    def pair(n, carry):
        picks = [pl.ds(2 * n + i, chips, stride=chans) for i in range(2)]
        parts = [
            jnp.concatenate([r_ref[col, part * blocks + k, pick, :] for k in range(blocks)], axis=1)
            for pick in picks
            for part in range(2)
            for col in range(2)
        ]
        turned = jnp.concatenate(parts, axis=0).astype(BF16)
        s = jnp.dot(a_ref[...], turned, preferred_element_type=F32)
        f_re, f_im = f_ref[:, :rows], f_ref[:, rows:]
        filtered = []
        for i in range(2):
            s_re = s[2 * i * half : (2 * i + 1) * half]
            s_im = s[(2 * i + 1) * half : (2 * i + 2) * half]
            filtered += [s_re * f_re - s_im * f_im, s_re * f_im + s_im * f_re]
        filtered = jnp.concatenate(filtered, axis=0).astype(BF16)
        back = jnp.dot(ai_ref[...], filtered, preferred_element_type=F32)
        edge = jnp.dot(m_ref[...], turned[:, :128], preferred_element_type=F32)
        head = jnp.where(lane == 0, edge, back[:, :128])
        back = jnp.concatenate([head, back[:, 128:]], axis=1)
        cos, sin = tw_ref[:, :rows], tw_ref[:, rows:]
        for i, pick in enumerate(picks):
            b_re = back[2 * i * half : (2 * i + 1) * half]
            b_im = back[(2 * i + 1) * half : (2 * i + 2) * half]
            out_re = b_re * cos - b_im * sin
            out_im = b_im * cos + b_re * sin
            for col in range(2):
                part = slice(col * chips, (col + 1) * chips)
                for k in range(blocks):
                    q_ref[col, k, pick, :] = out_re[part, k * 128 : (k + 1) * 128]
                    q_ref[col, blocks + k, pick, :] = out_im[part, k * 128 : (k + 1) * 128]
        return carry

    lax.fori_loop(0, chans // 2, pair, 0, unroll=4)
    copies[2].wait()
    for col in range(2):
        q = jnp.concatenate([q_ref[col, k].astype(BF16) for k in range(2 * blocks)], axis=1)
        y = jnp.dot(q, inv_ref[...], preferred_element_type=F32)
        y_ref[:, :, col * rows : (col + 1) * rows] = y.astype(BF16).reshape(chips, chans, rows)


def long_conv(x, fwd, inv, tw, a, ai, m, f):
    chips, chans, both = x.shape
    vmem = pl.BlockSpec(memory_space=pltpu.VMEM)
    hbm = pl.BlockSpec(memory_space=pl.ANY)
    return pl.pallas_call(
        conv_kernel,
        in_specs=[vmem, hbm, hbm, hbm, vmem, vmem, vmem, vmem],
        out_specs=vmem,
        out_shape=jax.ShapeDtypeStruct(x.shape, BF16),
        scratch_shapes=[
            pltpu.VMEM(fwd.shape, BF16),
            pltpu.VMEM(inv.shape, BF16),
            pltpu.VMEM(tw.shape, F32),
            pltpu.VMEM((2, both // 128, chips * chans, 128), F32),
            pltpu.VMEM((2, both // 128, chips * chans, 128), F32),
            pltpu.SemaphoreType.DMA((3,)),
        ],
        compiler_params=pltpu.CompilerParams(vmem_limit_bytes=VMEM),
        cost_estimate=pl.CostEstimate(flops=8 * 10**9, bytes_accessed=8 * 2**20, transcendentals=0),
        name="long_conv",
    )(x, fwd, inv, tw, a, ai, m, f)


def cos_sin(product, modulus):
    phase = (product % modulus).astype(F32) * (2.0 * math.pi / modulus)
    return jnp.cos(phase), jnp.sin(phase)


def twice(t):
    zero = jnp.zeros_like(t)
    return jnp.block([[t, zero], [zero, t]])


def column_tables(core, rows, cols, padded):
    i = lax.iota(jnp.int32, cols)
    b = 2 * (i % CHIPS) + ((i // CHIPS) ^ core)
    k1 = lax.iota(jnp.int32, rows)
    tw = jnp.concatenate(cos_sin(b[:, None] * k1[None, :], padded), axis=1)
    k2 = lax.iota(jnp.int32, cols)
    c, s = cos_sin(k2[:, None] * b[None, :], cols)
    a = jnp.block([[c, s], [-s, c]])
    twist = jnp.stack(cos_sin(jnp.mod((b[:, None] - b[None, :]) * rows, padded), padded))

    return tw, twice(a.astype(BF16)), twice(a.T.astype(BF16)), jnp.stack([c, s]), twist


def gather_line(block, axis):
    d1 = send(block, **{axis: -1})
    d3 = send(block, **{axis: 1})
    d2 = send(block, **{axis: 2})
    return jnp.concatenate([block, d1, d2, d3], axis=0)


def per_device(tokens, in_weight, filter_spectrum, skip_bias, out_weight):
    rows, _, width = tokens.shape
    cols = SEQ
    padded = 2 * rows * cols
    s = lax.axis_index("seq")
    h = lax.axis_index("ch")
    z, y, x, core = coords(s)
    chan = in_weight.shape[2] // 2
    depth = in_weight.shape[0]

    mine = tokens.reshape(rows, width)
    filt = jnp.transpose(filter_spectrum, (3, 1, 0, 2)).reshape(4, -1, 2 * cols)
    filt = jnp.concatenate(split_table(filt), axis=1)

    def half_for(c):
        w = lax.dynamic_slice_in_dim(in_weight, c * chan, chan, 2)
        return jnp.transpose(w, (1, 0, 2)).reshape(3 * depth, chan)

    def load(w, c, z_to):
        f = lax.dynamic_index_in_dim(filt, 2 * c + z_to, 0, keepdims=False)
        return jnp.concatenate([w, jnp.pad(f, ((0, 0), (0, chan - 2 * cols)))], axis=0)

    keep, give = half_for(core), half_for(1 - core)
    far = send(load(keep, core, 1 - z), dz=1)
    far_near = send(load(give, 1 - core, 1 - z), dz=1, dc=1)
    near = send(load(give, 1 - core, z), dc=1)
    keep = load(keep, core, z)
    other = send(mine, dc=1)

    def ordered(own, partner, axis=0):
        return jnp.concatenate(
            [jnp.where(core == 0, own, partner), jnp.where(core == 0, partner, own)], axis=axis
        )

    def block_of(n):
        part = slice(n * depth, (n + 1) * depth)
        w = jnp.concatenate([ordered(keep[part], near[part]), ordered(far[part], far_near[part])], axis=0)
        part, lanes = slice(0, depth), slice((n - 1) * chan // 2, n * chan // 2)
        g = jnp.concatenate(
            [
                ordered(keep[part, lanes], near[part, lanes]),
                ordered(far[part, lanes], far_near[part, lanes]),
            ],
            axis=0,
        )
        part, lanes = slice(3 * depth + 16 * (n - 1), 3 * depth + 16 * n), slice(0, 2 * cols)
        f = jnp.concatenate(
            [
                ordered(keep[part, lanes], near[part, lanes], 1),
                ordered(far[part, lanes], far_near[part, lanes], 1),
            ],
            axis=1,
        )
        return jnp.concatenate(
            [jnp.concatenate([w, f], axis=0), jnp.pad(g, ((0, 16), (0, 0)))], axis=1
        )

    half_ow = out_weight.shape[0] // 2
    ow_part = lax.dynamic_slice_in_dim(out_weight, core * half_ow, half_ow, 0)
    key_block, value_block, other, ow_part = lax.optimization_barrier(
        (block_of(1), block_of(2), other, ow_part)
    )
    key_line, value_line, ow_part = lax.optimization_barrier(
        (gather_line(key_block, "dx"), gather_line(value_block, "dy"), ow_part)
    )

    order = np.arange(32)
    p_, q_, dz = order // 8, (order // 2) % 4, order % 2
    key_order = ((z ^ dz) * 4 + (y + p_) % 4) * 4 + (x + q_) % 4
    value_order = ((z ^ dz) * 4 + (y + q_) % 4) * 4 + (x + p_) % 4
    order = jnp.stack([key_order, value_order])
    first = sum_part(first_kernel, "first_part", order, mine, other, [], [key_line, value_line], True)
    near_lines = [send(key_line, dy=-1), send(key_line, dy=1), send(value_line, dx=-1), send(value_line, dx=1)]
    tables = column_tables(core, rows, cols, padded)
    near_lines, first, tables = lax.optimization_barrier((near_lines, first, tables))
    halves = cut_halves(near_lines)
    last_lines = [
        send(halves[0], dy=-1),
        send(halves[1], dy=1),
        send(halves[2], dx=-1),
        send(halves[3], dx=1),
    ]
    totals = sum_part(second_kernel, "second_part", order, mine, other, first[:2], near_lines, False)

    perm = []
    for t in range(SEQ):
        tz, ty, tx, tc = coords(t)
        for th in range(2):
            perm.append((t * 2 + th, index_of(tz ^ tc, ty, tx, tc) * 2 + 1 - th))
    ow_same = lax.ppermute(ow_part, ("seq", "ch"), perm)

    last_lines, ow_same = lax.optimization_barrier((last_lines, ow_same))
    source, gate = last_part(totals, first[2:], last_lines)
    packed = source.reshape(CHIPS, chan // CHIPS, 2 * rows)
    mine_ch = lax.all_to_all(packed, "seq", 0, 0, axis_index_groups=SAME_CORE)

    tw, a, ai, cs, twist = tables
    k1_, k3_, v1_, v3_ = near_lines
    f, m = filter_part(
        order,
        [key_line, k1_, last_lines[0], last_lines[1], k3_],
        [value_line, v1_, last_lines[2], last_lines[3], v3_],
        cs,
        twist,
    )
    forward, inverse = row_tables(rows, padded)
    fwd = jnp.asarray(forward.astype(np.float32).astype(ml_dtypes.bfloat16))
    inv = jnp.asarray(inverse.astype(np.float32).astype(ml_dtypes.bfloat16))
    mine_ch, f, m = lax.optimization_barrier((mine_ch, f, m))
    conv = long_conv(mine_ch, fwd, inv, tw, a, ai, m, f)
    conv = lax.all_to_all(conv, "seq", 0, 0, axis_index_groups=SAME_CORE)
    conv = conv.reshape(chan, 2 * rows).astype(F32)

    gate = gate.astype(F32)
    skip = lax.dynamic_slice_in_dim(skip_bias, core * chan, chan, 0)[:, None]
    gated = (gate * (conv + skip * source.astype(F32))).astype(BF16)

    kept = rows // 2
    own_here = lax.dynamic_slice(gated, (0, h * kept), (chan, kept))
    own_there = lax.dynamic_slice(gated, (0, (1 - h) * kept), (chan, kept))
    oth_here = lax.dynamic_slice(gated, (0, rows + h * kept), (chan, kept))
    oth_there = lax.dynamic_slice(gated, (0, rows + (1 - h) * kept), (chan, kept))
    swap_ch = [(0, 1), (1, 0)]
    from_h = lax.ppermute(own_there, "ch", swap_ch)
    perm2 = []
    for t in range(SEQ):
        for th in range(2):
            perm2.append((t * 2 + th, (t ^ 1) * 2 + 1 - th))
    from_hc = lax.ppermute(oth_there, ("seq", "ch"), perm2)
    from_c = send(oth_here, dc=1)
    from_c, ow_same = lax.optimization_barrier((from_c, ow_same))
    ow_cross = send(ow_same, dc=1)
    here = ordered(own_here, from_c)

    mixed = mix_part(None, [here], [out_weight])
    mixed = mix_part(mixed, [from_h, from_hc], [ow_same, ow_cross])
    return mixed.reshape(kept, 1, width)


def solution(mesh):
    in_specs = (
        P(None, "seq", None),
        P("seq", None, "ch"),
        P(None, "seq", None, "ch"),
        P("ch"),
        P("ch", None),
    )
    return jax.shard_map(
        per_device, mesh=mesh, in_specs=in_specs, out_specs=P("ch", "seq", None), check_vma=False
    )
```

```python
import functools
import math

import jax
import jax.numpy as jnp
import ml_dtypes
import numpy as np
from jax import lax
from jax.experimental import pallas as pl
from jax.experimental.pallas import tpu as pltpu
from jax.sharding import PartitionSpec as P

BF16 = jnp.bfloat16
F32 = jnp.float32
HIGH = lax.Precision.HIGHEST
SEQ = 64
VMEM = 60 * 2**20
CHIPS = 32
SAME_CORE = [[2 * p + j for p in range(CHIPS)] for j in range(2)]


def coords(s):
    return s // 32, (s // 8) % 4, (s // 2) % 4, s % 2


def index_of(z, y, x, c):
    return ((z * 4 + y) * 4 + x) * 2 + c


def send(value, dz=0, dy=0, dx=0, dc=0):
    perm = []
    for s in range(SEQ):
        z, y, x, c = coords(s)
        perm.append((s, index_of((z + dz) % 2, (y + dy) % 4, (x + dx) % 4, c ^ dc)))
    return lax.ppermute(value, "seq", perm)


def split_table(table):
    upper = table.astype(BF16)
    lower = (table - upper.astype(F32)).astype(BF16)
    return upper, lower


def row_tables(rows, padded):
    points = 2 * rows
    a = np.arange(rows)
    k = np.arange(rows)
    phase = 2.0 * np.pi * ((a[:, None] * k[None, :]) % points) / points
    re, im = np.cos(phase), -np.sin(phase)
    im[:, 0] = np.where(a % 2 == 0, 1.0, -1.0)
    forward = np.concatenate([re, im], axis=1)
    scale = np.full((rows,), 2.0)
    scale[0] = 1.0
    inverse = np.concatenate([re * scale, im * scale], axis=1).T / padded
    return forward, inverse


def picked(order_ref, row, group, tok_ref):
    blocks = [
        tok_ref[:, pl.ds(pl.multiple_of(order_ref[row, group * 8 + i] * 128, 128), 128)]
        for i in range(8)
    ]
    return jnp.concatenate(blocks, axis=1)


def by_column(run, mine_ref, other_ref):
    step = pl.program_id(0)

    @pl.when(step < 2)
    def _():
        run(mine_ref)

    @pl.when(step >= 2)
    def _():
        run(other_ref)


def first_kernel(order_ref, mine_ref, other_ref, key_line, value_line, *outs):
    key_ref, value_ref, key_tok_ref, value_tok_ref = outs

    def run(tok_ref):
        for row, line, total_ref, last_ref in (
            (0, key_line, key_ref, key_tok_ref),
            (1, value_line, value_ref, value_tok_ref),
        ):
            total_ref[...] = jnp.dot(
                picked(order_ref, row, 0, tok_ref), line[...], preferred_element_type=F32
            )
            last_ref[...] = picked(order_ref, row, 2, tok_ref)

    by_column(run, mine_ref, other_ref)


def second_kernel(order_ref, mine_ref, other_ref, key_in, value_in, k1, k3, v1, v3, key_ref, value_ref):
    def run(tok_ref):
        for row, before, e1, e3, total_ref in (
            (0, key_in, k1, k3, key_ref),
            (1, value_in, v1, v3, value_ref),
        ):
            total = before[...]
            total += jnp.dot(picked(order_ref, row, 1, tok_ref), e1[...], preferred_element_type=F32)
            total += jnp.dot(picked(order_ref, row, 3, tok_ref), e3[...], preferred_element_type=F32)
            total_ref[...] = total

    by_column(run, mine_ref, other_ref)


def sum_part(kernel, name, order, mine, other, totals, weights, last):
    rows, width = mine.shape
    chan = weights[0].shape[1]
    tile = rows // 2
    quarter = width // 4
    by_row = [pl.BlockSpec((tile, chan), lambda i, o: (i, 0))] * 2
    tokens_out = [pl.BlockSpec((tile, quarter), lambda i, o: (i, 0))] * 2
    shapes = [jax.ShapeDtypeStruct((2 * rows, chan), F32)] * 2
    token_shapes = [jax.ShapeDtypeStruct((2 * rows, quarter), BF16)] * 2
    return pl.pallas_call(
        kernel,
        grid_spec=pltpu.PrefetchScalarGridSpec(
            num_scalar_prefetch=1,
            grid=(4,),
            in_specs=[
                pl.BlockSpec((tile, width), lambda i, o: (jnp.minimum(i, 1), 0)),
                pl.BlockSpec((tile, width), lambda i, o: (jnp.maximum(i - 2, 0), 0)),
            ]
            + by_row[: len(totals)]
            + [pl.BlockSpec((quarter, chan), lambda i, o: (0, 0))] * len(weights),
            out_specs=by_row + (tokens_out if last else []),
        ),
        out_shape=shapes + (token_shapes if last else []),
        compiler_params=pltpu.CompilerParams(vmem_limit_bytes=VMEM),
        cost_estimate=pl.CostEstimate(
            flops=2 * 2 * rows * quarter * chan * len(weights), bytes_accessed=18 * 2**20, transcendentals=0
        ),
        name=name,
    )(order, mine, other, *totals, *weights)


def cut_kernel(*refs):
    for src, dst in zip(refs[:4], refs[4:], strict=True):
        dst[...] = src[...]


def cut_halves(lines):
    rows, width = lines[0].shape
    tile = rows // 4
    upper = pl.BlockSpec((tile, width), lambda i: (i, 0))
    lower = pl.BlockSpec((tile, width), lambda i: (i + 2, 0))
    return pl.pallas_call(
        cut_kernel,
        grid=(2,),
        in_specs=[upper, lower, upper, lower],
        out_specs=[upper] * 4,
        out_shape=[jax.ShapeDtypeStruct((rows // 2, width), BF16)] * 4,
        compiler_params=pltpu.CompilerParams(vmem_limit_bytes=VMEM),
        cost_estimate=pl.CostEstimate(flops=0, bytes_accessed=4 * rows * width * 2, transcendentals=0),
        name="cut_halves",
    )(*lines)


def last_kernel(key_ref, value_ref, key_tok_ref, value_tok_ref, ka, kb, va, vb, send_ref):
    half = ka.shape[0]

    def finish(total_ref, tok_ref, wa, wb):
        total = total_ref[...]
        total += jnp.dot(tok_ref[:, :half], wa[...], preferred_element_type=F32)
        total += jnp.dot(tok_ref[:, half:], wb[...], preferred_element_type=F32)
        return total.astype(BF16).astype(F32)

    source = finish(key_ref, key_tok_ref, ka, kb) * finish(value_ref, value_tok_ref, va, vb)
    send_ref[...] = source.T.astype(BF16)


def last_part(totals, tokens, weights):
    total, chan = totals[0].shape
    quarter = tokens[0].shape[1]
    tile = total // 4
    return pl.pallas_call(
        last_kernel,
        grid=(4,),
        in_specs=[pl.BlockSpec((tile, chan), lambda i: (i, 0))] * 2
        + [pl.BlockSpec((tile, quarter), lambda i: (i, 0))] * 2
        + [pl.BlockSpec((quarter // 2, chan), lambda i: (0, 0))] * 4,
        out_specs=pl.BlockSpec((chan, tile), lambda i: (0, i)),
        out_shape=jax.ShapeDtypeStruct((chan, total), BF16),
        compiler_params=pltpu.CompilerParams(vmem_limit_bytes=VMEM),
        cost_estimate=pl.CostEstimate(
            flops=2 * 2 * total * quarter * chan, bytes_accessed=13 * 2**20, transcendentals=0
        ),
        name="last_part",
    )(*totals, *tokens, *weights)


def gate_kernel(mine_ref, other_ref, weight_ref, out_ref):
    chips, deep, chan = weight_ref.shape

    def run(tok_ref):
        weight = weight_ref[...].reshape(chips * deep, chan)
        gate = jnp.dot(tok_ref[...], weight, preferred_element_type=F32)
        out_ref[...] = gate.T.astype(BF16)

    by_column(run, mine_ref, other_ref)


def gate_part(mine, other, gathered):
    rows, width = mine.shape
    chips, _, chan = gathered.shape
    tile = rows // 2
    return pl.pallas_call(
        gate_kernel,
        grid=(4,),
        in_specs=[
            pl.BlockSpec((tile, width), lambda i: (jnp.minimum(i, 1), 0)),
            pl.BlockSpec((tile, width), lambda i: (jnp.maximum(i - 2, 0), 0)),
            pl.BlockSpec((chips, width // chips, chan), lambda i: (0, 0, 0)),
        ],
        out_specs=pl.BlockSpec((chan, tile), lambda i: (0, i)),
        out_shape=jax.ShapeDtypeStruct((chan, 2 * rows), BF16),
        compiler_params=pltpu.CompilerParams(vmem_limit_bytes=VMEM),
        cost_estimate=pl.CostEstimate(
            flops=2 * 2 * rows * width * chan, bytes_accessed=13 * 2**20, transcendentals=0
        ),
        name="gate_part",
    )(mine, other, gathered)


def turn(ref):
    return ref[...].astype(F32).T.astype(BF16)


def mix_kernel(here, w_here, out_ref, lhs_ref):
    @pl.when(pl.program_id(0) == 0)
    def _():
        lhs_ref[...] = turn(here)

    out_ref[...] = jnp.dot(lhs_ref[...], w_here[...], preferred_element_type=F32)


def mix_more_kernel(total_ref, near_h, far_h, w_near, w_far, out_ref, lhs_ref):
    m = near_h.shape[0]

    @pl.when(pl.program_id(0) == 0)
    def _():
        lhs_ref[:, :m] = turn(near_h)
        lhs_ref[:, m:] = turn(far_h)

    total = total_ref[...]
    total += jnp.dot(lhs_ref[:, :m], w_near[...], preferred_element_type=F32)
    total += jnp.dot(lhs_ref[:, m:], w_far[...], preferred_element_type=F32)
    out_ref[...] = total.astype(BF16)


def mix_part(total, parts, weights):
    rows = parts[0].shape[1]
    width = weights[0].shape[1]
    tile = width // 4
    depth = sum(p.shape[0] for p in parts)
    totals = [] if total is None else [total]

    def whole(g):
        return pl.BlockSpec(g.shape, lambda i: (0, 0))

    def tiled(w):
        return pl.BlockSpec((w.shape[0], tile), lambda i: (0, i))

    return pl.pallas_call(
        mix_kernel if total is None else mix_more_kernel,
        grid=(4,),
        in_specs=[tiled(t) for t in totals] + [whole(p) for p in parts] + [tiled(w) for w in weights],
        out_specs=pl.BlockSpec((rows, tile), lambda i: (0, i)),
        out_shape=jax.ShapeDtypeStruct((rows, width), F32 if total is None else BF16),
        scratch_shapes=[pltpu.VMEM((rows, depth), BF16)],
        compiler_params=pltpu.CompilerParams(vmem_limit_bytes=VMEM),
        cost_estimate=pl.CostEstimate(
            flops=2 * rows * depth * width, bytes_accessed=12 * 2**20, transcendentals=0
        ),
        name="mix_part" if total is None else "mix_more",
    )(*totals, *parts, *weights)


def filter_kernel(z_ref, x_ref, cs_ref, twist_ref, f_ref, m_ref):
    chips, _, lanes = x_ref.shape
    lanes = lanes // 2
    points = 2 * chips * 16
    rows, cols = points // 2, lanes // 2

    def part(n):
        rows_of = slice(16 * n, 16 * (n + 1))
        cores = [x_ref[:, rows_of, c * lanes : (c + 1) * lanes] for c in range(2)]
        return jnp.stack(cores, axis=1).reshape(points, lanes)

    upper, lower = part(0), part(1)
    whole = (upper.astype(F32) + lower.astype(F32)).T
    i = lax.broadcasted_iota(jnp.int32, (rows, rows), 0)
    j = lax.broadcasted_iota(jnp.int32, (rows, rows), 1)
    mirror = (i + j == rows).astype(F32).astype(BF16)
    i = lax.broadcasted_iota(jnp.int32, (lanes, lanes), 0)
    j = lax.broadcasted_iota(jnp.int32, (lanes, lanes), 1)
    flip = ((i // cols == j // cols) & (i % cols + j % cols == cols - 1)).astype(F32).astype(BF16)

    def mirrored(part):
        turned = jnp.dot(flip, part[:, rows:], preferred_element_type=F32).astype(BF16)
        return jnp.dot(turned, mirror, preferred_element_type=F32)

    other = mirrored(upper.astype(F32).T.astype(BF16)) + mirrored(lower.astype(F32).T.astype(BF16))
    f_ref[:, :rows] = 0.5 * (whole[:cols, :rows] + other[:cols])
    f_ref[:, rows:] = 0.5 * (whole[cols:, :rows] - other[cols:])
    c, s = cs_ref[0], cs_ref[1]

    def contract(left, right):
        return lax.dot_general(
            left, right, (((0,), (0,)), ((), ())), precision=HIGH, preferred_element_type=F32
        )

    m_ref[...] = jnp.zeros_like(m_ref)
    for n, k in enumerate((0, rows)):
        e_re, e_im = whole[:cols, k : k + 1], whole[cols:, k : k + 1]
        u = c * e_re - s * e_im
        v = s * e_re + c * e_im
        g = contract(u, c) + contract(v, s)
        if n:
            g = g * twist_ref[0] - (contract(v, c) - contract(u, s)) * twist_ref[1]
        for start in (n * cols, lanes + n * cols):
            spot = slice(start, start + cols)
            m_ref[spot, spot] = g.astype(BF16)


def filter_part(z, gathered, cs, twist):
    chips = gathered.shape[0]
    cols = cs.shape[1]
    rows = chips * 16
    lanes = 2 * cols
    return pl.pallas_call(
        filter_kernel,
        grid_spec=pltpu.PrefetchScalarGridSpec(
            num_scalar_prefetch=1,
            grid=(1,),
            in_specs=[
                pl.BlockSpec((chips, 32, 2 * lanes), lambda i, z: (0, 4, z[0])),
                pl.BlockSpec(cs.shape, lambda i, z: (0, 0, 0)),
                pl.BlockSpec(twist.shape, lambda i, z: (0, 0, 0)),
            ],
            out_specs=[
                pl.BlockSpec((cols, 2 * rows), lambda i, z: (0, 0)),
                pl.BlockSpec((2 * lanes, 2 * lanes), lambda i, z: (0, 0)),
            ],
        ),
        out_shape=[
            jax.ShapeDtypeStruct((cols, 2 * rows), F32),
            jax.ShapeDtypeStruct((2 * lanes, 2 * lanes), BF16),
        ],
        compiler_params=pltpu.CompilerParams(vmem_limit_bytes=VMEM),
        cost_estimate=pl.CostEstimate(flops=10**9, bytes_accessed=2**20, transcendentals=0),
        name="filter_part",
    )(z.reshape(1), gathered, cs, twist)


def conv_kernel(
    x_ref, fwd_hbm, inv_hbm, tw_hbm, a_ref, ai_ref, m_ref, f_ref, y_ref, fwd_ref, inv_ref, tw_ref, r_ref, q_ref, sems
):
    copies = [
        pltpu.make_async_copy(src, dst, sems.at[i])
        for i, (src, dst) in enumerate(((fwd_hbm, fwd_ref), (tw_hbm, tw_ref), (inv_hbm, inv_ref)))
    ]
    for copy in copies:
        copy.start()
    chips, chans, both = x_ref.shape
    rows = both // 2
    blocks = rows // 128
    half = 2 * chips
    copies[0].wait()
    for col in range(2):
        x = x_ref[:, :, col * rows : (col + 1) * rows].reshape(chips * chans, rows)
        r = jnp.dot(x, fwd_ref[...], preferred_element_type=F32)
        r = r.reshape(chips, chans, 2 * rows)
        if col == 0:
            copies[1].wait()
        tw = tw_ref[col * chips : (col + 1) * chips, :]
        cos = tw[:, None, :rows]
        sin = tw[:, None, rows:]
        re, im = r[:, :, :rows], r[:, :, rows:]
        turned_re = (re * cos + im * sin).reshape(chips * chans, rows)
        turned_im = (im * cos - re * sin).reshape(chips * chans, rows)
        for k in range(blocks):
            r_ref[col, k] = turned_re[:, k * 128 : (k + 1) * 128]
            r_ref[col, blocks + k] = turned_im[:, k * 128 : (k + 1) * 128]
    lane = lax.broadcasted_iota(jnp.int32, (4 * half, 128), 1)

    def pair(n, carry):
        picks = [pl.ds(2 * n + i, chips, stride=chans) for i in range(2)]
        parts = [
            jnp.concatenate([r_ref[col, part * blocks + k, pick, :] for k in range(blocks)], axis=1)
            for pick in picks
            for part in range(2)
            for col in range(2)
        ]
        turned = jnp.concatenate(parts, axis=0).astype(BF16)
        s = jnp.dot(a_ref[...], turned, preferred_element_type=F32)
        f_re, f_im = f_ref[:, :rows], f_ref[:, rows:]
        filtered = []
        for i in range(2):
            s_re = s[2 * i * half : (2 * i + 1) * half]
            s_im = s[(2 * i + 1) * half : (2 * i + 2) * half]
            filtered += [s_re * f_re - s_im * f_im, s_re * f_im + s_im * f_re]
        filtered = jnp.concatenate(filtered, axis=0).astype(BF16)
        back = jnp.dot(ai_ref[...], filtered, preferred_element_type=F32)
        edge = jnp.dot(m_ref[...], turned[:, :128], preferred_element_type=F32)
        head = jnp.where(lane == 0, edge, back[:, :128])
        back = jnp.concatenate([head, back[:, 128:]], axis=1)
        cos, sin = tw_ref[:, :rows], tw_ref[:, rows:]
        for i, pick in enumerate(picks):
            b_re = back[2 * i * half : (2 * i + 1) * half]
            b_im = back[(2 * i + 1) * half : (2 * i + 2) * half]
            out_re = b_re * cos - b_im * sin
            out_im = b_im * cos + b_re * sin
            for col in range(2):
                part = slice(col * chips, (col + 1) * chips)
                for k in range(blocks):
                    q_ref[col, k, pick, :] = out_re[part, k * 128 : (k + 1) * 128]
                    q_ref[col, blocks + k, pick, :] = out_im[part, k * 128 : (k + 1) * 128]
        return carry

    lax.fori_loop(0, chans // 2, pair, 0, unroll=4)
    copies[2].wait()
    for col in range(2):
        q = jnp.concatenate([q_ref[col, k].astype(BF16) for k in range(2 * blocks)], axis=1)
        y = jnp.dot(q, inv_ref[...], preferred_element_type=F32)
        y_ref[:, :, col * rows : (col + 1) * rows] = y.astype(BF16).reshape(chips, chans, rows)


def long_conv(x, fwd, inv, tw, a, ai, m, f):
    chips, chans, both = x.shape
    vmem = pl.BlockSpec(memory_space=pltpu.VMEM)
    hbm = pl.BlockSpec(memory_space=pl.ANY)
    return pl.pallas_call(
        conv_kernel,
        in_specs=[vmem, hbm, hbm, hbm, vmem, vmem, vmem, vmem],
        out_specs=vmem,
        out_shape=jax.ShapeDtypeStruct(x.shape, BF16),
        scratch_shapes=[
            pltpu.VMEM(fwd.shape, BF16),
            pltpu.VMEM(inv.shape, BF16),
            pltpu.VMEM(tw.shape, F32),
            pltpu.VMEM((2, both // 128, chips * chans, 128), F32),
            pltpu.VMEM((2, both // 128, chips * chans, 128), F32),
            pltpu.SemaphoreType.DMA((3,)),
        ],
        compiler_params=pltpu.CompilerParams(vmem_limit_bytes=VMEM),
        cost_estimate=pl.CostEstimate(flops=8 * 10**9, bytes_accessed=8 * 2**20, transcendentals=0),
        name="long_conv",
    )(x, fwd, inv, tw, a, ai, m, f)


def cos_sin(product, modulus):
    phase = (product % modulus).astype(F32) * (2.0 * math.pi / modulus)
    return jnp.cos(phase), jnp.sin(phase)


def twice(t):
    zero = jnp.zeros_like(t)
    return jnp.block([[t, zero], [zero, t]])


def column_tables(core, rows, cols, padded):
    i = lax.iota(jnp.int32, cols)
    b = 2 * (i % CHIPS) + ((i // CHIPS) ^ core)
    k1 = lax.iota(jnp.int32, rows)
    tw = jnp.concatenate(cos_sin(b[:, None] * k1[None, :], padded), axis=1)
    k2 = lax.iota(jnp.int32, cols)
    c, s = cos_sin(k2[:, None] * b[None, :], cols)
    a = jnp.block([[c, s], [-s, c]])
    twist = jnp.stack(cos_sin(jnp.mod((b[:, None] - b[None, :]) * rows, padded), padded))

    return tw, twice(a.astype(BF16)), twice(a.T.astype(BF16)), jnp.stack([c, s]), twist


def gather_line(block, axis):
    d1 = send(block, **{axis: -1})
    d3 = send(block, **{axis: 1})
    d2 = send(block, **{axis: 2})
    return jnp.concatenate([block, d1, d2, d3], axis=0)


def per_device(tokens, in_weight, filter_spectrum, skip_bias, out_weight):
    rows, _, width = tokens.shape
    cols = SEQ
    padded = 2 * rows * cols
    s = lax.axis_index("seq")
    h = lax.axis_index("ch")
    z, y, x, core = coords(s)
    chan = in_weight.shape[2] // 2
    depth = in_weight.shape[0]

    mine = tokens.reshape(rows, width)
    filt = jnp.transpose(filter_spectrum, (3, 1, 0, 2)).reshape(4, -1, 2 * cols)
    filt = jnp.concatenate(split_table(filt), axis=1)

    def half_for(c):
        w = lax.dynamic_slice_in_dim(in_weight, c * chan, chan, 2)
        f = lax.dynamic_slice_in_dim(filt, 2 * c, 2, 0)
        return jnp.transpose(w, (1, 0, 2)).reshape(3 * depth, chan), jnp.concatenate([f[0], f[1]], axis=1)

    keep, keep_f = half_for(core)
    give, give_f = half_for(1 - core)
    far_near = send(give[depth:], dz=1, dc=1)
    far = send(keep[depth:], dz=1)
    near = send(give, dc=1)
    near_f = send(give_f, dc=1)
    other = send(mine, dc=1)

    def ordered(own, partner, axis=0):
        return jnp.concatenate(
            [jnp.where(core == 0, own, partner), jnp.where(core == 0, partner, own)], axis=axis
        )

    def block_of(n):
        own, away = slice(n * depth, (n + 1) * depth), slice((n - 1) * depth, n * depth)
        return jnp.concatenate([ordered(keep[own], near[own]), ordered(far[away], far_near[away])], axis=0)

    key_block, value_block = block_of(1), block_of(2)
    f_lanes = 2 * cols
    gate_block = jnp.concatenate(
        [
            ordered(keep[:depth], near[:depth]),
            jnp.concatenate(
                [
                    ordered(keep_f[:, :f_lanes], near_f[:, :f_lanes], 1),
                    ordered(keep_f[:, f_lanes:], near_f[:, f_lanes:], 1),
                ],
                axis=1,
            ),
        ],
        axis=0,
    )
    gathered = lax.all_gather(gate_block, "seq", axis=0, axis_index_groups=SAME_CORE)
    key_block, value_block, other = lax.optimization_barrier((key_block, value_block, other))
    half_ow = out_weight.shape[0] // 2
    ow_part = lax.dynamic_slice_in_dim(out_weight, core * half_ow, half_ow, 0)
    key_line, value_line, ow_part = lax.optimization_barrier(
        (gather_line(key_block, "dx"), gather_line(value_block, "dy"), ow_part)
    )

    order = np.arange(32)
    p_, q_, dz = order // 8, (order // 2) % 4, order % 2
    key_order = ((z ^ dz) * 4 + (y + p_) % 4) * 4 + (x + q_) % 4
    value_order = ((z ^ dz) * 4 + (y + q_) % 4) * 4 + (x + p_) % 4
    order = jnp.stack([key_order, value_order])
    first = sum_part(first_kernel, "first_part", order, mine, other, [], [key_line, value_line], True)
    near_lines = [send(key_line, dy=-1), send(key_line, dy=1), send(value_line, dx=-1), send(value_line, dx=1)]
    tables = column_tables(core, rows, cols, padded)
    near_lines, first, tables = lax.optimization_barrier((near_lines, first, tables))
    halves = cut_halves(near_lines)
    last_lines = [
        send(halves[0], dy=-1),
        send(halves[1], dy=1),
        send(halves[2], dx=-1),
        send(halves[3], dx=1),
    ]
    totals = sum_part(second_kernel, "second_part", order, mine, other, first[:2], near_lines, False)

    perm = []
    for t in range(SEQ):
        tz, ty, tx, tc = coords(t)
        for th in range(2):
            perm.append((t * 2 + th, index_of(tz ^ tc, ty, tx, tc) * 2 + 1 - th))
    ow_same = lax.ppermute(ow_part, ("seq", "ch"), perm)

    source = last_part(totals, first[2:], last_lines)
    packed = source.reshape(CHIPS, chan // CHIPS, 2 * rows)
    mine_ch = lax.all_to_all(packed, "seq", 0, 0, axis_index_groups=SAME_CORE)

    tw, a, ai, cs, twist = tables
    f, m = filter_part(z, gathered, cs, twist)
    forward, inverse = row_tables(rows, padded)
    fwd = jnp.asarray(forward.astype(np.float32).astype(ml_dtypes.bfloat16))
    inv = jnp.asarray(inverse.astype(np.float32).astype(ml_dtypes.bfloat16))
    mine_ch, ow_same, f, m = lax.optimization_barrier((mine_ch, ow_same, f, m))
    conv = long_conv(mine_ch, fwd, inv, tw, a, ai, m, f)
    conv = lax.all_to_all(conv, "seq", 0, 0, axis_index_groups=SAME_CORE)
    conv = conv.reshape(chan, 2 * rows).astype(F32)

    gate = gate_part(mine, other, gathered).astype(F32)
    skip = lax.dynamic_slice_in_dim(skip_bias, core * chan, chan, 0)[:, None]
    gated = (gate * (conv + skip * source.astype(F32))).astype(BF16)

    kept = rows // 2
    own_here = lax.dynamic_slice(gated, (0, h * kept), (chan, kept))
    own_there = lax.dynamic_slice(gated, (0, (1 - h) * kept), (chan, kept))
    oth_here = lax.dynamic_slice(gated, (0, rows + h * kept), (chan, kept))
    oth_there = lax.dynamic_slice(gated, (0, rows + (1 - h) * kept), (chan, kept))
    swap_ch = [(0, 1), (1, 0)]
    from_h = lax.ppermute(own_there, "ch", swap_ch)
    perm2 = []
    for t in range(SEQ):
        for th in range(2):
            perm2.append((t * 2 + th, (t ^ 1) * 2 + 1 - th))
    from_hc = lax.ppermute(oth_there, ("seq", "ch"), perm2)
    from_c = send(oth_here, dc=1)
    from_c, ow_same = lax.optimization_barrier((from_c, ow_same))
    ow_cross = send(ow_same, dc=1)
    here = ordered(own_here, from_c)

    mixed = mix_part(None, [here], [out_weight])
    mixed = mix_part(mixed, [from_h, from_hc], [ow_same, ow_cross])
    return mixed.reshape(kept, 1, width)


def solution(mesh):
    in_specs = (
        P(None, "seq", None),
        P("seq", None, "ch"),
        P(None, "seq", None, "ch"),
        P("ch"),
        P("ch", None),
    )
    return jax.shard_map(
        per_device, mesh=mesh, in_specs=in_specs, out_specs=P("ch", "seq", None), check_vma=False
    )
```

```python
import functools
import math

import jax
import jax.numpy as jnp
import ml_dtypes
import numpy as np
from jax import lax
from jax.experimental import pallas as pl
from jax.experimental.pallas import tpu as pltpu
from jax.sharding import PartitionSpec as P

BF16 = jnp.bfloat16
F32 = jnp.float32
HIGH = lax.Precision.HIGHEST
SEQ = 64
VMEM = 60 * 2**20
CHIPS = 32
SAME_CORE = [[2 * p + j for p in range(CHIPS)] for j in range(2)]


def coords(s):
    return s // 32, (s // 8) % 4, (s // 2) % 4, s % 2


def index_of(z, y, x, c):
    return ((z * 4 + y) * 4 + x) * 2 + c


def send(value, dz=0, dy=0, dx=0, dc=0):
    perm = []
    for s in range(SEQ):
        z, y, x, c = coords(s)
        perm.append((s, index_of((z + dz) % 2, (y + dy) % 4, (x + dx) % 4, c ^ dc)))
    return lax.ppermute(value, "seq", perm)


def split_table(table):
    upper = table.astype(BF16)
    lower = (table - upper.astype(F32)).astype(BF16)
    return upper, lower


def row_tables(rows, padded):
    points = 2 * rows
    a = np.arange(rows)
    k = np.arange(rows)
    phase = 2.0 * np.pi * ((a[:, None] * k[None, :]) % points) / points
    re, im = np.cos(phase), -np.sin(phase)
    im[:, 0] = np.where(a % 2 == 0, 1.0, -1.0)
    forward = np.concatenate([re, im], axis=1)
    scale = np.full((rows,), 2.0)
    scale[0] = 1.0
    inverse = np.concatenate([re * scale, im * scale], axis=1).T / padded
    return forward, inverse


def picked(order_ref, row, group, tok_ref):
    blocks = [
        tok_ref[:, pl.ds(pl.multiple_of(order_ref[row, group * 8 + i] * 128, 128), 128)]
        for i in range(8)
    ]
    return jnp.concatenate(blocks, axis=1)


def by_column(run, mine_ref, other_ref):
    step = pl.program_id(0)

    @pl.when(step < 2)
    def _():
        run(mine_ref)

    @pl.when(step >= 2)
    def _():
        run(other_ref)


def first_kernel(order_ref, mine_ref, other_ref, key_line, value_line, *outs):
    key_ref, value_ref, key_tok_ref, value_tok_ref = outs

    def run(tok_ref):
        for row, line, total_ref, last_ref in (
            (0, key_line, key_ref, key_tok_ref),
            (1, value_line, value_ref, value_tok_ref),
        ):
            total_ref[...] = jnp.dot(
                picked(order_ref, row, 0, tok_ref), line[...], preferred_element_type=F32
            )
            last_ref[...] = picked(order_ref, row, 2, tok_ref)

    by_column(run, mine_ref, other_ref)


def second_kernel(order_ref, mine_ref, other_ref, key_in, value_in, k1, k3, v1, v3, key_ref, value_ref):
    def run(tok_ref):
        for row, before, e1, e3, total_ref in (
            (0, key_in, k1, k3, key_ref),
            (1, value_in, v1, v3, value_ref),
        ):
            total = before[...]
            total += jnp.dot(picked(order_ref, row, 1, tok_ref), e1[...], preferred_element_type=F32)
            total += jnp.dot(picked(order_ref, row, 3, tok_ref), e3[...], preferred_element_type=F32)
            total_ref[...] = total

    by_column(run, mine_ref, other_ref)


def sum_part(kernel, name, order, mine, other, totals, weights, last):
    rows, width = mine.shape
    chan = weights[0].shape[1]
    tile = rows // 2
    quarter = width // 4
    by_row = [pl.BlockSpec((tile, chan), lambda i, o: (i, 0))] * 2
    tokens_out = [pl.BlockSpec((tile, quarter), lambda i, o: (i, 0))] * 2
    shapes = [jax.ShapeDtypeStruct((2 * rows, chan), F32)] * 2
    token_shapes = [jax.ShapeDtypeStruct((2 * rows, quarter), BF16)] * 2
    return pl.pallas_call(
        kernel,
        grid_spec=pltpu.PrefetchScalarGridSpec(
            num_scalar_prefetch=1,
            grid=(4,),
            in_specs=[
                pl.BlockSpec((tile, width), lambda i, o: (jnp.minimum(i, 1), 0)),
                pl.BlockSpec((tile, width), lambda i, o: (jnp.maximum(i - 2, 0), 0)),
            ]
            + by_row[: len(totals)]
            + [pl.BlockSpec((quarter, chan), lambda i, o: (0, 0))] * len(weights),
            out_specs=by_row + (tokens_out if last else []),
        ),
        out_shape=shapes + (token_shapes if last else []),
        compiler_params=pltpu.CompilerParams(vmem_limit_bytes=VMEM),
        cost_estimate=pl.CostEstimate(
            flops=2 * 2 * rows * quarter * chan * len(weights), bytes_accessed=18 * 2**20, transcendentals=0
        ),
        name=name,
    )(order, mine, other, *totals, *weights)


def cut_kernel(*refs):
    for src, dst in zip(refs[:4], refs[4:], strict=True):
        dst[...] = src[...]


def cut_halves(lines):
    rows, width = lines[0].shape
    tile = rows // 4
    upper = pl.BlockSpec((tile, width), lambda i: (i, 0))
    lower = pl.BlockSpec((tile, width), lambda i: (i + 2, 0))
    return pl.pallas_call(
        cut_kernel,
        grid=(2,),
        in_specs=[upper, lower, upper, lower],
        out_specs=[upper] * 4,
        out_shape=[jax.ShapeDtypeStruct((rows // 2, width), BF16)] * 4,
        compiler_params=pltpu.CompilerParams(vmem_limit_bytes=VMEM),
        cost_estimate=pl.CostEstimate(flops=0, bytes_accessed=4 * rows * width * 2, transcendentals=0),
        name="cut_halves",
    )(*lines)


def last_kernel(key_ref, value_ref, key_tok_ref, value_tok_ref, ka, kb, va, vb, send_ref):
    half = ka.shape[0]

    def finish(total_ref, tok_ref, wa, wb):
        total = total_ref[...]
        total += jnp.dot(tok_ref[:, :half], wa[...], preferred_element_type=F32)
        total += jnp.dot(tok_ref[:, half:], wb[...], preferred_element_type=F32)
        return total.astype(BF16).astype(F32)

    source = finish(key_ref, key_tok_ref, ka, kb) * finish(value_ref, value_tok_ref, va, vb)
    send_ref[...] = source.T.astype(BF16)


def last_part(totals, tokens, weights):
    total, chan = totals[0].shape
    quarter = tokens[0].shape[1]
    tile = total // 8
    return pl.pallas_call(
        last_kernel,
        grid=(8,),
        in_specs=[pl.BlockSpec((tile, chan), lambda i: (i, 0))] * 2
        + [pl.BlockSpec((tile, quarter), lambda i: (i, 0))] * 2
        + [pl.BlockSpec((quarter // 2, chan), lambda i: (0, 0))] * 4,
        out_specs=pl.BlockSpec((chan, tile), lambda i: (0, i)),
        out_shape=jax.ShapeDtypeStruct((chan, total), BF16),
        compiler_params=pltpu.CompilerParams(vmem_limit_bytes=VMEM),
        cost_estimate=pl.CostEstimate(
            flops=2 * 2 * total * quarter * chan, bytes_accessed=13 * 2**20, transcendentals=0
        ),
        name="last_part",
    )(*totals, *tokens, *weights)


def gate_kernel(mine_ref, other_ref, weight_ref, out_ref):
    chips, deep, chan = weight_ref.shape

    def run(tok_ref):
        weight = weight_ref[...].reshape(chips * deep, chan)
        gate = jnp.dot(tok_ref[...], weight, preferred_element_type=F32)
        out_ref[...] = gate.T.astype(BF16)

    by_column(run, mine_ref, other_ref)


def gate_part(mine, other, gathered):
    rows, width = mine.shape
    chips, _, chan = gathered.shape
    tile = rows // 2
    return pl.pallas_call(
        gate_kernel,
        grid=(4,),
        in_specs=[
            pl.BlockSpec((tile, width), lambda i: (jnp.minimum(i, 1), 0)),
            pl.BlockSpec((tile, width), lambda i: (jnp.maximum(i - 2, 0), 0)),
            pl.BlockSpec((chips, width // chips, chan), lambda i: (0, 0, 0)),
        ],
        out_specs=pl.BlockSpec((chan, tile), lambda i: (0, i)),
        out_shape=jax.ShapeDtypeStruct((chan, 2 * rows), BF16),
        compiler_params=pltpu.CompilerParams(vmem_limit_bytes=VMEM),
        cost_estimate=pl.CostEstimate(
            flops=2 * 2 * rows * width * chan, bytes_accessed=13 * 2**20, transcendentals=0
        ),
        name="gate_part",
    )(mine, other, gathered)


def turn(ref):
    return ref[...].astype(F32).T.astype(BF16)


def mix_kernel(here, w_here, out_ref, lhs_ref):
    @pl.when(pl.program_id(0) == 0)
    def _():
        lhs_ref[...] = turn(here)

    out_ref[...] = jnp.dot(lhs_ref[...], w_here[...], preferred_element_type=F32)


def mix_more_kernel(total_ref, near_h, far_h, w_near, w_far, out_ref, lhs_ref):
    m = near_h.shape[0]

    @pl.when(pl.program_id(0) == 0)
    def _():
        lhs_ref[:, :m] = turn(near_h)
        lhs_ref[:, m:] = turn(far_h)

    total = total_ref[...]
    total += jnp.dot(lhs_ref[:, :m], w_near[...], preferred_element_type=F32)
    total += jnp.dot(lhs_ref[:, m:], w_far[...], preferred_element_type=F32)
    out_ref[...] = total.astype(BF16)


def mix_part(total, parts, weights):
    rows = parts[0].shape[1]
    width = weights[0].shape[1]
    tile = width // 8
    depth = sum(p.shape[0] for p in parts)
    totals = [] if total is None else [total]

    def whole(g):
        return pl.BlockSpec(g.shape, lambda i: (0, 0))

    def tiled(w):
        return pl.BlockSpec((w.shape[0], tile), lambda i: (0, i))

    return pl.pallas_call(
        mix_kernel if total is None else mix_more_kernel,
        grid=(8,),
        in_specs=[tiled(t) for t in totals] + [whole(p) for p in parts] + [tiled(w) for w in weights],
        out_specs=pl.BlockSpec((rows, tile), lambda i: (0, i)),
        out_shape=jax.ShapeDtypeStruct((rows, width), F32 if total is None else BF16),
        scratch_shapes=[pltpu.VMEM((rows, depth), BF16)],
        compiler_params=pltpu.CompilerParams(vmem_limit_bytes=VMEM),
        cost_estimate=pl.CostEstimate(
            flops=2 * rows * depth * width, bytes_accessed=12 * 2**20, transcendentals=0
        ),
        name="mix_part" if total is None else "mix_more",
    )(*totals, *parts, *weights)


def filter_kernel(z_ref, x_ref, cs_ref, twist_ref, f_ref, m_ref):
    chips, _, lanes = x_ref.shape
    lanes = lanes // 2
    points = 2 * chips * 16
    rows, cols = points // 2, lanes // 2

    def part(n):
        rows_of = slice(16 * n, 16 * (n + 1))
        cores = [x_ref[:, rows_of, c * lanes : (c + 1) * lanes] for c in range(2)]
        return jnp.stack(cores, axis=1).reshape(points, lanes)

    upper, lower = part(0), part(1)
    whole = (upper.astype(F32) + lower.astype(F32)).T
    i = lax.broadcasted_iota(jnp.int32, (rows, rows), 0)
    j = lax.broadcasted_iota(jnp.int32, (rows, rows), 1)
    mirror = (i + j == rows).astype(F32).astype(BF16)
    i = lax.broadcasted_iota(jnp.int32, (lanes, lanes), 0)
    j = lax.broadcasted_iota(jnp.int32, (lanes, lanes), 1)
    flip = ((i // cols == j // cols) & (i % cols + j % cols == cols - 1)).astype(F32).astype(BF16)

    def mirrored(part):
        turned = jnp.dot(flip, part[:, rows:], preferred_element_type=F32).astype(BF16)
        return jnp.dot(turned, mirror, preferred_element_type=F32)

    other = mirrored(upper.astype(F32).T.astype(BF16)) + mirrored(lower.astype(F32).T.astype(BF16))
    f_ref[:, :rows] = 0.5 * (whole[:cols, :rows] + other[:cols])
    f_ref[:, rows:] = 0.5 * (whole[cols:, :rows] - other[cols:])
    c, s = cs_ref[0], cs_ref[1]

    def contract(left, right):
        return lax.dot_general(
            left, right, (((0,), (0,)), ((), ())), precision=HIGH, preferred_element_type=F32
        )

    m_ref[...] = jnp.zeros_like(m_ref)
    for n, k in enumerate((0, rows)):
        e_re, e_im = whole[:cols, k : k + 1], whole[cols:, k : k + 1]
        u = c * e_re - s * e_im
        v = s * e_re + c * e_im
        g = contract(u, c) + contract(v, s)
        if n:
            g = g * twist_ref[0] - (contract(v, c) - contract(u, s)) * twist_ref[1]
        for start in (n * cols, lanes + n * cols):
            spot = slice(start, start + cols)
            m_ref[spot, spot] = g.astype(BF16)


def filter_part(z, gathered, cs, twist):
    chips = gathered.shape[0]
    cols = cs.shape[1]
    rows = chips * 16
    lanes = 2 * cols
    return pl.pallas_call(
        filter_kernel,
        grid_spec=pltpu.PrefetchScalarGridSpec(
            num_scalar_prefetch=1,
            grid=(1,),
            in_specs=[
                pl.BlockSpec((chips, 32, 2 * lanes), lambda i, z: (0, 4, z[0])),
                pl.BlockSpec(cs.shape, lambda i, z: (0, 0, 0)),
                pl.BlockSpec(twist.shape, lambda i, z: (0, 0, 0)),
            ],
            out_specs=[
                pl.BlockSpec((cols, 2 * rows), lambda i, z: (0, 0)),
                pl.BlockSpec((2 * lanes, 2 * lanes), lambda i, z: (0, 0)),
            ],
        ),
        out_shape=[
            jax.ShapeDtypeStruct((cols, 2 * rows), F32),
            jax.ShapeDtypeStruct((2 * lanes, 2 * lanes), BF16),
        ],
        compiler_params=pltpu.CompilerParams(vmem_limit_bytes=VMEM),
        cost_estimate=pl.CostEstimate(flops=10**9, bytes_accessed=2**20, transcendentals=0),
        name="filter_part",
    )(z.reshape(1), gathered, cs, twist)


def conv_kernel(
    x_ref, fwd_hbm, inv_hbm, tw_hbm, a_ref, ai_ref, m_ref, f_ref, y_ref, fwd_ref, inv_ref, tw_ref, r_ref, q_ref, sems
):
    copies = [
        pltpu.make_async_copy(src, dst, sems.at[i])
        for i, (src, dst) in enumerate(((fwd_hbm, fwd_ref), (tw_hbm, tw_ref), (inv_hbm, inv_ref)))
    ]
    for copy in copies:
        copy.start()
    chips, chans, both = x_ref.shape
    rows = both // 2
    blocks = rows // 128
    half = 2 * chips
    copies[0].wait()
    for col in range(2):
        x = x_ref[:, :, col * rows : (col + 1) * rows].reshape(chips * chans, rows)
        r = jnp.dot(x, fwd_ref[...], preferred_element_type=F32)
        r = r.reshape(chips, chans, 2 * rows)
        if col == 0:
            copies[1].wait()
        tw = tw_ref[col * chips : (col + 1) * chips, :]
        cos = tw[:, None, :rows]
        sin = tw[:, None, rows:]
        re, im = r[:, :, :rows], r[:, :, rows:]
        turned_re = (re * cos + im * sin).reshape(chips * chans, rows)
        turned_im = (im * cos - re * sin).reshape(chips * chans, rows)
        for k in range(blocks):
            r_ref[col, k] = turned_re[:, k * 128 : (k + 1) * 128]
            r_ref[col, blocks + k] = turned_im[:, k * 128 : (k + 1) * 128]
    lane = lax.broadcasted_iota(jnp.int32, (4 * half, 128), 1)

    def pair(n, carry):
        picks = [pl.ds(2 * n + i, chips, stride=chans) for i in range(2)]
        parts = [
            jnp.concatenate([r_ref[col, part * blocks + k, pick, :] for k in range(blocks)], axis=1)
            for pick in picks
            for part in range(2)
            for col in range(2)
        ]
        turned = jnp.concatenate(parts, axis=0).astype(BF16)
        s = jnp.dot(a_ref[...], turned, preferred_element_type=F32)
        f_re, f_im = f_ref[:, :rows], f_ref[:, rows:]
        filtered = []
        for i in range(2):
            s_re = s[2 * i * half : (2 * i + 1) * half]
            s_im = s[(2 * i + 1) * half : (2 * i + 2) * half]
            filtered += [s_re * f_re - s_im * f_im, s_re * f_im + s_im * f_re]
        filtered = jnp.concatenate(filtered, axis=0).astype(BF16)
        back = jnp.dot(ai_ref[...], filtered, preferred_element_type=F32)
        edge = jnp.dot(m_ref[...], turned[:, :128], preferred_element_type=F32)
        head = jnp.where(lane == 0, edge, back[:, :128])
        back = jnp.concatenate([head, back[:, 128:]], axis=1)
        cos, sin = tw_ref[:, :rows], tw_ref[:, rows:]
        for i, pick in enumerate(picks):
            b_re = back[2 * i * half : (2 * i + 1) * half]
            b_im = back[(2 * i + 1) * half : (2 * i + 2) * half]
            out_re = b_re * cos - b_im * sin
            out_im = b_im * cos + b_re * sin
            for col in range(2):
                part = slice(col * chips, (col + 1) * chips)
                for k in range(blocks):
                    q_ref[col, k, pick, :] = out_re[part, k * 128 : (k + 1) * 128]
                    q_ref[col, blocks + k, pick, :] = out_im[part, k * 128 : (k + 1) * 128]
        return carry

    lax.fori_loop(0, chans // 2, pair, 0, unroll=4)
    copies[2].wait()
    for col in range(2):
        q = jnp.concatenate([q_ref[col, k].astype(BF16) for k in range(2 * blocks)], axis=1)
        y = jnp.dot(q, inv_ref[...], preferred_element_type=F32)
        y_ref[:, :, col * rows : (col + 1) * rows] = y.astype(BF16).reshape(chips, chans, rows)


def long_conv(x, fwd, inv, tw, a, ai, m, f):
    chips, chans, both = x.shape
    vmem = pl.BlockSpec(memory_space=pltpu.VMEM)
    hbm = pl.BlockSpec(memory_space=pl.ANY)
    return pl.pallas_call(
        conv_kernel,
        in_specs=[vmem, hbm, hbm, hbm, vmem, vmem, vmem, vmem],
        out_specs=vmem,
        out_shape=jax.ShapeDtypeStruct(x.shape, BF16),
        scratch_shapes=[
            pltpu.VMEM(fwd.shape, BF16),
            pltpu.VMEM(inv.shape, BF16),
            pltpu.VMEM(tw.shape, F32),
            pltpu.VMEM((2, both // 128, chips * chans, 128), F32),
            pltpu.VMEM((2, both // 128, chips * chans, 128), F32),
            pltpu.SemaphoreType.DMA((3,)),
        ],
        compiler_params=pltpu.CompilerParams(vmem_limit_bytes=VMEM),
        cost_estimate=pl.CostEstimate(flops=8 * 10**9, bytes_accessed=8 * 2**20, transcendentals=0),
        name="long_conv",
    )(x, fwd, inv, tw, a, ai, m, f)


def cos_sin(product, modulus):
    phase = (product % modulus).astype(F32) * (2.0 * math.pi / modulus)
    return jnp.cos(phase), jnp.sin(phase)


def twice(t):
    zero = jnp.zeros_like(t)
    return jnp.block([[t, zero], [zero, t]])


def column_tables(core, rows, cols, padded):
    i = lax.iota(jnp.int32, cols)
    b = 2 * (i % CHIPS) + ((i // CHIPS) ^ core)
    k1 = lax.iota(jnp.int32, rows)
    tw = jnp.concatenate(cos_sin(b[:, None] * k1[None, :], padded), axis=1)
    k2 = lax.iota(jnp.int32, cols)
    c, s = cos_sin(k2[:, None] * b[None, :], cols)
    a = jnp.block([[c, s], [-s, c]])
    twist = jnp.stack(cos_sin(jnp.mod((b[:, None] - b[None, :]) * rows, padded), padded))

    return tw, twice(a.astype(BF16)), twice(a.T.astype(BF16)), jnp.stack([c, s]), twist


def gather_line(block, axis):
    d1 = send(block, **{axis: -1})
    d3 = send(block, **{axis: 1})
    d2 = send(block, **{axis: 2})
    return jnp.concatenate([block, d1, d2, d3], axis=0)


def per_device(tokens, in_weight, filter_spectrum, skip_bias, out_weight):
    rows, _, width = tokens.shape
    cols = SEQ
    padded = 2 * rows * cols
    s = lax.axis_index("seq")
    h = lax.axis_index("ch")
    z, y, x, core = coords(s)
    chan = in_weight.shape[2] // 2
    depth = in_weight.shape[0]

    mine = tokens.reshape(rows, width)
    filt = jnp.transpose(filter_spectrum, (3, 1, 0, 2)).reshape(4, -1, 2 * cols)
    filt = jnp.concatenate(split_table(filt), axis=1)

    def half_for(c):
        w = lax.dynamic_slice_in_dim(in_weight, c * chan, chan, 2)
        f = lax.dynamic_slice_in_dim(filt, 2 * c, 2, 0)
        return jnp.transpose(w, (1, 0, 2)).reshape(3 * depth, chan), jnp.concatenate([f[0], f[1]], axis=1)

    keep, keep_f = half_for(core)
    give, give_f = half_for(1 - core)
    far_near = send(give[depth:], dz=1, dc=1)
    far = send(keep[depth:], dz=1)
    near = send(give, dc=1)
    near_f = send(give_f, dc=1)
    other = send(mine, dc=1)

    def ordered(own, partner, axis=0):
        return jnp.concatenate(
            [jnp.where(core == 0, own, partner), jnp.where(core == 0, partner, own)], axis=axis
        )

    def block_of(n):
        own, away = slice(n * depth, (n + 1) * depth), slice((n - 1) * depth, n * depth)
        return jnp.concatenate([ordered(keep[own], near[own]), ordered(far[away], far_near[away])], axis=0)

    key_block, value_block = block_of(1), block_of(2)
    f_lanes = 2 * cols
    gate_block = jnp.concatenate(
        [
            ordered(keep[:depth], near[:depth]),
            jnp.concatenate(
                [
                    ordered(keep_f[:, :f_lanes], near_f[:, :f_lanes], 1),
                    ordered(keep_f[:, f_lanes:], near_f[:, f_lanes:], 1),
                ],
                axis=1,
            ),
        ],
        axis=0,
    )
    gathered = lax.all_gather(gate_block, "seq", axis=0, axis_index_groups=SAME_CORE)
    key_block, value_block, other = lax.optimization_barrier((key_block, value_block, other))
    half_ow = out_weight.shape[0] // 2
    ow_part = lax.dynamic_slice_in_dim(out_weight, core * half_ow, half_ow, 0)
    key_line, value_line, ow_part = lax.optimization_barrier(
        (gather_line(key_block, "dx"), gather_line(value_block, "dy"), ow_part)
    )

    order = np.arange(32)
    p_, q_, dz = order // 8, (order // 2) % 4, order % 2
    key_order = ((z ^ dz) * 4 + (y + p_) % 4) * 4 + (x + q_) % 4
    value_order = ((z ^ dz) * 4 + (y + q_) % 4) * 4 + (x + p_) % 4
    order = jnp.stack([key_order, value_order])
    first = sum_part(first_kernel, "first_part", order, mine, other, [], [key_line, value_line], True)
    near_lines = [send(key_line, dy=-1), send(key_line, dy=1), send(value_line, dx=-1), send(value_line, dx=1)]
    tables = column_tables(core, rows, cols, padded)
    near_lines, first, tables = lax.optimization_barrier((near_lines, first, tables))
    halves = cut_halves(near_lines)
    last_lines = [
        send(halves[0], dy=-1),
        send(halves[1], dy=1),
        send(halves[2], dx=-1),
        send(halves[3], dx=1),
    ]
    totals = sum_part(second_kernel, "second_part", order, mine, other, first[:2], near_lines, False)

    perm = []
    for t in range(SEQ):
        tz, ty, tx, tc = coords(t)
        for th in range(2):
            perm.append((t * 2 + th, index_of(tz ^ tc, ty, tx, tc) * 2 + 1 - th))
    ow_same = lax.ppermute(ow_part, ("seq", "ch"), perm)

    source = last_part(totals, first[2:], last_lines)
    packed = source.reshape(CHIPS, chan // CHIPS, 2 * rows)
    mine_ch = lax.all_to_all(packed, "seq", 0, 0, axis_index_groups=SAME_CORE)

    tw, a, ai, cs, twist = tables
    f, m = filter_part(z, gathered, cs, twist)
    forward, inverse = row_tables(rows, padded)
    fwd = jnp.asarray(forward.astype(np.float32).astype(ml_dtypes.bfloat16))
    inv = jnp.asarray(inverse.astype(np.float32).astype(ml_dtypes.bfloat16))
    mine_ch, ow_same, f, m = lax.optimization_barrier((mine_ch, ow_same, f, m))
    conv = long_conv(mine_ch, fwd, inv, tw, a, ai, m, f)
    conv = lax.all_to_all(conv, "seq", 0, 0, axis_index_groups=SAME_CORE)
    conv = conv.reshape(chan, 2 * rows).astype(F32)

    gate = gate_part(mine, other, gathered).astype(F32)
    skip = lax.dynamic_slice_in_dim(skip_bias, core * chan, chan, 0)[:, None]
    gated = (gate * (conv + skip * source.astype(F32))).astype(BF16)

    kept = rows // 2
    own_here = lax.dynamic_slice(gated, (0, h * kept), (chan, kept))
    own_there = lax.dynamic_slice(gated, (0, (1 - h) * kept), (chan, kept))
    oth_here = lax.dynamic_slice(gated, (0, rows + h * kept), (chan, kept))
    oth_there = lax.dynamic_slice(gated, (0, rows + (1 - h) * kept), (chan, kept))
    swap_ch = [(0, 1), (1, 0)]
    from_h = lax.ppermute(own_there, "ch", swap_ch)
    perm2 = []
    for t in range(SEQ):
        for th in range(2):
            perm2.append((t * 2 + th, (t ^ 1) * 2 + 1 - th))
    from_hc = lax.ppermute(oth_there, ("seq", "ch"), perm2)
    from_c = send(oth_here, dc=1)
    from_c, ow_same = lax.optimization_barrier((from_c, ow_same))
    ow_cross = send(ow_same, dc=1)
    here = ordered(own_here, from_c)

    mixed = mix_part(None, [here], [out_weight])
    mixed = mix_part(mixed, [from_h, from_hc], [ow_same, ow_cross])
    return mixed.reshape(kept, 1, width)


def solution(mesh):
    in_specs = (
        P(None, "seq", None),
        P("seq", None, "ch"),
        P(None, "seq", None, "ch"),
        P("ch"),
        P("ch", None),
    )
    return jax.shard_map(
        per_device, mesh=mesh, in_specs=in_specs, out_specs=P("ch", "seq", None), check_vma=False
    )
```

```python
import functools
import math

import jax
import jax.numpy as jnp
import ml_dtypes
import numpy as np
from jax import lax
from jax.experimental import pallas as pl
from jax.experimental.pallas import tpu as pltpu
from jax.sharding import PartitionSpec as P

BF16 = jnp.bfloat16
F32 = jnp.float32
HIGH = lax.Precision.HIGHEST
SEQ = 64
VMEM = 60 * 2**20
CHIPS = 32
SAME_CORE = [[2 * p + j for p in range(CHIPS)] for j in range(2)]


def coords(s):
    return s // 32, (s // 8) % 4, (s // 2) % 4, s % 2


def index_of(z, y, x, c):
    return ((z * 4 + y) * 4 + x) * 2 + c


def send(value, dz=0, dy=0, dx=0, dc=0):
    perm = []
    for s in range(SEQ):
        z, y, x, c = coords(s)
        perm.append((s, index_of((z + dz) % 2, (y + dy) % 4, (x + dx) % 4, c ^ dc)))
    return lax.ppermute(value, "seq", perm)


def split_table(table):
    upper = table.astype(BF16)
    lower = (table - upper.astype(F32)).astype(BF16)
    return upper, lower


def row_tables(rows, padded):
    points = 2 * rows
    a = np.arange(rows)
    k = np.arange(rows)
    phase = 2.0 * np.pi * ((a[:, None] * k[None, :]) % points) / points
    re, im = np.cos(phase), -np.sin(phase)
    im[:, 0] = np.where(a % 2 == 0, 1.0, -1.0)
    forward = np.concatenate([re, im], axis=1)
    scale = np.full((rows,), 2.0)
    scale[0] = 1.0
    inverse = np.concatenate([re * scale, im * scale], axis=1).T / padded
    return forward, inverse


def picked(order_ref, row, group, tok_ref):
    blocks = [
        tok_ref[:, pl.ds(pl.multiple_of(order_ref[row, group * 8 + i] * 128, 128), 128)]
        for i in range(8)
    ]
    return jnp.concatenate(blocks, axis=1)


def by_column(run, mine_ref, other_ref):
    step = pl.program_id(0)

    @pl.when(step < 2)
    def _():
        run(mine_ref)

    @pl.when(step >= 2)
    def _():
        run(other_ref)


def first_kernel(order_ref, mine_ref, other_ref, key_line, value_line, *outs):
    key_ref, value_ref, key_tok_ref, value_tok_ref = outs

    def run(tok_ref):
        for row, line, total_ref, last_ref in (
            (0, key_line, key_ref, key_tok_ref),
            (1, value_line, value_ref, value_tok_ref),
        ):
            total_ref[...] = jnp.dot(
                picked(order_ref, row, 0, tok_ref), line[...], preferred_element_type=F32
            )
            last_ref[...] = picked(order_ref, row, 2, tok_ref)

    by_column(run, mine_ref, other_ref)


def second_kernel(order_ref, mine_ref, other_ref, key_in, value_in, k1, k3, v1, v3, key_ref, value_ref):
    def run(tok_ref):
        for row, before, e1, e3, total_ref in (
            (0, key_in, k1, k3, key_ref),
            (1, value_in, v1, v3, value_ref),
        ):
            total = before[...]
            total += jnp.dot(picked(order_ref, row, 1, tok_ref), e1[...], preferred_element_type=F32)
            total += jnp.dot(picked(order_ref, row, 3, tok_ref), e3[...], preferred_element_type=F32)
            total_ref[...] = total

    by_column(run, mine_ref, other_ref)


def sum_part(kernel, name, order, mine, other, totals, weights, last):
    rows, width = mine.shape
    chan = weights[0].shape[1]
    tile = rows // 2
    quarter = width // 4
    by_row = [pl.BlockSpec((tile, chan), lambda i, o: (i, 0))] * 2
    tokens_out = [pl.BlockSpec((tile, quarter), lambda i, o: (i, 0))] * 2
    shapes = [jax.ShapeDtypeStruct((2 * rows, chan), F32)] * 2
    token_shapes = [jax.ShapeDtypeStruct((2 * rows, quarter), BF16)] * 2
    return pl.pallas_call(
        kernel,
        grid_spec=pltpu.PrefetchScalarGridSpec(
            num_scalar_prefetch=1,
            grid=(4,),
            in_specs=[
                pl.BlockSpec((tile, width), lambda i, o: (jnp.minimum(i, 1), 0)),
                pl.BlockSpec((tile, width), lambda i, o: (jnp.maximum(i - 2, 0), 0)),
            ]
            + by_row[: len(totals)]
            + [pl.BlockSpec((quarter, chan), lambda i, o: (0, 0))] * len(weights),
            out_specs=by_row + (tokens_out if last else []),
        ),
        out_shape=shapes + (token_shapes if last else []),
        compiler_params=pltpu.CompilerParams(vmem_limit_bytes=VMEM),
        cost_estimate=pl.CostEstimate(
            flops=2 * 2 * rows * quarter * chan * len(weights), bytes_accessed=18 * 2**20, transcendentals=0
        ),
        name=name,
    )(order, mine, other, *totals, *weights)


def cut_kernel(*refs):
    for src, dst in zip(refs[:4], refs[4:], strict=True):
        dst[...] = src[...]


def cut_halves(lines):
    rows, width = lines[0].shape
    tile = rows // 4
    upper = pl.BlockSpec((tile, width), lambda i: (i, 0))
    lower = pl.BlockSpec((tile, width), lambda i: (i + 2, 0))
    return pl.pallas_call(
        cut_kernel,
        grid=(2,),
        in_specs=[upper, lower, upper, lower],
        out_specs=[upper] * 4,
        out_shape=[jax.ShapeDtypeStruct((rows // 2, width), BF16)] * 4,
        compiler_params=pltpu.CompilerParams(vmem_limit_bytes=VMEM),
        cost_estimate=pl.CostEstimate(flops=0, bytes_accessed=4 * rows * width * 2, transcendentals=0),
        name="cut_halves",
    )(*lines)


def last_kernel(key_ref, value_ref, key_tok_ref, value_tok_ref, ka, kb, va, vb, send_ref):
    half = ka.shape[0]

    def finish(total_ref, tok_ref, wa, wb):
        total = total_ref[...]
        total += jnp.dot(tok_ref[:, :half], wa[...], preferred_element_type=F32)
        total += jnp.dot(tok_ref[:, half:], wb[...], preferred_element_type=F32)
        return total.astype(BF16).astype(F32)

    source = finish(key_ref, key_tok_ref, ka, kb) * finish(value_ref, value_tok_ref, va, vb)
    send_ref[...] = source.T.astype(BF16)


def last_part(totals, tokens, weights):
    total, chan = totals[0].shape
    quarter = tokens[0].shape[1]
    tile = total // 4
    return pl.pallas_call(
        last_kernel,
        grid=(4,),
        in_specs=[pl.BlockSpec((tile, chan), lambda i: (i, 0))] * 2
        + [pl.BlockSpec((tile, quarter), lambda i: (i, 0))] * 2
        + [pl.BlockSpec((quarter // 2, chan), lambda i: (0, 0))] * 4,
        out_specs=pl.BlockSpec((chan, tile), lambda i: (0, i)),
        out_shape=jax.ShapeDtypeStruct((chan, total), BF16),
        compiler_params=pltpu.CompilerParams(vmem_limit_bytes=VMEM),
        cost_estimate=pl.CostEstimate(
            flops=2 * 2 * total * quarter * chan, bytes_accessed=13 * 2**20, transcendentals=0
        ),
        name="last_part",
    )(*totals, *tokens, *weights)


def gate_kernel(mine_ref, other_ref, weight_ref, out_ref):
    chips, deep, chan = weight_ref.shape

    def run(tok_ref):
        weight = weight_ref[...].reshape(chips * deep, chan)
        gate = jnp.dot(tok_ref[...], weight, preferred_element_type=F32)
        out_ref[...] = gate.T.astype(BF16)

    by_column(run, mine_ref, other_ref)


def gate_part(mine, other, gathered):
    rows, width = mine.shape
    chips, _, chan = gathered.shape
    tile = rows // 2
    return pl.pallas_call(
        gate_kernel,
        grid=(4,),
        in_specs=[
            pl.BlockSpec((tile, width), lambda i: (jnp.minimum(i, 1), 0)),
            pl.BlockSpec((tile, width), lambda i: (jnp.maximum(i - 2, 0), 0)),
            pl.BlockSpec((chips, width // chips, chan), lambda i: (0, 0, 0)),
        ],
        out_specs=pl.BlockSpec((chan, tile), lambda i: (0, i)),
        out_shape=jax.ShapeDtypeStruct((chan, 2 * rows), BF16),
        compiler_params=pltpu.CompilerParams(vmem_limit_bytes=VMEM),
        cost_estimate=pl.CostEstimate(
            flops=2 * 2 * rows * width * chan, bytes_accessed=13 * 2**20, transcendentals=0
        ),
        name="gate_part",
    )(mine, other, gathered)


def turn(ref):
    return ref[...].astype(F32).T.astype(BF16)


def mix_kernel(here, w_here, out_ref, lhs_ref):
    @pl.when(pl.program_id(0) == 0)
    def _():
        lhs_ref[...] = turn(here)

    out_ref[...] = jnp.dot(lhs_ref[...], w_here[...], preferred_element_type=F32)


def mix_more_kernel(total_ref, near_h, far_h, w_near, w_far, out_ref, lhs_ref):
    m = near_h.shape[0]

    @pl.when(pl.program_id(0) == 0)
    def _():
        lhs_ref[:, :m] = turn(near_h)
        lhs_ref[:, m:] = turn(far_h)

    total = total_ref[...]
    total += jnp.dot(lhs_ref[:, :m], w_near[...], preferred_element_type=F32)
    total += jnp.dot(lhs_ref[:, m:], w_far[...], preferred_element_type=F32)
    out_ref[...] = total.astype(BF16)


def mix_part(total, parts, weights):
    rows = parts[0].shape[1]
    width = weights[0].shape[1]
    tile = width // 2
    depth = sum(p.shape[0] for p in parts)
    totals = [] if total is None else [total]

    def whole(g):
        return pl.BlockSpec(g.shape, lambda i: (0, 0))

    def tiled(w):
        return pl.BlockSpec((w.shape[0], tile), lambda i: (0, i))

    return pl.pallas_call(
        mix_kernel if total is None else mix_more_kernel,
        grid=(2,),
        in_specs=[tiled(t) for t in totals] + [whole(p) for p in parts] + [tiled(w) for w in weights],
        out_specs=pl.BlockSpec((rows, tile), lambda i: (0, i)),
        out_shape=jax.ShapeDtypeStruct((rows, width), F32 if total is None else BF16),
        scratch_shapes=[pltpu.VMEM((rows, depth), BF16)],
        compiler_params=pltpu.CompilerParams(vmem_limit_bytes=VMEM),
        cost_estimate=pl.CostEstimate(
            flops=2 * rows * depth * width, bytes_accessed=12 * 2**20, transcendentals=0
        ),
        name="mix_part" if total is None else "mix_more",
    )(*totals, *parts, *weights)


def filter_kernel(z_ref, x_ref, cs_ref, twist_ref, f_ref, m_ref):
    chips, _, lanes = x_ref.shape
    lanes = lanes // 2
    points = 2 * chips * 16
    rows, cols = points // 2, lanes // 2

    def part(n):
        rows_of = slice(16 * n, 16 * (n + 1))
        cores = [x_ref[:, rows_of, c * lanes : (c + 1) * lanes] for c in range(2)]
        return jnp.stack(cores, axis=1).reshape(points, lanes)

    upper, lower = part(0), part(1)
    whole = (upper.astype(F32) + lower.astype(F32)).T
    i = lax.broadcasted_iota(jnp.int32, (rows, rows), 0)
    j = lax.broadcasted_iota(jnp.int32, (rows, rows), 1)
    mirror = (i + j == rows).astype(F32).astype(BF16)
    i = lax.broadcasted_iota(jnp.int32, (lanes, lanes), 0)
    j = lax.broadcasted_iota(jnp.int32, (lanes, lanes), 1)
    flip = ((i // cols == j // cols) & (i % cols + j % cols == cols - 1)).astype(F32).astype(BF16)

    def mirrored(part):
        turned = jnp.dot(flip, part[:, rows:], preferred_element_type=F32).astype(BF16)
        return jnp.dot(turned, mirror, preferred_element_type=F32)

    other = mirrored(upper.astype(F32).T.astype(BF16)) + mirrored(lower.astype(F32).T.astype(BF16))
    f_ref[:, :rows] = 0.5 * (whole[:cols, :rows] + other[:cols])
    f_ref[:, rows:] = 0.5 * (whole[cols:, :rows] - other[cols:])
    c, s = cs_ref[0], cs_ref[1]

    def contract(left, right):
        return lax.dot_general(
            left, right, (((0,), (0,)), ((), ())), precision=HIGH, preferred_element_type=F32
        )

    m_ref[...] = jnp.zeros_like(m_ref)
    for n, k in enumerate((0, rows)):
        e_re, e_im = whole[:cols, k : k + 1], whole[cols:, k : k + 1]
        u = c * e_re - s * e_im
        v = s * e_re + c * e_im
        g = contract(u, c) + contract(v, s)
        if n:
            g = g * twist_ref[0] - (contract(v, c) - contract(u, s)) * twist_ref[1]
        for start in (n * cols, lanes + n * cols):
            spot = slice(start, start + cols)
            m_ref[spot, spot] = g.astype(BF16)


def filter_part(z, gathered, cs, twist):
    chips = gathered.shape[0]
    cols = cs.shape[1]
    rows = chips * 16
    lanes = 2 * cols
    return pl.pallas_call(
        filter_kernel,
        grid_spec=pltpu.PrefetchScalarGridSpec(
            num_scalar_prefetch=1,
            grid=(1,),
            in_specs=[
                pl.BlockSpec((chips, 32, 2 * lanes), lambda i, z: (0, 4, z[0])),
                pl.BlockSpec(cs.shape, lambda i, z: (0, 0, 0)),
                pl.BlockSpec(twist.shape, lambda i, z: (0, 0, 0)),
            ],
            out_specs=[
                pl.BlockSpec((cols, 2 * rows), lambda i, z: (0, 0)),
                pl.BlockSpec((2 * lanes, 2 * lanes), lambda i, z: (0, 0)),
            ],
        ),
        out_shape=[
            jax.ShapeDtypeStruct((cols, 2 * rows), F32),
            jax.ShapeDtypeStruct((2 * lanes, 2 * lanes), BF16),
        ],
        compiler_params=pltpu.CompilerParams(vmem_limit_bytes=VMEM),
        cost_estimate=pl.CostEstimate(flops=10**9, bytes_accessed=2**20, transcendentals=0),
        name="filter_part",
    )(z.reshape(1), gathered, cs, twist)


def conv_kernel(
    x_ref, fwd_hbm, inv_hbm, tw_hbm, a_ref, ai_ref, m_ref, f_ref, y_ref, fwd_ref, inv_ref, tw_ref, r_ref, q_ref, sems
):
    copies = [
        pltpu.make_async_copy(src, dst, sems.at[i])
        for i, (src, dst) in enumerate(((fwd_hbm, fwd_ref), (tw_hbm, tw_ref), (inv_hbm, inv_ref)))
    ]
    for copy in copies:
        copy.start()
    chips, chans, both = x_ref.shape
    rows = both // 2
    blocks = rows // 128
    half = 2 * chips
    copies[0].wait()
    for col in range(2):
        x = x_ref[:, :, col * rows : (col + 1) * rows].reshape(chips * chans, rows)
        r = jnp.dot(x, fwd_ref[...], preferred_element_type=F32)
        r = r.reshape(chips, chans, 2 * rows)
        if col == 0:
            copies[1].wait()
        tw = tw_ref[col * chips : (col + 1) * chips, :]
        cos = tw[:, None, :rows]
        sin = tw[:, None, rows:]
        re, im = r[:, :, :rows], r[:, :, rows:]
        turned_re = (re * cos + im * sin).reshape(chips * chans, rows)
        turned_im = (im * cos - re * sin).reshape(chips * chans, rows)
        for k in range(blocks):
            r_ref[col, k] = turned_re[:, k * 128 : (k + 1) * 128]
            r_ref[col, blocks + k] = turned_im[:, k * 128 : (k + 1) * 128]
    lane = lax.broadcasted_iota(jnp.int32, (4 * half, 128), 1)

    def pair(n, carry):
        picks = [pl.ds(2 * n + i, chips, stride=chans) for i in range(2)]
        parts = [
            jnp.concatenate([r_ref[col, part * blocks + k, pick, :] for k in range(blocks)], axis=1)
            for pick in picks
            for part in range(2)
            for col in range(2)
        ]
        turned = jnp.concatenate(parts, axis=0).astype(BF16)
        s = jnp.dot(a_ref[...], turned, preferred_element_type=F32)
        f_re, f_im = f_ref[:, :rows], f_ref[:, rows:]
        filtered = []
        for i in range(2):
            s_re = s[2 * i * half : (2 * i + 1) * half]
            s_im = s[(2 * i + 1) * half : (2 * i + 2) * half]
            filtered += [s_re * f_re - s_im * f_im, s_re * f_im + s_im * f_re]
        filtered = jnp.concatenate(filtered, axis=0).astype(BF16)
        back = jnp.dot(ai_ref[...], filtered, preferred_element_type=F32)
        edge = jnp.dot(m_ref[...], turned[:, :128], preferred_element_type=F32)
        head = jnp.where(lane == 0, edge, back[:, :128])
        back = jnp.concatenate([head, back[:, 128:]], axis=1)
        cos, sin = tw_ref[:, :rows], tw_ref[:, rows:]
        for i, pick in enumerate(picks):
            b_re = back[2 * i * half : (2 * i + 1) * half]
            b_im = back[(2 * i + 1) * half : (2 * i + 2) * half]
            out_re = b_re * cos - b_im * sin
            out_im = b_im * cos + b_re * sin
            for col in range(2):
                part = slice(col * chips, (col + 1) * chips)
                for k in range(blocks):
                    q_ref[col, k, pick, :] = out_re[part, k * 128 : (k + 1) * 128]
                    q_ref[col, blocks + k, pick, :] = out_im[part, k * 128 : (k + 1) * 128]
        return carry

    lax.fori_loop(0, chans // 2, pair, 0, unroll=4)
    copies[2].wait()
    for col in range(2):
        q = jnp.concatenate([q_ref[col, k].astype(BF16) for k in range(2 * blocks)], axis=1)
        y = jnp.dot(q, inv_ref[...], preferred_element_type=F32)
        y_ref[:, :, col * rows : (col + 1) * rows] = y.astype(BF16).reshape(chips, chans, rows)


def long_conv(x, fwd, inv, tw, a, ai, m, f):
    chips, chans, both = x.shape
    vmem = pl.BlockSpec(memory_space=pltpu.VMEM)
    hbm = pl.BlockSpec(memory_space=pl.ANY)
    return pl.pallas_call(
        conv_kernel,
        in_specs=[vmem, hbm, hbm, hbm, vmem, vmem, vmem, vmem],
        out_specs=vmem,
        out_shape=jax.ShapeDtypeStruct(x.shape, BF16),
        scratch_shapes=[
            pltpu.VMEM(fwd.shape, BF16),
            pltpu.VMEM(inv.shape, BF16),
            pltpu.VMEM(tw.shape, F32),
            pltpu.VMEM((2, both // 128, chips * chans, 128), F32),
            pltpu.VMEM((2, both // 128, chips * chans, 128), F32),
            pltpu.SemaphoreType.DMA((3,)),
        ],
        compiler_params=pltpu.CompilerParams(vmem_limit_bytes=VMEM),
        cost_estimate=pl.CostEstimate(flops=8 * 10**9, bytes_accessed=8 * 2**20, transcendentals=0),
        name="long_conv",
    )(x, fwd, inv, tw, a, ai, m, f)


def cos_sin(product, modulus):
    phase = (product % modulus).astype(F32) * (2.0 * math.pi / modulus)
    return jnp.cos(phase), jnp.sin(phase)


def twice(t):
    zero = jnp.zeros_like(t)
    return jnp.block([[t, zero], [zero, t]])


def column_tables(core, rows, cols, padded):
    i = lax.iota(jnp.int32, cols)
    b = 2 * (i % CHIPS) + ((i // CHIPS) ^ core)
    k1 = lax.iota(jnp.int32, rows)
    tw = jnp.concatenate(cos_sin(b[:, None] * k1[None, :], padded), axis=1)
    k2 = lax.iota(jnp.int32, cols)
    c, s = cos_sin(k2[:, None] * b[None, :], cols)
    a = jnp.block([[c, s], [-s, c]])
    twist = jnp.stack(cos_sin(jnp.mod((b[:, None] - b[None, :]) * rows, padded), padded))

    return tw, twice(a.astype(BF16)), twice(a.T.astype(BF16)), jnp.stack([c, s]), twist


def gather_line(block, axis):
    d1 = send(block, **{axis: -1})
    d3 = send(block, **{axis: 1})
    d2 = send(block, **{axis: 2})
    return jnp.concatenate([block, d1, d2, d3], axis=0)


def per_device(tokens, in_weight, filter_spectrum, skip_bias, out_weight):
    rows, _, width = tokens.shape
    cols = SEQ
    padded = 2 * rows * cols
    s = lax.axis_index("seq")
    h = lax.axis_index("ch")
    z, y, x, core = coords(s)
    chan = in_weight.shape[2] // 2
    depth = in_weight.shape[0]

    mine = tokens.reshape(rows, width)
    filt = jnp.transpose(filter_spectrum, (3, 1, 0, 2)).reshape(4, -1, 2 * cols)
    filt = jnp.concatenate(split_table(filt), axis=1)

    def half_for(c):
        w = lax.dynamic_slice_in_dim(in_weight, c * chan, chan, 2)
        f = lax.dynamic_slice_in_dim(filt, 2 * c, 2, 0)
        return jnp.transpose(w, (1, 0, 2)).reshape(3 * depth, chan), jnp.concatenate([f[0], f[1]], axis=1)

    keep, keep_f = half_for(core)
    give, give_f = half_for(1 - core)
    far_near = send(give[depth:], dz=1, dc=1)
    far = send(keep[depth:], dz=1)
    near = send(give, dc=1)
    near_f = send(give_f, dc=1)
    other = send(mine, dc=1)

    def ordered(own, partner, axis=0):
        return jnp.concatenate(
            [jnp.where(core == 0, own, partner), jnp.where(core == 0, partner, own)], axis=axis
        )

    def block_of(n):
        own, away = slice(n * depth, (n + 1) * depth), slice((n - 1) * depth, n * depth)
        return jnp.concatenate([ordered(keep[own], near[own]), ordered(far[away], far_near[away])], axis=0)

    key_block, value_block = block_of(1), block_of(2)
    f_lanes = 2 * cols
    gate_block = jnp.concatenate(
        [
            ordered(keep[:depth], near[:depth]),
            jnp.concatenate(
                [
                    ordered(keep_f[:, :f_lanes], near_f[:, :f_lanes], 1),
                    ordered(keep_f[:, f_lanes:], near_f[:, f_lanes:], 1),
                ],
                axis=1,
            ),
        ],
        axis=0,
    )
    gathered = lax.all_gather(gate_block, "seq", axis=0, axis_index_groups=SAME_CORE)
    key_block, value_block, other = lax.optimization_barrier((key_block, value_block, other))
    half_ow = out_weight.shape[0] // 2
    ow_part = lax.dynamic_slice_in_dim(out_weight, core * half_ow, half_ow, 0)
    key_line, value_line, ow_part = lax.optimization_barrier(
        (gather_line(key_block, "dx"), gather_line(value_block, "dy"), ow_part)
    )

    order = np.arange(32)
    p_, q_, dz = order // 8, (order // 2) % 4, order % 2
    key_order = ((z ^ dz) * 4 + (y + p_) % 4) * 4 + (x + q_) % 4
    value_order = ((z ^ dz) * 4 + (y + q_) % 4) * 4 + (x + p_) % 4
    order = jnp.stack([key_order, value_order])
    first = sum_part(first_kernel, "first_part", order, mine, other, [], [key_line, value_line], True)
    near_lines = [send(key_line, dy=-1), send(key_line, dy=1), send(value_line, dx=-1), send(value_line, dx=1)]
    tables = column_tables(core, rows, cols, padded)
    near_lines, first, tables = lax.optimization_barrier((near_lines, first, tables))
    halves = cut_halves(near_lines)
    last_lines = [
        send(halves[0], dy=-1),
        send(halves[1], dy=1),
        send(halves[2], dx=-1),
        send(halves[3], dx=1),
    ]
    totals = sum_part(second_kernel, "second_part", order, mine, other, first[:2], near_lines, False)

    perm = []
    for t in range(SEQ):
        tz, ty, tx, tc = coords(t)
        for th in range(2):
            perm.append((t * 2 + th, index_of(tz ^ tc, ty, tx, tc) * 2 + 1 - th))
    ow_same = lax.ppermute(ow_part, ("seq", "ch"), perm)

    source = last_part(totals, first[2:], last_lines)
    packed = source.reshape(CHIPS, chan // CHIPS, 2 * rows)
    mine_ch = lax.all_to_all(packed, "seq", 0, 0, axis_index_groups=SAME_CORE)

    tw, a, ai, cs, twist = tables
    f, m = filter_part(z, gathered, cs, twist)
    forward, inverse = row_tables(rows, padded)
    fwd = jnp.asarray(forward.astype(np.float32).astype(ml_dtypes.bfloat16))
    inv = jnp.asarray(inverse.astype(np.float32).astype(ml_dtypes.bfloat16))
    mine_ch, ow_same, f, m = lax.optimization_barrier((mine_ch, ow_same, f, m))
    conv = long_conv(mine_ch, fwd, inv, tw, a, ai, m, f)
    conv = lax.all_to_all(conv, "seq", 0, 0, axis_index_groups=SAME_CORE)
    conv = conv.reshape(chan, 2 * rows).astype(F32)

    gate = gate_part(mine, other, gathered).astype(F32)
    skip = lax.dynamic_slice_in_dim(skip_bias, core * chan, chan, 0)[:, None]
    gated = (gate * (conv + skip * source.astype(F32))).astype(BF16)

    kept = rows // 2
    own_here = lax.dynamic_slice(gated, (0, h * kept), (chan, kept))
    own_there = lax.dynamic_slice(gated, (0, (1 - h) * kept), (chan, kept))
    oth_here = lax.dynamic_slice(gated, (0, rows + h * kept), (chan, kept))
    oth_there = lax.dynamic_slice(gated, (0, rows + (1 - h) * kept), (chan, kept))
    swap_ch = [(0, 1), (1, 0)]
    from_h = lax.ppermute(own_there, "ch", swap_ch)
    perm2 = []
    for t in range(SEQ):
        for th in range(2):
            perm2.append((t * 2 + th, (t ^ 1) * 2 + 1 - th))
    from_hc = lax.ppermute(oth_there, ("seq", "ch"), perm2)
    from_c = send(oth_here, dc=1)
    from_c, ow_same = lax.optimization_barrier((from_c, ow_same))
    ow_cross = send(ow_same, dc=1)
    here = ordered(own_here, from_c)

    mixed = mix_part(None, [here], [out_weight])
    mixed = mix_part(mixed, [from_h, from_hc], [ow_same, ow_cross])
    return mixed.reshape(kept, 1, width)


def solution(mesh):
    in_specs = (
        P(None, "seq", None),
        P("seq", None, "ch"),
        P(None, "seq", None, "ch"),
        P("ch"),
        P("ch", None),
    )
    return jax.shard_map(
        per_device, mesh=mesh, in_specs=in_specs, out_specs=P("ch", "seq", None), check_vma=False
    )
```
